32 devices in a mesh: clips: 2 (over y), tm: 4 (over z), rows: 4 (over x, core).
Axes of the slice: x: 2, y: 2, z: 4, core: 2. Of those that a mesh axis runs over, the one named last changes fastest.
Arguments:
- latents: bfloat16 [32, 8, 192, 128], P(('clips', 'tm'), 'rows'), parts along dimension 0, may hold values from -6 to 6
- conv_weight: bfloat16 [3, 27, 192, 192], replicated, may hold values from -0.078125 to 0.078125
- norm_gains: float32 [3, 192], replicated, may hold values from 0.5 to 1.5
- biases: float32 [3, 192], replicated, may hold values from -3 to 3
Outputs:
- decoded: bfloat16 [32, 8, 192, 128], P(('clips', 'tm'), 'rows'), parts along dimension 0
The draws below stay inside these ranges and needn't reach their ends.
There are 2 independent parts, one for each index of `clips`. The reference program is written for one: setup_inputs(seed, part) draws one part's arguments, and reference() takes and returns one part's arrays. A program takes and returns all parts, laid end to end along the dimension named above; an argument that names none is the same for every part. Nothing has to cross between parts.
All inputs are finite; a program needn't handle non-finite values.
Results may differ from the reference program's by a relative error of at most 0.011.
Values may be sent and summed in bfloat16 or wider, within the bound.
No kernel may reach another device: no remote copies, remote signals or barrier semaphores. Data moves between devices by JAX's collectives and lax.ppermute only.
A program may use at most 64 MiB of HBM per device.

```python
import jax
import jax.numpy as jnp
from jax import lax

C = 192
W = 128
LAYERS = 3
FRAMES = 16
HEIGHT = 8


def block_levels(stream_key, dims, pieces, low, top_value):
    def one(axis_at, parts):
        draws = jax.random.uniform(jax.random.fold_in(jax.random.fold_in(stream_key, 6), axis_at), (parts,), jnp.float32, low / len(pieces), top_value / len(pieces))
        return jnp.repeat(jnp.exp(draws), dims[axis_at] // parts).reshape((-1,) + (1,) * (len(dims) - axis_at - 1))

    gain = one(*pieces[0])
    for cut in pieces[1:]:
        gain = gain * one(*cut)
    return gain


def normal_values(stream_key, shape, spread, bound, split=(), held_as=jnp.bfloat16):
    entries = jax.random.normal(stream_key, shape, jnp.float32) * spread
    if len(split) > 0:
        entries = block_levels(stream_key, shape, split, -0.22, 0.18) * entries
    return jnp.clip(entries, min=-bound, max=bound).astype(held_as)


def setup_inputs(seed: int = 0, part: int = 0) -> dict:
    streams_of = jax.random.split(jax.random.key(seed), 5)
    own_keys = jax.random.split(jax.random.fold_in(streams_of[4], part), 5)
    return {
        "latents": normal_values(own_keys[0], (FRAMES, HEIGHT, C, W), 1.0, 6.0, ((0, 4), (1, 4))),
        "conv_weight": normal_values(streams_of[1], (LAYERS, 27, C, C), (27 * C) ** -0.5, 0.078125),
        "norm_gains": jnp.clip(jax.random.uniform(streams_of[2], (LAYERS, C), jnp.float32, 0.5, 1.5), 0.5, 1.5),
        "biases": normal_values(streams_of[3], (LAYERS, C), 0.5, 3.0, (), jnp.float32),
    }


EPSILON = 1e-06

def activate(values, gain_row):
    widened = values.astype(jnp.float32)
    squares = lax.optimization_barrier(jnp.mean(widened * widened, axis=2, keepdims=True))
    normed = widened * lax.rsqrt(squares + EPSILON) * gain_row[None, None, :, None]
    return jax.nn.silu(normed).astype(jnp.bfloat16)

def one_layer(values, gain_row, weight, bias_row):
    rounded = activate(values, gain_row)
    padded = jnp.pad(lax.optimization_barrier(rounded).astype(jnp.float32), ((2, 0), (1, 1), (0, 0), (1, 1)))
    frames = values.shape[0]
    height = values.shape[1]
    columns = values.shape[3]
    total = jnp.zeros(values.shape, jnp.float32)
    for time_tap in range(3):
        for row_tap in range(3):
            for column_tap in range(3):
                window = padded[time_tap:time_tap + frames, row_tap:row_tap + height, :, column_tap:column_tap + columns]
                kernel = weight[9 * time_tap + 3 * row_tap + column_tap].astype(jnp.float32)
                total = total + jnp.einsum('oc,fhcw->fhow', kernel, window, precision=lax.Precision.HIGHEST)
    summed = values.astype(jnp.float32) + total + bias_row[None, None, :, None]
    return summed.astype(jnp.bfloat16)

def reference(latents, conv_weight, norm_gains, biases):
    values = latents
    for layer_index in range(LAYERS):
        values = one_layer(values, norm_gains[layer_index], conv_weight[layer_index], biases[layer_index])
    return values
```

```python
import functools

import jax
import jax.numpy as jnp
from jax import lax
from jax.experimental import pallas as pl
from jax.experimental.pallas import tpu as pltpu
from jax.sharding import PartitionSpec as P

EPSILON = 1e-06
TIME_HALO = 2
VMEM = pl.BlockSpec(memory_space=pltpu.VMEM)
SMEM = pl.BlockSpec(memory_space=pltpu.SMEM)
LIMIT = 24 * 1024 * 1024


def column(row, width):
    return jnp.transpose(jnp.broadcast_to(row, (width, row.shape[1])))


def activated(values, gain):
    squares = jnp.mean(values * values, axis=0, keepdims=True)
    normed = values * lax.rsqrt(squares + EPSILON) * gain
    return (normed / (1.0 + jnp.exp(-normed))).astype(jnp.bfloat16)


def prepare_kernel(values_ref, gains_ref, act_ref, send_ref):
    frames, rows, _, width = values_ref.shape
    gain = column(gains_ref[0:1, :], width)
    for f in range(frames):
        for r in range(rows):
            act = activated(values_ref[f, r].astype(jnp.float32), gain)
            act_ref[f, r] = act
            if f >= frames - TIME_HALO:
                send_ref[f - (frames - TIME_HALO), r] = act


def prepare(latents, gains):
    frames, rows, channels, width = latents.shape
    return pl.pallas_call(
        prepare_kernel,
        out_shape=(
            jax.ShapeDtypeStruct(latents.shape, jnp.bfloat16),
            jax.ShapeDtypeStruct((TIME_HALO, rows, channels, width), jnp.bfloat16),
        ),
        in_specs=[VMEM] * 2,
        out_specs=(VMEM, VMEM),
        compiler_params=pltpu.CompilerParams(vmem_limit_bytes=LIMIT),
        cost_estimate=pl.CostEstimate(flops=8 * latents.size, bytes_accessed=4 * latents.size, transcendentals=latents.size),
        name="prepare",
    )(latents, gains)


def weights_kernel(w_ref, out_ref):
    _, outs, ins = w_ref.shape
    for tap in range(9):
        out_ref[:, tap * ins : (tap + 1) * ins] = w_ref[3 * tap : 3 * tap + 3].reshape(3 * outs, ins)


def weights(conv_weight):
    layers, taps, outs, ins = conv_weight.shape
    return pl.pallas_call(
        weights_kernel,
        grid=(layers,),
        out_shape=jax.ShapeDtypeStruct((layers, 3 * outs, 9 * ins), conv_weight.dtype),
        in_specs=[pl.BlockSpec((None, taps, outs, ins), lambda l: (l, 0, 0, 0))],
        out_specs=pl.BlockSpec((None, 3 * outs, 9 * ins), lambda l: (l, 0, 0)),
        compiler_params=pltpu.CompilerParams(vmem_limit_bytes=LIMIT),
        cost_estimate=pl.CostEstimate(flops=0, bytes_accessed=4 * conv_weight.size, transcendentals=0),
        name="weights",
    )(conv_weight)


def layer_kernel(
    layer, last, odd_ref, values_ref, act_ref, before_ref, pair_ref, other_ref, w_ref, biases_ref, gains_ref, *refs
):
    outs, x_ref = refs[:-1], refs[-1]
    frames, rows, channels, width = values_ref.shape
    odd = odd_ref[0] == 1
    for f in range(frames + TIME_HALO):
        pair, other = pair_ref[f], other_ref[f]
        middle = before_ref[f] if f < TIME_HALO else act_ref[f - TIME_HALO]
        lines = [jnp.where(odd, pair, other)] + [middle[r] for r in range(rows)] + [jnp.where(odd, other, pair)]
        for tap in range(3):
            for r in range(rows):
                x_ref[f, tap, :, r * width : (r + 1) * width] = lines[tap + r]
    bias = column(biases_ref[layer : layer + 1, :], width)
    lane = lax.broadcasted_iota(jnp.int32, (channels, width), 1)
    if not last:
        gain = column(gains_ref[layer + 1 : layer + 2, :], width)
    for f in range(frames):
        window = x_ref[f : f + 3].reshape(9 * channels, rows * width)
        sums = jnp.dot(w_ref[...], window, preferred_element_type=jnp.float32)
        for r in range(rows):
            part = sums[:, r * width : (r + 1) * width]
            from_left = jnp.where(lane == 0, 0.0, pltpu.roll(part[:channels], 1, 1))
            from_right = jnp.where(lane == width - 1, 0.0, pltpu.roll(part[2 * channels :], width - 1, 1))
            conv = from_left + part[channels : 2 * channels] + from_right
            total = (values_ref[f, r].astype(jnp.float32) + conv + bias).astype(jnp.bfloat16)
            outs[0][f, r] = total
            if not last:
                act = activated(total.astype(jnp.float32), gain)
                outs[1][f, r] = act
                if f >= frames - TIME_HALO:
                    outs[2][f - (frames - TIME_HALO), r] = act


def one_layer(layer, last, odd, values, act, before, pair, other, weight, biases, gains):
    frames, rows, channels, width = values.shape
    whole = jax.ShapeDtypeStruct(values.shape, jnp.bfloat16)
    send = jax.ShapeDtypeStruct((TIME_HALO, rows, channels, width), jnp.bfloat16)
    out_shape = (whole,) if last else (whole, whole, send)
    weight_spec = pl.BlockSpec((None,) + weight.shape[1:], lambda i: (layer, 0, 0))
    return pl.pallas_call(
        functools.partial(layer_kernel, layer, last),
        grid=(1,),
        out_shape=out_shape,
        in_specs=[SMEM] + [VMEM] * 5 + [weight_spec] + [VMEM] * 2,
        out_specs=(VMEM,) * len(out_shape),
        scratch_shapes=[pltpu.VMEM((frames + TIME_HALO, 3, channels, rows * width), jnp.bfloat16)],
        compiler_params=pltpu.CompilerParams(vmem_limit_bytes=LIMIT),
        cost_estimate=pl.CostEstimate(
            flops=54 * channels * values.size, bytes_accessed=2 * weight.size // 3, transcendentals=values.size
        ),
        name=f"conv_layer_{layer}",
    )(odd, values, act, before, pair, other, weight, biases, gains)


def swaps(count, first):
    pairs = [(i, i + 1) for i in range(first, count - 1, 2)]
    return pairs + [(b, a) for a, b in pairs]


def on_device(latents, conv_weight, norm_gains, biases):
    layers = conv_weight.shape[0]
    strips = lax.axis_size("rows")
    blocks = lax.axis_size("tm")
    odd = lax.rem(lax.axis_index("rows"), 2).astype(jnp.int32)
    values = latents
    act, send = prepare(latents, norm_gains)
    weight = weights(conv_weight)
    for layer in range(layers):
        before = lax.ppermute(send, "tm", [(i, i + 1) for i in range(blocks - 1)])
        top = jnp.concatenate([before[:, 0], act[:, 0]], axis=0)
        bottom = jnp.concatenate([before[:, -1], act[:, -1]], axis=0)
        pair = lax.ppermute(jnp.where(odd == 1, top, bottom), "rows", swaps(strips, 0))
        other = lax.ppermute(jnp.where(odd == 1, bottom, top), "rows", swaps(strips, 1))
        last = layer == layers - 1
        result = one_layer(layer, last, odd.reshape(1), values, act, before, pair, other, weight, biases, norm_gains)
        if not last:
            values, act, send = result
    return result[0]


def solution(mesh):
    in_specs = (P(("clips", "tm"), "rows", None, None), P(), P(), P())
    out_specs = P(("clips", "tm"), "rows", None, None)
    return jax.shard_map(on_device, mesh=mesh, in_specs=in_specs, out_specs=out_specs, check_vma=False)
```

```python
import functools

import jax
import jax.numpy as jnp
from jax import lax
from jax.experimental import pallas as pl
from jax.experimental.pallas import tpu as pltpu
from jax.sharding import PartitionSpec as P

EPSILON = 1e-06
TIME_HALO = 2
VMEM = pl.BlockSpec(memory_space=pltpu.VMEM)
SMEM = pl.BlockSpec(memory_space=pltpu.SMEM)
LIMIT = 24 * 1024 * 1024


def column(row, width):
    return jnp.transpose(jnp.broadcast_to(row, (width, row.shape[1])))


def activated(values, gain):
    squares = jnp.mean(values * values, axis=0, keepdims=True)
    normed = values * lax.rsqrt(squares + EPSILON) * gain
    return (normed / (1.0 + jnp.exp(-normed))).astype(jnp.bfloat16)


def prepare_kernel(values_ref, gains_ref, act_ref, send_ref):
    frames, rows, _, width = values_ref.shape
    gain = column(gains_ref[0:1, :], width)
    for f in range(frames):
        for r in range(rows):
            act = activated(values_ref[f, r].astype(jnp.float32), gain)
            act_ref[f, r] = act
            if f >= frames - TIME_HALO:
                send_ref[f - (frames - TIME_HALO), r] = act


def prepare(latents, gains):
    frames, rows, channels, width = latents.shape
    return pl.pallas_call(
        prepare_kernel,
        out_shape=(
            jax.ShapeDtypeStruct(latents.shape, jnp.bfloat16),
            jax.ShapeDtypeStruct((TIME_HALO, rows, channels, width), jnp.bfloat16),
        ),
        in_specs=[VMEM] * 2,
        out_specs=(VMEM, VMEM),
        compiler_params=pltpu.CompilerParams(vmem_limit_bytes=LIMIT),
        cost_estimate=pl.CostEstimate(flops=8 * latents.size, bytes_accessed=4 * latents.size, transcendentals=latents.size),
        name="prepare",
    )(latents, gains)


def weights_kernel(w_ref, out_ref):
    _, outs, ins = w_ref.shape
    for tap in range(9):
        out_ref[:, tap * ins : (tap + 1) * ins] = w_ref[3 * tap : 3 * tap + 3].reshape(3 * outs, ins)


def weights(conv_weight):
    layers, taps, outs, ins = conv_weight.shape
    return pl.pallas_call(
        weights_kernel,
        grid=(layers,),
        out_shape=jax.ShapeDtypeStruct((layers, 3 * outs, 9 * ins), conv_weight.dtype),
        in_specs=[pl.BlockSpec((None, taps, outs, ins), lambda l: (l, 0, 0, 0))],
        out_specs=pl.BlockSpec((None, 3 * outs, 9 * ins), lambda l: (l, 0, 0)),
        compiler_params=pltpu.CompilerParams(vmem_limit_bytes=LIMIT),
        cost_estimate=pl.CostEstimate(flops=0, bytes_accessed=4 * conv_weight.size, transcendentals=0),
        name="weights",
    )(conv_weight)


def layer_kernel(
    layer, last, odd_ref, values_ref, act_ref, before_ref, pair_ref, other_ref, w_ref, biases_ref, gains_ref, *refs
):
    outs, x_ref = refs[:-1], refs[-1]
    frames, rows, channels, width = values_ref.shape
    odd = odd_ref[0] == 1
    pair_zero = jnp.zeros((channels, width), jnp.bfloat16)
    for f in range(frames + TIME_HALO):
        pair = pair_ref[1 - odd_ref[0], f]
        other = jnp.where(odd_ref[1] == 1, pair_zero, other_ref[odd_ref[0], f])
        middle = before_ref[f] if f < TIME_HALO else act_ref[f - TIME_HALO]
        lines = [jnp.where(odd, pair, other)] + [middle[r] for r in range(rows)] + [jnp.where(odd, other, pair)]
        for tap in range(3):
            for r in range(rows):
                x_ref[f, tap, :, r * width : (r + 1) * width] = lines[tap + r]
    bias = column(biases_ref[layer : layer + 1, :], width)
    lane = lax.broadcasted_iota(jnp.int32, (channels, width), 1)
    if not last:
        gain = column(gains_ref[layer + 1 : layer + 2, :], width)
    for f in range(frames):
        window = x_ref[f : f + 3].reshape(9 * channels, rows * width)
        sums = jnp.dot(w_ref[...], window, preferred_element_type=jnp.float32)
        for r in range(rows):
            part = sums[:, r * width : (r + 1) * width]
            from_left = jnp.where(lane == 0, 0.0, pltpu.roll(part[:channels], 1, 1))
            from_right = jnp.where(lane == width - 1, 0.0, pltpu.roll(part[2 * channels :], width - 1, 1))
            conv = from_left + part[channels : 2 * channels] + from_right
            total = (values_ref[f, r].astype(jnp.float32) + conv + bias).astype(jnp.bfloat16)
            outs[0][f, r] = total
            if not last:
                act = activated(total.astype(jnp.float32), gain)
                outs[1][f, r] = act
                if f >= frames - TIME_HALO:
                    outs[2][f - (frames - TIME_HALO), r] = act


def one_layer(layer, last, odd, values, act, before, pair, other, weight, biases, gains):
    frames, rows, channels, width = values.shape
    whole = jax.ShapeDtypeStruct(values.shape, jnp.bfloat16)
    send = jax.ShapeDtypeStruct((TIME_HALO, rows, channels, width), jnp.bfloat16)
    out_shape = (whole,) if last else (whole, whole, send)
    weight_spec = pl.BlockSpec((None,) + weight.shape[1:], lambda i: (layer, 0, 0))
    return pl.pallas_call(
        functools.partial(layer_kernel, layer, last),
        grid=(1,),
        out_shape=out_shape,
        in_specs=[SMEM] + [VMEM] * 5 + [weight_spec] + [VMEM] * 2,
        out_specs=(VMEM,) * len(out_shape),
        scratch_shapes=[pltpu.VMEM((frames + TIME_HALO, 3, channels, rows * width), jnp.bfloat16)],
        compiler_params=pltpu.CompilerParams(vmem_limit_bytes=LIMIT),
        cost_estimate=pl.CostEstimate(
            flops=54 * channels * values.size, bytes_accessed=2 * weight.size // 3, transcendentals=values.size
        ),
        name=f"conv_layer_{layer}",
    )(odd, values, act, before, pair, other, weight, biases, gains)


def on_device(latents, conv_weight, norm_gains, biases):
    layers = conv_weight.shape[0]
    strips = lax.axis_size("rows")
    blocks = lax.axis_size("tm")
    strip = lax.axis_index("rows")
    odd = lax.rem(strip, 2).astype(jnp.int32)
    edge = ((strip == 0) | (strip == strips - 1)).astype(jnp.int32)
    place = jnp.stack([odd, edge])
    pairs = [[i, i + 1] for i in range(0, strips, 2)]
    others = [[i, (i + 1) % strips] for i in range(1, strips, 2)]
    values = latents
    act, send = prepare(latents, norm_gains)
    weight = weights(conv_weight)
    for layer in range(layers):
        before = lax.ppermute(send, "tm", [(i, i + 1) for i in range(blocks - 1)])
        if layer == 0:
            before, weight = lax.optimization_barrier((before, weight))
        top = jnp.concatenate([before[:, 0], act[:, 0]], axis=0)
        bottom = jnp.concatenate([before[:, -1], act[:, -1]], axis=0)
        pair = lax.all_gather(jnp.where(odd == 1, top, bottom), "rows", axis_index_groups=pairs)
        other = lax.all_gather(jnp.where(odd == 1, bottom, top), "rows", axis_index_groups=others)
        last = layer == layers - 1
        result = one_layer(layer, last, place, values, act, before, pair, other, weight, biases, norm_gains)
        if not last:
            values, act, send = result
    return result[0]


def solution(mesh):
    in_specs = (P(("clips", "tm"), "rows", None, None), P(), P(), P())
    out_specs = P(("clips", "tm"), "rows", None, None)
    return jax.shard_map(on_device, mesh=mesh, in_specs=in_specs, out_specs=out_specs, check_vma=False)
```

```python
import functools

import jax
import jax.numpy as jnp
from jax import lax
from jax.experimental import pallas as pl
from jax.experimental.pallas import tpu as pltpu
from jax.sharding import PartitionSpec as P

EPSILON = 1e-06
PAIR = 2
LANES = 128
VMEM = pl.BlockSpec(memory_space=pltpu.VMEM)
SMEM = pl.BlockSpec(memory_space=pltpu.SMEM)
LIMIT = 24 * 1024 * 1024


def rounded(lanes):
    return -(-lanes // LANES) * LANES


def column(row):
    return jnp.transpose(jnp.broadcast_to(row, (LANES, row.shape[1])))


def lane_of(lanes):
    return lax.broadcasted_iota(jnp.int32, (1, lanes), 1)


def filled(lanes, pitch):
    lane = lane_of(lanes)
    gaps = lane < 0
    for end in range(pitch - 1, lanes, pitch):
        gaps = gaps | (lane == end)
    return jnp.where(gaps, 0.0, 1.0)


def activated(values, gain, mask):
    squares = jnp.mean(values * values, axis=0, keepdims=True)
    normed = values * (lax.rsqrt(squares + EPSILON) * mask) * gain
    return (normed / (1.0 + jnp.exp(-normed))).astype(jnp.bfloat16)


def weights_kernel(place_ref, w_ref, out_ref):
    _, outs, ins = w_ref.shape
    flipped = place_ref[1]
    for time_tap in range(3):
        for row_tap in range(3):
            source = 9 * time_tap + 3 * (row_tap + flipped * (2 - 2 * row_tap))
            at = (3 * time_tap + row_tap) * ins
            out_ref[:, at : at + ins] = w_ref[pl.ds(source, 3)].reshape(3 * outs, ins)


def weights(place, conv_weight):
    layers, taps, outs, ins = conv_weight.shape
    return pl.pallas_call(
        weights_kernel,
        grid=(layers,),
        out_shape=jax.ShapeDtypeStruct((layers, 3 * outs, 9 * ins), conv_weight.dtype),
        in_specs=[SMEM, pl.BlockSpec((None, taps, outs, ins), lambda l: (l, 0, 0, 0))],
        out_specs=pl.BlockSpec((None, 3 * outs, 9 * ins), lambda l: (l, 0, 0)),
        compiler_params=pltpu.CompilerParams(vmem_limit_bytes=LIMIT),
        cost_estimate=pl.CostEstimate(flops=0, bytes_accessed=4 * conv_weight.size, transcendentals=0),
        name="weights",
    )(place, conv_weight)


def pack_kernel(halo, keep, place_ref, own_ref, mate_ref, far_ref, far_mate_ref, gains_ref, *out_refs):
    frames, rows, _, width = own_ref.shape
    core, group, outer = place_ref[0], place_ref[1], place_ref[2] == 1
    window = width // 2 + halo
    pitch = window + 1
    lanes = out_refs[0].shape[2]
    lane = lane_of(LANES)
    gain = column(gains_ref[0:1, :])
    mask = filled(lanes, pitch)
    first = core * (width - window)
    count = 2 * rows + halo
    for f in range(frames):
        blocks = [None] * (lanes // LANES)
        for row in range(count):
            near = row < 2 * rows
            local = row if near else 4 * rows - 1 - row
            at = local % rows
            side = group if near else 1 - group
            index = at + side * (rows - 1 - 2 * at)
            outermost = local < rows
            own, mate = (own_ref, mate_ref) if near else (far_mate_ref, far_ref)
            if not outermost:
                own, mate = mate, own
            line = jnp.where(outer, own[f, index], mate[f, index]).astype(jnp.float32)
            offset = row * pitch
            shift = lax.rem(offset % LANES + LANES - first, LANES)
            turned = pltpu.roll(line, shift, 1)
            low = offset % LANES
            block = offset // LANES
            here = (lane >= low) & (lane < low + window)
            piece = jnp.where(here, turned, 0.0)
            blocks[block] = piece if blocks[block] is None else blocks[block] + piece
            if low + window > LANES:
                piece = jnp.where(lane < low + window - LANES, turned, 0.0)
                blocks[block + 1] = piece
        for b, values in enumerate(blocks):
            part = slice(b * LANES, (b + 1) * LANES)
            out_refs[-1][f, :, part] = activated(values, gain, mask[:, part])
            if keep:
                out_refs[0][f, :, part] = values.astype(jnp.bfloat16)


def pack(halo, keep, place, own, mate, far, far_mate, gains):
    frames, rows, channels, width = own.shape
    lanes = rounded((2 * rows + halo) * (width // 2 + halo + 1))
    out = jax.ShapeDtypeStruct((frames, channels, lanes), jnp.bfloat16)
    return pl.pallas_call(
        functools.partial(pack_kernel, halo, keep),
        out_shape=(out,) * (1 + keep),
        in_specs=[SMEM] + [VMEM] * 5,
        out_specs=(VMEM,) * (1 + keep),
        compiler_params=pltpu.CompilerParams(vmem_limit_bytes=LIMIT),
        cost_estimate=pl.CostEstimate(
            flops=20 * frames * channels * lanes, bytes_accessed=8 * own.size, transcendentals=frames * channels * lanes
        ),
        name="pack",
    )(place, own, mate, far, far_mate, gains)


def conv_kernel(
    layer, last, pitch, half, place_ref, earlier_ref, act_ref, values_ref, w_ref, biases_ref, gains_ref, *refs
):
    outs, x_ref = refs[:-1], refs[-1]
    _, channels, lanes_in = act_ref.shape
    lanes = x_ref.shape[3] // PAIR
    first_row = lane_of(lanes_in) < pitch
    for j in range(2 * PAIR):
        ref = earlier_ref if j < PAIR else act_ref
        middle = ref[j % PAIR]
        wide = middle.astype(jnp.float32)
        above = jnp.where(first_row, 0.0, pltpu.roll(wide, pitch, 1)).astype(jnp.bfloat16)
        below = pltpu.roll(wide, lanes_in - pitch, 1).astype(jnp.bfloat16)
        for t in range(PAIR):
            if 0 <= j - t < 3:
                for tap, lines in enumerate((above, middle, below)):
                    x_ref[j - t, tap, :, t * lanes : (t + 1) * lanes] = lines[:, :lanes]
    sums = jnp.dot(
        w_ref[...], x_ref[...].reshape(9 * channels, PAIR * lanes), preferred_element_type=jnp.float32
    )
    bias = column(biases_ref[layer : layer + 1, :])
    start = lane_of(lanes) == 0
    if not last:
        gain = column(gains_ref[layer + 1 : layer + 2, :])
        mask = filled(lanes, pitch)
    for t in range(PAIR):
        part = sums[:, t * lanes : (t + 1) * lanes]
        conv = (
            jnp.where(start, 0.0, pltpu.roll(part[:channels], 1, 1))
            + part[channels : 2 * channels]
            + pltpu.roll(part[2 * channels :], lanes - 1, 1)
        )
        totals = []
        for b in range(lanes // LANES):
            at = slice(b * LANES, (b + 1) * LANES)
            total = (values_ref[t, :, at].astype(jnp.float32) + conv[:, at] + bias).astype(jnp.bfloat16)
            totals.append(total.astype(jnp.float32))
            if not last:
                outs[0][t, :, at] = total
                outs[1][t, :, at] = activated(totals[-1], gain, mask[:, at])
        if last:
            whole = jnp.concatenate(totals, axis=1)
            halo = pitch - 1 - half
            whole = jnp.where(place_ref[0] == 1, pltpu.roll(whole, lanes - halo, 1), whole)
            left = lane_of(LANES) < half

            def rows_of(row):
                one = whole if row == 0 else pltpu.roll(whole, lanes - row * pitch, 1)
                two = pltpu.roll(whole, lanes - (row + 1) * pitch + half, 1)
                return jnp.where(left, one[:, :LANES], two[:, :LANES])

            outermost, inner = rows_of(0), rows_of(2)
            outer = place_ref[2] == 1
            outs[0][t] = jnp.where(outer, outermost, inner).astype(jnp.bfloat16)
            outs[1][t] = jnp.where(outer, inner, outermost).astype(jnp.bfloat16)


def conv(layer, last, pitch, rows_left, half, place, earlier, act, values, weight, biases, gains):
    _, channels, _ = act.shape
    lanes = rounded(rows_left * pitch)
    out = jax.ShapeDtypeStruct((PAIR, channels, LANES if last else lanes), jnp.bfloat16)
    weight_spec = pl.BlockSpec((None,) + weight.shape[1:], lambda i: (layer, 0, 0))
    return pl.pallas_call(
        functools.partial(conv_kernel, layer, last, pitch, half),
        grid=(1,),
        out_shape=(out, out),
        in_specs=[SMEM] + [VMEM] * 3 + [weight_spec] + [VMEM] * 2,
        out_specs=(VMEM, VMEM),
        scratch_shapes=[pltpu.VMEM((3, 3, channels, PAIR * lanes), jnp.bfloat16)],
        compiler_params=pltpu.CompilerParams(vmem_limit_bytes=LIMIT),
        cost_estimate=pl.CostEstimate(
            flops=54 * channels * channels * PAIR * lanes,
            bytes_accessed=2 * weight.size // weight.shape[0],
            transcendentals=PAIR * channels * lanes,
        ),
        name=f"conv_{layer}",
    )(place, earlier, act, values, weight, biases, gains)


def join_kernel(place_ref, *refs):
    out_ref = refs[-1]
    kept, got = refs[: len(refs) // 2], refs[len(refs) // 2 : -1]
    _, rows, _, width = out_ref.shape
    half = width // 2
    first, group = place_ref[0] == 0, place_ref[1]
    left_half = lane_of(width) < half
    for p in range(len(kept)):
        for t in range(PAIR):
            mine, theirs = kept[p][t].astype(jnp.float32), got[p][t].astype(jnp.float32)
            left, right = jnp.where(first, mine, theirs), jnp.where(first, theirs, mine)
            lines = (
                jnp.where(left_half, left, pltpu.roll(right, half, 1)),
                jnp.where(left_half, pltpu.roll(left, half, 1), right),
            )
            for j in range(rows):
                out_ref[PAIR * p + t, j + group * (rows - 1 - 2 * j)] = lines[j].astype(jnp.bfloat16)


def join(place, kept, got, shape):
    return pl.pallas_call(
        join_kernel,
        out_shape=jax.ShapeDtypeStruct(shape, jnp.bfloat16),
        in_specs=[SMEM] + [VMEM] * (2 * len(kept)),
        out_specs=VMEM,
        compiler_params=pltpu.CompilerParams(vmem_limit_bytes=LIMIT),
        name="join",
    )(place, *kept, *got)


def on_device(latents, conv_weight, norm_gains, biases):
    layers = conv_weight.shape[0]
    frames, rows, channels, width = latents.shape
    strips, blocks = lax.axis_size("rows"), lax.axis_size("tm")
    assert strips == 4 and rows == 2 and frames % PAIR == 0 and width == LANES
    strip = lax.axis_index("rows").astype(jnp.int32)
    core, group = strip & 1, strip >> 1
    place = jnp.stack([core, group, (core == group).astype(jnp.int32)])

    def mate_of(block):
        return lax.ppermute(block, "rows", [(i, i ^ 1) for i in range(strips)])

    def earlier_of(block):
        return lax.ppermute(block, "tm", [(i, i + 1) for i in range(blocks - 1)])

    tail = latents[frames - PAIR :]
    far = lax.ppermute(latents, "rows", [(i, i ^ 2) for i in range(strips)])
    mate = mate_of(latents)
    before = earlier_of(tail)
    across = [
        (z * strips + r, (z + 1) * strips + (r ^ 2)) for z in range(blocks - 1) for r in range(strips)
    ]
    far_before = lax.ppermute(tail, ("tm", "rows"), across)
    weight = weights(place, conv_weight)
    far_mate = mate_of(far)
    both = jnp.concatenate([before, far_before], axis=0)
    both_mate = mate_of(both)

    values, act = pack(layers, True, place, latents, mate, far, far_mate, norm_gains)
    halo = pack(layers, False, place, before, both_mate[:PAIR], far_before, both_mate[PAIR:], norm_gains)[0]
    pitch = width // 2 + layers + 1
    pairs = frames // PAIR
    values = [values[PAIR * p : PAIR * (p + 1)] for p in range(pairs)]
    act = [act[PAIR * p : PAIR * (p + 1)] for p in range(pairs)]
    for layer in range(layers):
        last = layer == layers - 1
        rows_left = 2 * rows + layers - 1 - layer
        results = [None] * pairs
        next_halo = None
        for p in reversed(range(pairs)):
            earlier = act[p - 1] if p else halo
            results[p] = conv(
                layer, last, pitch, rows_left, width // 2, place, earlier, act[p], values[p], weight, biases, norm_gains
            )
            if p == pairs - 1 and not last:
                next_halo = earlier_of(results[p][1])
        values, act = [r[0] for r in results], [r[1] for r in results]
        halo = next_halo
    got = [mate_of(send) for send in act]
    return join(place, values, got, latents.shape)


def solution(mesh):
    in_specs = (P(("clips", "tm"), "rows", None, None), P(), P(), P())
    out_specs = P(("clips", "tm"), "rows", None, None)
    return jax.shard_map(on_device, mesh=mesh, in_specs=in_specs, out_specs=out_specs, check_vma=False)
```

```python
import functools

import jax
import jax.numpy as jnp
from jax import lax
from jax.experimental import pallas as pl
from jax.experimental.pallas import tpu as pltpu
from jax.sharding import PartitionSpec as P

EPSILON = 1e-06
PAIR = 2
LANES = 128
TILE = 256
VMEM = pl.BlockSpec(memory_space=pltpu.VMEM)
SMEM = pl.BlockSpec(memory_space=pltpu.SMEM)
LIMIT = 24 * 1024 * 1024


def rounded(lanes):
    return -(-lanes // LANES) * LANES


def column(row):
    return jnp.transpose(jnp.broadcast_to(row, (LANES, row.shape[1])))


def lane_of(lanes):
    return lax.broadcasted_iota(jnp.int32, (1, lanes), 1)


def filled(lanes, pitch):
    lane = lane_of(lanes)
    gaps = lane < 0
    for end in range(pitch - 1, lanes, pitch):
        gaps = gaps | (lane == end)
    return jnp.where(gaps, 0.0, 1.0)


def activated(values, gain, mask):
    squares = jnp.mean(values * values, axis=0, keepdims=True)
    halved = values * (lax.rsqrt(squares + EPSILON) * (0.5 * mask)) * gain
    return (halved + halved * jnp.tanh(halved)).astype(jnp.bfloat16)


def weights_kernel(place_ref, w_ref, gains_ref, biases_ref, out_ref, columns_ref):
    _, outs, ins = w_ref.shape
    flipped = place_ref[1]
    for time_tap in range(3):
        for row_tap in range(3):
            source = 9 * time_tap + 3 * (row_tap + flipped * (2 - 2 * row_tap))
            at = (3 * time_tap + row_tap) * ins
            out_ref[:, at : at + ins] = w_ref[pl.ds(source, 3)].reshape(3 * outs, ins)
    layer = pl.program_id(0)
    columns_ref[0] = column(gains_ref[pl.ds(layer, 1), :])
    columns_ref[1] = column(biases_ref[pl.ds(layer, 1), :])


def weights(place, conv_weight, gains, biases):
    layers, taps, outs, ins = conv_weight.shape
    return pl.pallas_call(
        weights_kernel,
        grid=(layers,),
        out_shape=(
            jax.ShapeDtypeStruct((layers, 3 * outs, 9 * ins), conv_weight.dtype),
            jax.ShapeDtypeStruct((layers, 2, outs, LANES), jnp.float32),
        ),
        in_specs=[SMEM, pl.BlockSpec((None, taps, outs, ins), lambda l: (l, 0, 0, 0)), VMEM, VMEM],
        out_specs=(
            pl.BlockSpec((None, 3 * outs, 9 * ins), lambda l: (l, 0, 0)),
            pl.BlockSpec((None, 2, outs, LANES), lambda l: (l, 0, 0, 0)),
        ),
        compiler_params=pltpu.CompilerParams(vmem_limit_bytes=LIMIT),
        cost_estimate=pl.CostEstimate(flops=0, bytes_accessed=4 * conv_weight.size, transcendentals=0),
        name="weights",
    )(place, conv_weight, gains, biases)


def placed(blocks, place_ref, row, window, line):
    pitch, width = window + 1, line.shape[1]
    lane = lane_of(LANES)
    block, low = divmod(row * pitch, LANES)
    shift = lax.rem(low + LANES - place_ref[0] * (width - window), LANES)
    turned = pltpu.roll(line, shift, 1)
    here = (lane >= low) & (lane < low + window)
    blocks[block] = blocks.get(block, 0.0) + jnp.where(here, turned, 0.0)
    if low + window > LANES:
        blocks[block + 1] = blocks.get(block + 1, 0.0) + jnp.where(lane < low + window - LANES, turned, 0.0)


def near_kernel(halo, place_ref, own_ref, mate_ref, gains_ref, values_ref, act_ref):
    frames, rows, _, width = own_ref.shape
    window = width // 2 + halo
    group, outer = place_ref[1], place_ref[2] == 1
    gain = column(gains_ref[0:1, :])
    mask = filled(act_ref.shape[2], window + 1)
    for f in range(frames):
        blocks = {}
        for row in range(2 * rows):
            at = row % rows
            index = at + group * (rows - 1 - 2 * at)
            one, two = (own_ref, mate_ref) if row < rows else (mate_ref, own_ref)
            line = jnp.where(outer, one[f, index], two[f, index]).astype(jnp.float32)
            placed(blocks, place_ref, row, window, line)
        for b in blocks:
            part = slice(b * LANES, (b + 1) * LANES)
            values_ref[f, :, part] = blocks[b].astype(jnp.bfloat16)
            if part.stop <= act_ref.shape[2]:
                act_ref[f, :, part] = activated(blocks[b], gain, mask[:, part])


def near(halo, place, own, mate, gains):
    frames, rows, channels, width = own.shape
    lanes = 2 * rows * (width // 2 + halo + 1)
    return pl.pallas_call(
        functools.partial(near_kernel, halo),
        out_shape=(
            jax.ShapeDtypeStruct((frames, channels, rounded(lanes)), jnp.bfloat16),
            jax.ShapeDtypeStruct((frames, channels, lanes // LANES * LANES), jnp.bfloat16),
        ),
        in_specs=[SMEM] + [VMEM] * 3,
        out_specs=(VMEM, VMEM),
        compiler_params=pltpu.CompilerParams(vmem_limit_bytes=LIMIT),
        cost_estimate=pl.CostEstimate(flops=40 * own.size, bytes_accessed=8 * own.size, transcendentals=2 * own.size),
        name="near",
    )(place, own, mate, gains)


def far_kernel(halo, place_ref, far_ref, mate_ref, near_ref, act_ref, columns_ref, *out_refs):
    frames, rows, _, width = far_ref.shape
    window = width // 2 + halo
    group, outer = place_ref[1], place_ref[2] == 1
    lanes, done = out_refs[0].shape[2], act_ref.shape[2]
    mask = filled(lanes, window + 1)
    for f in range(frames):
        values_ref, act_out_ref = out_refs[2 * (f // PAIR)], out_refs[2 * (f // PAIR) + 1]
        t = f % PAIR
        values_ref[t, :, :done] = near_ref[f, :, :done]
        act_out_ref[t, :, :done] = act_ref[f]
        blocks = {done // LANES: near_ref[f, :, done:].astype(jnp.float32)}
        for row in range(2 * rows, 2 * rows + halo):
            local = 4 * rows - 1 - row
            at = local % rows
            index = at + (1 - group) * (rows - 1 - 2 * at)
            one, two = (mate_ref, far_ref) if local < rows else (far_ref, mate_ref)
            line = jnp.where(outer, one[f, index], two[f, index]).astype(jnp.float32)
            placed(blocks, place_ref, row, window, line)
        for b in blocks:
            part = slice(b * LANES, (b + 1) * LANES)
            values_ref[t, :, part] = blocks[b].astype(jnp.bfloat16)
            act_out_ref[t, :, part] = activated(blocks[b], columns_ref[0, 0], mask[:, part])


def beyond(halo, place, far, mate, near_values, near_act, columns):
    frames, rows, channels, width = far.shape
    lanes = rounded((2 * rows + halo) * (width // 2 + halo + 1))
    out = jax.ShapeDtypeStruct((PAIR, channels, lanes), jnp.bfloat16)
    count = 2 * (frames // PAIR)
    outs = pl.pallas_call(
        functools.partial(far_kernel, halo),
        out_shape=(out,) * count,
        in_specs=[SMEM] + [VMEM] * 5,
        out_specs=(VMEM,) * count,
        compiler_params=pltpu.CompilerParams(vmem_limit_bytes=LIMIT),
        cost_estimate=pl.CostEstimate(flops=40 * far.size, bytes_accessed=8 * far.size, transcendentals=2 * far.size),
        name="beyond",
    )(place, far, mate, near_values, near_act, columns)
    return list(outs[0::2]), list(outs[1::2])


def conv_kernel(layer, last, pitch, half, place_ref, earlier_ref, act_ref, values_ref, w_ref, columns_ref, *refs):
    outs, x_ref = refs[:-1], refs[-1]
    _, channels, lanes_in = act_ref.shape
    lanes = x_ref.shape[3] // PAIR
    chunks = lanes // LANES
    lane = lane_of(LANES)
    for j in range(2 * PAIR):
        ref = earlier_ref if j < PAIR else act_ref
        middle = ref[j % PAIR]
        above = pltpu.roll(middle, pitch, 1)
        edge = jnp.where(lane < pitch, 0.0, above[:, :LANES].astype(jnp.float32)).astype(jnp.bfloat16)
        below = pltpu.roll(middle, lanes_in - pitch, 1)
        for t in range(PAIR):
            if 0 <= j - t < 3:
                for tap, lines in enumerate((above, middle, below)):
                    x_ref[j - t, tap, :, t * lanes : (t + 1) * lanes] = lines[:, :lanes]
                x_ref[j - t, 0, :, t * lanes : t * lanes + LANES] = edge
    tiles = [
        jnp.dot(
            w_ref[...],
            x_ref[:, :, :, at : at + TILE].reshape(9 * channels, TILE),
            preferred_element_type=jnp.float32,
        )
        for at in range(0, PAIR * lanes, TILE)
    ]
    bias = columns_ref[layer, 1]
    if not last:
        mask = filled(lanes, pitch)
        gain = columns_ref[layer + 1, 0]
    for t in range(PAIR):

        def sums(tap, b):
            tile, at = divmod((t * chunks + b) * LANES, TILE)
            return tiles[tile][tap * channels : (tap + 1) * channels, at : at + LANES]

        totals = []
        from_left = 0.0
        from_right = pltpu.roll(sums(2, 0), LANES - 1, 1)
        for b in range(chunks):
            at = slice(b * LANES, (b + 1) * LANES)
            left = pltpu.roll(sums(0, b), 1, 1)
            right = pltpu.roll(sums(2, b + 1), LANES - 1, 1) if b + 1 < chunks else 0.0
            summed = (
                jnp.where(lane == 0, from_left, left) + sums(1, b) + jnp.where(lane == LANES - 1, right, from_right)
            )
            from_left, from_right = left, right
            total = (values_ref[t, :, at].astype(jnp.float32) + summed + bias).astype(jnp.bfloat16)
            totals.append(total.astype(jnp.float32))
            if not last:
                outs[0][t, :, at] = total
                outs[1][t, :, at] = activated(totals[-1], gain, mask[:, at])
        if last:
            whole = jnp.concatenate(totals, axis=1)
            halo = pitch - 1 - half
            whole = jnp.where(place_ref[0] == 1, pltpu.roll(whole, lanes - halo, 1), whole)
            left_half = lane < half

            def rows_of(row):
                one = whole if row == 0 else pltpu.roll(whole, lanes - row * pitch, 1)
                two = pltpu.roll(whole, lanes - (row + 1) * pitch + half, 1)
                return jnp.where(left_half, one[:, :LANES], two[:, :LANES])

            outermost, inner = rows_of(0), rows_of(2)
            outer = place_ref[2] == 1
            outs[0][t] = jnp.where(outer, outermost, inner).astype(jnp.bfloat16)
            outs[1][t] = jnp.where(outer, inner, outermost).astype(jnp.bfloat16)


def conv(layer, last, pitch, rows_left, half, place, earlier, act, values, weight, columns):
    _, channels, _ = act.shape
    lanes = rounded(rows_left * pitch)
    out = jax.ShapeDtypeStruct((PAIR, channels, LANES if last else lanes), jnp.bfloat16)
    weight_spec = pl.BlockSpec((None,) + weight.shape[1:], lambda i: (layer, 0, 0))
    return pl.pallas_call(
        functools.partial(conv_kernel, layer, last, pitch, half),
        grid=(1,),
        out_shape=(out, out),
        in_specs=[SMEM] + [VMEM] * 3 + [weight_spec, VMEM],
        out_specs=(VMEM, VMEM),
        scratch_shapes=[pltpu.VMEM((3, 3, channels, PAIR * lanes), jnp.bfloat16)],
        compiler_params=pltpu.CompilerParams(vmem_limit_bytes=LIMIT),
        cost_estimate=pl.CostEstimate(
            flops=54 * channels * channels * PAIR * lanes,
            bytes_accessed=2 * weight.size // weight.shape[0],
            transcendentals=PAIR * channels * lanes,
        ),
        name=f"conv_{layer}",
    )(place, earlier, act, values, weight, columns)


def join_kernel(place_ref, *refs):
    out_ref = refs[-1]
    kept, got = refs[: len(refs) // 2], refs[len(refs) // 2 : -1]
    _, rows, _, width = out_ref.shape
    half = width // 2
    first, group = place_ref[0] == 0, place_ref[1]
    left_half = lane_of(width) < half
    for p in range(len(kept)):
        for t in range(PAIR):
            mine, theirs = kept[p][t].astype(jnp.float32), got[p][t].astype(jnp.float32)
            left, right = jnp.where(first, mine, theirs), jnp.where(first, theirs, mine)
            lines = (
                jnp.where(left_half, left, pltpu.roll(right, half, 1)),
                jnp.where(left_half, pltpu.roll(left, half, 1), right),
            )
            for j in range(rows):
                out_ref[PAIR * p + t, j + group * (rows - 1 - 2 * j)] = lines[j].astype(jnp.bfloat16)


def join(place, kept, got, shape):
    return pl.pallas_call(
        join_kernel,
        out_shape=jax.ShapeDtypeStruct(shape, jnp.bfloat16),
        in_specs=[SMEM] + [VMEM] * (2 * len(kept)),
        out_specs=VMEM,
        compiler_params=pltpu.CompilerParams(vmem_limit_bytes=LIMIT),
        name="join",
    )(place, *kept, *got)


def on_device(latents, conv_weight, norm_gains, biases):
    layers = conv_weight.shape[0]
    frames, rows, channels, width = latents.shape
    strips, blocks = lax.axis_size("rows"), lax.axis_size("tm")
    assert strips == 4 and rows == 2 and frames % PAIR == 0 and width == LANES
    strip = lax.axis_index("rows").astype(jnp.int32)
    core, group = strip & 1, strip >> 1
    place = jnp.stack([core, group, (core == group).astype(jnp.int32)])

    def mate_of(block):
        return lax.ppermute(block, "rows", [(i, i ^ 1) for i in range(strips)])

    def earlier_of(block):
        return lax.ppermute(block, "tm", [(i, i + 1) for i in range(blocks - 1)])

    far = lax.ppermute(latents, "rows", [(i, i ^ 2) for i in range(strips)])
    mate = mate_of(latents)
    weight, columns = weights(place, conv_weight, norm_gains, biases)
    near_values, near_act = near(layers, place, latents, mate, norm_gains)
    far, weight, columns, near_values, near_act = lax.optimization_barrier(
        (far, weight, columns, near_values, near_act)
    )
    values, act = beyond(layers, place, far, mate_of(far), near_values, near_act, columns)
    pitch = width // 2 + layers + 1
    pairs = frames // PAIR
    for layer in range(layers):
        last = layer == layers - 1
        rows_left = 2 * rows + layers - 1 - layer
        halo = earlier_of(act[-1])
        results = [None] * pairs
        for p in reversed(range(pairs)):
            earlier = act[p - 1] if p else halo
            results[p] = conv(
                layer, last, pitch, rows_left, width // 2, place, earlier, act[p], values[p], weight, columns
            )
        values, act = [r[0] for r in results], [r[1] for r in results]
    got = [mate_of(send) for send in act]
    return join(place, values, got, latents.shape)


def solution(mesh):
    in_specs = (P(("clips", "tm"), "rows", None, None), P(), P(), P())
    out_specs = P(("clips", "tm"), "rows", None, None)
    return jax.shard_map(on_device, mesh=mesh, in_specs=in_specs, out_specs=out_specs, check_vma=False)
```

```python
import functools

import jax
import jax.numpy as jnp
from jax import lax
from jax.experimental import pallas as pl
from jax.experimental.pallas import tpu as pltpu
from jax.sharding import PartitionSpec as P

EPSILON = 1e-06
PAIR = 2
LANES = 128
TILE = 256
VMEM = pl.BlockSpec(memory_space=pltpu.VMEM)
SMEM = pl.BlockSpec(memory_space=pltpu.SMEM)
LIMIT = 24 * 1024 * 1024


def rounded(lanes):
    return -(-lanes // LANES) * LANES


def column(row):
    return jnp.transpose(jnp.broadcast_to(row, (LANES, row.shape[1])))


def lane_of(lanes):
    return lax.broadcasted_iota(jnp.int32, (1, lanes), 1)


def filled(lanes, pitch):
    lane = lane_of(lanes)
    gaps = lane < 0
    for end in range(pitch - 1, lanes, pitch):
        gaps = gaps | (lane == end)
    return jnp.where(gaps, 0.0, 1.0)


def activated(values, gain, mask):
    squares = jnp.mean(values * values, axis=0, keepdims=True)
    halved = values * (lax.rsqrt(squares + EPSILON) * (0.5 * mask)) * gain
    return (halved + halved * jnp.tanh(halved)).astype(jnp.bfloat16)


def weights_kernel(place_ref, w_ref, gains_ref, biases_ref, *refs):
    layers, _, outs, ins = w_ref.shape
    flipped = place_ref[1]
    for layer in range(layers):
        for time_tap in range(3):
            for row_tap in range(3):
                source = 9 * time_tap + 3 * (row_tap + flipped * (2 - 2 * row_tap))
                at = (3 * time_tap + row_tap) * ins
                refs[layer][:, at : at + ins] = w_ref[layer, pl.ds(source, 3)].reshape(3 * outs, ins)
        refs[-1][layer, 0] = column(gains_ref[layer : layer + 1, :])
        refs[-1][layer, 1] = column(biases_ref[layer : layer + 1, :])


def weights(place, conv_weight, gains, biases):
    layers, _, outs, ins = conv_weight.shape
    one = jax.ShapeDtypeStruct((3 * outs, 9 * ins), conv_weight.dtype)
    results = pl.pallas_call(
        weights_kernel,
        out_shape=(one,) * layers + (jax.ShapeDtypeStruct((layers, 2, outs, LANES), jnp.float32),),
        in_specs=[SMEM] + [VMEM] * 3,
        out_specs=(VMEM,) * (layers + 1),
        compiler_params=pltpu.CompilerParams(vmem_limit_bytes=LIMIT),
        cost_estimate=pl.CostEstimate(flops=0, bytes_accessed=4 * conv_weight.size, transcendentals=0),
        name="weights",
    )(place, conv_weight, gains, biases)
    return results[:-1], results[-1]


def placed(blocks, place_ref, row, window, line):
    pitch, width = window + 1, line.shape[1]
    lane = lane_of(LANES)
    block, low = divmod(row * pitch, LANES)
    shift = lax.rem(low + LANES - place_ref[0] * (width - window), LANES)
    turned = pltpu.roll(line, shift, 1)
    here = (lane >= low) & (lane < low + window)
    blocks[block] = blocks.get(block, 0.0) + jnp.where(here, turned, 0.0)
    if low + window > LANES:
        blocks[block + 1] = blocks.get(block + 1, 0.0) + jnp.where(lane < low + window - LANES, turned, 0.0)


def near_kernel(halo, place_ref, own_ref, mate_ref, gains_ref, values_ref, *act_refs):
    frames, rows, _, width = own_ref.shape
    window = width // 2 + halo
    group, outer = place_ref[1], place_ref[2] == 1
    gain = column(gains_ref[0:1, :])
    done = act_refs[0].shape[2]
    mask = filled(done, window + 1)
    for f in range(frames):
        blocks = {}
        for row in range(2 * rows):
            at = row % rows
            index = at + group * (rows - 1 - 2 * at)
            one, two = (own_ref, mate_ref) if row < rows else (mate_ref, own_ref)
            line = jnp.where(outer, one[f, index], two[f, index]).astype(jnp.float32)
            placed(blocks, place_ref, row, window, line)
        for b in blocks:
            part = slice(b * LANES, (b + 1) * LANES)
            values_ref[f, :, part] = blocks[b].astype(jnp.bfloat16)
            if part.stop <= done:
                act_refs[f // PAIR][f % PAIR, :, part] = activated(blocks[b], gain, mask[:, part])


def near(halo, place, own, mate, gains):
    frames, rows, channels, width = own.shape
    lanes = 2 * rows * (width // 2 + halo + 1)
    pairs = frames // PAIR
    outs = pl.pallas_call(
        functools.partial(near_kernel, halo),
        out_shape=(jax.ShapeDtypeStruct((frames, channels, rounded(lanes)), jnp.bfloat16),)
        + (jax.ShapeDtypeStruct((PAIR, channels, lanes // LANES * LANES), jnp.bfloat16),) * pairs,
        in_specs=[SMEM] + [VMEM] * 3,
        out_specs=(VMEM,) * (1 + pairs),
        compiler_params=pltpu.CompilerParams(vmem_limit_bytes=LIMIT),
        cost_estimate=pl.CostEstimate(flops=40 * own.size, bytes_accessed=8 * own.size, transcendentals=2 * own.size),
        name="near",
    )(place, own, mate, gains)
    return outs[0], outs[1:]


def far_kernel(halo, pairs, place_ref, far_ref, mate_ref, near_ref, columns_ref, *refs):
    act_refs, value_refs, out_refs, send_ref = refs[:pairs], refs[pairs : 2 * pairs], refs[2 * pairs : -1], refs[-1]
    frames, rows, _, width = far_ref.shape
    window = width // 2 + halo
    group, outer = place_ref[1], place_ref[2] == 1
    lanes, done = out_refs[0].shape[2], act_refs[0].shape[2]
    mask = filled(lanes, window + 1)
    for f in range(frames):
        p, t = divmod(f, PAIR)
        value_refs[p][t, :, :done] = near_ref[f, :, :done]
        out_refs[p][t, :, :done] = act_refs[p][t]
        blocks = {done // LANES: near_ref[f, :, done:].astype(jnp.float32)}
        for row in range(2 * rows, 2 * rows + halo):
            local = 4 * rows - 1 - row
            at = local % rows
            index = at + (1 - group) * (rows - 1 - 2 * at)
            one, two = (mate_ref, far_ref) if local < rows else (far_ref, mate_ref)
            line = jnp.where(outer, one[f, index], two[f, index]).astype(jnp.float32)
            placed(blocks, place_ref, row, window, line)
        for b in blocks:
            part = slice(b * LANES, (b + 1) * LANES)
            value_refs[p][t, :, part] = blocks[b].astype(jnp.bfloat16)
            act = activated(blocks[b], columns_ref[0, 0], mask[:, part])
            out_refs[p][t, :, part] = act
            if p == pairs - 1:
                send_ref[t, :, part.start - done : part.stop - done] = act


def beyond(halo, place, far, mate, near_values, near_act, columns):
    frames, rows, channels, width = far.shape
    lanes = rounded((2 * rows + halo) * (width // 2 + halo + 1))
    out = jax.ShapeDtypeStruct((PAIR, channels, lanes), jnp.bfloat16)
    send = jax.ShapeDtypeStruct((PAIR, channels, lanes - near_act[0].shape[2]), jnp.bfloat16)
    pairs = frames // PAIR
    outs = pl.pallas_call(
        functools.partial(far_kernel, halo, pairs),
        out_shape=(out,) * (2 * pairs) + (send,),
        in_specs=[SMEM] + [VMEM] * (4 + pairs),
        out_specs=(VMEM,) * (2 * pairs + 1),
        compiler_params=pltpu.CompilerParams(vmem_limit_bytes=LIMIT),
        cost_estimate=pl.CostEstimate(flops=40 * far.size, bytes_accessed=8 * far.size, transcendentals=2 * far.size),
        name="beyond",
    )(place, far, mate, near_values, columns, *near_act)
    return outs[:pairs], outs[pairs : 2 * pairs], outs[-1]


def conv_kernel(layer, last, pitch, half, place_ref, act_ref, values_ref, w_ref, columns_ref, *refs):
    earlier_refs, outs, x_ref = refs[:-3], refs[-3:-1], refs[-1]
    _, channels, lanes_in = act_ref.shape
    lanes = x_ref.shape[3] // PAIR
    chunks = lanes // LANES
    lane = lane_of(LANES)
    for j in range(2 * PAIR):
        parts = [ref[j % PAIR] for ref in (earlier_refs if j < PAIR else (act_ref,))]
        middle = parts[0] if len(parts) == 1 else jnp.concatenate(parts, axis=1)
        above = pltpu.roll(middle, pitch, 1)
        edge = jnp.where(lane < pitch, 0.0, above[:, :LANES].astype(jnp.float32)).astype(jnp.bfloat16)
        below = pltpu.roll(middle, lanes_in - pitch, 1)
        for t in range(PAIR):
            if 0 <= j - t < 3:
                for tap, lines in enumerate((above, middle, below)):
                    x_ref[j - t, tap, :, t * lanes : (t + 1) * lanes] = lines[:, :lanes]
                x_ref[j - t, 0, :, t * lanes : t * lanes + LANES] = edge
    tiles = [
        jnp.dot(
            w_ref[...],
            x_ref[:, :, :, at : at + TILE].reshape(9 * channels, TILE),
            preferred_element_type=jnp.float32,
        )
        for at in range(0, PAIR * lanes, TILE)
    ]
    bias = columns_ref[layer, 1]
    if not last:
        mask = filled(lanes, pitch)
        gain = columns_ref[layer + 1, 0]
    for t in range(PAIR):

        def sums(tap, b):
            tile, at = divmod((t * chunks + b) * LANES, TILE)
            return tiles[tile][tap * channels : (tap + 1) * channels, at : at + LANES]

        totals = []
        from_left = 0.0
        from_right = pltpu.roll(sums(2, 0), LANES - 1, 1)
        for b in range(chunks):
            at = slice(b * LANES, (b + 1) * LANES)
            left = pltpu.roll(sums(0, b), 1, 1)
            right = pltpu.roll(sums(2, b + 1), LANES - 1, 1) if b + 1 < chunks else 0.0
            summed = (
                jnp.where(lane == 0, from_left, left) + sums(1, b) + jnp.where(lane == LANES - 1, right, from_right)
            )
            from_left, from_right = left, right
            total = (values_ref[t, :, at].astype(jnp.float32) + summed + bias).astype(jnp.bfloat16)
            totals.append(total.astype(jnp.float32))
            if not last:
                outs[0][t, :, at] = total
                outs[1][t, :, at] = activated(totals[-1], gain, mask[:, at])
        if last:
            whole = jnp.concatenate(totals, axis=1)
            halo = pitch - 1 - half
            whole = jnp.where(place_ref[0] == 1, pltpu.roll(whole, lanes - halo, 1), whole)
            left_half = lane < half

            def rows_of(row):
                one = whole if row == 0 else pltpu.roll(whole, lanes - row * pitch, 1)
                two = pltpu.roll(whole, lanes - (row + 1) * pitch + half, 1)
                return jnp.where(left_half, one[:, :LANES], two[:, :LANES])

            outermost, inner = rows_of(0), rows_of(2)
            outer = place_ref[2] == 1
            outs[0][t] = jnp.where(outer, outermost, inner).astype(jnp.bfloat16)
            outs[1][t] = jnp.where(outer, inner, outermost).astype(jnp.bfloat16)


def conv(layer, last, pitch, rows_left, half, place, earlier, act, values, weight, columns):
    _, channels, _ = act.shape
    lanes = rounded(rows_left * pitch)
    out = jax.ShapeDtypeStruct((PAIR, channels, LANES if last else lanes), jnp.bfloat16)
    return pl.pallas_call(
        functools.partial(conv_kernel, layer, last, pitch, half),
        out_shape=(out, out),
        in_specs=[SMEM] + [VMEM] * (4 + len(earlier)),
        out_specs=(VMEM, VMEM),
        scratch_shapes=[pltpu.VMEM((3, 3, channels, PAIR * lanes), jnp.bfloat16)],
        compiler_params=pltpu.CompilerParams(vmem_limit_bytes=LIMIT),
        cost_estimate=pl.CostEstimate(
            flops=54 * channels * channels * PAIR * lanes,
            bytes_accessed=2 * weight.size,
            transcendentals=PAIR * channels * lanes,
        ),
        name=f"conv_{layer}",
    )(place, act, values, weight, columns, *earlier)


def join_kernel(place_ref, *refs):
    out_ref = refs[-1]
    kept, got = refs[: len(refs) // 2], refs[len(refs) // 2 : -1]
    _, rows, _, width = out_ref.shape
    half = width // 2
    first, group = place_ref[0] == 0, place_ref[1]
    left_half = lane_of(width) < half
    for p in range(len(kept)):
        for t in range(PAIR):
            mine, theirs = kept[p][t].astype(jnp.float32), got[p][t].astype(jnp.float32)
            left, right = jnp.where(first, mine, theirs), jnp.where(first, theirs, mine)
            lines = (
                jnp.where(left_half, left, pltpu.roll(right, half, 1)),
                jnp.where(left_half, pltpu.roll(left, half, 1), right),
            )
            for j in range(rows):
                out_ref[PAIR * p + t, j + group * (rows - 1 - 2 * j)] = lines[j].astype(jnp.bfloat16)


def join(place, kept, got, shape):
    return pl.pallas_call(
        join_kernel,
        out_shape=jax.ShapeDtypeStruct(shape, jnp.bfloat16),
        in_specs=[SMEM] + [VMEM] * (2 * len(kept)),
        out_specs=VMEM,
        compiler_params=pltpu.CompilerParams(vmem_limit_bytes=LIMIT),
        name="join",
    )(place, *kept, *got)


def on_device(latents, conv_weight, norm_gains, biases):
    layers = conv_weight.shape[0]
    frames, rows, channels, width = latents.shape
    strips, blocks = lax.axis_size("rows"), lax.axis_size("tm")
    assert strips == 4 and rows == 2 and frames % PAIR == 0 and width == LANES
    strip = lax.axis_index("rows").astype(jnp.int32)
    core, group = strip & 1, strip >> 1
    place = jnp.stack([core, group, (core == group).astype(jnp.int32)])

    def mate_of(block):
        return lax.ppermute(block, "rows", [(i, i ^ 1) for i in range(strips)])

    def earlier_of(block):
        return lax.ppermute(block, "tm", [(i, i + 1) for i in range(blocks - 1)])

    far = lax.ppermute(latents, "rows", [(i, i ^ 2) for i in range(strips)])
    mate = mate_of(latents)
    weight, columns = weights(place, conv_weight, norm_gains, biases)
    near_values, near_act = near(layers, place, latents, mate, norm_gains)
    halo_near = earlier_of(near_act[-1])
    far, weight, columns, near_values, near_act, halo_near = lax.optimization_barrier(
        (far, weight, columns, near_values, near_act, halo_near)
    )
    values, act, send = beyond(layers, place, far, mate_of(far), near_values, near_act, columns)
    halo = (halo_near, earlier_of(send))
    pitch = width // 2 + layers + 1
    pairs = frames // PAIR
    for layer in range(layers):
        last = layer == layers - 1
        rows_left = 2 * rows + layers - 1 - layer
        if layer:
            halo = (earlier_of(act[-1]),)
        results = [None] * pairs
        for p in reversed(range(pairs)):
            earlier = (act[p - 1],) if p else halo
            results[p] = conv(
                layer, last, pitch, rows_left, width // 2, place, earlier, act[p], values[p], weight[layer], columns
            )
        values, act = [r[0] for r in results], [r[1] for r in results]
    got = [mate_of(send) for send in act]
    return join(place, values, got, latents.shape)


def solution(mesh):
    in_specs = (P(("clips", "tm"), "rows", None, None), P(), P(), P())
    out_specs = P(("clips", "tm"), "rows", None, None)
    return jax.shard_map(on_device, mesh=mesh, in_specs=in_specs, out_specs=out_specs, check_vma=False)
```

```python
import functools

import jax
import jax.numpy as jnp
from jax import lax
from jax.experimental import pallas as pl
from jax.experimental.pallas import tpu as pltpu
from jax.sharding import PartitionSpec as P

EPSILON = 1e-06
PAIR = 2
LANES = 128
TILE = 256
VMEM = pl.BlockSpec(memory_space=pltpu.VMEM)
SMEM = pl.BlockSpec(memory_space=pltpu.SMEM)
ANY = pl.BlockSpec(memory_space=pl.ANY)
LIMIT = 24 * 1024 * 1024
LARGE = 48 * 1024 * 1024


def rounded(lanes):
    return -(-lanes // LANES) * LANES


def column(row):
    return jnp.transpose(jnp.broadcast_to(row, (LANES, row.shape[1])))


def lane_of(lanes):
    return lax.broadcasted_iota(jnp.int32, (1, lanes), 1)


def filled(lanes, pitch):
    lane = lane_of(lanes)
    gaps = lane < 0
    for end in range(pitch - 1, lanes, pitch):
        gaps = gaps | (lane == end)
    return jnp.where(gaps, 0.0, 1.0)


def activated(values, gain, mask):
    squares = jnp.mean(values * values, axis=0, keepdims=True)
    halved = values * (lax.rsqrt(squares + EPSILON) * (0.5 * mask)) * gain
    return (halved + halved * jnp.tanh(halved)).astype(jnp.bfloat16)


def fetched(pairs, sems):
    copies = [pltpu.make_async_copy(source, to, sems.at[i]) for i, (source, to) in enumerate(pairs)]
    for copy in copies:
        copy.start()
    return copies


def weights_kernel(first, columns, place_ref, w_ref, *refs):
    outs, held_ref, sems = refs[columns:-2], refs[-2], refs[-1]
    count, _, channels_out, ins = held_ref.shape
    copies = fetched([(w_ref.at[first + i], held_ref.at[i]) for i in range(count)], sems)
    flipped = place_ref[1]
    if columns:
        rows_ref = refs[0]
        layers = rows_ref.shape[0] // 2
        for layer in range(layers):
            outs[-1][layer, 0] = column(rows_ref[layer : layer + 1, :])
            outs[-1][layer, 1] = column(rows_ref[layers + layer : layers + layer + 1, :])
    for i in range(count):
        copies[i].wait()
        for time_tap in range(3):
            for row_tap in range(3):
                source = 9 * time_tap + 3 * (row_tap + flipped * (2 - 2 * row_tap))
                at = (3 * time_tap + row_tap) * ins
                outs[i][:, at : at + ins] = held_ref[i, pl.ds(source, 3)].reshape(3 * channels_out, ins)


def weights(first, count, place, conv_weight, *rows):
    layers, taps, outs, ins = conv_weight.shape
    one = jax.ShapeDtypeStruct((3 * outs, 9 * ins), conv_weight.dtype)
    columns = len(rows)
    results = pl.pallas_call(
        functools.partial(weights_kernel, first, columns),
        out_shape=(one,) * count + (jax.ShapeDtypeStruct((layers, 2, outs, LANES), jnp.float32),) * columns,
        in_specs=[SMEM, ANY] + [VMEM] * columns,
        out_specs=(VMEM,) * (count + columns),
        scratch_shapes=[
            pltpu.VMEM((count, taps, outs, ins), conv_weight.dtype),
            pltpu.SemaphoreType.DMA((count,)),
        ],
        compiler_params=pltpu.CompilerParams(vmem_limit_bytes=LARGE),
        cost_estimate=pl.CostEstimate(
            flops=0, bytes_accessed=4 * conv_weight.size * count // layers, transcendentals=0
        ),
        name="weights",
    )(place, conv_weight, *rows)
    return list(results[:count]), results[count:]


def spread(out_ref, index, act, pitch):
    lanes = out_ref.shape[3]
    above = pltpu.roll(act, pitch, 1)
    below = pltpu.roll(act, act.shape[1] - pitch, 1)
    edge = jnp.where(lane_of(LANES) < pitch, 0.0, above[:, :LANES].astype(jnp.float32))
    out_ref[index, 0, :, :LANES] = edge.astype(jnp.bfloat16)
    out_ref[index, 0, :, LANES:] = above[:, LANES:lanes]
    out_ref[index, 1] = act[:, :lanes]
    out_ref[index, 2] = below[:, :lanes]


def placed(blocks, place_ref, row, window, line):
    pitch, width = window + 1, line.shape[1]
    lane = lane_of(LANES)
    block, low = divmod(row * pitch, LANES)
    shift = lax.rem(low + LANES - place_ref[0] * (width - window), LANES)
    turned = pltpu.roll(line, shift, 1)
    here = (lane >= low) & (lane < low + window)
    blocks[block] = blocks.get(block, 0.0) + jnp.where(here, turned, 0.0)
    if low + window > LANES:
        blocks[block + 1] = blocks.get(block + 1, 0.0) + jnp.where(lane < low + window - LANES, turned, 0.0)


def near_kernel(halo, place_ref, own_ref, mate_ref, gains_ref, values_ref, *act_refs):
    frames, rows, _, width = own_ref.shape
    window = width // 2 + halo
    group, outer = place_ref[1], place_ref[2] == 1
    gain = column(gains_ref[0:1, :])
    done = act_refs[0].shape[2]
    mask = filled(done, window + 1)
    for f in range(frames):
        blocks = {}
        for row in range(2 * rows):
            at = row % rows
            index = at + group * (rows - 1 - 2 * at)
            one, two = (own_ref, mate_ref) if row < rows else (mate_ref, own_ref)
            line = jnp.where(outer, one[f, index], two[f, index]).astype(jnp.float32)
            placed(blocks, place_ref, row, window, line)
        for b in blocks:
            part = slice(b * LANES, (b + 1) * LANES)
            values_ref[f, :, part] = blocks[b].astype(jnp.bfloat16)
            if part.stop <= done:
                act_refs[f // PAIR][f % PAIR, :, part] = activated(blocks[b], gain, mask[:, part])


def near(halo, place, own, mate, gains):
    frames, rows, channels, width = own.shape
    lanes = 2 * rows * (width // 2 + halo + 1)
    pairs = frames // PAIR
    outs = pl.pallas_call(
        functools.partial(near_kernel, halo),
        out_shape=(jax.ShapeDtypeStruct((frames, channels, rounded(lanes)), jnp.bfloat16),)
        + (jax.ShapeDtypeStruct((PAIR, channels, lanes // LANES * LANES), jnp.bfloat16),) * pairs,
        in_specs=[SMEM] + [VMEM] * 3,
        out_specs=(VMEM,) * (1 + pairs),
        compiler_params=pltpu.CompilerParams(vmem_limit_bytes=LIMIT),
        cost_estimate=pl.CostEstimate(flops=40 * own.size, bytes_accessed=8 * own.size, transcendentals=2 * own.size),
        name="near",
    )(place, own, mate, gains)
    return outs[0], outs[1:]


def far_kernel(halo, pairs, place_ref, far_ref, mate_ref, near_ref, columns_ref, *refs):
    act_refs, value_refs, out_refs, send_ref = refs[:pairs], refs[pairs : 2 * pairs], refs[2 * pairs : -1], refs[-1]
    frames, rows, _, width = far_ref.shape
    window = width // 2 + halo
    group, outer = place_ref[1], place_ref[2] == 1
    lanes, done = value_refs[0].shape[2], act_refs[0].shape[2]
    mask = filled(lanes, window + 1)
    for f in range(frames):
        p, t = divmod(f, PAIR)
        value_refs[p][t, :, :done] = near_ref[f, :, :done]
        acts = [act_refs[p][t]]
        blocks = {done // LANES: near_ref[f, :, done:].astype(jnp.float32)}
        for row in range(2 * rows, 2 * rows + halo):
            local = 4 * rows - 1 - row
            at = local % rows
            index = at + (1 - group) * (rows - 1 - 2 * at)
            one, two = (mate_ref, far_ref) if local < rows else (far_ref, mate_ref)
            line = jnp.where(outer, one[f, index], two[f, index]).astype(jnp.float32)
            placed(blocks, place_ref, row, window, line)
        for b in sorted(blocks):
            part = slice(b * LANES, (b + 1) * LANES)
            value_refs[p][t, :, part] = blocks[b].astype(jnp.bfloat16)
            act = activated(blocks[b], columns_ref[0, 0], mask[:, part])
            acts.append(act)
            if p == pairs - 1:
                send_ref[t, :, part.start - done : part.stop - done] = act
        spread(out_refs[p], t, jnp.concatenate(acts, axis=1), window + 1)


def beyond(halo, place, far, mate, near_values, near_act, columns):
    frames, rows, channels, width = far.shape
    lanes = rounded((2 * rows + halo) * (width // 2 + halo + 1))
    out = jax.ShapeDtypeStruct((PAIR, channels, lanes), jnp.bfloat16)
    shifted = jax.ShapeDtypeStruct((PAIR, 3, channels, rounded((2 * rows + halo - 1) * (width // 2 + halo + 1))), jnp.bfloat16)
    send = jax.ShapeDtypeStruct((PAIR, channels, lanes - near_act[0].shape[2]), jnp.bfloat16)
    pairs = frames // PAIR
    outs = pl.pallas_call(
        functools.partial(far_kernel, halo, pairs),
        out_shape=(out,) * pairs + (shifted,) * pairs + (send,),
        in_specs=[SMEM] + [VMEM] * (4 + pairs),
        out_specs=(VMEM,) * (2 * pairs + 1),
        compiler_params=pltpu.CompilerParams(vmem_limit_bytes=LIMIT),
        cost_estimate=pl.CostEstimate(flops=40 * far.size, bytes_accessed=8 * far.size, transcendentals=2 * far.size),
        name="beyond",
    )(place, far, mate, near_values, columns, *near_act)
    return outs[:pairs], outs[pairs : 2 * pairs], outs[-1]


def conv_kernel(
    layer, last, sends, received, pitch, half, place_ref, shifted_ref, values_ref, w_ref, columns_ref, *refs
):
    scratch = refs[-1:] if received else ()
    outs = refs[received or 1 : len(refs) - len(scratch)]
    if received:
        earlier_ref = scratch[0]
        for t in range(PAIR):
            parts = [ref[t] for ref in refs[:received]]
            spread(earlier_ref, t, parts[0] if received == 1 else jnp.concatenate(parts, axis=1), pitch)
    else:
        earlier_ref = refs[0]
    _, _, channels, lanes = shifted_ref.shape
    chunks = lanes // LANES
    lane = lane_of(LANES)

    def window(t, b):
        taken = [(earlier_ref, t + a) if t + a < PAIR else (shifted_ref, t + a - PAIR) for a in range(3)]
        at = slice(b * LANES, (b + 1) * LANES)
        return jnp.concatenate([ref[j, :, :, at].reshape(3 * channels, LANES) for ref, j in taken], axis=0)

    places = [(t, b) for t in range(PAIR) for b in range(chunks)]
    side = TILE // LANES
    tiles = []
    for n in range(0, len(places), side):
        rhs = jnp.concatenate([window(t, b) for t, b in places[n : n + side]], axis=1)
        tiles.append(jnp.dot(w_ref[...], rhs, preferred_element_type=jnp.float32))
    bias = columns_ref[layer, 1]
    if not last:
        mask = filled(lanes, pitch)
        gain = columns_ref[layer + 1, 0]
    for t in range(PAIR):

        def sums(tap, b):
            tile, at = divmod((t * chunks + b) * LANES, TILE)
            return tiles[tile][tap * channels : (tap + 1) * channels, at : at + LANES]

        totals, acts = [], []
        from_left = 0.0
        from_right = pltpu.roll(sums(2, 0), LANES - 1, 1)
        for b in range(chunks):
            at = slice(b * LANES, (b + 1) * LANES)
            left = pltpu.roll(sums(0, b), 1, 1)
            right = pltpu.roll(sums(2, b + 1), LANES - 1, 1) if b + 1 < chunks else 0.0
            summed = (
                jnp.where(lane == 0, from_left, left) + sums(1, b) + jnp.where(lane == LANES - 1, right, from_right)
            )
            from_left, from_right = left, right
            total = (values_ref[t, :, at].astype(jnp.float32) + summed + bias).astype(jnp.bfloat16)
            totals.append(total.astype(jnp.float32))
            if not last:
                outs[0][t, :, at] = total
                acts.append(activated(totals[-1], gain, mask[:, at]))
                if sends:
                    outs[2][t, :, at] = acts[-1]
        if not last:
            spread(outs[1], t, jnp.concatenate(acts, axis=1), pitch)
        else:
            whole = jnp.concatenate(totals, axis=1)
            halo = pitch - 1 - half
            whole = jnp.where(place_ref[0] == 1, pltpu.roll(whole, lanes - halo, 1), whole)
            left_half = lane < half

            def rows_of(row):
                one = whole if row == 0 else pltpu.roll(whole, lanes - row * pitch, 1)
                two = pltpu.roll(whole, lanes - (row + 1) * pitch + half, 1)
                return jnp.where(left_half, one[:, :LANES], two[:, :LANES])

            outermost, inner = rows_of(0), rows_of(2)
            outer = place_ref[2] == 1
            outs[0][t] = jnp.where(outer, outermost, inner).astype(jnp.bfloat16)
            outs[1][t] = jnp.where(outer, inner, outermost).astype(jnp.bfloat16)


def conv(layer, last, sends, received, pitch, rows_left, half, place, earlier, shifted, values, weight, columns):
    _, _, channels, lanes = shifted.shape
    if last:
        out_shape = (jax.ShapeDtypeStruct((PAIR, channels, LANES), jnp.bfloat16),) * 2
    else:
        out_shape = (
            jax.ShapeDtypeStruct((PAIR, channels, lanes), jnp.bfloat16),
            jax.ShapeDtypeStruct((PAIR, 3, channels, rounded((rows_left - 1) * pitch)), jnp.bfloat16),
        )
        out_shape += out_shape[:1] * sends
    return pl.pallas_call(
        functools.partial(conv_kernel, layer, last, sends, received, pitch, half),
        out_shape=out_shape,
        in_specs=[SMEM] + [VMEM] * (4 + len(earlier)),
        out_specs=(VMEM,) * len(out_shape),
        scratch_shapes=[pltpu.VMEM((PAIR, 3, channels, lanes), jnp.bfloat16)] * (received > 0),
        compiler_params=pltpu.CompilerParams(vmem_limit_bytes=LIMIT),
        cost_estimate=pl.CostEstimate(
            flops=54 * channels * channels * PAIR * lanes,
            bytes_accessed=2 * weight.size,
            transcendentals=PAIR * channels * lanes,
        ),
        name=f"conv_{layer}",
    )(place, shifted, values, weight, columns, *earlier)


def join_kernel(place_ref, *refs):
    out_ref = refs[-1]
    kept, got = refs[: len(refs) // 2], refs[len(refs) // 2 : -1]
    _, rows, _, width = out_ref.shape
    half = width // 2
    first, group = place_ref[0] == 0, place_ref[1]
    left_half = lane_of(width) < half
    for p in range(len(kept)):
        for t in range(PAIR):
            mine, theirs = kept[p][t].astype(jnp.float32), got[p][t].astype(jnp.float32)
            left, right = jnp.where(first, mine, theirs), jnp.where(first, theirs, mine)
            lines = (
                jnp.where(left_half, left, pltpu.roll(right, half, 1)),
                jnp.where(left_half, pltpu.roll(left, half, 1), right),
            )
            for j in range(rows):
                out_ref[PAIR * p + t, j + group * (rows - 1 - 2 * j)] = lines[j].astype(jnp.bfloat16)


def join(place, kept, got, shape):
    return pl.pallas_call(
        join_kernel,
        out_shape=jax.ShapeDtypeStruct(shape, jnp.bfloat16),
        in_specs=[SMEM] + [VMEM] * (2 * len(kept)),
        out_specs=VMEM,
        compiler_params=pltpu.CompilerParams(vmem_limit_bytes=LIMIT),
        name="join",
    )(place, *kept, *got)


def on_device(latents, conv_weight, norm_gains, biases):
    layers = conv_weight.shape[0]
    frames, rows, channels, width = latents.shape
    strips, blocks = lax.axis_size("rows"), lax.axis_size("tm")
    assert strips == 4 and rows == 2 and frames % PAIR == 0 and width == LANES
    strip = lax.axis_index("rows").astype(jnp.int32)
    core, group = strip & 1, strip >> 1
    place = jnp.stack([core, group, (core == group).astype(jnp.int32)])

    def mate_of(block):
        return lax.ppermute(block, "rows", [(i, i ^ 1) for i in range(strips)])

    def earlier_of(block):
        return lax.ppermute(block, "tm", [(i, i + 1) for i in range(blocks - 1)])

    far = lax.ppermute(latents, "rows", [(i, i ^ 2) for i in range(strips)])
    mate = mate_of(latents)
    row_values = jnp.concatenate([norm_gains, biases], axis=0)
    weight, (columns,) = weights(0, layers - 1, place, conv_weight, row_values)
    near_values, near_act = near(layers, place, latents, mate, row_values)
    halo_near = earlier_of(near_act[-1])
    far, weight, columns, near_values, near_act, halo_near = lax.optimization_barrier(
        (far, weight, columns, near_values, near_act, halo_near)
    )
    last_weight, _ = weights(layers - 1, 1, place, conv_weight)
    far_mate, last_weight = lax.optimization_barrier((mate_of(far), last_weight))
    weight = weight + last_weight
    values, shifted, send = beyond(layers, place, far, far_mate, near_values, near_act, columns)
    halo = (halo_near, earlier_of(send))
    pitch = width // 2 + layers + 1
    pairs = frames // PAIR
    for layer in range(layers):
        last = layer == layers - 1
        rows_left = 2 * rows + layers - 1 - layer
        results = [None] * pairs
        for p in reversed(range(pairs)):
            earlier, received = ((shifted[p - 1],), 0) if p else (halo, len(halo))
            results[p] = conv(
                layer,
                last,
                p == pairs - 1,
                received,
                pitch,
                rows_left,
                width // 2,
                place,
                earlier,
                shifted[p],
                values[p],
                weight[layer],
                columns,
            )
        values, shifted = [r[0] for r in results], [r[1] for r in results]
        if not last:
            halo = (earlier_of(results[-1][2]),)
    got = [mate_of(send) for send in shifted]
    return join(place, values, got, latents.shape)


def solution(mesh):
    in_specs = (P(("clips", "tm"), "rows", None, None), P(), P(), P())
    out_specs = P(("clips", "tm"), "rows", None, None)
    return jax.shard_map(on_device, mesh=mesh, in_specs=in_specs, out_specs=out_specs, check_vma=False)
```

```python
import functools

import jax
import jax.numpy as jnp
from jax import lax
from jax.experimental import pallas as pl
from jax.experimental.pallas import tpu as pltpu
from jax.sharding import PartitionSpec as P

EPSILON = 1e-06
PAIR = 2
LANES = 128
TILE = 256
VMEM = pl.BlockSpec(memory_space=pltpu.VMEM)
SMEM = pl.BlockSpec(memory_space=pltpu.SMEM)
ANY = pl.BlockSpec(memory_space=pl.ANY)
LIMIT = 24 * 1024 * 1024
LARGE = 44 * 1024 * 1024


def rounded(lanes):
    return -(-lanes // LANES) * LANES


def column(row):
    return jnp.transpose(jnp.broadcast_to(row, (LANES, row.shape[1])))


def lane_of(lanes):
    return lax.broadcasted_iota(jnp.int32, (1, lanes), 1)


def filled(lanes, pitch):
    lane = lane_of(lanes)
    gaps = lane < 0
    for end in range(pitch - 1, lanes, pitch):
        gaps = gaps | (lane == end)
    return jnp.where(gaps, 0.0, 1.0)


def activated(values, gain, mask):
    squares = jnp.mean(values * values, axis=0, keepdims=True)
    halved = values * (lax.rsqrt(squares + EPSILON) * (0.5 * mask)) * gain
    return (halved + halved * jnp.tanh(halved)).astype(jnp.bfloat16)


def fetched(pairs, sems):
    copies = [pltpu.make_async_copy(source, to, sems.at[i]) for i, (source, to) in enumerate(pairs)]
    for copy in copies:
        copy.start()
    return copies


def weights_kernel(first, columns, place_ref, w_ref, *refs):
    outs, held_ref, sems = refs[columns:-2], refs[-2], refs[-1]
    count, _, channels_out, ins = held_ref.shape
    copies = fetched([(w_ref.at[first + i], held_ref.at[i]) for i in range(count)], sems)
    flipped = place_ref[1]
    if columns:
        rows_ref = refs[0]
        layers = rows_ref.shape[0] // 2
        for layer in range(layers):
            outs[-1][layer, 0] = column(rows_ref[layer : layer + 1, :])
            outs[-1][layer, 1] = column(rows_ref[layers + layer : layers + layer + 1, :])
    for i in range(count):
        copies[i].wait()
        for time_tap in range(3):
            for row_tap in range(3):
                source = 9 * time_tap + 3 * (row_tap + flipped * (2 - 2 * row_tap))
                at = (3 * time_tap + row_tap) * ins
                outs[i][:, at : at + ins] = held_ref[i, pl.ds(source, 3)].reshape(3 * channels_out, ins)


def weights(first, count, place, conv_weight, *rows):
    layers, taps, outs, ins = conv_weight.shape
    one = jax.ShapeDtypeStruct((3 * outs, 9 * ins), conv_weight.dtype)
    columns = len(rows)
    results = pl.pallas_call(
        functools.partial(weights_kernel, first, columns),
        out_shape=(one,) * count + (jax.ShapeDtypeStruct((layers, 2, outs, LANES), jnp.float32),) * columns,
        in_specs=[SMEM, ANY] + [VMEM] * columns,
        out_specs=(VMEM,) * (count + columns),
        scratch_shapes=[
            pltpu.VMEM((count, taps, outs, ins), conv_weight.dtype),
            pltpu.SemaphoreType.DMA((count,)),
        ],
        compiler_params=pltpu.CompilerParams(vmem_limit_bytes=LARGE),
        cost_estimate=pl.CostEstimate(
            flops=0, bytes_accessed=4 * conv_weight.size * count // layers, transcendentals=0
        ),
        name="weights",
    )(place, conv_weight, *rows)
    return list(results[:count]), results[count:]


def spread(out_ref, index, act, pitch):
    lanes = out_ref.shape[3]
    above = pltpu.roll(act, pitch, 1)
    below = pltpu.roll(act, act.shape[1] - pitch, 1)
    edge = jnp.where(lane_of(LANES) < pitch, 0.0, above[:, :LANES].astype(jnp.float32))
    out_ref[index, 0, :, :LANES] = edge.astype(jnp.bfloat16)
    out_ref[index, 0, :, LANES:] = above[:, LANES:lanes]
    out_ref[index, 1] = act[:, :lanes]
    out_ref[index, 2] = below[:, :lanes]


def placed(blocks, place_ref, row, window, line):
    pitch, width = window + 1, line.shape[1]
    lane = lane_of(LANES)
    block, low = divmod(row * pitch, LANES)
    shift = lax.rem(low + LANES - place_ref[0] * (width - window), LANES)
    turned = pltpu.roll(line, shift, 1)
    here = (lane >= low) & (lane < low + window)
    blocks[block] = blocks.get(block, 0.0) + jnp.where(here, turned, 0.0)
    if low + window > LANES:
        blocks[block + 1] = blocks.get(block + 1, 0.0) + jnp.where(lane < low + window - LANES, turned, 0.0)


def near_kernel(halo, place_ref, own_ref, mate_ref, gains_ref, values_ref, *act_refs):
    frames, rows, _, width = own_ref.shape
    window = width // 2 + halo
    group, outer = place_ref[1], place_ref[2] == 1
    gain = column(gains_ref[0:1, :])
    done = act_refs[0].shape[2]
    mask = filled(done, window + 1)
    for f in range(frames):
        blocks = {}
        for row in range(2 * rows):
            at = row % rows
            index = at + group * (rows - 1 - 2 * at)
            one, two = (own_ref, mate_ref) if row < rows else (mate_ref, own_ref)
            line = jnp.where(outer, one[f, index], two[f, index]).astype(jnp.float32)
            placed(blocks, place_ref, row, window, line)
        for b in blocks:
            part = slice(b * LANES, (b + 1) * LANES)
            values_ref[f, :, part] = blocks[b].astype(jnp.bfloat16)
            if part.stop <= done:
                act_refs[f // PAIR][f % PAIR, :, part] = activated(blocks[b], gain, mask[:, part])


def near(halo, place, own, mate, gains):
    frames, rows, channels, width = own.shape
    lanes = 2 * rows * (width // 2 + halo + 1)
    pairs = frames // PAIR
    outs = pl.pallas_call(
        functools.partial(near_kernel, halo),
        out_shape=(jax.ShapeDtypeStruct((frames, channels, rounded(lanes)), jnp.bfloat16),)
        + (jax.ShapeDtypeStruct((PAIR, channels, lanes // LANES * LANES), jnp.bfloat16),) * pairs,
        in_specs=[SMEM] + [VMEM] * 3,
        out_specs=(VMEM,) * (1 + pairs),
        compiler_params=pltpu.CompilerParams(vmem_limit_bytes=LIMIT),
        cost_estimate=pl.CostEstimate(flops=40 * own.size, bytes_accessed=8 * own.size, transcendentals=2 * own.size),
        name="near",
    )(place, own, mate, gains)
    return outs[0], outs[1:]


def far_kernel(halo, pairs, place_ref, far_ref, mate_ref, near_ref, columns_ref, *refs):
    act_refs, value_refs, out_refs, send_ref = refs[:pairs], refs[pairs : 2 * pairs], refs[2 * pairs : -1], refs[-1]
    frames, rows, _, width = far_ref.shape
    window = width // 2 + halo
    group, outer = place_ref[1], place_ref[2] == 1
    lanes, done = value_refs[0].shape[2], act_refs[0].shape[2]
    mask = filled(lanes, window + 1)
    for f in range(frames):
        p, t = divmod(f, PAIR)
        value_refs[p][t, :, :done] = near_ref[f, :, :done]
        acts = [act_refs[p][t]]
        blocks = {done // LANES: near_ref[f, :, done:].astype(jnp.float32)}
        for row in range(2 * rows, 2 * rows + halo):
            local = 4 * rows - 1 - row
            at = local % rows
            index = at + (1 - group) * (rows - 1 - 2 * at)
            one, two = (mate_ref, far_ref) if local < rows else (far_ref, mate_ref)
            line = jnp.where(outer, one[f, index], two[f, index]).astype(jnp.float32)
            placed(blocks, place_ref, row, window, line)
        for b in sorted(blocks):
            part = slice(b * LANES, (b + 1) * LANES)
            value_refs[p][t, :, part] = blocks[b].astype(jnp.bfloat16)
            act = activated(blocks[b], columns_ref[0, 0], mask[:, part])
            acts.append(act)
            if p == pairs - 1:
                send_ref[t, :, part.start - done : part.stop - done] = act
        spread(out_refs[p], t, jnp.concatenate(acts, axis=1), window + 1)


def beyond(halo, place, far, mate, near_values, near_act, columns):
    frames, rows, channels, width = far.shape
    lanes = rounded((2 * rows + halo) * (width // 2 + halo + 1))
    out = jax.ShapeDtypeStruct((PAIR, channels, lanes), jnp.bfloat16)
    shifted = jax.ShapeDtypeStruct((PAIR, 3, channels, rounded((2 * rows + halo - 1) * (width // 2 + halo + 1))), jnp.bfloat16)
    send = jax.ShapeDtypeStruct((PAIR, channels, lanes - near_act[0].shape[2]), jnp.bfloat16)
    pairs = frames // PAIR
    outs = pl.pallas_call(
        functools.partial(far_kernel, halo, pairs),
        out_shape=(out,) * pairs + (shifted,) * pairs + (send,),
        in_specs=[SMEM] + [VMEM] * (4 + pairs),
        out_specs=(VMEM,) * (2 * pairs + 1),
        compiler_params=pltpu.CompilerParams(vmem_limit_bytes=LIMIT),
        cost_estimate=pl.CostEstimate(flops=40 * far.size, bytes_accessed=8 * far.size, transcendentals=2 * far.size),
        name="beyond",
    )(place, far, mate, near_values, columns, *near_act)
    return outs[:pairs], outs[pairs : 2 * pairs], outs[-1]


def conv_kernel(
    layer, last, sends, received, pitch, half, place_ref, shifted_ref, values_ref, w_ref, columns_ref, *refs
):
    scratch = refs[-1:] if received else ()
    outs = refs[received or 1 : len(refs) - len(scratch)]
    if received:
        earlier_ref = scratch[0]
        for t in range(PAIR):
            parts = [ref[t] for ref in refs[:received]]
            spread(earlier_ref, t, parts[0] if received == 1 else jnp.concatenate(parts, axis=1), pitch)
    else:
        earlier_ref = refs[0]
    _, _, channels, lanes = shifted_ref.shape
    chunks = lanes // LANES
    lane = lane_of(LANES)

    def window(t, b):
        taken = [(earlier_ref, t + a) if t + a < PAIR else (shifted_ref, t + a - PAIR) for a in range(3)]
        at = slice(b * LANES, (b + 1) * LANES)
        return jnp.concatenate([ref[j, :, :, at].reshape(3 * channels, LANES) for ref, j in taken], axis=0)

    places = [(t, b) for t in range(PAIR) for b in range(chunks)]
    side = TILE // LANES
    tiles = []
    bias = columns_ref[layer, 1]
    if not last:
        mask = filled(lanes, pitch)
        gain = columns_ref[layer + 1, 0]

    def sums(t, tap, b):
        tile, at = divmod((t * chunks + b) * LANES, TILE)
        return tiles[tile][tap * channels : (tap + 1) * channels, at : at + LANES]

    def finish(t):
        totals, acts = [], []
        from_left = 0.0
        from_right = pltpu.roll(sums(t, 2, 0), LANES - 1, 1)
        for b in range(chunks):
            at = slice(b * LANES, (b + 1) * LANES)
            left = pltpu.roll(sums(t, 0, b), 1, 1)
            right = pltpu.roll(sums(t, 2, b + 1), LANES - 1, 1) if b + 1 < chunks else 0.0
            summed = (
                jnp.where(lane == 0, from_left, left) + sums(t, 1, b) + jnp.where(lane == LANES - 1, right, from_right)
            )
            from_left, from_right = left, right
            total = (values_ref[t, :, at].astype(jnp.float32) + summed + bias).astype(jnp.bfloat16)
            totals.append(total.astype(jnp.float32))
            if not last:
                outs[0][t, :, at] = total
                acts.append(activated(totals[-1], gain, mask[:, at]))
                if sends:
                    outs[2][t, :, at] = acts[-1]
        if not last:
            spread(outs[1], t, jnp.concatenate(acts, axis=1), pitch)
            return
        whole = jnp.concatenate(totals, axis=1)
        halo = pitch - 1 - half
        whole = jnp.where(place_ref[0] == 1, pltpu.roll(whole, lanes - halo, 1), whole)
        left_half = lane < half

        def rows_of(row):
            one = whole if row == 0 else pltpu.roll(whole, lanes - row * pitch, 1)
            two = pltpu.roll(whole, lanes - (row + 1) * pitch + half, 1)
            return jnp.where(left_half, one[:, :LANES], two[:, :LANES])

        outermost, inner = rows_of(0), rows_of(2)
        outer = place_ref[2] == 1
        outs[0][t] = jnp.where(outer, outermost, inner).astype(jnp.bfloat16)
        outs[1][t] = jnp.where(outer, inner, outermost).astype(jnp.bfloat16)

    finished = 0
    for n in range(0, len(places), side):
        rhs = jnp.concatenate([window(t, b) for t, b in places[n : n + side]], axis=1)
        tiles.append(jnp.dot(w_ref[...], rhs, preferred_element_type=jnp.float32))
        while finished < PAIR and (finished + 1) * chunks <= n + side:
            finish(finished)
            finished += 1


def conv(layer, last, sends, received, pitch, rows_left, half, place, earlier, shifted, values, weight, columns):
    _, _, channels, lanes = shifted.shape
    if last:
        out_shape = (jax.ShapeDtypeStruct((PAIR, channels, LANES), jnp.bfloat16),) * 2
    else:
        out_shape = (
            jax.ShapeDtypeStruct((PAIR, channels, lanes), jnp.bfloat16),
            jax.ShapeDtypeStruct((PAIR, 3, channels, rounded((rows_left - 1) * pitch)), jnp.bfloat16),
        )
        out_shape += out_shape[:1] * sends
    return pl.pallas_call(
        functools.partial(conv_kernel, layer, last, sends, received, pitch, half),
        out_shape=out_shape,
        in_specs=[SMEM] + [VMEM] * (4 + len(earlier)),
        out_specs=(VMEM,) * len(out_shape),
        scratch_shapes=[pltpu.VMEM((PAIR, 3, channels, lanes), jnp.bfloat16)] * (received > 0),
        compiler_params=pltpu.CompilerParams(vmem_limit_bytes=LIMIT),
        cost_estimate=pl.CostEstimate(
            flops=54 * channels * channels * PAIR * lanes,
            bytes_accessed=2 * weight.size,
            transcendentals=PAIR * channels * lanes,
        ),
        name=f"conv_{layer}",
    )(place, shifted, values, weight, columns, *earlier)


def join_kernel(pair, place_ref, kept_ref, got_ref, *refs):
    out_ref, lines_ref, sem = refs[-3:]
    _, rows, _, width = lines_ref.shape
    half = width // 2
    first, group = place_ref[0] == 0, place_ref[1]
    left_half = lane_of(width) < half
    for t in range(PAIR):
        mine, theirs = kept_ref[t].astype(jnp.float32), got_ref[t].astype(jnp.float32)
        left, right = jnp.where(first, mine, theirs), jnp.where(first, theirs, mine)
        lines = (
            jnp.where(left_half, left, pltpu.roll(right, half, 1)),
            jnp.where(left_half, pltpu.roll(left, half, 1), right),
        )
        for j in range(rows):
            lines_ref[t, j + group * (rows - 1 - 2 * j)] = lines[j].astype(jnp.bfloat16)
    copy = pltpu.make_async_copy(lines_ref, out_ref.at[pl.ds(PAIR * pair, PAIR)], sem)
    copy.start()
    copy.wait()


def join(place, pair, kept, got, shape, *so_far):
    return pl.pallas_call(
        functools.partial(join_kernel, pair),
        out_shape=jax.ShapeDtypeStruct(shape, jnp.bfloat16),
        in_specs=[SMEM, VMEM, VMEM] + [ANY] * len(so_far),
        out_specs=ANY,
        scratch_shapes=[pltpu.VMEM((PAIR,) + shape[1:], jnp.bfloat16), pltpu.SemaphoreType.DMA],
        input_output_aliases={3: 0} if so_far else {},
        compiler_params=pltpu.CompilerParams(vmem_limit_bytes=LIMIT),
        name="join",
    )(place, kept, got, *so_far)


def on_device(latents, conv_weight, norm_gains, biases):
    layers = conv_weight.shape[0]
    frames, rows, channels, width = latents.shape
    strips, blocks = lax.axis_size("rows"), lax.axis_size("tm")
    assert strips == 4 and rows == 2 and frames % PAIR == 0 and width == LANES
    strip = lax.axis_index("rows").astype(jnp.int32)
    core, group = strip & 1, strip >> 1
    place = jnp.stack([core, group, (core == group).astype(jnp.int32)])

    def mate_of(block):
        return lax.ppermute(block, "rows", [(i, i ^ 1) for i in range(strips)])

    def earlier_of(block):
        return lax.ppermute(block, "tm", [(i, i + 1) for i in range(blocks - 1)])

    far = lax.ppermute(latents, "rows", [(i, i ^ 2) for i in range(strips)])
    mate = mate_of(latents)
    row_values = jnp.concatenate([norm_gains, biases], axis=0)
    weight, (columns,) = weights(0, layers, place, conv_weight, row_values)
    near_values, near_act = near(layers, place, latents, mate, row_values)
    halo_near = earlier_of(near_act[-1])
    far, weight, columns, near_values, near_act, halo_near = lax.optimization_barrier(
        (far, weight, columns, near_values, near_act, halo_near)
    )
    values, shifted, send = beyond(layers, place, far, mate_of(far), near_values, near_act, columns)
    halo = (halo_near, earlier_of(send))
    pitch = width // 2 + layers + 1
    pairs = frames // PAIR
    for layer in range(layers):
        last = layer == layers - 1
        rows_left = 2 * rows + layers - 1 - layer
        results = [None] * pairs
        for p in reversed(range(pairs)):
            earlier, received = ((shifted[p - 1],), 0) if p else (halo, len(halo))
            results[p] = conv(
                layer,
                last,
                p == pairs - 1,
                received,
                pitch,
                rows_left,
                width // 2,
                place,
                earlier,
                shifted[p],
                values[p],
                weight[layer],
                columns,
            )
        values, shifted = [r[0] for r in results], [r[1] for r in results]
        if not last:
            halo = (earlier_of(results[-1][2]),)
    result = ()
    for p in reversed(range(pairs)):
        result = (join(place, p, values[p], mate_of(shifted[p]), latents.shape, *result),)
    return result[0]


def solution(mesh):
    in_specs = (P(("clips", "tm"), "rows", None, None), P(), P(), P())
    out_specs = P(("clips", "tm"), "rows", None, None)
    return jax.shard_map(on_device, mesh=mesh, in_specs=in_specs, out_specs=out_specs, check_vma=False)
```

```python
import functools

import jax
import jax.numpy as jnp
from jax import lax
from jax.experimental import pallas as pl
from jax.experimental.pallas import tpu as pltpu
from jax.sharding import PartitionSpec as P

EPSILON = 1e-06
PAIR = 2
LANES = 128
TILE = 256
VMEM = pl.BlockSpec(memory_space=pltpu.VMEM)
ANY = pl.BlockSpec(memory_space=pl.ANY)
LIMIT = 24 * 1024 * 1024
LARGE = 44 * 1024 * 1024


def place():
    strip = lax.axis_index("rows").astype(jnp.int32)
    core, group = strip & 1, strip >> 1
    return core, group, core == group


def rounded(lanes):
    return -(-lanes // LANES) * LANES


def column(row):
    return jnp.transpose(jnp.broadcast_to(row, (LANES, row.shape[1])))


def lane_of(lanes):
    return lax.broadcasted_iota(jnp.int32, (1, lanes), 1)


def filled(lanes, pitch):
    lane = lane_of(lanes)
    gaps = lane < 0
    for end in range(pitch - 1, lanes, pitch):
        gaps = gaps | (lane == end)
    return jnp.where(gaps, 0.0, 1.0)


def activated(values, gain, mask):
    squares = jnp.mean(values * values, axis=0, keepdims=True)
    halved = values * (lax.rsqrt(squares + EPSILON) * (0.5 * mask)) * gain
    return (halved + halved * jnp.tanh(halved)).astype(jnp.bfloat16)


def fetched(pairs, sems):
    copies = [pltpu.make_async_copy(source, to, sems.at[i]) for i, (source, to) in enumerate(pairs)]
    for copy in copies:
        copy.start()
    return copies


def weights_kernel(first, columns, w_ref, *refs):
    outs, held_ref, sems = refs[columns:-2], refs[-2], refs[-1]
    count, _, channels_out, ins = held_ref.shape
    copies = fetched([(w_ref.at[first + i], held_ref.at[i]) for i in range(count)], sems)
    _, flipped, _ = place()
    if columns:
        rows_ref = refs[0]
        layers = rows_ref.shape[0] // 2
        for layer in range(layers):
            outs[-1][layer, 0] = column(rows_ref[layer : layer + 1, :])
            outs[-1][layer, 1] = column(rows_ref[layers + layer : layers + layer + 1, :])
    for i in range(count):
        copies[i].wait()
        for time_tap in range(3):
            for row_tap in range(3):
                source = 9 * time_tap + 3 * (row_tap + flipped * (2 - 2 * row_tap))
                at = (3 * time_tap + row_tap) * ins
                outs[i][:, at : at + ins] = held_ref[i, pl.ds(source, 3)].reshape(3 * channels_out, ins)


def weights(first, count, conv_weight, *rows):
    layers, taps, outs, ins = conv_weight.shape
    one = jax.ShapeDtypeStruct((3 * outs, 9 * ins), conv_weight.dtype)
    columns = len(rows)
    results = pl.pallas_call(
        functools.partial(weights_kernel, first, columns),
        out_shape=(one,) * count + (jax.ShapeDtypeStruct((layers, 2, outs, LANES), jnp.float32),) * columns,
        in_specs=[ANY] + [VMEM] * columns,
        out_specs=(VMEM,) * (count + columns),
        scratch_shapes=[
            pltpu.VMEM((count, taps, outs, ins), conv_weight.dtype),
            pltpu.SemaphoreType.DMA((count,)),
        ],
        compiler_params=pltpu.CompilerParams(vmem_limit_bytes=LARGE),
        cost_estimate=pl.CostEstimate(
            flops=0, bytes_accessed=4 * conv_weight.size * count // layers, transcendentals=0
        ),
        name="weights",
    )(conv_weight, *rows)
    return list(results[:count]), results[count:]


def spread(out_ref, index, act, pitch):
    lanes = out_ref.shape[3]
    above = pltpu.roll(act, pitch, 1)
    below = pltpu.roll(act, act.shape[1] - pitch, 1)
    edge = jnp.where(lane_of(LANES) < pitch, 0.0, above[:, :LANES].astype(jnp.float32))
    out_ref[index, 0, :, :LANES] = edge.astype(jnp.bfloat16)
    out_ref[index, 0, :, LANES:] = above[:, LANES:lanes]
    out_ref[index, 1] = act[:, :lanes]
    out_ref[index, 2] = below[:, :lanes]


def placed(blocks, core, row, window, line):
    pitch, width = window + 1, line.shape[1]
    lane = lane_of(LANES)
    block, low = divmod(row * pitch, LANES)
    shift = lax.rem(low + LANES - core * (width - window), LANES)
    turned = pltpu.roll(line, shift, 1)
    here = (lane >= low) & (lane < low + window)
    blocks[block] = blocks.get(block, 0.0) + jnp.where(here, turned, 0.0)
    if low + window > LANES:
        blocks[block + 1] = blocks.get(block + 1, 0.0) + jnp.where(lane < low + window - LANES, turned, 0.0)


def near_kernel(halo, own_ref, mate_ref, gains_ref, values_ref, *act_refs):
    frames, rows, _, width = own_ref.shape
    window = width // 2 + halo
    core, group, outer = place()
    gain = column(gains_ref[0:1, :])
    done = act_refs[0].shape[2]
    mask = filled(done, window + 1)
    for f in range(frames):
        blocks = {}
        for row in range(2 * rows):
            at = row % rows
            index = at + group * (rows - 1 - 2 * at)
            one, two = (own_ref, mate_ref) if row < rows else (mate_ref, own_ref)
            line = jnp.where(outer, one[f, index], two[f, index]).astype(jnp.float32)
            placed(blocks, core, row, window, line)
        for b in blocks:
            part = slice(b * LANES, (b + 1) * LANES)
            values_ref[f, :, part] = blocks[b].astype(jnp.bfloat16)
            if part.stop <= done:
                act_refs[f // PAIR][f % PAIR, :, part] = activated(blocks[b], gain, mask[:, part])


def near(halo, own, mate, gains):
    frames, rows, channels, width = own.shape
    lanes = 2 * rows * (width // 2 + halo + 1)
    pairs = frames // PAIR
    outs = pl.pallas_call(
        functools.partial(near_kernel, halo),
        out_shape=(jax.ShapeDtypeStruct((frames, channels, rounded(lanes)), jnp.bfloat16),)
        + (jax.ShapeDtypeStruct((PAIR, channels, lanes // LANES * LANES), jnp.bfloat16),) * pairs,
        in_specs=[VMEM] * 3,
        out_specs=(VMEM,) * (1 + pairs),
        compiler_params=pltpu.CompilerParams(vmem_limit_bytes=LIMIT),
        cost_estimate=pl.CostEstimate(flops=40 * own.size, bytes_accessed=8 * own.size, transcendentals=2 * own.size),
        name="near",
    )(own, mate, gains)
    return outs[0], outs[1:]


def far_kernel(halo, pairs, far_ref, mate_ref, near_ref, columns_ref, *refs):
    act_refs, value_refs, out_refs, send_ref = refs[:pairs], refs[pairs : 2 * pairs], refs[2 * pairs : -1], refs[-1]
    frames, rows, _, width = far_ref.shape
    window = width // 2 + halo
    core, group, outer = place()
    lanes, done = value_refs[0].shape[2], act_refs[0].shape[2]
    mask = filled(lanes, window + 1)
    for f in range(frames):
        p, t = divmod(f, PAIR)
        value_refs[p][t, :, :done] = near_ref[f, :, :done]
        acts = [act_refs[p][t]]
        blocks = {done // LANES: near_ref[f, :, done:].astype(jnp.float32)}
        for row in range(2 * rows, 2 * rows + halo):
            local = 4 * rows - 1 - row
            at = local % rows
            index = at + (1 - group) * (rows - 1 - 2 * at)
            one, two = (mate_ref, far_ref) if local < rows else (far_ref, mate_ref)
            line = jnp.where(outer, one[f, index], two[f, index]).astype(jnp.float32)
            placed(blocks, core, row, window, line)
        for b in sorted(blocks):
            part = slice(b * LANES, (b + 1) * LANES)
            value_refs[p][t, :, part] = blocks[b].astype(jnp.bfloat16)
            act = activated(blocks[b], columns_ref[0, 0], mask[:, part])
            acts.append(act)
            if p == pairs - 1:
                send_ref[t, :, part.start - done : part.stop - done] = act
        spread(out_refs[p], t, jnp.concatenate(acts, axis=1), window + 1)


def beyond(halo, far, mate, near_values, near_act, columns):
    frames, rows, channels, width = far.shape
    lanes = rounded((2 * rows + halo) * (width // 2 + halo + 1))
    out = jax.ShapeDtypeStruct((PAIR, channels, lanes), jnp.bfloat16)
    shifted = jax.ShapeDtypeStruct((PAIR, 3, channels, rounded((2 * rows + halo - 1) * (width // 2 + halo + 1))), jnp.bfloat16)
    send = jax.ShapeDtypeStruct((PAIR, channels, lanes - near_act[0].shape[2]), jnp.bfloat16)
    pairs = frames // PAIR
    outs = pl.pallas_call(
        functools.partial(far_kernel, halo, pairs),
        out_shape=(out,) * pairs + (shifted,) * pairs + (send,),
        in_specs=[VMEM] * (4 + pairs),
        out_specs=(VMEM,) * (2 * pairs + 1),
        compiler_params=pltpu.CompilerParams(vmem_limit_bytes=LIMIT),
        cost_estimate=pl.CostEstimate(flops=40 * far.size, bytes_accessed=8 * far.size, transcendentals=2 * far.size),
        name="beyond",
    )(far, mate, near_values, columns, *near_act)
    return outs[:pairs], outs[pairs : 2 * pairs], outs[-1]


def conv_kernel(
    layer, last, sends, received, pitch, half, shifted_ref, values_ref, w_ref, columns_ref, *refs
):
    scratch = refs[-1:] if received else ()
    outs = refs[received or 1 : len(refs) - len(scratch)]
    if received:
        earlier_ref = scratch[0]
        for t in range(PAIR):
            parts = [ref[t] for ref in refs[:received]]
            spread(earlier_ref, t, parts[0] if received == 1 else jnp.concatenate(parts, axis=1), pitch)
    else:
        earlier_ref = refs[0]
    _, _, channels, lanes = shifted_ref.shape
    chunks = lanes // LANES
    lane = lane_of(LANES)

    def window(t, b):
        taken = [(earlier_ref, t + a) if t + a < PAIR else (shifted_ref, t + a - PAIR) for a in range(3)]
        at = slice(b * LANES, (b + 1) * LANES)
        return jnp.concatenate([ref[j, :, :, at].reshape(3 * channels, LANES) for ref, j in taken], axis=0)

    places = [(t, b) for t in range(PAIR) for b in range(chunks)]
    side = TILE // LANES
    tiles = []
    bias = columns_ref[layer, 1]
    if not last:
        mask = filled(lanes, pitch)
        gain = columns_ref[layer + 1, 0]

    def sums(t, tap, b):
        tile, at = divmod((t * chunks + b) * LANES, TILE)
        return tiles[tile][tap * channels : (tap + 1) * channels, at : at + LANES]

    def finish(t):
        totals, acts = [], []
        from_left = 0.0
        from_right = pltpu.roll(sums(t, 2, 0), LANES - 1, 1)
        for b in range(chunks):
            at = slice(b * LANES, (b + 1) * LANES)
            left = pltpu.roll(sums(t, 0, b), 1, 1)
            right = pltpu.roll(sums(t, 2, b + 1), LANES - 1, 1) if b + 1 < chunks else 0.0
            summed = (
                jnp.where(lane == 0, from_left, left) + sums(t, 1, b) + jnp.where(lane == LANES - 1, right, from_right)
            )
            from_left, from_right = left, right
            total = (values_ref[t, :, at].astype(jnp.float32) + summed + bias).astype(jnp.bfloat16)
            totals.append(total.astype(jnp.float32))
            if not last:
                outs[0][t, :, at] = total
                acts.append(activated(totals[-1], gain, mask[:, at]))
                if sends:
                    outs[2][t, :, at] = acts[-1]
        if not last:
            spread(outs[1], t, jnp.concatenate(acts, axis=1), pitch)
            return
        whole = jnp.concatenate(totals, axis=1)
        halo = pitch - 1 - half
        core, _, outer = place()
        whole = jnp.where(core == 1, pltpu.roll(whole, lanes - halo, 1), whole)
        left_half = lane < half

        def rows_of(row):
            one = whole if row == 0 else pltpu.roll(whole, lanes - row * pitch, 1)
            two = pltpu.roll(whole, lanes - (row + 1) * pitch + half, 1)
            return jnp.where(left_half, one[:, :LANES], two[:, :LANES])

        outermost, inner = rows_of(0), rows_of(2)
        outs[0][t] = jnp.where(outer, outermost, inner).astype(jnp.bfloat16)
        outs[1][t] = jnp.where(outer, inner, outermost).astype(jnp.bfloat16)

    finished = 0
    for n in range(0, len(places), side):
        rhs = jnp.concatenate([window(t, b) for t, b in places[n : n + side]], axis=1)
        tiles.append(jnp.dot(w_ref[...], rhs, preferred_element_type=jnp.float32))
        while finished < PAIR and (finished + 1) * chunks <= n + side:
            finish(finished)
            finished += 1


def conv(layer, last, sends, received, pitch, rows_left, half, earlier, shifted, values, weight, columns):
    _, _, channels, lanes = shifted.shape
    if last:
        out_shape = (jax.ShapeDtypeStruct((PAIR, channels, LANES), jnp.bfloat16),) * 2
    else:
        out_shape = (
            jax.ShapeDtypeStruct((PAIR, channels, lanes), jnp.bfloat16),
            jax.ShapeDtypeStruct((PAIR, 3, channels, rounded((rows_left - 1) * pitch)), jnp.bfloat16),
        )
        out_shape += out_shape[:1] * sends
    return pl.pallas_call(
        functools.partial(conv_kernel, layer, last, sends, received, pitch, half),
        out_shape=out_shape,
        in_specs=[VMEM] * (4 + len(earlier)),
        out_specs=(VMEM,) * len(out_shape),
        scratch_shapes=[pltpu.VMEM((PAIR, 3, channels, lanes), jnp.bfloat16)] * (received > 0),
        compiler_params=pltpu.CompilerParams(vmem_limit_bytes=LIMIT),
        cost_estimate=pl.CostEstimate(
            flops=54 * channels * channels * PAIR * lanes,
            bytes_accessed=2 * weight.size,
            transcendentals=PAIR * channels * lanes,
        ),
        name=f"conv_{layer}",
    )(shifted, values, weight, columns, *earlier)


def join_kernel(pair, kept_ref, got_ref, *refs):
    out_ref, lines_ref, sem = refs[-3:]
    _, rows, _, width = lines_ref.shape
    half = width // 2
    core, group, _ = place()
    first = core == 0
    left_half = lane_of(width) < half
    for t in range(PAIR):
        mine, theirs = kept_ref[t].astype(jnp.float32), got_ref[t].astype(jnp.float32)
        left, right = jnp.where(first, mine, theirs), jnp.where(first, theirs, mine)
        lines = (
            jnp.where(left_half, left, pltpu.roll(right, half, 1)),
            jnp.where(left_half, pltpu.roll(left, half, 1), right),
        )
        for j in range(rows):
            lines_ref[t, j + group * (rows - 1 - 2 * j)] = lines[j].astype(jnp.bfloat16)
    copy = pltpu.make_async_copy(lines_ref, out_ref.at[pl.ds(PAIR * pair, PAIR)], sem)
    copy.start()
    copy.wait()


def join(pair, kept, got, shape, *so_far):
    return pl.pallas_call(
        functools.partial(join_kernel, pair),
        out_shape=jax.ShapeDtypeStruct(shape, jnp.bfloat16),
        in_specs=[VMEM, VMEM] + [ANY] * len(so_far),
        out_specs=ANY,
        scratch_shapes=[pltpu.VMEM((PAIR,) + shape[1:], jnp.bfloat16), pltpu.SemaphoreType.DMA],
        input_output_aliases={2: 0} if so_far else {},
        compiler_params=pltpu.CompilerParams(vmem_limit_bytes=LIMIT),
        name="join",
    )(kept, got, *so_far)


def on_device(latents, conv_weight, norm_gains, biases):
    layers = conv_weight.shape[0]
    frames, rows, channels, width = latents.shape
    strips, blocks = lax.axis_size("rows"), lax.axis_size("tm")
    assert strips == 4 and rows == 2 and frames % PAIR == 0 and width == LANES

    def mate_of(block):
        return lax.ppermute(block, "rows", [(i, i ^ 1) for i in range(strips)])

    def earlier_of(block):
        return lax.ppermute(block, "tm", [(i, i + 1) for i in range(blocks - 1)])

    far = lax.ppermute(latents, "rows", [(i, i ^ 2) for i in range(strips)])
    mate = mate_of(latents)
    row_values = jnp.concatenate([norm_gains, biases], axis=0)
    weight, (columns,) = weights(0, layers, conv_weight, row_values)
    near_values, near_act = near(layers, latents, mate, row_values)
    halo_near = earlier_of(near_act[-1])
    far, weight, columns, near_values, near_act, halo_near = lax.optimization_barrier(
        (far, weight, columns, near_values, near_act, halo_near)
    )
    values, shifted, send = beyond(layers, far, mate_of(far), near_values, near_act, columns)
    halo = (halo_near, earlier_of(send))
    pitch = width // 2 + layers + 1
    pairs = frames // PAIR
    for layer in range(layers):
        last = layer == layers - 1
        rows_left = 2 * rows + layers - 1 - layer
        results = [None] * pairs
        for p in reversed(range(pairs)):
            earlier, received = ((shifted[p - 1],), 0) if p else (halo, len(halo))
            results[p] = conv(
                layer,
                last,
                p == pairs - 1,
                received,
                pitch,
                rows_left,
                width // 2,
                earlier,
                shifted[p],
                values[p],
                weight[layer],
                columns,
            )
        values, shifted = [r[0] for r in results], [r[1] for r in results]
        if not last:
            halo = (earlier_of(results[-1][2]),)
    result = ()
    for p in reversed(range(pairs)):
        result = (join(p, values[p], mate_of(shifted[p]), latents.shape, *result),)
    return result[0]


def solution(mesh):
    in_specs = (P(("clips", "tm"), "rows", None, None), P(), P(), P())
    out_specs = P(("clips", "tm"), "rows", None, None)
    return jax.shard_map(on_device, mesh=mesh, in_specs=in_specs, out_specs=out_specs, check_vma=False)
```

```python
import functools

import jax
import jax.numpy as jnp
from jax import lax
from jax.experimental import pallas as pl
from jax.experimental.pallas import tpu as pltpu
from jax.sharding import PartitionSpec as P

EPSILON = 1e-06
PAIR = 2
LANES = 128
TILE = 256
IN_FLIGHT = 3
VMEM = pl.BlockSpec(memory_space=pltpu.VMEM)
ANY = pl.BlockSpec(memory_space=pl.ANY)
LIMIT = 24 * 1024 * 1024
LARGE = 44 * 1024 * 1024


def place():
    strip = lax.axis_index("rows").astype(jnp.int32)
    core, group = strip & 1, strip >> 1
    return core, group, core == group


def rounded(lanes):
    return -(-lanes // LANES) * LANES


def column(row):
    return jnp.transpose(jnp.broadcast_to(row, (LANES, row.shape[1])))


def lane_of(lanes):
    return lax.broadcasted_iota(jnp.int32, (1, lanes), 1)


def filled(lanes, pitch):
    lane = lane_of(lanes)
    gaps = lane < 0
    for end in range(pitch - 1, lanes, pitch):
        gaps = gaps | (lane == end)
    return jnp.where(gaps, 0.0, 1.0)


def activated(values, gain, mask):
    squares = jnp.mean(values * values, axis=0, keepdims=True)
    halved = values * (lax.rsqrt(squares + EPSILON) * (0.5 * mask)) * gain
    return (halved + halved * jnp.tanh(halved)).astype(jnp.bfloat16)


def weights_kernel(w_ref, rows_ref, *refs):
    outs, columns_ref, held_ref, sems = refs[:-3], refs[-3], refs[-2], refs[-1]
    layers, taps, channels_out, ins = w_ref.shape
    step = taps // 3
    places = [(layer, time_tap) for layer in range(layers) for time_tap in range(3)]
    copies = []
    for n, (layer, time_tap) in enumerate(places):
        part = pl.ds(step * time_tap, step)
        copies.append(pltpu.make_async_copy(w_ref.at[layer, part], held_ref.at[n], sems.at[n]))
    for copy in copies[:IN_FLIGHT]:
        copy.start()
    _, flipped, _ = place()
    for layer in range(layers):
        columns_ref[layer, 0] = column(rows_ref[layer : layer + 1, :])
        columns_ref[layer, 1] = column(rows_ref[layers + layer : layers + layer + 1, :])
    for n, (layer, time_tap) in enumerate(places):
        copies[n].wait()
        if n + IN_FLIGHT < len(copies):
            copies[n + IN_FLIGHT].start()
        for row_tap in range(3):
            source = 3 * (row_tap + flipped * (2 - 2 * row_tap))
            at = (3 * time_tap + row_tap) * ins
            outs[layer][:, at : at + ins] = held_ref[n, pl.ds(source, 3)].reshape(3 * channels_out, ins)


def weights(conv_weight, rows):
    layers, taps, outs, ins = conv_weight.shape
    one = jax.ShapeDtypeStruct((3 * outs, 9 * ins), conv_weight.dtype)
    results = pl.pallas_call(
        weights_kernel,
        out_shape=(one,) * layers + (jax.ShapeDtypeStruct((layers, 2, outs, LANES), jnp.float32),),
        in_specs=[ANY, VMEM],
        out_specs=(VMEM,) * (layers + 1),
        scratch_shapes=[
            pltpu.VMEM((3 * layers, taps // 3, outs, ins), conv_weight.dtype),
            pltpu.SemaphoreType.DMA((3 * layers,)),
        ],
        compiler_params=pltpu.CompilerParams(vmem_limit_bytes=LARGE),
        cost_estimate=pl.CostEstimate(flops=0, bytes_accessed=4 * conv_weight.size, transcendentals=0),
        name="weights",
    )(conv_weight, rows)
    return results[:-1], results[-1]


def joined(valid):
    rest = valid % LANES
    return rest if 0 < PAIR * rest <= LANES else 0


def spread(out_ref, index, act, pitch):
    lanes = out_ref.shape[3]
    above = pltpu.roll(act, pitch, 1)
    below = pltpu.roll(act, act.shape[1] - pitch, 1)
    edge = jnp.where(lane_of(LANES) < pitch, 0.0, above[:, :LANES].astype(jnp.float32))
    out_ref[index, 0, :, :LANES] = edge.astype(jnp.bfloat16)
    out_ref[index, 0, :, LANES:] = above[:, LANES:lanes]
    out_ref[index, 1] = act[:, :lanes]
    out_ref[index, 2] = below[:, :lanes]


def placed(blocks, core, row, window, line):
    pitch, width = window + 1, line.shape[1]
    lane = lane_of(LANES)
    block, low = divmod(row * pitch, LANES)
    shift = lax.rem(low + LANES - core * (width - window), LANES)
    turned = pltpu.roll(line, shift, 1)
    here = (lane >= low) & (lane < low + window)
    blocks[block] = blocks.get(block, 0.0) + jnp.where(here, turned, 0.0)
    if low + window > LANES:
        blocks[block + 1] = blocks.get(block + 1, 0.0) + jnp.where(lane < low + window - LANES, turned, 0.0)


def near_kernel(halo, own_ref, mate_ref, gains_ref, values_ref, *act_refs):
    frames, rows, _, width = own_ref.shape
    window = width // 2 + halo
    core, group, outer = place()
    gain = column(gains_ref[0:1, :])
    done = act_refs[0].shape[2]
    mask = filled(done, window + 1)
    for f in range(frames):
        blocks = {}
        for row in range(2 * rows):
            at = row % rows
            index = at + group * (rows - 1 - 2 * at)
            one, two = (own_ref, mate_ref) if row < rows else (mate_ref, own_ref)
            line = jnp.where(outer, one[f, index], two[f, index]).astype(jnp.float32)
            placed(blocks, core, row, window, line)
        for b in blocks:
            part = slice(b * LANES, (b + 1) * LANES)
            values_ref[f, :, part] = blocks[b].astype(jnp.bfloat16)
            if part.stop <= done:
                act_refs[f // PAIR][f % PAIR, :, part] = activated(blocks[b], gain, mask[:, part])


def near(halo, own, mate, gains):
    frames, rows, channels, width = own.shape
    lanes = 2 * rows * (width // 2 + halo + 1)
    pairs = frames // PAIR
    outs = pl.pallas_call(
        functools.partial(near_kernel, halo),
        out_shape=(jax.ShapeDtypeStruct((frames, channels, rounded(lanes)), jnp.bfloat16),)
        + (jax.ShapeDtypeStruct((PAIR, channels, lanes // LANES * LANES), jnp.bfloat16),) * pairs,
        in_specs=[VMEM] * 3,
        out_specs=(VMEM,) * (1 + pairs),
        compiler_params=pltpu.CompilerParams(vmem_limit_bytes=LIMIT),
        cost_estimate=pl.CostEstimate(flops=40 * own.size, bytes_accessed=8 * own.size, transcendentals=2 * own.size),
        name="near",
    )(own, mate, gains)
    return outs[0], outs[1:]


def far_kernel(halo, pairs, far_ref, mate_ref, near_ref, columns_ref, *refs):
    act_refs, value_refs, out_refs, send_ref = refs[:pairs], refs[pairs : 2 * pairs], refs[2 * pairs : -1], refs[-1]
    frames, rows, _, width = far_ref.shape
    window = width // 2 + halo
    core, group, outer = place()
    lanes, done = value_refs[0].shape[2], act_refs[0].shape[2]
    mask = filled(lanes, window + 1)
    for f in range(frames):
        p, t = divmod(f, PAIR)
        value_refs[p][t, :, :done] = near_ref[f, :, :done]
        acts = [act_refs[p][t]]
        blocks = {done // LANES: near_ref[f, :, done:].astype(jnp.float32)}
        for row in range(2 * rows, 2 * rows + halo):
            local = 4 * rows - 1 - row
            at = local % rows
            index = at + (1 - group) * (rows - 1 - 2 * at)
            one, two = (mate_ref, far_ref) if local < rows else (far_ref, mate_ref)
            line = jnp.where(outer, one[f, index], two[f, index]).astype(jnp.float32)
            placed(blocks, core, row, window, line)
        for b in sorted(blocks):
            part = slice(b * LANES, (b + 1) * LANES)
            value_refs[p][t, :, part] = blocks[b].astype(jnp.bfloat16)
            act = activated(blocks[b], columns_ref[0, 0], mask[:, part])
            acts.append(act)
            if p == pairs - 1:
                send_ref[t, :, part.start - done : part.stop - done] = act
        spread(out_refs[p], t, jnp.concatenate(acts, axis=1), window + 1)


def beyond(halo, far, mate, near_values, near_act, columns):
    frames, rows, channels, width = far.shape
    lanes = rounded((2 * rows + halo) * (width // 2 + halo + 1))
    out = jax.ShapeDtypeStruct((PAIR, channels, lanes), jnp.bfloat16)
    shifted = jax.ShapeDtypeStruct((PAIR, 3, channels, rounded((2 * rows + halo - 1) * (width // 2 + halo + 1))), jnp.bfloat16)
    send = jax.ShapeDtypeStruct((PAIR, channels, lanes - near_act[0].shape[2]), jnp.bfloat16)
    pairs = frames // PAIR
    outs = pl.pallas_call(
        functools.partial(far_kernel, halo, pairs),
        out_shape=(out,) * pairs + (shifted,) * pairs + (send,),
        in_specs=[VMEM] * (4 + pairs),
        out_specs=(VMEM,) * (2 * pairs + 1),
        compiler_params=pltpu.CompilerParams(vmem_limit_bytes=LIMIT),
        cost_estimate=pl.CostEstimate(flops=40 * far.size, bytes_accessed=8 * far.size, transcendentals=2 * far.size),
        name="beyond",
    )(far, mate, near_values, columns, *near_act)
    return outs[:pairs], outs[pairs : 2 * pairs], outs[-1]


def conv_kernel(
    layer, last, sends, rest_sent, received, rest, pitch, half, shifted_ref, values_ref, w_ref, columns_ref, *refs
):
    scratch = refs[-1:] if received else ()
    outs = refs[received or 1 : len(refs) - len(scratch)]
    if received:
        earlier_ref = scratch[0]
        for t in range(PAIR):
            if rest:
                whole = (refs[0].shape[1] - LANES) // PAIR
                tail = refs[0][:, PAIR * whole :].astype(jnp.float32)
                tail = tail if t == 0 else pltpu.roll(tail, LANES - t * (LANES // PAIR), 1)
                tail = jnp.where(lane_of(LANES) < rest, tail, 0.0).astype(jnp.bfloat16)
                parts = [refs[0][:, t * whole : (t + 1) * whole], tail]
            else:
                parts = [ref[t] for ref in refs[:received]]
            spread(earlier_ref, t, parts[0] if len(parts) == 1 else jnp.concatenate(parts, axis=1), pitch)
    else:
        earlier_ref = refs[0]
    _, _, channels, lanes = shifted_ref.shape
    chunks = lanes // LANES
    lane = lane_of(LANES)

    def window(t, b):
        taken = [(earlier_ref, t + a) if t + a < PAIR else (shifted_ref, t + a - PAIR) for a in range(3)]
        at = slice(b * LANES, (b + 1) * LANES)
        return jnp.concatenate([ref[j, :, :, at].reshape(3 * channels, LANES) for ref, j in taken], axis=0)

    places = [(t, b) for t in range(PAIR) for b in range(chunks)]
    side = TILE // LANES
    tiles = []
    bias = columns_ref[layer, 1]
    if not last:
        mask = filled(lanes, pitch)
        gain = columns_ref[layer + 1, 0]

    def sums(t, tap, b):
        tile, at = divmod((t * chunks + b) * LANES, TILE)
        return tiles[tile][tap][:, at : at + LANES]

    tails = []

    def finish(t):
        totals, acts = [], []
        from_left = 0.0
        from_right = pltpu.roll(sums(t, 2, 0), LANES - 1, 1)
        for b in range(chunks):
            at = slice(b * LANES, (b + 1) * LANES)
            left = pltpu.roll(sums(t, 0, b), 1, 1)
            right = pltpu.roll(sums(t, 2, b + 1), LANES - 1, 1) if b + 1 < chunks else 0.0
            summed = (
                jnp.where(lane == 0, from_left, left) + sums(t, 1, b) + jnp.where(lane == LANES - 1, right, from_right)
            )
            from_left, from_right = left, right
            total = (values_ref[t, :, at].astype(jnp.float32) + summed + bias).astype(jnp.bfloat16)
            totals.append(total.astype(jnp.float32))
            if not last:
                outs[0][t, :, at] = total
                acts.append(activated(totals[-1], gain, mask[:, at]))
                if not sends:
                    continue
                if not rest_sent:
                    outs[2][t, :, at] = acts[-1]
                elif b < chunks - 1:
                    outs[2][:, (t * (chunks - 1) + b) * LANES : (t * (chunks - 1) + b + 1) * LANES] = acts[-1]
                else:
                    tail = jnp.where(lane < rest_sent, acts[-1].astype(jnp.float32), 0.0)
                    tails.append(tail if t == 0 else pltpu.roll(tail, t * (LANES // PAIR), 1))
        if not last:
            spread(outs[1], t, jnp.concatenate(acts, axis=1), pitch)
            return
        whole = jnp.concatenate(totals, axis=1)
        halo = pitch - 1 - half
        core, _, outer = place()
        whole = jnp.where(core == 1, pltpu.roll(whole, lanes - halo, 1), whole)
        left_half = lane < half

        def rows_of(row):
            one = whole if row == 0 else pltpu.roll(whole, lanes - row * pitch, 1)
            two = pltpu.roll(whole, lanes - (row + 1) * pitch + half, 1)
            return jnp.where(left_half, one[:, :LANES], two[:, :LANES])

        outermost, inner = rows_of(0), rows_of(2)
        outs[0][t] = jnp.where(outer, outermost, inner).astype(jnp.bfloat16)
        outs[1][t] = jnp.where(outer, inner, outermost).astype(jnp.bfloat16)

    finished = 0
    for n in range(0, len(places), side):
        rhs = jnp.concatenate([window(t, b) for t, b in places[n : n + side]], axis=1)
        tiles.append(
            [
                jnp.dot(w_ref[tap * channels : (tap + 1) * channels], rhs, preferred_element_type=jnp.float32)
                for tap in range(3)
            ]
        )
        while finished < PAIR and (finished + 1) * chunks <= n + side:
            finish(finished)
            finished += 1
    if sends and rest_sent:
        outs[2][:, PAIR * (chunks - 1) * LANES :] = sum(tails).astype(jnp.bfloat16)


def conv(layer, last, sends, received, rest, pitch, rows_left, half, earlier, shifted, values, weight, columns):
    _, _, channels, lanes = shifted.shape
    rest_sent = joined(rows_left * pitch)
    if last:
        out_shape = (jax.ShapeDtypeStruct((PAIR, channels, LANES), jnp.bfloat16),) * 2
    else:
        out_shape = (
            jax.ShapeDtypeStruct((PAIR, channels, lanes), jnp.bfloat16),
            jax.ShapeDtypeStruct((PAIR, 3, channels, rounded((rows_left - 1) * pitch)), jnp.bfloat16),
        )
        if sends and rest_sent:
            sent = PAIR * (lanes - LANES) + LANES
            out_shape += (jax.ShapeDtypeStruct((channels, sent), jnp.bfloat16),)
        elif sends:
            out_shape += out_shape[:1]
    return pl.pallas_call(
        functools.partial(conv_kernel, layer, last, sends and not last, rest_sent, received, rest, pitch, half),
        out_shape=out_shape,
        in_specs=[VMEM] * (4 + len(earlier)),
        out_specs=(VMEM,) * len(out_shape),
        scratch_shapes=[pltpu.VMEM((PAIR, 3, channels, lanes), jnp.bfloat16)] * (received > 0),
        compiler_params=pltpu.CompilerParams(vmem_limit_bytes=LIMIT),
        cost_estimate=pl.CostEstimate(
            flops=54 * channels * channels * PAIR * lanes,
            bytes_accessed=2 * weight.size,
            transcendentals=PAIR * channels * lanes,
        ),
        name=f"conv_{layer}",
    )(shifted, values, weight, columns, *earlier)


def join_kernel(pair, kept_ref, got_ref, *refs):
    out_ref, lines_ref, sem = refs[-3:]
    _, rows, _, width = lines_ref.shape
    half = width // 2
    core, group, _ = place()
    first = core == 0
    left_half = lane_of(width) < half
    for t in range(PAIR):
        mine, theirs = kept_ref[t].astype(jnp.float32), got_ref[t].astype(jnp.float32)
        left, right = jnp.where(first, mine, theirs), jnp.where(first, theirs, mine)
        lines = (
            jnp.where(left_half, left, pltpu.roll(right, half, 1)),
            jnp.where(left_half, pltpu.roll(left, half, 1), right),
        )
        for j in range(rows):
            lines_ref[t, j + group * (rows - 1 - 2 * j)] = lines[j].astype(jnp.bfloat16)
    copy = pltpu.make_async_copy(lines_ref, out_ref.at[pl.ds(PAIR * pair, PAIR)], sem)
    copy.start()
    copy.wait()


def join(pair, kept, got, shape, *so_far):
    return pl.pallas_call(
        functools.partial(join_kernel, pair),
        out_shape=jax.ShapeDtypeStruct(shape, jnp.bfloat16),
        in_specs=[VMEM, VMEM] + [ANY] * len(so_far),
        out_specs=ANY,
        scratch_shapes=[pltpu.VMEM((PAIR,) + shape[1:], jnp.bfloat16), pltpu.SemaphoreType.DMA],
        input_output_aliases={2: 0} if so_far else {},
        compiler_params=pltpu.CompilerParams(vmem_limit_bytes=LIMIT),
        name="join",
    )(kept, got, *so_far)


def on_device(latents, conv_weight, norm_gains, biases):
    layers = conv_weight.shape[0]
    frames, rows, channels, width = latents.shape
    strips, blocks = lax.axis_size("rows"), lax.axis_size("tm")
    assert strips == 4 and rows == 2 and frames % PAIR == 0 and width == LANES

    def mate_of(block):
        return lax.ppermute(block, "rows", [(i, i ^ 1) for i in range(strips)])

    def earlier_of(block):
        return lax.ppermute(block, "tm", [(i, i + 1) for i in range(blocks - 1)])

    far = lax.ppermute(latents, "rows", [(i, i ^ 2) for i in range(strips)])
    mate = mate_of(latents)
    row_values = jnp.concatenate([norm_gains, biases], axis=0)
    weight, columns = weights(conv_weight, row_values)
    near_values, near_act = near(layers, latents, mate, row_values)
    halo_near = earlier_of(near_act[-1])
    far, weight, columns, near_values, near_act, halo_near = lax.optimization_barrier(
        (far, weight, columns, near_values, near_act, halo_near)
    )
    values, shifted, send = beyond(layers, far, mate_of(far), near_values, near_act, columns)
    halo, rest = (halo_near, earlier_of(send)), 0
    pitch = width // 2 + layers + 1
    pairs = frames // PAIR
    for layer in range(layers):
        last = layer == layers - 1
        rows_left = 2 * rows + layers - 1 - layer
        results = [None] * pairs
        for p in reversed(range(pairs)):
            earlier, received = ((shifted[p - 1],), 0) if p else (halo, len(halo))
            results[p] = conv(
                layer,
                last,
                p == pairs - 1,
                received,
                rest if received else 0,
                pitch,
                rows_left,
                width // 2,
                earlier,
                shifted[p],
                values[p],
                weight[layer],
                columns,
            )
        values, shifted = [r[0] for r in results], [r[1] for r in results]
        if not last:
            halo, rest = (earlier_of(results[-1][2]),), joined(rows_left * pitch)
    result = ()
    for p in reversed(range(pairs)):
        result = (join(p, values[p], mate_of(shifted[p]), latents.shape, *result),)
    return result[0]


def solution(mesh):
    in_specs = (P(("clips", "tm"), "rows", None, None), P(), P(), P())
    out_specs = P(("clips", "tm"), "rows", None, None)
    return jax.shard_map(on_device, mesh=mesh, in_specs=in_specs, out_specs=out_specs, check_vma=False)
```

```python
import functools

import jax
import jax.numpy as jnp
from jax import lax
from jax.experimental import pallas as pl
from jax.experimental.pallas import tpu as pltpu
from jax.sharding import PartitionSpec as P

EPSILON = 1e-06
PAIR = 2
LANES = 128
TILE = 256
VMEM = pl.BlockSpec(memory_space=pltpu.VMEM)
ANY = pl.BlockSpec(memory_space=pl.ANY)
LIMIT = 24 * 1024 * 1024
LARGE = 44 * 1024 * 1024


def place():
    strip = lax.axis_index("rows").astype(jnp.int32)
    core, group = strip & 1, strip >> 1
    return core, group, core == group


def rounded(lanes):
    return -(-lanes // LANES) * LANES


def column(row):
    return jnp.transpose(jnp.broadcast_to(row, (LANES, row.shape[1])))


def lane_of(lanes):
    return lax.broadcasted_iota(jnp.int32, (1, lanes), 1)


def filled(lanes, pitch):
    lane = lane_of(lanes)
    gaps = lane < 0
    for end in range(pitch - 1, lanes, pitch):
        gaps = gaps | (lane == end)
    return jnp.where(gaps, 0.0, 1.0)


def activated(values, gain, mask):
    squares = jnp.mean(values * values, axis=0, keepdims=True)
    halved = values * (lax.rsqrt(squares + EPSILON) * (0.5 * mask)) * gain
    return (halved + halved * jnp.tanh(halved)).astype(jnp.bfloat16)


def weights_kernel(w_ref, rows_ref, *refs):
    outs, turned_ref, columns_ref, held_ref, sems = refs[:-4], refs[-4], refs[-3], refs[-2], refs[-1]
    layers, taps, channels_out, ins = w_ref.shape
    step = taps // 3
    places = [(layer, time_tap) for layer in range(layers) for time_tap in range(3)]
    copies = []
    for n, (layer, time_tap) in enumerate(places):
        part = pl.ds(step * time_tap, step)
        copies.append(pltpu.make_async_copy(w_ref.at[layer, part], held_ref.at[n], sems.at[n]))
    for copy in copies:
        copy.start()
    _, flipped, _ = place()
    for layer in range(layers):
        columns_ref[layer, 0] = column(rows_ref[layer : layer + 1, :])
        columns_ref[layer, 1] = column(rows_ref[layers + layer : layers + layer + 1, :])
    for n, (layer, time_tap) in enumerate(places):
        copies[n].wait()
        for row_tap in range(3):
            source = 3 * (row_tap + flipped * (2 - 2 * row_tap))
            at = (3 * time_tap + row_tap) * ins
            block = held_ref[n, pl.ds(source, 3)].reshape(3 * channels_out, ins)
            outs[layer][:, at : at + ins] = block
            if layer == layers - 1 and time_tap > 0:
                at = (3 * (2 - time_tap) + row_tap) * ins
                turned_ref[:, at : at + ins] = block


def weights(conv_weight, rows):
    layers, taps, outs, ins = conv_weight.shape
    one = jax.ShapeDtypeStruct((3 * outs, 9 * ins), conv_weight.dtype)
    results = pl.pallas_call(
        weights_kernel,
        out_shape=(one,) * layers
        + (
            jax.ShapeDtypeStruct((3 * outs, 6 * ins), conv_weight.dtype),
            jax.ShapeDtypeStruct((layers, 2, outs, LANES), jnp.float32),
        ),
        in_specs=[ANY, VMEM],
        out_specs=(VMEM,) * (layers + 2),
        scratch_shapes=[
            pltpu.VMEM((3 * layers, taps // 3, outs, ins), conv_weight.dtype),
            pltpu.SemaphoreType.DMA((3 * layers,)),
        ],
        compiler_params=pltpu.CompilerParams(vmem_limit_bytes=LARGE),
        cost_estimate=pl.CostEstimate(flops=0, bytes_accessed=4 * conv_weight.size, transcendentals=0),
        name="weights",
    )(conv_weight, rows)
    return results[:-2], results[-2], results[-1]


def joined(valid):
    rest = valid % LANES
    return rest if 0 < PAIR * rest <= LANES else 0


def spread(out_ref, index, act, pitch):
    lanes = out_ref.shape[3]
    above = pltpu.roll(act, pitch, 1)
    below = pltpu.roll(act, act.shape[1] - pitch, 1)
    edge = jnp.where(lane_of(LANES) < pitch, 0.0, above[:, :LANES].astype(jnp.float32))
    out_ref[index, 0, :, :LANES] = edge.astype(jnp.bfloat16)
    out_ref[index, 0, :, LANES:] = above[:, LANES:lanes]
    out_ref[index, 1] = act[:, :lanes]
    out_ref[index, 2] = below[:, :lanes]


def placed(blocks, core, row, window, line):
    pitch, width = window + 1, line.shape[1]
    lane = lane_of(LANES)
    block, low = divmod(row * pitch, LANES)
    shift = lax.rem(low + LANES - core * (width - window), LANES)
    turned = pltpu.roll(line, shift, 1)
    here = (lane >= low) & (lane < low + window)
    blocks[block] = blocks.get(block, 0.0) + jnp.where(here, turned, 0.0)
    if low + window > LANES:
        blocks[block + 1] = blocks.get(block + 1, 0.0) + jnp.where(lane < low + window - LANES, turned, 0.0)


def near_kernel(halo, own_ref, mate_ref, gains_ref, values_ref, *act_refs):
    frames, rows, _, width = own_ref.shape
    window = width // 2 + halo
    core, group, outer = place()
    gain = column(gains_ref[0:1, :])
    done = act_refs[0].shape[2]
    mask = filled(done, window + 1)
    for f in range(frames):
        blocks = {}
        for row in range(2 * rows):
            at = row % rows
            index = at + group * (rows - 1 - 2 * at)
            one, two = (own_ref, mate_ref) if row < rows else (mate_ref, own_ref)
            line = jnp.where(outer, one[f, index], two[f, index]).astype(jnp.float32)
            placed(blocks, core, row, window, line)
        for b in blocks:
            part = slice(b * LANES, (b + 1) * LANES)
            values_ref[f, :, part] = blocks[b].astype(jnp.bfloat16)
            if part.stop <= done:
                act_refs[f // PAIR][f % PAIR, :, part] = activated(blocks[b], gain, mask[:, part])


def near(halo, own, mate, gains):
    frames, rows, channels, width = own.shape
    lanes = 2 * rows * (width // 2 + halo + 1)
    pairs = frames // PAIR
    outs = pl.pallas_call(
        functools.partial(near_kernel, halo),
        out_shape=(jax.ShapeDtypeStruct((frames, channels, rounded(lanes)), jnp.bfloat16),)
        + (jax.ShapeDtypeStruct((PAIR, channels, lanes // LANES * LANES), jnp.bfloat16),) * pairs,
        in_specs=[VMEM] * 3,
        out_specs=(VMEM,) * (1 + pairs),
        compiler_params=pltpu.CompilerParams(vmem_limit_bytes=LIMIT),
        cost_estimate=pl.CostEstimate(flops=40 * own.size, bytes_accessed=8 * own.size, transcendentals=2 * own.size),
        name="near",
    )(own, mate, gains)
    return outs[0], outs[1:]


def far_kernel(halo, pairs, far_ref, mate_ref, near_ref, columns_ref, *refs):
    act_refs, value_refs, out_refs, send_ref = refs[:pairs], refs[pairs : 2 * pairs], refs[2 * pairs : -1], refs[-1]
    frames, rows, _, width = far_ref.shape
    window = width // 2 + halo
    core, group, outer = place()
    lanes, done = value_refs[0].shape[2], act_refs[0].shape[2]
    mask = filled(lanes, window + 1)
    for f in range(frames):
        p, t = divmod(f, PAIR)
        value_refs[p][t, :, :done] = near_ref[f, :, :done]
        acts = [act_refs[p][t]]
        blocks = {done // LANES: near_ref[f, :, done:].astype(jnp.float32)}
        for row in range(2 * rows, 2 * rows + halo):
            local = 4 * rows - 1 - row
            at = local % rows
            index = at + (1 - group) * (rows - 1 - 2 * at)
            one, two = (mate_ref, far_ref) if local < rows else (far_ref, mate_ref)
            line = jnp.where(outer, one[f, index], two[f, index]).astype(jnp.float32)
            placed(blocks, core, row, window, line)
        for b in sorted(blocks):
            part = slice(b * LANES, (b + 1) * LANES)
            value_refs[p][t, :, part] = blocks[b].astype(jnp.bfloat16)
            act = activated(blocks[b], columns_ref[0, 0], mask[:, part])
            acts.append(act)
            if p == pairs - 1:
                send_ref[t, :, part.start - done : part.stop - done] = act
        spread(out_refs[p], t, jnp.concatenate(acts, axis=1), window + 1)


def beyond(halo, far, mate, near_values, near_act, columns):
    frames, rows, channels, width = far.shape
    lanes = rounded((2 * rows + halo) * (width // 2 + halo + 1))
    out = jax.ShapeDtypeStruct((PAIR, channels, lanes), jnp.bfloat16)
    shifted = jax.ShapeDtypeStruct((PAIR, 3, channels, rounded((2 * rows + halo - 1) * (width // 2 + halo + 1))), jnp.bfloat16)
    send = jax.ShapeDtypeStruct((PAIR, channels, lanes - near_act[0].shape[2]), jnp.bfloat16)
    pairs = frames // PAIR
    outs = pl.pallas_call(
        functools.partial(far_kernel, halo, pairs),
        out_shape=(out,) * pairs + (shifted,) * pairs + (send,),
        in_specs=[VMEM] * (4 + pairs),
        out_specs=(VMEM,) * (2 * pairs + 1),
        compiler_params=pltpu.CompilerParams(vmem_limit_bytes=LIMIT),
        cost_estimate=pl.CostEstimate(flops=40 * far.size, bytes_accessed=8 * far.size, transcendentals=2 * far.size),
        name="beyond",
    )(far, mate, near_values, columns, *near_act)
    return outs[:pairs], outs[pairs : 2 * pairs], outs[-1]


def lines_of(ref, frame, lanes):
    return ref[frame, :, :, lanes].reshape(3 * ref.shape[2], -1)


def column_sums(taps):
    lane = lane_of(LANES)
    left, middle, right = taps
    lefts = [pltpu.roll(block, 1, 1) for block in left]
    rights = [pltpu.roll(block, LANES - 1, 1) for block in right] + [0.0]
    return [
        jnp.where(lane == 0, lefts[b - 1] if b else 0.0, lefts[b])
        + middle[b]
        + jnp.where(lane == LANES - 1, rights[b + 1], rights[b])
        for b in range(len(middle))
    ]


def by_taps(sums):
    channels, lanes = sums.shape[0] // 3, sums.shape[1]
    return [
        [sums[tap * channels : (tap + 1) * channels, at : at + LANES] for at in range(0, lanes, LANES)]
        for tap in range(3)
    ]


def own_columns(blocks, pitch, half):
    core, _, _ = place()
    halo = pitch - 1 - half
    lanes = len(blocks) * LANES
    whole = jnp.concatenate(blocks, axis=1)
    whole = jnp.where(core == 1, pltpu.roll(whole, lanes - halo, 1), whole)
    left_half = lane_of(LANES) < half

    def rows_of(row):
        one = whole if row == 0 else pltpu.roll(whole, lanes - row * pitch, 1)
        two = pltpu.roll(whole, lanes - (row + 1) * pitch + half, 1)
        return jnp.where(left_half, one[:, :LANES], two[:, :LANES])

    return rows_of(0), rows_of(2)


def given(outermost, inner, kept_ref, sent_ref, t):
    _, _, outer = place()
    kept_ref[t] = jnp.where(outer, outermost, inner).astype(jnp.bfloat16)
    sent_ref[t] = jnp.where(outer, inner, outermost).astype(jnp.bfloat16)


def conv_kernel(plan, shifted_ref, values_ref, w_ref, columns_ref, *refs):
    layer, pitch, half, received = plan["layer"], plan["pitch"], plan["half"], plan["received"]
    last, sends, rest, rest_sent = plan["last"], plan["sends"], plan["rest"], plan["rest_sent"]
    refs = list(refs)
    earlier_refs = [refs.pop(0) for _ in range(received or 1)]
    next_w_ref = refs.pop(0) if sends == "sums" else None
    if received:
        earlier_ref = refs.pop()
        for t in range(PAIR):
            if rest:
                whole = (earlier_refs[0].shape[1] - LANES) // PAIR
                tail = earlier_refs[0][:, PAIR * whole :].astype(jnp.float32)
                tail = tail if t == 0 else pltpu.roll(tail, LANES - t * (LANES // PAIR), 1)
                tail = jnp.where(lane_of(LANES) < rest, tail, 0.0).astype(jnp.bfloat16)
                parts = [earlier_refs[0][:, t * whole : (t + 1) * whole], tail]
            else:
                parts = [ref[t] for ref in earlier_refs]
            spread(earlier_ref, t, parts[0] if len(parts) == 1 else jnp.concatenate(parts, axis=1), pitch)
    else:
        earlier_ref = earlier_refs[0]
    outs = refs
    _, _, channels, lanes = shifted_ref.shape
    chunks = lanes // LANES
    lane = lane_of(LANES)

    def window(t, b):
        taken = [(earlier_ref, t + a) if t + a < PAIR else (shifted_ref, t + a - PAIR) for a in range(3)]
        at = slice(b * LANES, (b + 1) * LANES)
        return jnp.concatenate([lines_of(ref, j, at) for ref, j in taken], axis=0)

    places = [(t, b) for t in range(PAIR) for b in range(chunks)]
    side = TILE // LANES
    sums = {}
    tails = []
    bias = columns_ref[layer, 1]
    if not last:
        mask = filled(lanes, pitch)
        gain = columns_ref[layer + 1, 0]

    def finish(t):
        convs = column_sums([[sums[t, b][tap] for b in range(chunks)] for tap in range(3)])
        totals, acts = [], []
        for b in range(chunks):
            at = slice(b * LANES, (b + 1) * LANES)
            total = (values_ref[t, :, at].astype(jnp.float32) + convs[b] + bias).astype(jnp.bfloat16)
            totals.append(total.astype(jnp.float32))
            if last:
                continue
            outs[0][t, :, at] = total
            acts.append(activated(totals[-1], gain, mask[:, at]))
            if sends != "act":
                continue
            if not rest_sent:
                outs[2][t, :, at] = acts[-1]
            elif b < chunks - 1:
                outs[2][:, (t * (chunks - 1) + b) * LANES : (t * (chunks - 1) + b + 1) * LANES] = acts[-1]
            else:
                tail = jnp.where(lane < rest_sent, acts[-1].astype(jnp.float32), 0.0)
                tails.append(tail if t == 0 else pltpu.roll(tail, t * (LANES // PAIR), 1))
        if last:
            given(*own_columns(totals, pitch, half), *outs, t)
        else:
            spread(outs[1], t, jnp.concatenate(acts, axis=1), pitch)

    finished = 0
    for n in range(0, len(places), side):
        rhs = jnp.concatenate([window(t, b) for t, b in places[n : n + side]], axis=1)
        tile = jnp.dot(w_ref[...], rhs, preferred_element_type=jnp.float32)
        taps = by_taps(tile)
        for i, key in enumerate(places[n : n + side]):
            sums[key] = [taps[tap][i] for tap in range(3)]
        while finished < PAIR and (finished + 1) * chunks <= n + side:
            finish(finished)
            finished += 1
    if sends == "act" and rest_sent:
        outs[2][:, PAIR * (chunks - 1) * LANES :] = sum(tails).astype(jnp.bfloat16)
    if sends == "sums":
        depth = 3 * channels
        for t in range(PAIR):
            frames = range(t, PAIR)
            rhs = jnp.concatenate([lines_of(outs[1], j, slice(None)) for j in frames], axis=0)
            added = jnp.dot(next_w_ref[:, : len(frames) * depth], rhs, preferred_element_type=jnp.float32)
            pieces = own_columns(column_sums(by_taps(added)), pitch, half)
            for i, piece in enumerate(pieces):
                outs[2][t, :, i * LANES : (i + 1) * LANES] = piece.astype(jnp.bfloat16)


def conv(plan, earlier, shifted, values, weight, next_weight, columns):
    _, _, channels, lanes = shifted.shape
    pitch, sends, received = plan["pitch"], plan["sends"], plan["received"]
    if plan["last"]:
        out_shape = (jax.ShapeDtypeStruct((PAIR, channels, LANES), jnp.bfloat16),) * 2
    else:
        out_shape = (
            jax.ShapeDtypeStruct((PAIR, channels, lanes), jnp.bfloat16),
            jax.ShapeDtypeStruct((PAIR, 3, channels, rounded((plan["rows"] - 1) * pitch)), jnp.bfloat16),
        )
        if sends == "sums":
            out_shape += (jax.ShapeDtypeStruct((PAIR, channels, 2 * LANES), jnp.bfloat16),)
        elif sends and plan["rest_sent"]:
            out_shape += (jax.ShapeDtypeStruct((channels, PAIR * (lanes - LANES) + LANES), jnp.bfloat16),)
        elif sends:
            out_shape += out_shape[:1]
    extra = (next_weight,) if sends == "sums" else ()
    return pl.pallas_call(
        functools.partial(conv_kernel, plan),
        out_shape=out_shape,
        in_specs=[VMEM] * (4 + len(earlier) + len(extra)),
        out_specs=(VMEM,) * len(out_shape),
        scratch_shapes=[pltpu.VMEM((PAIR, 3, channels, lanes), jnp.bfloat16)] * (received > 0),
        compiler_params=pltpu.CompilerParams(vmem_limit_bytes=LIMIT),
        cost_estimate=pl.CostEstimate(
            flops=54 * channels * channels * PAIR * lanes,
            bytes_accessed=2 * weight.size,
            transcendentals=PAIR * channels * lanes,
        ),
        name=f"conv_{plan['layer']}",
    )(shifted, values, weight, columns, *earlier, *extra)


def own_kernel(layer, pitch, half, shifted_ref, values_ref, w_ref, columns_ref, out_ref):
    _, _, channels, lanes = shifted_ref.shape
    bias = columns_ref[layer, 1]
    for t in range(PAIR):
        rhs = jnp.concatenate([lines_of(shifted_ref, j, slice(None)) for j in range(t, -1, -1)], axis=0)
        added = jnp.dot(w_ref[:, : (t + 1) * 3 * channels], rhs, preferred_element_type=jnp.float32)
        convs = column_sums(by_taps(added))
        totals = [
            values_ref[t, :, b * LANES : (b + 1) * LANES].astype(jnp.float32) + convs[b] + bias
            for b in range(lanes // LANES)
        ]
        for i, piece in enumerate(own_columns(totals, pitch, half)):
            out_ref[t, :, i * LANES : (i + 1) * LANES] = piece


def own(layer, pitch, half, shifted, values, weight, columns):
    _, _, channels, lanes = shifted.shape
    return pl.pallas_call(
        functools.partial(own_kernel, layer, pitch, half),
        out_shape=jax.ShapeDtypeStruct((PAIR, channels, 2 * LANES), jnp.float32),
        in_specs=[VMEM] * 4,
        out_specs=VMEM,
        compiler_params=pltpu.CompilerParams(vmem_limit_bytes=LIMIT),
        cost_estimate=pl.CostEstimate(
            flops=27 * channels * channels * PAIR * lanes, bytes_accessed=2 * weight.size, transcendentals=0
        ),
        name="own",
    )(shifted, values, weight, columns)


def total_kernel(own_ref, came_ref, kept_ref, sent_ref):
    for t in range(PAIR):
        whole = own_ref[t] + came_ref[t].astype(jnp.float32)
        given(whole[:, :LANES], whole[:, LANES:], kept_ref, sent_ref, t)


def total(owned, came):
    pair, channels, _ = owned.shape
    return pl.pallas_call(
        total_kernel,
        out_shape=(jax.ShapeDtypeStruct((pair, channels, LANES), jnp.bfloat16),) * 2,
        in_specs=[VMEM] * 2,
        out_specs=(VMEM,) * 2,
        compiler_params=pltpu.CompilerParams(vmem_limit_bytes=LIMIT),
        cost_estimate=pl.CostEstimate(flops=2 * owned.size, bytes_accessed=8 * owned.size, transcendentals=0),
        name="total",
    )(owned, came)


def join_kernel(pair, kept_ref, got_ref, *refs):
    out_ref, lines_ref, sem = refs[-3:]
    _, rows, _, width = lines_ref.shape
    half = width // 2
    core, group, _ = place()
    first = core == 0
    left_half = lane_of(width) < half
    for t in range(PAIR):
        mine, theirs = kept_ref[t].astype(jnp.float32), got_ref[t].astype(jnp.float32)
        left, right = jnp.where(first, mine, theirs), jnp.where(first, theirs, mine)
        lines = (
            jnp.where(left_half, left, pltpu.roll(right, half, 1)),
            jnp.where(left_half, pltpu.roll(left, half, 1), right),
        )
        for j in range(rows):
            lines_ref[t, j + group * (rows - 1 - 2 * j)] = lines[j].astype(jnp.bfloat16)
    copy = pltpu.make_async_copy(lines_ref, out_ref.at[pl.ds(PAIR * pair, PAIR)], sem)
    copy.start()
    copy.wait()


def join(pair, kept, got, shape, *so_far):
    return pl.pallas_call(
        functools.partial(join_kernel, pair),
        out_shape=jax.ShapeDtypeStruct(shape, jnp.bfloat16),
        in_specs=[VMEM, VMEM] + [ANY] * len(so_far),
        out_specs=ANY,
        scratch_shapes=[pltpu.VMEM((PAIR,) + shape[1:], jnp.bfloat16), pltpu.SemaphoreType.DMA],
        input_output_aliases={2: 0} if so_far else {},
        compiler_params=pltpu.CompilerParams(vmem_limit_bytes=LIMIT),
        name="join",
    )(kept, got, *so_far)


def on_device(latents, conv_weight, norm_gains, biases):
    layers = conv_weight.shape[0]
    frames, rows, channels, width = latents.shape
    strips, blocks = lax.axis_size("rows"), lax.axis_size("tm")
    assert layers > 1 and strips == 4 and rows == 2 and frames % PAIR == 0 and width == LANES

    def mate_of(block):
        return lax.ppermute(block, "rows", [(i, i ^ 1) for i in range(strips)])

    def earlier_of(block):
        return lax.ppermute(block, "tm", [(i, i + 1) for i in range(blocks - 1)])

    far = lax.ppermute(latents, "rows", [(i, i ^ 2) for i in range(strips)])
    mate = mate_of(latents)
    row_values = jnp.concatenate([norm_gains, biases], axis=0)
    weight, turned, columns = weights(conv_weight, row_values)
    near_values, near_act = near(layers, latents, mate, row_values)
    halo_near = earlier_of(near_act[-1])
    far, weight, turned, columns, near_values, near_act, halo_near = lax.optimization_barrier(
        (far, weight, turned, columns, near_values, near_act, halo_near)
    )
    values, shifted, send = beyond(layers, far, mate_of(far), near_values, near_act, columns)
    halo, rest = (halo_near, earlier_of(send)), 0
    half = width // 2
    pitch = half + layers + 1
    pairs = frames // PAIR
    for layer in range(layers):
        last = layer == layers - 1
        rows_left = 2 * rows + layers - 1 - layer
        results = [None] * pairs
        for p in reversed(range(pairs)):
            if last and p == 0:
                owned = own(layer, pitch, half, shifted[p], values[p], turned, columns)
                results[p] = total(owned, halo[0])
                continue
            sends = "" if last or p < pairs - 1 else "act" if layer < layers - 2 else "sums"
            plan = {
                "layer": layer,
                "last": last,
                "sends": sends,
                "rest_sent": joined(rows_left * pitch),
                "received": 0 if p else len(halo),
                "rest": 0 if p else rest,
                "pitch": pitch,
                "half": half,
                "rows": rows_left,
            }
            earlier = (shifted[p - 1],) if p else halo
            results[p] = conv(plan, earlier, shifted[p], values[p], weight[layer], weight[-1], columns)
            if sends:
                arriving = earlier_of(results[p][2])
        values, shifted = [r[0] for r in results], [r[1] for r in results]
        if not last:
            halo, rest = (arriving,), joined(rows_left * pitch)
    result = ()
    for p in reversed(range(pairs)):
        result = (join(p, values[p], mate_of(shifted[p]), latents.shape, *result),)
    return result[0]


def solution(mesh):
    in_specs = (P(("clips", "tm"), "rows", None, None), P(), P(), P())
    out_specs = P(("clips", "tm"), "rows", None, None)
    return jax.shard_map(on_device, mesh=mesh, in_specs=in_specs, out_specs=out_specs, check_vma=False)
```

```python
import functools

import jax
import jax.numpy as jnp
from jax import lax
from jax.experimental import pallas as pl
from jax.experimental.pallas import tpu as pltpu
from jax.sharding import PartitionSpec as P

EPSILON = 1e-06
PAIR = 2
LANES = 128
TILE = 256
VMEM = pl.BlockSpec(memory_space=pltpu.VMEM)
ANY = pl.BlockSpec(memory_space=pl.ANY)
LIMIT = 44 * 1024 * 1024


def place():
    strip = lax.axis_index("rows").astype(jnp.int32)
    core, group = strip & 1, strip >> 1
    return core, group, core == group


def rounded(lanes):
    return -(-lanes // LANES) * LANES


def column(row):
    return jnp.transpose(jnp.broadcast_to(row, (LANES, row.shape[1])))


def lane_of(lanes):
    return lax.broadcasted_iota(jnp.int32, (1, lanes), 1)


def filled(lanes, pitch):
    lane = lane_of(lanes)
    gaps = lane < 0
    for end in range(pitch - 1, lanes, pitch):
        gaps = gaps | (lane == end)
    return jnp.where(gaps, 0.0, 1.0)


def activated(values, gain, mask):
    squares = jnp.mean(values * values, axis=0, keepdims=True)
    halved = values * (lax.rsqrt(squares + EPSILON) * (0.5 * mask)) * gain
    return (halved + halved * jnp.tanh(halved)).astype(jnp.bfloat16)


def fetches(layer, w_ref, held_ref, sems):
    step = w_ref.shape[1] // 3
    return [
        pltpu.make_async_copy(w_ref.at[layer, pl.ds(step * tap, step)], held_ref.at[tap], sems.at[tap]) for tap in range(3)
    ]


def laid_out(copies, held_ref, out_ref):
    _, _, outs, ins = held_ref.shape
    _, flipped, _ = place()
    for time_tap in range(3):
        copies[time_tap].wait()
        for row_tap in range(3):
            source = 3 * (row_tap + flipped * (2 - 2 * row_tap))
            at = (3 * time_tap + row_tap) * ins
            out_ref[:, at : at + ins] = held_ref[time_tap, pl.ds(source, 3)].reshape(3 * outs, ins)


def held(conv_weight):
    _, taps, outs, ins = conv_weight.shape
    return [pltpu.VMEM((3, taps // 3, outs, ins), conv_weight.dtype), pltpu.SemaphoreType.DMA((3,))]


def laid_shape(conv_weight):
    _, _, outs, ins = conv_weight.shape
    return jax.ShapeDtypeStruct((3 * outs, 9 * ins), conv_weight.dtype)


def weights_kernel(w_ref, rows_ref, out_ref, columns_ref, held_ref, sems):
    copies = fetches(0, w_ref, held_ref, sems)
    for copy in copies:
        copy.start()
    layers = w_ref.shape[0]
    for layer in range(layers):
        columns_ref[layer, 0] = column(rows_ref[layer : layer + 1, :])
        columns_ref[layer, 1] = column(rows_ref[layers + layer : layers + layer + 1, :])
    laid_out(copies, held_ref, out_ref)


def weights(conv_weight, rows):
    layers, _, outs, _ = conv_weight.shape
    return pl.pallas_call(
        weights_kernel,
        out_shape=(laid_shape(conv_weight), jax.ShapeDtypeStruct((layers, 2, outs, LANES), jnp.float32)),
        in_specs=[ANY, VMEM],
        out_specs=(VMEM, VMEM),
        scratch_shapes=held(conv_weight),
        compiler_params=pltpu.CompilerParams(vmem_limit_bytes=LIMIT),
        cost_estimate=pl.CostEstimate(flops=0, bytes_accessed=4 * conv_weight.size // layers, transcendentals=0),
        name="weights",
    )(conv_weight, rows)


def split_kernel(in_ref, *out_refs):
    for p, out_ref in enumerate(out_refs):
        out_ref[...] = in_ref[PAIR * p : PAIR * (p + 1)]


def split(latents):
    pairs = latents.shape[0] // PAIR
    return pl.pallas_call(
        split_kernel,
        out_shape=(jax.ShapeDtypeStruct((PAIR,) + latents.shape[1:], latents.dtype),) * pairs,
        in_specs=[VMEM],
        out_specs=(VMEM,) * pairs,
        compiler_params=pltpu.CompilerParams(vmem_limit_bytes=LIMIT),
        name="split",
    )(latents)


def joined(valid):
    rest = valid % LANES
    return rest if 0 < PAIR * rest <= LANES else 0


def spread(out_ref, index, act, pitch):
    lanes = out_ref.shape[3]
    above = pltpu.roll(act, pitch, 1)
    below = pltpu.roll(act, act.shape[1] - pitch, 1)
    edge = jnp.where(lane_of(LANES) < pitch, 0.0, above[:, :LANES].astype(jnp.float32))
    out_ref[index, 0, :, :LANES] = edge.astype(jnp.bfloat16)
    out_ref[index, 0, :, LANES:] = above[:, LANES:lanes]
    out_ref[index, 1] = act[:, :lanes]
    out_ref[index, 2] = below[:, :lanes]


def placed(blocks, core, row, window, line):
    pitch, width = window + 1, line.shape[1]
    lane = lane_of(LANES)
    block, low = divmod(row * pitch, LANES)
    shift = lax.rem(low + LANES - core * (width - window), LANES)
    turned = pltpu.roll(line, shift, 1)
    here = (lane >= low) & (lane < low + window)
    blocks[block] = blocks.get(block, 0.0) + jnp.where(here, turned, 0.0)
    if low + window > LANES:
        blocks[block + 1] = blocks.get(block + 1, 0.0) + jnp.where(lane < low + window - LANES, turned, 0.0)


def near_kernel(halo, pairs, mate_ref, gains_ref, *refs):
    own_refs, value_refs, act_refs = refs[:pairs], refs[pairs : 2 * pairs], refs[2 * pairs :]
    frames, rows, _, width = mate_ref.shape
    window = width // 2 + halo
    core, group, outer = place()
    gain = column(gains_ref[0:1, :])
    done = act_refs[0].shape[2]
    mask = filled(done, window + 1)
    for f in range(frames):
        p, t = divmod(f, PAIR)
        blocks = {}
        for row in range(2 * rows):
            at = row % rows
            index = at + group * (rows - 1 - 2 * at)
            own, mate = own_refs[p][t, index], mate_ref[f, index]
            one, two = (own, mate) if row < rows else (mate, own)
            placed(blocks, core, row, window, jnp.where(outer, one, two).astype(jnp.float32))
        for b in blocks:
            part = slice(b * LANES, (b + 1) * LANES)
            value_refs[p][t, :, part] = blocks[b].astype(jnp.bfloat16)
            if part.stop <= done:
                act_refs[p][t, :, part] = activated(blocks[b], gain, mask[:, part])


def near(halo, mate, gains, own):
    frames, rows, channels, width = mate.shape
    lanes = 2 * rows * (width // 2 + halo + 1)
    pairs = len(own)
    outs = pl.pallas_call(
        functools.partial(near_kernel, halo, pairs),
        out_shape=(jax.ShapeDtypeStruct((PAIR, channels, rounded(lanes)), jnp.bfloat16),) * pairs
        + (jax.ShapeDtypeStruct((PAIR, channels, lanes // LANES * LANES), jnp.bfloat16),) * pairs,
        in_specs=[VMEM] * (2 + pairs),
        out_specs=(VMEM,) * (2 * pairs),
        compiler_params=pltpu.CompilerParams(vmem_limit_bytes=LIMIT),
        cost_estimate=pl.CostEstimate(flops=40 * mate.size, bytes_accessed=8 * mate.size, transcendentals=2 * mate.size),
        name="near",
    )(mate, gains, *own)
    return outs[:pairs], outs[pairs:]


def add_far(halo, far_ref, mate_ref, near_ref, act_ref, columns_ref, values_ref, shifted_ref, send_ref=None):
    pair, rows, _, width = far_ref.shape
    window = width // 2 + halo
    core, group, outer = place()
    lanes, done = values_ref.shape[2], act_ref.shape[2]
    mask = filled(lanes, window + 1)
    for t in range(pair):
        values_ref[t, :, :done] = near_ref[t, :, :done]
        acts = [act_ref[t]]
        blocks = {done // LANES: near_ref[t, :, done:].astype(jnp.float32)}
        for row in range(2 * rows, 2 * rows + halo):
            local = 4 * rows - 1 - row
            at = local % rows
            index = at + (1 - group) * (rows - 1 - 2 * at)
            one, two = (mate_ref, far_ref) if local < rows else (far_ref, mate_ref)
            line = jnp.where(outer, one[t, index], two[t, index]).astype(jnp.float32)
            placed(blocks, core, row, window, line)
        for b in sorted(blocks):
            part = slice(b * LANES, (b + 1) * LANES)
            values_ref[t, :, part] = blocks[b].astype(jnp.bfloat16)
            acts.append(activated(blocks[b], columns_ref[0, 0], mask[:, part]))
        act = jnp.concatenate(acts, axis=1)
        spread(shifted_ref, t, act, window + 1)
        if send_ref is not None:
            send_ref[t] = act


def far_shapes(rows, halo, channels, half):
    pitch = half + halo + 1
    return (
        jax.ShapeDtypeStruct((PAIR, channels, rounded((2 * rows + halo) * pitch)), jnp.bfloat16),
        jax.ShapeDtypeStruct((PAIR, 3, channels, rounded((2 * rows + halo - 1) * pitch)), jnp.bfloat16),
    )


def beyond(halo, columns, *parts):
    far = parts[0]
    _, rows, channels, width = far.shape
    values, shifted = far_shapes(rows, halo, channels, width // 2)

    def kernel(columns_ref, far_ref, mate_ref, near_ref, act_ref, *outs):
        add_far(halo, far_ref, mate_ref, near_ref, act_ref, columns_ref, *outs)

    return pl.pallas_call(
        kernel,
        out_shape=(values, shifted, values),
        in_specs=[VMEM] * 5,
        out_specs=(VMEM,) * 3,
        compiler_params=pltpu.CompilerParams(vmem_limit_bytes=LIMIT),
        cost_estimate=pl.CostEstimate(flops=40 * far.size, bytes_accessed=8 * far.size, transcendentals=2 * far.size),
        name="beyond",
    )(columns, *parts)


def conv_kernel(plan, shifted_ref, values_ref, w_ref, columns_ref, *refs):
    layer, pitch, half, received = plan["layer"], plan["pitch"], plan["half"], plan["received"]
    last, sends, rest, rest_sent = plan["last"], plan["sends"], plan["rest"], plan["rest_sent"]
    refs = list(refs)
    earlier_refs = [refs.pop(0) for _ in range(plan["inputs"])]
    if plan["fetches"]:
        next_ref, sems, held_ref = refs.pop(0), refs.pop(), refs.pop()
        copies = fetches(layer + 1, next_ref, held_ref, sems)
        for copy in copies:
            copy.start()
    earlier_ref = refs.pop() if received else earlier_refs[0]
    if received:
        for t in range(PAIR):
            if rest:
                whole = (earlier_refs[0].shape[1] - LANES) // PAIR
                tail = earlier_refs[0][:, PAIR * whole :].astype(jnp.float32)
                tail = tail if t == 0 else pltpu.roll(tail, LANES - t * (LANES // PAIR), 1)
                tail = jnp.where(lane_of(LANES) < rest, tail, 0.0).astype(jnp.bfloat16)
                act = jnp.concatenate([earlier_refs[0][:, t * whole : (t + 1) * whole], tail], axis=1)
            else:
                act = earlier_refs[0][t]
            spread(earlier_ref, t, act, pitch)
    outs = refs
    if plan["fetches"]:
        laid_ref = outs.pop()
    if plan["builds"]:
        earlier_ref = outs.pop()
        add_far(pitch - 1 - half, *earlier_refs, columns_ref, outs.pop(), earlier_ref)
    _, _, channels, lanes = shifted_ref.shape
    chunks = lanes // LANES
    lane = lane_of(LANES)

    def window(t, b):
        taken = [(earlier_ref, t + a) if t + a < PAIR else (shifted_ref, t + a - PAIR) for a in range(3)]
        at = slice(b * LANES, (b + 1) * LANES)
        return jnp.concatenate([ref[j, :, :, at].reshape(3 * channels, LANES) for ref, j in taken], axis=0)

    places = [(t, b) for t in range(PAIR) for b in range(chunks)]
    side = TILE // LANES
    tiles = []
    bias = columns_ref[layer, 1]
    if not last:
        mask = filled(lanes, pitch)
        gain = columns_ref[layer + 1, 0]

    def sums(t, tap, b):
        tile, at = divmod((t * chunks + b) * LANES, TILE)
        return tiles[tile][tap * channels : (tap + 1) * channels, at : at + LANES]

    tails = []

    def finish(t):
        totals, acts = [], []
        from_left = 0.0
        from_right = pltpu.roll(sums(t, 2, 0), LANES - 1, 1)
        for b in range(chunks):
            at = slice(b * LANES, (b + 1) * LANES)
            left = pltpu.roll(sums(t, 0, b), 1, 1)
            right = pltpu.roll(sums(t, 2, b + 1), LANES - 1, 1) if b + 1 < chunks else 0.0
            summed = (
                jnp.where(lane == 0, from_left, left) + sums(t, 1, b) + jnp.where(lane == LANES - 1, right, from_right)
            )
            from_left, from_right = left, right
            total = (values_ref[t, :, at].astype(jnp.float32) + summed + bias).astype(jnp.bfloat16)
            totals.append(total.astype(jnp.float32))
            if not last:
                outs[0][t, :, at] = total
                acts.append(activated(totals[-1], gain, mask[:, at]))
                if not sends:
                    continue
                if not rest_sent:
                    outs[2][t, :, at] = acts[-1]
                elif b < chunks - 1:
                    outs[2][:, (t * (chunks - 1) + b) * LANES : (t * (chunks - 1) + b + 1) * LANES] = acts[-1]
                else:
                    tail = jnp.where(lane < rest_sent, acts[-1].astype(jnp.float32), 0.0)
                    tails.append(tail if t == 0 else pltpu.roll(tail, t * (LANES // PAIR), 1))
        if not last:
            spread(outs[1], t, jnp.concatenate(acts, axis=1), pitch)
            return
        whole = jnp.concatenate(totals, axis=1)
        halo = pitch - 1 - half
        core, _, outer = place()
        whole = jnp.where(core == 1, pltpu.roll(whole, lanes - halo, 1), whole)
        left_half = lane < half

        def rows_of(row):
            one = whole if row == 0 else pltpu.roll(whole, lanes - row * pitch, 1)
            two = pltpu.roll(whole, lanes - (row + 1) * pitch + half, 1)
            return jnp.where(left_half, one[:, :LANES], two[:, :LANES])

        outermost, inner = rows_of(0), rows_of(2)
        outs[0][t] = jnp.where(outer, outermost, inner).astype(jnp.bfloat16)
        outs[1][t] = jnp.where(outer, inner, outermost).astype(jnp.bfloat16)

    finished = 0
    for n in range(0, len(places), side):
        rhs = jnp.concatenate([window(t, b) for t, b in places[n : n + side]], axis=1)
        tiles.append(jnp.dot(w_ref[...], rhs, preferred_element_type=jnp.float32))
        while finished < PAIR and (finished + 1) * chunks <= n + side:
            finish(finished)
            finished += 1
    if plan["fetches"]:
        laid_out(copies, held_ref, laid_ref)
    if sends and rest_sent:
        outs[2][:, PAIR * (chunks - 1) * LANES :] = sum(tails).astype(jnp.bfloat16)


def conv(plan, earlier, shifted, values, weight, columns, conv_weight):
    _, _, channels, lanes = shifted.shape
    pitch, half, received = plan["pitch"], plan["half"], plan["received"]
    if plan["last"]:
        out_shape = (jax.ShapeDtypeStruct((PAIR, channels, LANES), jnp.bfloat16),) * 2
    else:
        out_shape = (
            jax.ShapeDtypeStruct((PAIR, channels, lanes), jnp.bfloat16),
            jax.ShapeDtypeStruct((PAIR, 3, channels, rounded((plan["rows"] - 1) * pitch)), jnp.bfloat16),
        )
        if plan["sends"] and plan["rest_sent"]:
            out_shape += (jax.ShapeDtypeStruct((channels, PAIR * (lanes - LANES) + LANES), jnp.bfloat16),)
        elif plan["sends"]:
            out_shape += out_shape[:1]
    scratch = [pltpu.VMEM((PAIR, 3, channels, lanes), jnp.bfloat16)] * received
    extra = ()
    if plan["builds"]:
        out_shape += far_shapes(earlier[0].shape[1], pitch - 1 - half, channels, half)
    if plan["fetches"]:
        extra = (conv_weight,)
        out_shape += (laid_shape(conv_weight),)
        scratch += held(conv_weight)
    return pl.pallas_call(
        functools.partial(conv_kernel, plan),
        out_shape=out_shape,
        in_specs=[VMEM] * (4 + len(earlier)) + [ANY] * len(extra),
        out_specs=(VMEM,) * len(out_shape),
        scratch_shapes=scratch,
        compiler_params=pltpu.CompilerParams(vmem_limit_bytes=LIMIT),
        cost_estimate=pl.CostEstimate(
            flops=54 * channels * channels * PAIR * lanes,
            bytes_accessed=2 * weight.size,
            transcendentals=PAIR * channels * lanes,
        ),
        name=f"conv_{plan['layer']}",
    )(shifted, values, weight, columns, *earlier, *extra)


def join_kernel(pair, kept_ref, got_ref, *refs):
    out_ref, lines_ref, sem = refs[-3:]
    _, rows, _, width = lines_ref.shape
    half = width // 2
    core, group, _ = place()
    first = core == 0
    left_half = lane_of(width) < half
    for t in range(PAIR):
        mine, theirs = kept_ref[t].astype(jnp.float32), got_ref[t].astype(jnp.float32)
        left, right = jnp.where(first, mine, theirs), jnp.where(first, theirs, mine)
        lines = (
            jnp.where(left_half, left, pltpu.roll(right, half, 1)),
            jnp.where(left_half, pltpu.roll(left, half, 1), right),
        )
        for j in range(rows):
            lines_ref[t, j + group * (rows - 1 - 2 * j)] = lines[j].astype(jnp.bfloat16)
    copy = pltpu.make_async_copy(lines_ref, out_ref.at[pl.ds(PAIR * pair, PAIR)], sem)
    copy.start()
    copy.wait()


def join(pair, kept, got, shape, *so_far):
    return pl.pallas_call(
        functools.partial(join_kernel, pair),
        out_shape=jax.ShapeDtypeStruct(shape, jnp.bfloat16),
        in_specs=[VMEM, VMEM] + [ANY] * len(so_far),
        out_specs=ANY,
        scratch_shapes=[pltpu.VMEM((PAIR,) + shape[1:], jnp.bfloat16), pltpu.SemaphoreType.DMA],
        input_output_aliases={2: 0} if so_far else {},
        compiler_params=pltpu.CompilerParams(vmem_limit_bytes=LIMIT),
        name="join",
    )(kept, got, *so_far)


def on_device(latents, conv_weight, norm_gains, biases):
    layers = conv_weight.shape[0]
    frames, rows, channels, width = latents.shape
    strips, blocks = lax.axis_size("rows"), lax.axis_size("tm")
    assert strips == 4 and rows == 2 and frames % PAIR == 0 and width == LANES

    def mate_of(block):
        return lax.ppermute(block, "rows", [(i, i ^ 1) for i in range(strips)])

    def earlier_of(block):
        return lax.ppermute(block, "tm", [(i, i + 1) for i in range(blocks - 1)])

    def beyond_of(block):
        return lax.ppermute(block, "rows", [(i, i ^ 2) for i in range(strips)])

    mate = mate_of(latents)
    pairs = frames // PAIR
    own = split(latents)
    far = [beyond_of(own[p]) for p in reversed(range(pairs))][::-1]
    row_values = jnp.concatenate([norm_gains, biases], axis=0)
    weight, columns = weights(conv_weight, row_values)
    near_values, near_act = near(layers, mate, row_values, own)
    far[-1], weight, columns, near_values, near_act = lax.optimization_barrier(
        (far[-1], weight, columns, near_values, near_act)
    )
    parts = [(far[p], mate_of(far[p]), near_values[p], near_act[p]) for p in reversed(range(pairs))][::-1]
    values, shifted = [None] * pairs, [None] * pairs
    values[-1], shifted[-1], send = beyond(layers, columns, *parts[-1])
    halo, rest = earlier_of(send), 0
    half = width // 2
    pitch = half + layers + 1
    for layer in range(layers):
        last = layer == layers - 1
        rows_left = 2 * rows + layers - 1 - layer
        results = [None] * pairs
        for p in reversed(range(pairs)):
            builds = layer == 0 and p > 0
            earlier = (halo,) if p == 0 else parts[p - 1] if builds else (shifted[p - 1],)
            plan = {
                "layer": layer,
                "last": last,
                "sends": p == pairs - 1 and not last,
                "rest_sent": joined(rows_left * pitch),
                "received": p == 0,
                "rest": 0 if p else rest,
                "builds": builds,
                "fetches": p == 0 and not last,
                "inputs": len(earlier),
                "pitch": pitch,
                "half": half,
                "rows": rows_left,
            }
            outs = list(conv(plan, earlier, shifted[p], values[p], weight, columns, conv_weight))
            if plan["fetches"]:
                next_weight = outs.pop()
            if builds:
                shifted[p - 1], values[p - 1] = outs.pop(), outs.pop()
            results[p] = outs
            if plan["sends"]:
                arriving = earlier_of(outs[2])
        values, shifted = [r[0] for r in results], [r[1] for r in results]
        if not last:
            halo, rest, weight = arriving, joined(rows_left * pitch), next_weight
    result = ()
    for p in reversed(range(pairs)):
        result = (join(p, values[p], mate_of(shifted[p]), latents.shape, *result),)
    return result[0]


def solution(mesh):
    in_specs = (P(("clips", "tm"), "rows", None, None), P(), P(), P())
    out_specs = P(("clips", "tm"), "rows", None, None)
    return jax.shard_map(on_device, mesh=mesh, in_specs=in_specs, out_specs=out_specs, check_vma=False)
```

```python
import functools

import jax
import jax.numpy as jnp
from jax import lax
from jax.experimental import pallas as pl
from jax.experimental.pallas import tpu as pltpu
from jax.sharding import PartitionSpec as P

EPSILON = 1e-06
PAIR = 2
LANES = 128
TILE = 256
VMEM = pl.BlockSpec(memory_space=pltpu.VMEM)
ANY = pl.BlockSpec(memory_space=pl.ANY)
LIMIT = 24 * 1024 * 1024
LARGE = 44 * 1024 * 1024


def place():
    strip = lax.axis_index("rows").astype(jnp.int32)
    core, group = strip & 1, strip >> 1
    return core, group, core == group


def rounded(lanes):
    return -(-lanes // LANES) * LANES


def column(row):
    return jnp.transpose(jnp.broadcast_to(row, (LANES, row.shape[1])))


def lane_of(lanes):
    return lax.broadcasted_iota(jnp.int32, (1, lanes), 1)


def filled(lanes, pitch):
    lane = lane_of(lanes)
    gaps = lane < 0
    for end in range(pitch - 1, lanes, pitch):
        gaps = gaps | (lane == end)
    return jnp.where(gaps, 0.0, 1.0)


def activated(values, gain, mask):
    squares = jnp.mean(values * values, axis=0, keepdims=True)
    halved = values * (lax.rsqrt(squares + EPSILON) * (0.5 * mask)) * gain
    return (halved + halved * jnp.tanh(halved)).astype(jnp.bfloat16)


def weights_kernel(w_ref, rows_ref, *refs):
    outs, columns_ref, held_ref, sems = refs[:-3], refs[-3], refs[-2], refs[-1]
    layers, taps, channels_out, ins = w_ref.shape
    step = taps // 3
    places = [(layer, time_tap) for layer in range(layers) for time_tap in range(3)]
    copies = []
    for n, (layer, time_tap) in enumerate(places):
        part = pl.ds(step * time_tap, step)
        copies.append(pltpu.make_async_copy(w_ref.at[layer, part], held_ref.at[n], sems.at[n]))
        copies[-1].start()
    _, flipped, _ = place()
    for layer in range(layers):
        columns_ref[layer, 0] = column(rows_ref[layer : layer + 1, :])
        columns_ref[layer, 1] = column(rows_ref[layers + layer : layers + layer + 1, :])
    for n, (layer, time_tap) in enumerate(places):
        copies[n].wait()
        for row_tap in range(3):
            source = 3 * (row_tap + flipped * (2 - 2 * row_tap))
            at = (3 * time_tap + row_tap) * ins
            outs[layer][:, at : at + ins] = held_ref[n, pl.ds(source, 3)].reshape(3 * channels_out, ins)


def weights(conv_weight, rows):
    layers, taps, outs, ins = conv_weight.shape
    one = jax.ShapeDtypeStruct((3 * outs, 9 * ins), conv_weight.dtype)
    results = pl.pallas_call(
        weights_kernel,
        out_shape=(one,) * layers + (jax.ShapeDtypeStruct((layers, 2, outs, LANES), jnp.float32),),
        in_specs=[ANY, VMEM],
        out_specs=(VMEM,) * (layers + 1),
        scratch_shapes=[
            pltpu.VMEM((3 * layers, taps // 3, outs, ins), conv_weight.dtype),
            pltpu.SemaphoreType.DMA((3 * layers,)),
        ],
        compiler_params=pltpu.CompilerParams(vmem_limit_bytes=LARGE),
        cost_estimate=pl.CostEstimate(flops=0, bytes_accessed=4 * conv_weight.size, transcendentals=0),
        name="weights",
    )(conv_weight, rows)
    return results[:-1], results[-1]


def split_kernel(in_ref, *out_refs):
    for p, out_ref in enumerate(out_refs):
        out_ref[...] = in_ref[PAIR * p : PAIR * (p + 1)]


def split(latents):
    pairs = latents.shape[0] // PAIR
    return pl.pallas_call(
        split_kernel,
        out_shape=(jax.ShapeDtypeStruct((PAIR,) + latents.shape[1:], latents.dtype),) * pairs,
        in_specs=[VMEM],
        out_specs=(VMEM,) * pairs,
        compiler_params=pltpu.CompilerParams(vmem_limit_bytes=LIMIT),
        name="split",
    )(latents)


def joined(valid):
    rest = valid % LANES
    return rest if 0 < PAIR * rest <= LANES else 0


def spread(out_ref, index, act, pitch):
    lanes = out_ref.shape[3]
    above = pltpu.roll(act, pitch, 1)
    below = pltpu.roll(act, act.shape[1] - pitch, 1)
    edge = jnp.where(lane_of(LANES) < pitch, 0.0, above[:, :LANES].astype(jnp.float32))
    out_ref[index, 0, :, :LANES] = edge.astype(jnp.bfloat16)
    out_ref[index, 0, :, LANES:] = above[:, LANES:lanes]
    out_ref[index, 1] = act[:, :lanes]
    out_ref[index, 2] = below[:, :lanes]


def placed(blocks, core, row, window, line):
    pitch, width = window + 1, line.shape[1]
    lane = lane_of(LANES)
    block, low = divmod(row * pitch, LANES)
    shift = lax.rem(low + LANES - core * (width - window), LANES)
    turned = pltpu.roll(line, shift, 1)
    here = (lane >= low) & (lane < low + window)
    blocks[block] = blocks.get(block, 0.0) + jnp.where(here, turned, 0.0)
    if low + window > LANES:
        blocks[block + 1] = blocks.get(block + 1, 0.0) + jnp.where(lane < low + window - LANES, turned, 0.0)


def near_kernel(halo, pairs, mate_ref, gains_ref, *refs):
    own_refs, value_refs, act_refs = refs[:pairs], refs[pairs : 2 * pairs], refs[2 * pairs :]
    frames, rows, _, width = mate_ref.shape
    window = width // 2 + halo
    core, group, outer = place()
    gain = column(gains_ref[0:1, :])
    done = act_refs[0].shape[2]
    mask = filled(done, window + 1)
    for f in range(frames):
        p, t = divmod(f, PAIR)
        blocks = {}
        for row in range(2 * rows):
            at = row % rows
            index = at + group * (rows - 1 - 2 * at)
            own, mate = own_refs[p][t, index], mate_ref[f, index]
            one, two = (own, mate) if row < rows else (mate, own)
            placed(blocks, core, row, window, jnp.where(outer, one, two).astype(jnp.float32))
        for b in blocks:
            part = slice(b * LANES, (b + 1) * LANES)
            value_refs[p][t, :, part] = blocks[b].astype(jnp.bfloat16)
            if part.stop <= done:
                act_refs[p][t, :, part] = activated(blocks[b], gain, mask[:, part])


def near(halo, mate, gains, own):
    frames, rows, channels, width = mate.shape
    lanes = 2 * rows * (width // 2 + halo + 1)
    pairs = len(own)
    outs = pl.pallas_call(
        functools.partial(near_kernel, halo, pairs),
        out_shape=(jax.ShapeDtypeStruct((PAIR, channels, rounded(lanes)), jnp.bfloat16),) * pairs
        + (jax.ShapeDtypeStruct((PAIR, channels, lanes // LANES * LANES), jnp.bfloat16),) * pairs,
        in_specs=[VMEM] * (2 + pairs),
        out_specs=(VMEM,) * (2 * pairs),
        compiler_params=pltpu.CompilerParams(vmem_limit_bytes=LIMIT),
        cost_estimate=pl.CostEstimate(flops=40 * mate.size, bytes_accessed=8 * mate.size, transcendentals=2 * mate.size),
        name="near",
    )(mate, gains, *own)
    return outs[:pairs], outs[pairs:]


def add_far(halo, far_ref, mate_ref, near_ref, act_ref, columns_ref, values_ref, shifted_ref, send_ref=None):
    pair, rows, _, width = far_ref.shape
    window = width // 2 + halo
    core, group, outer = place()
    lanes, done = values_ref.shape[2], act_ref.shape[2]
    mask = filled(lanes, window + 1)
    for t in range(pair):
        values_ref[t, :, :done] = near_ref[t, :, :done]
        acts = [act_ref[t]]
        blocks = {done // LANES: near_ref[t, :, done:].astype(jnp.float32)}
        for row in range(2 * rows, 2 * rows + halo):
            local = 4 * rows - 1 - row
            at = local % rows
            index = at + (1 - group) * (rows - 1 - 2 * at)
            one, two = (mate_ref, far_ref) if local < rows else (far_ref, mate_ref)
            line = jnp.where(outer, one[t, index], two[t, index]).astype(jnp.float32)
            placed(blocks, core, row, window, line)
        for b in sorted(blocks):
            part = slice(b * LANES, (b + 1) * LANES)
            values_ref[t, :, part] = blocks[b].astype(jnp.bfloat16)
            acts.append(activated(blocks[b], columns_ref[0, 0], mask[:, part]))
        act = jnp.concatenate(acts, axis=1)
        spread(shifted_ref, t, act, window + 1)
        if send_ref is not None:
            send_ref[t] = act


def far_shapes(rows, halo, channels, half):
    pitch = half + halo + 1
    return (
        jax.ShapeDtypeStruct((PAIR, channels, rounded((2 * rows + halo) * pitch)), jnp.bfloat16),
        jax.ShapeDtypeStruct((PAIR, 3, channels, rounded((2 * rows + halo - 1) * pitch)), jnp.bfloat16),
    )


def beyond(halo, columns, *parts):
    far = parts[0]
    _, rows, channels, width = far.shape
    values, shifted = far_shapes(rows, halo, channels, width // 2)

    def kernel(columns_ref, far_ref, mate_ref, near_ref, act_ref, *outs):
        add_far(halo, far_ref, mate_ref, near_ref, act_ref, columns_ref, *outs)

    return pl.pallas_call(
        kernel,
        out_shape=(values, shifted, values),
        in_specs=[VMEM] * 5,
        out_specs=(VMEM,) * 3,
        compiler_params=pltpu.CompilerParams(vmem_limit_bytes=LIMIT),
        cost_estimate=pl.CostEstimate(flops=40 * far.size, bytes_accessed=8 * far.size, transcendentals=2 * far.size),
        name="beyond",
    )(columns, *parts)


def conv_kernel(plan, shifted_ref, values_ref, w_ref, columns_ref, *refs):
    layer, pitch, half, received = plan["layer"], plan["pitch"], plan["half"], plan["received"]
    last, sends, rest, rest_sent = plan["last"], plan["sends"], plan["rest"], plan["rest_sent"]
    refs = list(refs)
    earlier_refs = [refs.pop(0) for _ in range(plan["inputs"])]
    earlier_ref = refs.pop() if received else earlier_refs[0]
    if received:
        for t in range(PAIR):
            if rest:
                whole = (earlier_refs[0].shape[1] - LANES) // PAIR
                tail = earlier_refs[0][:, PAIR * whole :].astype(jnp.float32)
                tail = tail if t == 0 else pltpu.roll(tail, LANES - t * (LANES // PAIR), 1)
                tail = jnp.where(lane_of(LANES) < rest, tail, 0.0).astype(jnp.bfloat16)
                act = jnp.concatenate([earlier_refs[0][:, t * whole : (t + 1) * whole], tail], axis=1)
            else:
                act = earlier_refs[0][t]
            spread(earlier_ref, t, act, pitch)
    outs = refs
    if plan["builds"]:
        earlier_ref = outs.pop()
        add_far(pitch - 1 - half, *earlier_refs, columns_ref, outs.pop(), earlier_ref)
    _, _, channels, lanes = shifted_ref.shape
    chunks = lanes // LANES
    lane = lane_of(LANES)

    def window(t, b):
        taken = [(earlier_ref, t + a) if t + a < PAIR else (shifted_ref, t + a - PAIR) for a in range(3)]
        at = slice(b * LANES, (b + 1) * LANES)
        return jnp.concatenate([ref[j, :, :, at].reshape(3 * channels, LANES) for ref, j in taken], axis=0)

    places = [(t, b) for t in range(PAIR) for b in range(chunks)]
    side = TILE // LANES
    tiles = []
    bias = columns_ref[layer, 1]
    if not last:
        mask = filled(lanes, pitch)
        gain = columns_ref[layer + 1, 0]

    def sums(t, tap, b):
        tile, at = divmod((t * chunks + b) * LANES, TILE)
        return tiles[tile][tap * channels : (tap + 1) * channels, at : at + LANES]

    tails = []

    def finish(t):
        totals, acts = [], []
        from_left = 0.0
        from_right = pltpu.roll(sums(t, 2, 0), LANES - 1, 1)
        for b in range(chunks):
            at = slice(b * LANES, (b + 1) * LANES)
            left = pltpu.roll(sums(t, 0, b), 1, 1)
            right = pltpu.roll(sums(t, 2, b + 1), LANES - 1, 1) if b + 1 < chunks else 0.0
            summed = (
                jnp.where(lane == 0, from_left, left) + sums(t, 1, b) + jnp.where(lane == LANES - 1, right, from_right)
            )
            from_left, from_right = left, right
            total = (values_ref[t, :, at].astype(jnp.float32) + summed + bias).astype(jnp.bfloat16)
            totals.append(total.astype(jnp.float32))
            if not last:
                outs[0][t, :, at] = total
                acts.append(activated(totals[-1], gain, mask[:, at]))
                if not sends:
                    continue
                if not rest_sent:
                    outs[2][t, :, at] = acts[-1]
                elif b < chunks - 1:
                    outs[2][:, (t * (chunks - 1) + b) * LANES : (t * (chunks - 1) + b + 1) * LANES] = acts[-1]
                else:
                    tail = jnp.where(lane < rest_sent, acts[-1].astype(jnp.float32), 0.0)
                    tails.append(tail if t == 0 else pltpu.roll(tail, t * (LANES // PAIR), 1))
        if not last:
            spread(outs[1], t, jnp.concatenate(acts, axis=1), pitch)
            return
        whole = jnp.concatenate(totals, axis=1)
        halo = pitch - 1 - half
        core, _, outer = place()
        whole = jnp.where(core == 1, pltpu.roll(whole, lanes - halo, 1), whole)
        left_half = lane < half

        def rows_of(row):
            one = whole if row == 0 else pltpu.roll(whole, lanes - row * pitch, 1)
            two = pltpu.roll(whole, lanes - (row + 1) * pitch + half, 1)
            return jnp.where(left_half, one[:, :LANES], two[:, :LANES])

        outermost, inner = rows_of(0), rows_of(2)
        outs[0][t] = jnp.where(outer, outermost, inner).astype(jnp.bfloat16)
        outs[1][t] = jnp.where(outer, inner, outermost).astype(jnp.bfloat16)

    finished = 0
    for n in range(0, len(places), side):
        rhs = jnp.concatenate([window(t, b) for t, b in places[n : n + side]], axis=1)
        tiles.append(jnp.dot(w_ref[...], rhs, preferred_element_type=jnp.float32))
        while finished < PAIR and (finished + 1) * chunks <= n + side:
            finish(finished)
            finished += 1
    if sends and rest_sent:
        outs[2][:, PAIR * (chunks - 1) * LANES :] = sum(tails).astype(jnp.bfloat16)


def conv(plan, earlier, shifted, values, weight, columns):
    _, _, channels, lanes = shifted.shape
    pitch, half, received = plan["pitch"], plan["half"], plan["received"]
    if plan["last"]:
        out_shape = (jax.ShapeDtypeStruct((PAIR, channels, LANES), jnp.bfloat16),) * 2
    else:
        out_shape = (
            jax.ShapeDtypeStruct((PAIR, channels, lanes), jnp.bfloat16),
            jax.ShapeDtypeStruct((PAIR, 3, channels, rounded((plan["rows"] - 1) * pitch)), jnp.bfloat16),
        )
        if plan["sends"] and plan["rest_sent"]:
            out_shape += (jax.ShapeDtypeStruct((channels, PAIR * (lanes - LANES) + LANES), jnp.bfloat16),)
        elif plan["sends"]:
            out_shape += out_shape[:1]
    scratch = [pltpu.VMEM((PAIR, 3, channels, lanes), jnp.bfloat16)] * received
    if plan["builds"]:
        out_shape += far_shapes(earlier[0].shape[1], pitch - 1 - half, channels, half)
    return pl.pallas_call(
        functools.partial(conv_kernel, plan),
        out_shape=out_shape,
        in_specs=[VMEM] * (4 + len(earlier)),
        out_specs=(VMEM,) * len(out_shape),
        scratch_shapes=scratch,
        compiler_params=pltpu.CompilerParams(vmem_limit_bytes=LIMIT),
        cost_estimate=pl.CostEstimate(
            flops=54 * channels * channels * PAIR * lanes,
            bytes_accessed=2 * weight.size,
            transcendentals=PAIR * channels * lanes,
        ),
        name=f"conv_{plan['layer']}",
    )(shifted, values, weight, columns, *earlier)


def join_kernel(pair, kept_ref, got_ref, *refs):
    out_ref, lines_ref, sem = refs[-3:]
    _, rows, _, width = lines_ref.shape
    half = width // 2
    core, group, _ = place()
    first = core == 0
    left_half = lane_of(width) < half
    for t in range(PAIR):
        mine, theirs = kept_ref[t].astype(jnp.float32), got_ref[t].astype(jnp.float32)
        left, right = jnp.where(first, mine, theirs), jnp.where(first, theirs, mine)
        lines = (
            jnp.where(left_half, left, pltpu.roll(right, half, 1)),
            jnp.where(left_half, pltpu.roll(left, half, 1), right),
        )
        for j in range(rows):
            lines_ref[t, j + group * (rows - 1 - 2 * j)] = lines[j].astype(jnp.bfloat16)
    copy = pltpu.make_async_copy(lines_ref, out_ref.at[pl.ds(PAIR * pair, PAIR)], sem)
    copy.start()
    copy.wait()


def join(pair, kept, got, shape, *so_far):
    return pl.pallas_call(
        functools.partial(join_kernel, pair),
        out_shape=jax.ShapeDtypeStruct(shape, jnp.bfloat16),
        in_specs=[VMEM, VMEM] + [ANY] * len(so_far),
        out_specs=ANY,
        scratch_shapes=[pltpu.VMEM((PAIR,) + shape[1:], jnp.bfloat16), pltpu.SemaphoreType.DMA],
        input_output_aliases={2: 0} if so_far else {},
        compiler_params=pltpu.CompilerParams(vmem_limit_bytes=LIMIT),
        name="join",
    )(kept, got, *so_far)


def on_device(latents, conv_weight, norm_gains, biases):
    layers = conv_weight.shape[0]
    frames, rows, channels, width = latents.shape
    strips, blocks = lax.axis_size("rows"), lax.axis_size("tm")
    assert strips == 4 and rows == 2 and frames % PAIR == 0 and width == LANES

    def mate_of(block):
        return lax.ppermute(block, "rows", [(i, i ^ 1) for i in range(strips)])

    def earlier_of(block):
        return lax.ppermute(block, "tm", [(i, i + 1) for i in range(blocks - 1)])

    def beyond_of(block):
        return lax.ppermute(block, "rows", [(i, i ^ 2) for i in range(strips)])

    mate = mate_of(latents)
    pairs = frames // PAIR
    own = split(latents)
    far = [beyond_of(own[p]) for p in reversed(range(pairs))][::-1]
    row_values = jnp.concatenate([norm_gains, biases], axis=0)
    weight, columns = weights(conv_weight, row_values)
    near_values, near_act = near(layers, mate, row_values, own)
    far[-1], weight, columns, near_values, near_act = lax.optimization_barrier(
        (far[-1], weight, columns, near_values, near_act)
    )
    parts = [(far[p], mate_of(far[p]), near_values[p], near_act[p]) for p in reversed(range(pairs))][::-1]
    values, shifted = [None] * pairs, [None] * pairs
    values[-1], shifted[-1], send = beyond(layers, columns, *parts[-1])
    halo, rest = earlier_of(send), 0
    half = width // 2
    pitch = half + layers + 1
    for layer in range(layers):
        last = layer == layers - 1
        rows_left = 2 * rows + layers - 1 - layer
        results = [None] * pairs
        for p in reversed(range(pairs)):
            builds = layer == 0 and p > 0
            earlier = (halo,) if p == 0 else parts[p - 1] if builds else (shifted[p - 1],)
            plan = {
                "layer": layer,
                "last": last,
                "sends": p == pairs - 1 and not last,
                "rest_sent": joined(rows_left * pitch),
                "received": p == 0,
                "rest": 0 if p else rest,
                "builds": builds,
                "inputs": len(earlier),
                "pitch": pitch,
                "half": half,
                "rows": rows_left,
            }
            outs = list(conv(plan, earlier, shifted[p], values[p], weight[layer], columns))
            if builds:
                shifted[p - 1], values[p - 1] = outs.pop(), outs.pop()
            results[p] = outs
            if plan["sends"]:
                arriving = earlier_of(outs[2])
        values, shifted = [r[0] for r in results], [r[1] for r in results]
        if not last:
            halo, rest = arriving, joined(rows_left * pitch)
    result = ()
    for p in reversed(range(pairs)):
        result = (join(p, values[p], mate_of(shifted[p]), latents.shape, *result),)
    return result[0]


def solution(mesh):
    in_specs = (P(("clips", "tm"), "rows", None, None), P(), P(), P())
    out_specs = P(("clips", "tm"), "rows", None, None)
    return jax.shard_map(on_device, mesh=mesh, in_specs=in_specs, out_specs=out_specs, check_vma=False)
```

```python
import functools

import jax
import jax.numpy as jnp
from jax import lax
from jax.experimental import pallas as pl
from jax.experimental.pallas import tpu as pltpu
from jax.sharding import PartitionSpec as P

EPSILON = 1e-06
PAIR = 2
LANES = 128
TILE = 256
VMEM = pl.BlockSpec(memory_space=pltpu.VMEM)
ANY = pl.BlockSpec(memory_space=pl.ANY)
LIMIT = 24 * 1024 * 1024
LARGE = 44 * 1024 * 1024


def place():
    strip = lax.axis_index("rows").astype(jnp.int32)
    core, group = strip & 1, strip >> 1
    return core, group, core == group


def rounded(lanes):
    return -(-lanes // LANES) * LANES


def column(row):
    return jnp.transpose(jnp.broadcast_to(row, (LANES, row.shape[1])))


def lane_of(lanes):
    return lax.broadcasted_iota(jnp.int32, (1, lanes), 1)


def filled(lanes, pitch):
    lane = lane_of(lanes)
    gaps = lane < 0
    for end in range(pitch - 1, lanes, pitch):
        gaps = gaps | (lane == end)
    return jnp.where(gaps, 0.0, 1.0)


def activated(values, gain, mask):
    squares = jnp.mean(values * values, axis=0, keepdims=True)
    halved = values * (lax.rsqrt(squares + EPSILON) * (0.5 * mask)) * gain
    return (halved + halved * jnp.tanh(halved)).astype(jnp.bfloat16)


def weights_kernel(w_ref, rows_ref, *refs):
    outs, columns_ref, held_ref, sems = refs[:-3], refs[-3], refs[-2], refs[-1]
    layers, taps, channels_out, ins = w_ref.shape
    step = taps // 3
    places = [(layer, time_tap) for layer in range(layers) for time_tap in range(3)]
    copies = []
    for n, (layer, time_tap) in enumerate(places):
        part = pl.ds(step * time_tap, step)
        copies.append(pltpu.make_async_copy(w_ref.at[layer, part], held_ref.at[n], sems.at[n]))
        copies[-1].start()
    _, flipped, _ = place()
    for layer in range(layers):
        columns_ref[layer, 0] = column(rows_ref[layer : layer + 1, :])
        columns_ref[layer, 1] = column(rows_ref[layers + layer : layers + layer + 1, :])
    for n, (layer, time_tap) in enumerate(places):
        copies[n].wait()
        for row_tap in range(3):
            source = 3 * (row_tap + flipped * (2 - 2 * row_tap))
            at = (3 * (2 - time_tap) + row_tap) * ins
            outs[layer][:, at : at + ins] = held_ref[n, pl.ds(source, 3)].reshape(3 * channels_out, ins)


def weights(conv_weight, rows):
    layers, taps, outs, ins = conv_weight.shape
    one = jax.ShapeDtypeStruct((3 * outs, 9 * ins), conv_weight.dtype)
    results = pl.pallas_call(
        weights_kernel,
        out_shape=(one,) * layers + (jax.ShapeDtypeStruct((layers, 2, outs, LANES), jnp.float32),),
        in_specs=[ANY, VMEM],
        out_specs=(VMEM,) * (layers + 1),
        scratch_shapes=[
            pltpu.VMEM((3 * layers, taps // 3, outs, ins), conv_weight.dtype),
            pltpu.SemaphoreType.DMA((3 * layers,)),
        ],
        compiler_params=pltpu.CompilerParams(vmem_limit_bytes=LARGE),
        cost_estimate=pl.CostEstimate(flops=0, bytes_accessed=4 * conv_weight.size, transcendentals=0),
        name="weights",
    )(conv_weight, rows)
    return results[:-1], results[-1]


def split_kernel(in_ref, *out_refs):
    for p, out_ref in enumerate(out_refs):
        out_ref[...] = in_ref[PAIR * p : PAIR * (p + 1)]


def split(latents):
    pairs = latents.shape[0] // PAIR
    return pl.pallas_call(
        split_kernel,
        out_shape=(jax.ShapeDtypeStruct((PAIR,) + latents.shape[1:], latents.dtype),) * pairs,
        in_specs=[VMEM],
        out_specs=(VMEM,) * pairs,
        compiler_params=pltpu.CompilerParams(vmem_limit_bytes=LIMIT),
        name="split",
    )(latents)


def joined(valid):
    rest = valid % LANES
    return rest if 0 < PAIR * rest <= LANES else 0


def spread(out_ref, index, act, pitch):
    lanes = out_ref.shape[3]
    above = pltpu.roll(act, pitch, 1)
    below = pltpu.roll(act, act.shape[1] - pitch, 1)
    edge = jnp.where(lane_of(LANES) < pitch, 0.0, above[:, :LANES].astype(jnp.float32))
    out_ref[index, 0, :, :LANES] = edge.astype(jnp.bfloat16)
    out_ref[index, 0, :, LANES:] = above[:, LANES:lanes]
    out_ref[index, 1] = act[:, :lanes]
    out_ref[index, 2] = below[:, :lanes]


def placed(blocks, core, row, window, line):
    pitch, width = window + 1, line.shape[1]
    lane = lane_of(LANES)
    block, low = divmod(row * pitch, LANES)
    shift = lax.rem(low + LANES - core * (width - window), LANES)
    turned = pltpu.roll(line, shift, 1)
    here = (lane >= low) & (lane < low + window)
    blocks[block] = blocks.get(block, 0.0) + jnp.where(here, turned, 0.0)
    if low + window > LANES:
        blocks[block + 1] = blocks.get(block + 1, 0.0) + jnp.where(lane < low + window - LANES, turned, 0.0)


def near_kernel(halo, pairs, mate_ref, gains_ref, *refs):
    own_refs, value_refs, act_refs = refs[:pairs], refs[pairs : 2 * pairs], refs[2 * pairs :]
    frames, rows, _, width = mate_ref.shape
    window = width // 2 + halo
    core, group, outer = place()
    gain = column(gains_ref[0:1, :])
    done = act_refs[0].shape[2]
    mask = filled(done, window + 1)
    for f in range(frames):
        p, t = divmod(f, PAIR)
        blocks = {}
        for row in range(2 * rows):
            at = row % rows
            index = at + group * (rows - 1 - 2 * at)
            own, mate = own_refs[p][t, index], mate_ref[f, index]
            one, two = (own, mate) if row < rows else (mate, own)
            placed(blocks, core, row, window, jnp.where(outer, one, two).astype(jnp.float32))
        for b in blocks:
            part = slice(b * LANES, (b + 1) * LANES)
            value_refs[p][t, :, part] = blocks[b].astype(jnp.bfloat16)
            if part.stop <= done:
                act_refs[p][t, :, part] = activated(blocks[b], gain, mask[:, part])


def near(halo, mate, gains, own):
    frames, rows, channels, width = mate.shape
    lanes = 2 * rows * (width // 2 + halo + 1)
    pairs = len(own)
    outs = pl.pallas_call(
        functools.partial(near_kernel, halo, pairs),
        out_shape=(jax.ShapeDtypeStruct((PAIR, channels, rounded(lanes)), jnp.bfloat16),) * pairs
        + (jax.ShapeDtypeStruct((PAIR, channels, lanes // LANES * LANES), jnp.bfloat16),) * pairs,
        in_specs=[VMEM] * (2 + pairs),
        out_specs=(VMEM,) * (2 * pairs),
        compiler_params=pltpu.CompilerParams(vmem_limit_bytes=LIMIT),
        cost_estimate=pl.CostEstimate(flops=40 * mate.size, bytes_accessed=8 * mate.size, transcendentals=2 * mate.size),
        name="near",
    )(mate, gains, *own)
    return outs[:pairs], outs[pairs:]


def add_far(halo, far_ref, mate_ref, near_ref, act_ref, columns_ref, values_ref, shifted_ref, send_ref=None):
    pair, rows, _, width = far_ref.shape
    window = width // 2 + halo
    core, group, outer = place()
    lanes, done = values_ref.shape[2], act_ref.shape[2]
    mask = filled(lanes, window + 1)
    for t in range(pair):
        values_ref[t, :, :done] = near_ref[t, :, :done]
        acts = [act_ref[t]]
        blocks = {done // LANES: near_ref[t, :, done:].astype(jnp.float32)}
        for row in range(2 * rows, 2 * rows + halo):
            local = 4 * rows - 1 - row
            at = local % rows
            index = at + (1 - group) * (rows - 1 - 2 * at)
            one, two = (mate_ref, far_ref) if local < rows else (far_ref, mate_ref)
            line = jnp.where(outer, one[t, index], two[t, index]).astype(jnp.float32)
            placed(blocks, core, row, window, line)
        for b in sorted(blocks):
            part = slice(b * LANES, (b + 1) * LANES)
            values_ref[t, :, part] = blocks[b].astype(jnp.bfloat16)
            acts.append(activated(blocks[b], columns_ref[0, 0], mask[:, part]))
        act = jnp.concatenate(acts, axis=1)
        spread(shifted_ref, t, act, window + 1)
        if send_ref is not None:
            send_ref[t] = act


def far_shapes(rows, halo, channels, half):
    pitch = half + halo + 1
    return (
        jax.ShapeDtypeStruct((PAIR, channels, rounded((2 * rows + halo) * pitch)), jnp.bfloat16),
        jax.ShapeDtypeStruct((PAIR, 3, channels, rounded((2 * rows + halo - 1) * pitch)), jnp.bfloat16),
    )


def beyond(halo, columns, *parts):
    far = parts[0]
    _, rows, channels, width = far.shape
    values, shifted = far_shapes(rows, halo, channels, width // 2)

    def kernel(columns_ref, far_ref, mate_ref, near_ref, act_ref, *outs):
        add_far(halo, far_ref, mate_ref, near_ref, act_ref, columns_ref, *outs)

    return pl.pallas_call(
        kernel,
        out_shape=(values, shifted, values),
        in_specs=[VMEM] * 5,
        out_specs=(VMEM,) * 3,
        compiler_params=pltpu.CompilerParams(vmem_limit_bytes=LIMIT),
        cost_estimate=pl.CostEstimate(flops=40 * far.size, bytes_accessed=8 * far.size, transcendentals=2 * far.size),
        name="beyond",
    )(columns, *parts)


def lines_of(ref, frame):
    return ref[frame].reshape(3 * ref.shape[2], ref.shape[3])


def by_taps(sums):
    channels, lanes = sums.shape[0] // 3, sums.shape[1]
    return [
        [sums[tap * channels : (tap + 1) * channels, at : at + LANES] for at in range(0, lanes, LANES)]
        for tap in range(3)
    ]


def column_sums(taps):
    lane = lane_of(LANES)
    left, middle, right = taps
    lefts = [pltpu.roll(block, 1, 1) for block in left]
    rights = [pltpu.roll(block, LANES - 1, 1) for block in right] + [0.0]
    return [
        jnp.where(lane == 0, lefts[b - 1] if b else 0.0, lefts[b])
        + middle[b]
        + jnp.where(lane == LANES - 1, rights[b + 1], rights[b])
        for b in range(len(middle))
    ]


def begin_kernel(shifted_ref, w_ref, out_ref):
    depth = 3 * shifted_ref.shape[2]
    for t in range(PAIR):
        rhs = jnp.concatenate([lines_of(shifted_ref, j) for j in range(t, -1, -1)], axis=0)
        sums = jnp.dot(w_ref[:, : (t + 1) * depth], rhs, preferred_element_type=jnp.float32)
        for b, block in enumerate(column_sums(by_taps(sums))):
            out_ref[t, :, b * LANES : (b + 1) * LANES] = block


def begin(shifted, weight):
    _, _, channels, lanes = shifted.shape
    return pl.pallas_call(
        begin_kernel,
        out_shape=jax.ShapeDtypeStruct((PAIR, channels, lanes), jnp.float32),
        in_specs=[VMEM] * 2,
        out_specs=VMEM,
        compiler_params=pltpu.CompilerParams(vmem_limit_bytes=LIMIT),
        cost_estimate=pl.CostEstimate(flops=0, bytes_accessed=0, transcendentals=0),
        name="begin",
    )(shifted, weight)


def conv_kernel(plan, shifted_ref, values_ref, w_ref, columns_ref, *refs):
    layer, pitch, half, received = plan["layer"], plan["pitch"], plan["half"], plan["received"]
    last, sends, rest, rest_sent = plan["last"], plan["sends"], plan["rest"], plan["rest_sent"]
    refs = list(refs)
    begun_ref = refs.pop(0) if plan["begun"] else None
    earlier_refs = [refs.pop(0) for _ in range(plan["inputs"])]
    earlier_ref = refs.pop() if received else earlier_refs[0]
    if received:
        for t in range(PAIR):
            if rest:
                whole = (earlier_refs[0].shape[1] - LANES) // PAIR
                tail = earlier_refs[0][:, PAIR * whole :].astype(jnp.float32)
                tail = tail if t == 0 else pltpu.roll(tail, LANES - t * (LANES // PAIR), 1)
                tail = jnp.where(lane_of(LANES) < rest, tail, 0.0).astype(jnp.bfloat16)
                act = jnp.concatenate([earlier_refs[0][:, t * whole : (t + 1) * whole], tail], axis=1)
            else:
                act = earlier_refs[0][t]
            spread(earlier_ref, t, act, pitch)
    outs = refs
    if plan["builds"]:
        earlier_ref = outs.pop()
        add_far(pitch - 1 - half, *earlier_refs, columns_ref, outs.pop(), earlier_ref)
    _, _, channels, lanes = shifted_ref.shape
    chunks = lanes // LANES
    lane = lane_of(LANES)

    def window(t, b):
        taken = [(earlier_ref, t + a) if t + a < PAIR else (shifted_ref, t + a - PAIR) for a in (2, 1, 0)]
        at = slice(b * LANES, (b + 1) * LANES)
        return jnp.concatenate([ref[j, :, :, at].reshape(3 * channels, LANES) for ref, j in taken], axis=0)

    bias = columns_ref[layer, 1]
    tails = []
    if not last:
        mask = filled(lanes, pitch)
        gain = columns_ref[layer + 1, 0]

    def finish(t, taps):
        totals, acts = [], []
        for b, conv in enumerate(column_sums(taps)):
            at = slice(b * LANES, (b + 1) * LANES)
            if begun_ref is not None:
                conv = conv + begun_ref[t, :, at]
            total = (values_ref[t, :, at].astype(jnp.float32) + conv + bias).astype(jnp.bfloat16)
            totals.append(total.astype(jnp.float32))
            if last:
                continue
            outs[0][t, :, at] = total
            acts.append(activated(totals[-1], gain, mask[:, at]))
            if not sends:
                continue
            if not rest_sent:
                outs[2][t, :, at] = acts[-1]
            elif b < chunks - 1:
                outs[2][:, (t * (chunks - 1) + b) * LANES : (t * (chunks - 1) + b + 1) * LANES] = acts[-1]
            else:
                tail = jnp.where(lane < rest_sent, acts[-1].astype(jnp.float32), 0.0)
                tails.append(tail if t == 0 else pltpu.roll(tail, t * (LANES // PAIR), 1))
        if not last:
            spread(outs[1], t, jnp.concatenate(acts, axis=1), pitch)
            return
        whole = jnp.concatenate(totals, axis=1)
        halo = pitch - 1 - half
        core, _, outer = place()
        whole = jnp.where(core == 1, pltpu.roll(whole, lanes - halo, 1), whole)
        left_half = lane < half

        def rows_of(row):
            one = whole if row == 0 else pltpu.roll(whole, lanes - row * pitch, 1)
            two = pltpu.roll(whole, lanes - (row + 1) * pitch + half, 1)
            return jnp.where(left_half, one[:, :LANES], two[:, :LANES])

        outermost, inner = rows_of(0), rows_of(2)
        outs[0][t] = jnp.where(outer, outermost, inner).astype(jnp.bfloat16)
        outs[1][t] = jnp.where(outer, inner, outermost).astype(jnp.bfloat16)

    if plan["begun"]:
        depth = 3 * channels
        for t in range(PAIR):
            at = (t + 1) * depth
            lead = at % LANES
            lines = [lines_of(earlier_ref, j) for j in range(PAIR - 1, t - 1, -1)]
            if lead:
                lines.insert(0, jnp.zeros((lead, lanes), jnp.bfloat16))
            sums = jnp.dot(w_ref[:, at - lead :], jnp.concatenate(lines, axis=0), preferred_element_type=jnp.float32)
            finish(t, by_taps(sums))
    else:
        places = [(t, b) for t in range(PAIR) for b in range(chunks)]
        side = TILE // LANES
        taps = {t: [[], [], []] for t in range(PAIR)}
        finished = 0
        for n in range(0, len(places), side):
            rhs = jnp.concatenate([window(t, b) for t, b in places[n : n + side]], axis=1)
            sums = by_taps(jnp.dot(w_ref[...], rhs, preferred_element_type=jnp.float32))
            for i, (t, _) in enumerate(places[n : n + side]):
                for tap in range(3):
                    taps[t][tap].append(sums[tap][i])
            while finished < PAIR and (finished + 1) * chunks <= n + side:
                finish(finished, taps[finished])
                finished += 1
    if sends and rest_sent:
        outs[2][:, PAIR * (chunks - 1) * LANES :] = sum(tails).astype(jnp.bfloat16)


def conv(plan, begun, earlier, shifted, values, weight, columns):
    _, _, channels, lanes = shifted.shape
    pitch, half, received = plan["pitch"], plan["half"], plan["received"]
    if plan["last"]:
        out_shape = (jax.ShapeDtypeStruct((PAIR, channels, LANES), jnp.bfloat16),) * 2
    else:
        out_shape = (
            jax.ShapeDtypeStruct((PAIR, channels, lanes), jnp.bfloat16),
            jax.ShapeDtypeStruct((PAIR, 3, channels, rounded((plan["rows"] - 1) * pitch)), jnp.bfloat16),
        )
        if plan["sends"] and plan["rest_sent"]:
            out_shape += (jax.ShapeDtypeStruct((channels, PAIR * (lanes - LANES) + LANES), jnp.bfloat16),)
        elif plan["sends"]:
            out_shape += out_shape[:1]
    scratch = [pltpu.VMEM((PAIR, 3, channels, lanes), jnp.bfloat16)] * received
    if plan["builds"]:
        out_shape += far_shapes(earlier[0].shape[1], pitch - 1 - half, channels, half)
    return pl.pallas_call(
        functools.partial(conv_kernel, plan),
        out_shape=out_shape,
        in_specs=[VMEM] * (4 + len(begun) + len(earlier)),
        out_specs=(VMEM,) * len(out_shape),
        scratch_shapes=scratch,
        compiler_params=pltpu.CompilerParams(vmem_limit_bytes=LIMIT),
        cost_estimate=pl.CostEstimate(
            flops=54 * channels * channels * PAIR * lanes,
            bytes_accessed=2 * weight.size,
            transcendentals=PAIR * channels * lanes,
        ),
        name=f"conv_{plan['layer']}",
    )(shifted, values, weight, columns, *begun, *earlier)


def join_kernel(pair, kept_ref, got_ref, *refs):
    out_ref, lines_ref, sem = refs[-3:]
    _, rows, _, width = lines_ref.shape
    half = width // 2
    core, group, _ = place()
    first = core == 0
    left_half = lane_of(width) < half
    for t in range(PAIR):
        mine, theirs = kept_ref[t].astype(jnp.float32), got_ref[t].astype(jnp.float32)
        left, right = jnp.where(first, mine, theirs), jnp.where(first, theirs, mine)
        lines = (
            jnp.where(left_half, left, pltpu.roll(right, half, 1)),
            jnp.where(left_half, pltpu.roll(left, half, 1), right),
        )
        for j in range(rows):
            lines_ref[t, j + group * (rows - 1 - 2 * j)] = lines[j].astype(jnp.bfloat16)
    copy = pltpu.make_async_copy(lines_ref, out_ref.at[pl.ds(PAIR * pair, PAIR)], sem)
    copy.start()
    copy.wait()


def join(pair, kept, got, shape, *so_far):
    return pl.pallas_call(
        functools.partial(join_kernel, pair),
        out_shape=jax.ShapeDtypeStruct(shape, jnp.bfloat16),
        in_specs=[VMEM, VMEM] + [ANY] * len(so_far),
        out_specs=ANY,
        scratch_shapes=[pltpu.VMEM((PAIR,) + shape[1:], jnp.bfloat16), pltpu.SemaphoreType.DMA],
        input_output_aliases={2: 0} if so_far else {},
        compiler_params=pltpu.CompilerParams(vmem_limit_bytes=LIMIT),
        name="join",
    )(kept, got, *so_far)


def on_device(latents, conv_weight, norm_gains, biases):
    layers = conv_weight.shape[0]
    frames, rows, channels, width = latents.shape
    strips, blocks = lax.axis_size("rows"), lax.axis_size("tm")
    assert strips == 4 and rows == 2 and frames % PAIR == 0 and width == LANES

    def mate_of(block):
        return lax.ppermute(block, "rows", [(i, i ^ 1) for i in range(strips)])

    def earlier_of(block):
        return lax.ppermute(block, "tm", [(i, i + 1) for i in range(blocks - 1)])

    def beyond_of(block):
        return lax.ppermute(block, "rows", [(i, i ^ 2) for i in range(strips)])

    mate = mate_of(latents)
    pairs = frames // PAIR
    own = split(latents)
    far = [beyond_of(own[p]) for p in reversed(range(pairs))][::-1]
    row_values = jnp.concatenate([norm_gains, biases], axis=0)
    weight, columns = weights(conv_weight, row_values)
    near_values, near_act = near(layers, mate, row_values, own)
    far[-1], weight, columns, near_values, near_act = lax.optimization_barrier(
        (far[-1], weight, columns, near_values, near_act)
    )
    values, shifted = [None] * pairs, [None] * pairs
    values[-1], shifted[-1], send = beyond(
        layers, columns, far[-1], mate_of(far[-1]), near_values[-1], near_act[-1]
    )
    halo, rest = earlier_of(send), 0
    first_begun = begin(shifted[-1], weight[0])
    *far[:-1], first_begun = lax.optimization_barrier((*far[:-1], first_begun))
    parts = [(far[p], mate_of(far[p]), near_values[p], near_act[p]) for p in reversed(range(pairs - 1))][::-1]
    half = width // 2
    pitch = half + layers + 1
    for layer in range(layers):
        last = layer == layers - 1
        rows_left = 2 * rows + layers - 1 - layer
        results = [None] * pairs
        for p in reversed(range(pairs)):
            builds = layer == 0 and p > 0
            earlier = (halo,) if p == 0 else parts[p - 1] if builds else (shifted[p - 1],)
            waits = builds or (last and p == 0)
            if builds and p == pairs - 1:
                begun = (first_begun,)
            else:
                begun = (begin(shifted[p], weight[layer]),) if waits else ()
            plan = {
                "layer": layer,
                "begun": waits,
                "last": last,
                "sends": p == pairs - 1 and not last,
                "rest_sent": joined(rows_left * pitch),
                "received": p == 0,
                "rest": 0 if p else rest,
                "builds": builds,
                "inputs": len(earlier),
                "pitch": pitch,
                "half": half,
                "rows": rows_left,
            }
            outs = list(conv(plan, begun, earlier, shifted[p], values[p], weight[layer], columns))
            if builds:
                shifted[p - 1], values[p - 1] = outs.pop(), outs.pop()
            results[p] = outs
            if plan["sends"]:
                arriving = earlier_of(outs[2])
        values, shifted = [r[0] for r in results], [r[1] for r in results]
        if not last:
            halo, rest = arriving, joined(rows_left * pitch)
    result = ()
    for p in reversed(range(pairs)):
        result = (join(p, values[p], mate_of(shifted[p]), latents.shape, *result),)
    return result[0]


def solution(mesh):
    in_specs = (P(("clips", "tm"), "rows", None, None), P(), P(), P())
    out_specs = P(("clips", "tm"), "rows", None, None)
    return jax.shard_map(on_device, mesh=mesh, in_specs=in_specs, out_specs=out_specs, check_vma=False)
```

```python
import functools

import jax
import jax.numpy as jnp
from jax import lax
from jax.experimental import pallas as pl
from jax.experimental.pallas import tpu as pltpu
from jax.sharding import PartitionSpec as P

EPSILON = 1e-06
PAIR = 2
LANES = 128
TILE = 256
VMEM = pl.BlockSpec(memory_space=pltpu.VMEM)
ANY = pl.BlockSpec(memory_space=pl.ANY)
LIMIT = 24 * 1024 * 1024
LARGE = 44 * 1024 * 1024


def place():
    strip = lax.axis_index("rows").astype(jnp.int32)
    core, group = strip & 1, strip >> 1
    return core, group, core == group


def rounded(lanes):
    return -(-lanes // LANES) * LANES


def column(row):
    return jnp.transpose(jnp.broadcast_to(row, (LANES, row.shape[1])))


def lane_of(lanes):
    return lax.broadcasted_iota(jnp.int32, (1, lanes), 1)


def filled(lanes, pitch):
    lane = lane_of(lanes)
    gaps = lane < 0
    for end in range(pitch - 1, lanes, pitch):
        gaps = gaps | (lane == end)
    return jnp.where(gaps, 0.0, 1.0)


def activated(values, gain, mask):
    squares = jnp.mean(values * values, axis=0, keepdims=True)
    halved = values * (lax.rsqrt(squares + EPSILON) * (0.5 * mask)) * gain
    return (halved + halved * jnp.tanh(halved)).astype(jnp.bfloat16)


def weights_kernel(w_ref, rows_ref, *refs):
    outs, columns_ref, held_ref, sems = refs[:-3], refs[-3], refs[-2], refs[-1]
    layers, taps, channels_out, ins = w_ref.shape
    step = taps // 3
    places = [(layer, time_tap) for layer in range(layers) for time_tap in range(3)]
    copies = []
    for n, (layer, time_tap) in enumerate(places):
        part = pl.ds(step * time_tap, step)
        copies.append(pltpu.make_async_copy(w_ref.at[layer, part], held_ref.at[n], sems.at[n]))
        copies[-1].start()
    _, flipped, _ = place()
    for layer in range(layers):
        columns_ref[layer, 0] = column(rows_ref[layer : layer + 1, :])
        columns_ref[layer, 1] = column(rows_ref[layers + layer : layers + layer + 1, :])
    for n, (layer, time_tap) in enumerate(places):
        copies[n].wait()
        for row_tap in range(3):
            source = 3 * (row_tap + flipped * (2 - 2 * row_tap))
            at = (3 * (2 - time_tap) + row_tap) * ins
            outs[layer][:, at : at + ins] = held_ref[n, pl.ds(source, 3)].reshape(3 * channels_out, ins)


def weights(conv_weight, rows):
    layers, taps, outs, ins = conv_weight.shape
    one = jax.ShapeDtypeStruct((3 * outs, 9 * ins), conv_weight.dtype)
    results = pl.pallas_call(
        weights_kernel,
        out_shape=(one,) * layers + (jax.ShapeDtypeStruct((layers, 2, outs, LANES), jnp.float32),),
        in_specs=[ANY, VMEM],
        out_specs=(VMEM,) * (layers + 1),
        scratch_shapes=[
            pltpu.VMEM((3 * layers, taps // 3, outs, ins), conv_weight.dtype),
            pltpu.SemaphoreType.DMA((3 * layers,)),
        ],
        compiler_params=pltpu.CompilerParams(vmem_limit_bytes=LARGE),
        cost_estimate=pl.CostEstimate(flops=0, bytes_accessed=4 * conv_weight.size, transcendentals=0),
        name="weights",
    )(conv_weight, rows)
    return results[:-1], results[-1]


def split_kernel(in_ref, *out_refs):
    for p, out_ref in enumerate(out_refs):
        out_ref[...] = in_ref[PAIR * p : PAIR * (p + 1)]


def split(latents):
    pairs = latents.shape[0] // PAIR
    return pl.pallas_call(
        split_kernel,
        out_shape=(jax.ShapeDtypeStruct((PAIR,) + latents.shape[1:], latents.dtype),) * pairs,
        in_specs=[VMEM],
        out_specs=(VMEM,) * pairs,
        compiler_params=pltpu.CompilerParams(vmem_limit_bytes=LIMIT),
        name="split",
    )(latents)


def joined(valid):
    rest = valid % LANES
    return rest if 0 < PAIR * rest <= LANES else 0


def spread(out_ref, index, act, pitch):
    lanes = out_ref.shape[3]
    above = pltpu.roll(act, pitch, 1)
    below = pltpu.roll(act, act.shape[1] - pitch, 1)
    edge = jnp.where(lane_of(LANES) < pitch, 0.0, above[:, :LANES].astype(jnp.float32))
    out_ref[index, 0, :, :LANES] = edge.astype(jnp.bfloat16)
    out_ref[index, 0, :, LANES:] = above[:, LANES:lanes]
    out_ref[index, 1] = act[:, :lanes]
    out_ref[index, 2] = below[:, :lanes]


def placed(blocks, core, row, window, line):
    pitch, width = window + 1, line.shape[1]
    lane = lane_of(LANES)
    block, low = divmod(row * pitch, LANES)
    shift = lax.rem(low + LANES - core * (width - window), LANES)
    turned = pltpu.roll(line, shift, 1)
    here = (lane >= low) & (lane < low + window)
    blocks[block] = blocks.get(block, 0.0) + jnp.where(here, turned, 0.0)
    if low + window > LANES:
        blocks[block + 1] = blocks.get(block + 1, 0.0) + jnp.where(lane < low + window - LANES, turned, 0.0)


def near_kernel(halo, pairs, mate_ref, gains_ref, *refs):
    own_refs, value_refs, act_refs = refs[:pairs], refs[pairs : 2 * pairs], refs[2 * pairs :]
    frames, rows, _, width = mate_ref.shape
    window = width // 2 + halo
    core, group, outer = place()
    gain = column(gains_ref[0:1, :])
    done = act_refs[0].shape[2]
    mask = filled(done, window + 1)
    for f in range(frames):
        p, t = divmod(f, PAIR)
        blocks = {}
        for row in range(2 * rows):
            at = row % rows
            index = at + group * (rows - 1 - 2 * at)
            own, mate = own_refs[p][t, index], mate_ref[f, index]
            one, two = (own, mate) if row < rows else (mate, own)
            placed(blocks, core, row, window, jnp.where(outer, one, two).astype(jnp.float32))
        for b in blocks:
            part = slice(b * LANES, (b + 1) * LANES)
            value_refs[p][t, :, part] = blocks[b].astype(jnp.bfloat16)
            if part.stop <= done:
                act_refs[p][t, :, part] = activated(blocks[b], gain, mask[:, part])


def near(halo, mate, gains, own):
    frames, rows, channels, width = mate.shape
    lanes = 2 * rows * (width // 2 + halo + 1)
    pairs = len(own)
    outs = pl.pallas_call(
        functools.partial(near_kernel, halo, pairs),
        out_shape=(jax.ShapeDtypeStruct((PAIR, channels, rounded(lanes)), jnp.bfloat16),) * pairs
        + (jax.ShapeDtypeStruct((PAIR, channels, lanes // LANES * LANES), jnp.bfloat16),) * pairs,
        in_specs=[VMEM] * (2 + pairs),
        out_specs=(VMEM,) * (2 * pairs),
        compiler_params=pltpu.CompilerParams(vmem_limit_bytes=LIMIT),
        cost_estimate=pl.CostEstimate(flops=40 * mate.size, bytes_accessed=8 * mate.size, transcendentals=2 * mate.size),
        name="near",
    )(mate, gains, *own)
    return outs[:pairs], outs[pairs:]


def add_far(halo, far_ref, mate_ref, near_ref, act_ref, columns_ref, values_ref, shifted_ref, send_ref=None):
    pair, rows, _, width = far_ref.shape
    window = width // 2 + halo
    core, group, outer = place()
    lanes, done = values_ref.shape[2], act_ref.shape[2]
    mask = filled(lanes, window + 1)
    for t in range(pair):
        values_ref[t, :, :done] = near_ref[t, :, :done]
        acts = [act_ref[t]]
        blocks = {done // LANES: near_ref[t, :, done:].astype(jnp.float32)}
        for row in range(2 * rows, 2 * rows + halo):
            local = 4 * rows - 1 - row
            at = local % rows
            index = at + (1 - group) * (rows - 1 - 2 * at)
            one, two = (mate_ref, far_ref) if local < rows else (far_ref, mate_ref)
            line = jnp.where(outer, one[t, index], two[t, index]).astype(jnp.float32)
            placed(blocks, core, row, window, line)
        for b in sorted(blocks):
            part = slice(b * LANES, (b + 1) * LANES)
            values_ref[t, :, part] = blocks[b].astype(jnp.bfloat16)
            acts.append(activated(blocks[b], columns_ref[0, 0], mask[:, part]))
        act = jnp.concatenate(acts, axis=1)
        spread(shifted_ref, t, act, window + 1)
        if send_ref is not None:
            send_ref[t] = act


def far_shapes(rows, halo, channels, half):
    pitch = half + halo + 1
    return (
        jax.ShapeDtypeStruct((PAIR, channels, rounded((2 * rows + halo) * pitch)), jnp.bfloat16),
        jax.ShapeDtypeStruct((PAIR, 3, channels, rounded((2 * rows + halo - 1) * pitch)), jnp.bfloat16),
    )


def beyond(halo, columns, *parts):
    far = parts[0]
    _, rows, channels, width = far.shape
    values, shifted = far_shapes(rows, halo, channels, width // 2)

    def kernel(columns_ref, far_ref, mate_ref, near_ref, act_ref, *outs):
        add_far(halo, far_ref, mate_ref, near_ref, act_ref, columns_ref, *outs)

    return pl.pallas_call(
        kernel,
        out_shape=(values, shifted, values),
        in_specs=[VMEM] * 5,
        out_specs=(VMEM,) * 3,
        compiler_params=pltpu.CompilerParams(vmem_limit_bytes=LIMIT),
        cost_estimate=pl.CostEstimate(flops=40 * far.size, bytes_accessed=8 * far.size, transcendentals=2 * far.size),
        name="beyond",
    )(columns, *parts)


def lines_of(ref, frame):
    return ref[frame].reshape(3 * ref.shape[2], ref.shape[3])


def by_taps(sums):
    channels, lanes = sums.shape[0] // 3, sums.shape[1]
    return [
        [sums[tap * channels : (tap + 1) * channels, at : at + LANES] for at in range(0, lanes, LANES)]
        for tap in range(3)
    ]


def column_sums(taps):
    lane = lane_of(LANES)
    left, middle, right = taps
    lefts = [pltpu.roll(block, 1, 1) for block in left]
    rights = [pltpu.roll(block, LANES - 1, 1) for block in right] + [0.0]
    return [
        jnp.where(lane == 0, lefts[b - 1] if b else 0.0, lefts[b])
        + middle[b]
        + jnp.where(lane == LANES - 1, rights[b + 1], rights[b])
        for b in range(len(middle))
    ]


def begin_kernel(shifted_ref, w_ref, out_ref):
    depth = 3 * shifted_ref.shape[2]
    for t in range(PAIR):
        rhs = jnp.concatenate([lines_of(shifted_ref, j) for j in range(t, -1, -1)], axis=0)
        sums = jnp.dot(w_ref[:, : (t + 1) * depth], rhs, preferred_element_type=jnp.float32)
        for b, block in enumerate(column_sums(by_taps(sums))):
            out_ref[t, :, b * LANES : (b + 1) * LANES] = block


def begin(shifted, weight):
    _, _, channels, lanes = shifted.shape
    return pl.pallas_call(
        begin_kernel,
        out_shape=jax.ShapeDtypeStruct((PAIR, channels, lanes), jnp.float32),
        in_specs=[VMEM] * 2,
        out_specs=VMEM,
        compiler_params=pltpu.CompilerParams(vmem_limit_bytes=LIMIT),
        cost_estimate=pl.CostEstimate(flops=0, bytes_accessed=0, transcendentals=0),
        name="begin",
    )(shifted, weight)


def conv_kernel(plan, shifted_ref, values_ref, w_ref, columns_ref, *refs):
    layer, pitch, half, received = plan["layer"], plan["pitch"], plan["half"], plan["received"]
    last, sends, rest, rest_sent = plan["last"], plan["sends"], plan["rest"], plan["rest_sent"]
    refs = list(refs)
    begun_ref = refs.pop(0) if plan["begun"] else None
    earlier_refs = [refs.pop(0) for _ in range(plan["inputs"])]
    earlier_ref = refs.pop() if received else earlier_refs[0]
    if received:
        for t in range(PAIR):
            if rest:
                whole = (earlier_refs[0].shape[1] - LANES) // PAIR
                tail = earlier_refs[0][:, PAIR * whole :].astype(jnp.float32)
                tail = tail if t == 0 else pltpu.roll(tail, LANES - t * (LANES // PAIR), 1)
                tail = jnp.where(lane_of(LANES) < rest, tail, 0.0).astype(jnp.bfloat16)
                act = jnp.concatenate([earlier_refs[0][:, t * whole : (t + 1) * whole], tail], axis=1)
            else:
                act = earlier_refs[0][t]
            spread(earlier_ref, t, act, pitch)
    outs = refs
    if plan["builds"]:
        earlier_ref = outs.pop()
        add_far(pitch - 1 - half, *earlier_refs, columns_ref, outs.pop(), earlier_ref)
    _, _, channels, lanes = shifted_ref.shape
    chunks = lanes // LANES
    lane = lane_of(LANES)

    def frame_of(j):
        return (earlier_ref, j) if j < PAIR else (shifted_ref, j - PAIR)

    def rows_of_frames(frames, blocks):
        at = slice(blocks[0] * LANES, (blocks[-1] + 1) * LANES)
        taken = [frame_of(j) for j in frames]
        return [ref[j, :, :, at].reshape(3 * channels, len(blocks) * LANES) for ref, j in taken]

    bias = columns_ref[layer, 1]
    tails = []
    if not last:
        mask = filled(lanes, pitch)
        gain = columns_ref[layer + 1, 0]
    sums = {}
    done = {t: [] for t in range(PAIR)}

    def finish(t, b):
        left = jnp.where(lane == 0, sums["left", t, b - 1] if b else 0.0, sums["left", t, b])
        follows = sums["right", t, b + 1] if b < chunks - 1 else 0.0
        conv = left + sums["middle", t, b] + jnp.where(lane == LANES - 1, follows, sums["right", t, b])
        at = slice(b * LANES, (b + 1) * LANES)
        if begun_ref is not None:
            conv = conv + begun_ref[t, :, at]
        total = (values_ref[t, :, at].astype(jnp.float32) + conv + bias).astype(jnp.bfloat16)
        if last:
            done[t].append(total.astype(jnp.float32))
            return
        outs[0][t, :, at] = total
        act = activated(total.astype(jnp.float32), gain, mask[:, at])
        done[t].append(act)
        if not sends:
            return
        if not rest_sent:
            outs[2][t, :, at] = act
        elif b < chunks - 1:
            outs[2][:, (t * (chunks - 1) + b) * LANES : (t * (chunks - 1) + b + 1) * LANES] = act
        else:
            tail = jnp.where(lane < rest_sent, act.astype(jnp.float32), 0.0)
            tails.append(tail if t == 0 else pltpu.roll(tail, t * (LANES // PAIR), 1))

    def finish_frame(t):
        whole = jnp.concatenate(done[t], axis=1)
        if not last:
            spread(outs[1], t, whole, pitch)
            return
        halo = pitch - 1 - half
        core, _, outer = place()
        whole = jnp.where(core == 1, pltpu.roll(whole, lanes - halo, 1), whole)
        left_half = lane < half

        def rows_of(row):
            one = whole if row == 0 else pltpu.roll(whole, lanes - row * pitch, 1)
            two = pltpu.roll(whole, lanes - (row + 1) * pitch + half, 1)
            return jnp.where(left_half, one[:, :LANES], two[:, :LANES])

        outermost, inner = rows_of(0), rows_of(2)
        outs[0][t] = jnp.where(outer, outermost, inner).astype(jnp.bfloat16)
        outs[1][t] = jnp.where(outer, inner, outermost).astype(jnp.bfloat16)

    side = TILE // LANES
    tiles = []
    if plan["begun"]:
        for t in range(PAIR):
            for b in range(0, chunks, side):
                places = [(t, c) for c in range(b, min(b + side, chunks))]
                tiles.append((places, list(range(PAIR - 1, t - 1, -1)), (t + 1) * 3 * channels))
    else:
        places = [(t, b) for t in range(PAIR) for b in range(chunks)]
        tiles = [(places[n : n + side], None, 0) for n in range(0, len(places), side)]
    waiting = []
    for places, frames, start in tiles:
        if frames is None:
            columns = [jnp.concatenate(rows_of_frames((t + 2, t + 1, t), [b]), axis=0) for t, b in places]
            rhs = jnp.concatenate(columns, axis=1)
            lead = 0
        else:
            lead = start % LANES
            lines = rows_of_frames(frames, [b for _, b in places])
            zeros = [jnp.zeros((lead, len(places) * LANES), jnp.bfloat16)] if lead else []
            rhs = jnp.concatenate(zeros + lines, axis=0)
        share = -(-len(waiting) // 3)
        for tap, name in enumerate(("left", "middle", "right")):
            rows = slice(tap * channels, (tap + 1) * channels)
            product = jnp.dot(w_ref[rows, start - lead :], rhs, preferred_element_type=jnp.float32)
            for i, (t, b) in enumerate(places):
                part = product[:, i * LANES : (i + 1) * LANES]
                turn = {"left": 1, "right": LANES - 1}.get(name)
                sums[name, t, b] = part if turn is None else pltpu.roll(part, turn, 1)
            for work in waiting[tap * share : (tap + 1) * share]:
                work()
        waiting = []
        for t, b in places:
            if b:
                waiting.append(functools.partial(finish, t, b - 1))
            if b == chunks - 1:
                waiting.append(functools.partial(finish, t, b))
                waiting.append(functools.partial(finish_frame, t))
    for work in waiting:
        work()
    if sends and rest_sent:
        outs[2][:, PAIR * (chunks - 1) * LANES :] = sum(tails).astype(jnp.bfloat16)


def conv(plan, begun, earlier, shifted, values, weight, columns):
    _, _, channels, lanes = shifted.shape
    pitch, half, received = plan["pitch"], plan["half"], plan["received"]
    if plan["last"]:
        out_shape = (jax.ShapeDtypeStruct((PAIR, channels, LANES), jnp.bfloat16),) * 2
    else:
        out_shape = (
            jax.ShapeDtypeStruct((PAIR, channels, lanes), jnp.bfloat16),
            jax.ShapeDtypeStruct((PAIR, 3, channels, rounded((plan["rows"] - 1) * pitch)), jnp.bfloat16),
        )
        if plan["sends"] and plan["rest_sent"]:
            out_shape += (jax.ShapeDtypeStruct((channels, PAIR * (lanes - LANES) + LANES), jnp.bfloat16),)
        elif plan["sends"]:
            out_shape += out_shape[:1]
    scratch = [pltpu.VMEM((PAIR, 3, channels, lanes), jnp.bfloat16)] * received
    if plan["builds"]:
        out_shape += far_shapes(earlier[0].shape[1], pitch - 1 - half, channels, half)
    return pl.pallas_call(
        functools.partial(conv_kernel, plan),
        out_shape=out_shape,
        in_specs=[VMEM] * (4 + len(begun) + len(earlier)),
        out_specs=(VMEM,) * len(out_shape),
        scratch_shapes=scratch,
        compiler_params=pltpu.CompilerParams(vmem_limit_bytes=LIMIT),
        cost_estimate=pl.CostEstimate(
            flops=54 * channels * channels * PAIR * lanes,
            bytes_accessed=2 * weight.size,
            transcendentals=PAIR * channels * lanes,
        ),
        name=f"conv_{plan['layer']}",
    )(shifted, values, weight, columns, *begun, *earlier)


def join_kernel(pair, kept_ref, got_ref, *refs):
    out_ref, lines_ref, sem = refs[-3:]
    _, rows, _, width = lines_ref.shape
    half = width // 2
    core, group, _ = place()
    first = core == 0
    left_half = lane_of(width) < half
    for t in range(PAIR):
        mine, theirs = kept_ref[t].astype(jnp.float32), got_ref[t].astype(jnp.float32)
        left, right = jnp.where(first, mine, theirs), jnp.where(first, theirs, mine)
        lines = (
            jnp.where(left_half, left, pltpu.roll(right, half, 1)),
            jnp.where(left_half, pltpu.roll(left, half, 1), right),
        )
        for j in range(rows):
            lines_ref[t, j + group * (rows - 1 - 2 * j)] = lines[j].astype(jnp.bfloat16)
    copy = pltpu.make_async_copy(lines_ref, out_ref.at[pl.ds(PAIR * pair, PAIR)], sem)
    copy.start()
    copy.wait()


def join(pair, kept, got, shape, *so_far):
    return pl.pallas_call(
        functools.partial(join_kernel, pair),
        out_shape=jax.ShapeDtypeStruct(shape, jnp.bfloat16),
        in_specs=[VMEM, VMEM] + [ANY] * len(so_far),
        out_specs=ANY,
        scratch_shapes=[pltpu.VMEM((PAIR,) + shape[1:], jnp.bfloat16), pltpu.SemaphoreType.DMA],
        input_output_aliases={2: 0} if so_far else {},
        compiler_params=pltpu.CompilerParams(vmem_limit_bytes=LIMIT),
        name="join",
    )(kept, got, *so_far)


def on_device(latents, conv_weight, norm_gains, biases):
    layers = conv_weight.shape[0]
    frames, rows, channels, width = latents.shape
    strips, blocks = lax.axis_size("rows"), lax.axis_size("tm")
    assert strips == 4 and rows == 2 and frames % PAIR == 0 and width == LANES

    def mate_of(block):
        return lax.ppermute(block, "rows", [(i, i ^ 1) for i in range(strips)])

    def earlier_of(block):
        return lax.ppermute(block, "tm", [(i, i + 1) for i in range(blocks - 1)])

    def beyond_of(block):
        return lax.ppermute(block, "rows", [(i, i ^ 2) for i in range(strips)])

    mate = mate_of(latents)
    pairs = frames // PAIR
    own = split(latents)
    far = [beyond_of(own[p]) for p in reversed(range(pairs))][::-1]
    row_values = jnp.concatenate([norm_gains, biases], axis=0)
    weight, columns = weights(conv_weight, row_values)
    near_values, near_act = near(layers, mate, row_values, own)
    far[-1], weight, columns, near_values, near_act = lax.optimization_barrier(
        (far[-1], weight, columns, near_values, near_act)
    )
    values, shifted = [None] * pairs, [None] * pairs
    values[-1], shifted[-1], send = beyond(
        layers, columns, far[-1], mate_of(far[-1]), near_values[-1], near_act[-1]
    )
    halo, rest = earlier_of(send), 0
    first_begun = begin(shifted[-1], weight[0])
    *far[:-1], first_begun = lax.optimization_barrier((*far[:-1], first_begun))
    parts = [(far[p], mate_of(far[p]), near_values[p], near_act[p]) for p in reversed(range(pairs - 1))][::-1]
    half = width // 2
    pitch = half + layers + 1
    for layer in range(layers):
        last = layer == layers - 1
        rows_left = 2 * rows + layers - 1 - layer
        results = [None] * pairs
        for p in reversed(range(pairs)):
            builds = layer == 0 and p > 0
            earlier = (halo,) if p == 0 else parts[p - 1] if builds else (shifted[p - 1],)
            waits = builds or (last and p == 0)
            if builds and p == pairs - 1:
                begun = (first_begun,)
            else:
                begun = (begin(shifted[p], weight[layer]),) if waits else ()
            plan = {
                "layer": layer,
                "begun": waits,
                "last": last,
                "sends": p == pairs - 1 and not last,
                "rest_sent": joined(rows_left * pitch),
                "received": p == 0,
                "rest": 0 if p else rest,
                "builds": builds,
                "inputs": len(earlier),
                "pitch": pitch,
                "half": half,
                "rows": rows_left,
            }
            outs = list(conv(plan, begun, earlier, shifted[p], values[p], weight[layer], columns))
            if builds:
                shifted[p - 1], values[p - 1] = outs.pop(), outs.pop()
            results[p] = outs
            if plan["sends"]:
                arriving = earlier_of(outs[2])
        values, shifted = [r[0] for r in results], [r[1] for r in results]
        if not last:
            halo, rest = arriving, joined(rows_left * pitch)
    result = ()
    for p in reversed(range(pairs)):
        result = (join(p, values[p], mate_of(shifted[p]), latents.shape, *result),)
    return result[0]


def solution(mesh):
    in_specs = (P(("clips", "tm"), "rows", None, None), P(), P(), P())
    out_specs = P(("clips", "tm"), "rows", None, None)
    return jax.shard_map(on_device, mesh=mesh, in_specs=in_specs, out_specs=out_specs, check_vma=False)
```

```python
import functools

import jax
import jax.numpy as jnp
from jax import lax
from jax.experimental import pallas as pl
from jax.experimental.pallas import tpu as pltpu
from jax.sharding import PartitionSpec as P

EPSILON = 1e-06
PAIR = 2
LANES = 128
TILE = 256
VMEM = pl.BlockSpec(memory_space=pltpu.VMEM)
ANY = pl.BlockSpec(memory_space=pl.ANY)
LIMIT = 24 * 1024 * 1024
LARGE = 44 * 1024 * 1024


def place():
    strip = lax.axis_index("rows").astype(jnp.int32)
    core, group = strip & 1, strip >> 1
    return core, group, core == group


def rounded(lanes):
    return -(-lanes // LANES) * LANES


def column(row):
    return jnp.transpose(jnp.broadcast_to(row, (LANES, row.shape[1])))


def lane_of(lanes):
    return lax.broadcasted_iota(jnp.int32, (1, lanes), 1)


def filled(lanes, pitch):
    lane = lane_of(lanes)
    gaps = lane < 0
    for end in range(pitch - 1, lanes, pitch):
        gaps = gaps | (lane == end)
    return jnp.where(gaps, 0.0, 1.0)


def activated(values, gain, mask):
    squares = jnp.mean(values * values, axis=0, keepdims=True)
    halved = values * (lax.rsqrt(squares + EPSILON) * (0.5 * mask)) * gain
    return (halved + halved * jnp.tanh(halved)).astype(jnp.bfloat16)


def weights_kernel(w_ref, rows_ref, *refs):
    outs, columns_ref, held_ref, sems = refs[:-3], refs[-3], refs[-2], refs[-1]
    layers, taps, channels_out, ins = w_ref.shape
    step = taps // 3
    places = [(layer, time_tap) for layer in range(layers) for time_tap in range(3)]
    copies = []
    for n, (layer, time_tap) in enumerate(places):
        part = pl.ds(step * time_tap, step)
        copies.append(pltpu.make_async_copy(w_ref.at[layer, part], held_ref.at[n], sems.at[n]))
        copies[-1].start()
    _, flipped, _ = place()
    for layer in range(layers):
        columns_ref[layer, 0] = column(rows_ref[layer : layer + 1, :])
        columns_ref[layer, 1] = column(rows_ref[layers + layer : layers + layer + 1, :])
    for n, (layer, time_tap) in enumerate(places):
        copies[n].wait()
        for row_tap in range(3):
            source = 3 * (row_tap + flipped * (2 - 2 * row_tap))
            at = (3 * (2 - time_tap) + row_tap) * ins
            outs[layer][:, at : at + ins] = held_ref[n, pl.ds(source, 3)].reshape(3 * channels_out, ins)


def weights(conv_weight, rows):
    layers, taps, outs, ins = conv_weight.shape
    one = jax.ShapeDtypeStruct((3 * outs, 9 * ins), conv_weight.dtype)
    results = pl.pallas_call(
        weights_kernel,
        out_shape=(one,) * layers + (jax.ShapeDtypeStruct((layers, 2, outs, LANES), jnp.float32),),
        in_specs=[ANY, VMEM],
        out_specs=(VMEM,) * (layers + 1),
        scratch_shapes=[
            pltpu.VMEM((3 * layers, taps // 3, outs, ins), conv_weight.dtype),
            pltpu.SemaphoreType.DMA((3 * layers,)),
        ],
        compiler_params=pltpu.CompilerParams(vmem_limit_bytes=LARGE),
        cost_estimate=pl.CostEstimate(flops=0, bytes_accessed=4 * conv_weight.size, transcendentals=0),
        name="weights",
    )(conv_weight, rows)
    return results[:-1], results[-1]


def split_kernel(in_ref, *out_refs):
    for p, out_ref in enumerate(out_refs):
        out_ref[...] = in_ref[PAIR * p : PAIR * (p + 1)]


def split(latents):
    pairs = latents.shape[0] // PAIR
    return pl.pallas_call(
        split_kernel,
        out_shape=(jax.ShapeDtypeStruct((PAIR,) + latents.shape[1:], latents.dtype),) * pairs,
        in_specs=[VMEM],
        out_specs=(VMEM,) * pairs,
        compiler_params=pltpu.CompilerParams(vmem_limit_bytes=LIMIT),
        name="split",
    )(latents)


def joined(valid):
    rest = valid % LANES
    return rest if 0 < PAIR * rest <= LANES else 0


def spread(out_ref, index, act, pitch):
    lanes = out_ref.shape[3]
    above = pltpu.roll(act, pitch, 1)
    below = pltpu.roll(act, act.shape[1] - pitch, 1)
    edge = jnp.where(lane_of(LANES) < pitch, 0.0, above[:, :LANES].astype(jnp.float32))
    out_ref[index, 0, :, :LANES] = edge.astype(jnp.bfloat16)
    out_ref[index, 0, :, LANES:] = above[:, LANES:lanes]
    out_ref[index, 1] = act[:, :lanes]
    out_ref[index, 2] = below[:, :lanes]


def placed(blocks, core, row, window, line):
    pitch, width = window + 1, line.shape[1]
    lane = lane_of(LANES)
    block, low = divmod(row * pitch, LANES)
    shift = lax.rem(low + LANES - core * (width - window), LANES)
    turned = pltpu.roll(line, shift, 1)
    here = (lane >= low) & (lane < low + window)
    blocks[block] = blocks.get(block, 0.0) + jnp.where(here, turned, 0.0)
    if low + window > LANES:
        blocks[block + 1] = blocks.get(block + 1, 0.0) + jnp.where(lane < low + window - LANES, turned, 0.0)


def near_kernel(halo, pairs, mate_ref, gains_ref, *refs):
    own_refs, value_refs, act_refs = refs[:pairs], refs[pairs : 2 * pairs], refs[2 * pairs : 3 * pairs]
    send_refs = refs[3 * pairs :]
    frames, rows, _, width = mate_ref.shape
    window = width // 2 + halo
    core, group, outer = place()
    gain = column(gains_ref[0:1, :])
    done = act_refs[0].shape[2]
    mask = filled(done, window + 1)
    for f in range(frames):
        p, t = divmod(f, PAIR)
        blocks, sent = {}, {}
        for row in range(2 * rows):
            at = row % rows
            index = at + group * (rows - 1 - 2 * at)
            own, mate = own_refs[p][t, index], mate_ref[f, index]
            one, two = (own, mate) if row < rows else (mate, own)
            line = jnp.where(outer, one, two).astype(jnp.float32)
            placed(blocks, core, row, window, line)
            there = 4 * rows - 1 - row
            if p < pairs - 1 and there < 2 * rows + halo:
                placed(sent, core, there, window, line)
        for b in sent:
            send_refs[p][t, :, b * LANES - done : (b + 1) * LANES - done] = sent[b].astype(jnp.bfloat16)
        for b in blocks:
            part = slice(b * LANES, (b + 1) * LANES)
            value_refs[p][t, :, part] = blocks[b].astype(jnp.bfloat16)
            if part.stop <= done:
                act_refs[p][t, :, part] = activated(blocks[b], gain, mask[:, part])


def near(halo, mate, gains, own):
    frames, rows, channels, width = mate.shape
    pitch = width // 2 + halo + 1
    lanes = 2 * rows * pitch
    done = lanes // LANES * LANES
    pairs = len(own)
    sent = jax.ShapeDtypeStruct((PAIR, channels, rounded(lanes + halo * pitch) - done), jnp.bfloat16)
    outs = pl.pallas_call(
        functools.partial(near_kernel, halo, pairs),
        out_shape=(jax.ShapeDtypeStruct((PAIR, channels, rounded(lanes)), jnp.bfloat16),) * pairs
        + (jax.ShapeDtypeStruct((PAIR, channels, done), jnp.bfloat16),) * pairs
        + (sent,) * (pairs - 1),
        in_specs=[VMEM] * (2 + pairs),
        out_specs=(VMEM,) * (3 * pairs - 1),
        compiler_params=pltpu.CompilerParams(vmem_limit_bytes=LIMIT),
        cost_estimate=pl.CostEstimate(flops=40 * mate.size, bytes_accessed=8 * mate.size, transcendentals=2 * mate.size),
        name="near",
    )(mate, gains, *own)
    return outs[:pairs], outs[pairs : 2 * pairs], outs[2 * pairs :]


def far_blocks(halo, far_ref, mate_ref, t, blocks):
    _, rows, _, width = far_ref.shape
    core, group, outer = place()
    for row in range(2 * rows, 2 * rows + halo):
        local = 4 * rows - 1 - row
        at = local % rows
        index = at + (1 - group) * (rows - 1 - 2 * at)
        one, two = (mate_ref, far_ref) if local < rows else (far_ref, mate_ref)
        line = jnp.where(outer, one[t, index], two[t, index]).astype(jnp.float32)
        placed(blocks, core, row, width // 2 + halo, line)


def add_far(pitch, add, near_ref, act_ref, columns_ref, values_ref, shifted_ref, send_ref=None):
    lanes, done = values_ref.shape[2], act_ref.shape[2]
    mask = filled(lanes, pitch)
    for t in range(PAIR):
        values_ref[t, :, :done] = near_ref[t, :, :done]
        acts = [act_ref[t]]
        blocks = {done // LANES: near_ref[t, :, done:].astype(jnp.float32)}
        add(t, blocks)
        for b in sorted(blocks):
            part = slice(b * LANES, (b + 1) * LANES)
            values_ref[t, :, part] = blocks[b].astype(jnp.bfloat16)
            acts.append(activated(blocks[b], columns_ref[0, 0], mask[:, part]))
        act = jnp.concatenate(acts, axis=1)
        spread(shifted_ref, t, act, pitch)
        if send_ref is not None:
            send_ref[t] = act


def far_shapes(rows, halo, channels, half):
    pitch = half + halo + 1
    return (
        jax.ShapeDtypeStruct((PAIR, channels, rounded((2 * rows + halo) * pitch)), jnp.bfloat16),
        jax.ShapeDtypeStruct((PAIR, 3, channels, rounded((2 * rows + halo - 1) * pitch)), jnp.bfloat16),
    )


def beyond(halo, columns, *parts):
    far = parts[0]
    _, rows, channels, width = far.shape
    values, shifted = far_shapes(rows, halo, channels, width // 2)

    def kernel(columns_ref, far_ref, mate_ref, near_ref, act_ref, *outs):
        add = functools.partial(far_blocks, halo, far_ref, mate_ref)
        add_far(width // 2 + halo + 1, add, near_ref, act_ref, columns_ref, *outs)

    return pl.pallas_call(
        kernel,
        out_shape=(values, shifted, values),
        in_specs=[VMEM] * 5,
        out_specs=(VMEM,) * 3,
        compiler_params=pltpu.CompilerParams(vmem_limit_bytes=LIMIT),
        cost_estimate=pl.CostEstimate(flops=40 * far.size, bytes_accessed=8 * far.size, transcendentals=2 * far.size),
        name="beyond",
    )(columns, *parts)


def lines_of(ref, frame):
    return ref[frame].reshape(3 * ref.shape[2], ref.shape[3])


def by_taps(sums):
    channels, lanes = sums.shape[0] // 3, sums.shape[1]
    return [
        [sums[tap * channels : (tap + 1) * channels, at : at + LANES] for at in range(0, lanes, LANES)]
        for tap in range(3)
    ]


def column_sums(taps):
    lane = lane_of(LANES)
    left, middle, right = taps
    lefts = [pltpu.roll(block, 1, 1) for block in left]
    rights = [pltpu.roll(block, LANES - 1, 1) for block in right] + [0.0]
    return [
        jnp.where(lane == 0, lefts[b - 1] if b else 0.0, lefts[b])
        + middle[b]
        + jnp.where(lane == LANES - 1, rights[b + 1], rights[b])
        for b in range(len(middle))
    ]


def begin_kernel(shifted_ref, w_ref, out_ref):
    depth = 3 * shifted_ref.shape[2]
    for t in range(PAIR):
        rhs = jnp.concatenate([lines_of(shifted_ref, j) for j in range(t, -1, -1)], axis=0)
        sums = jnp.dot(w_ref[:, : (t + 1) * depth], rhs, preferred_element_type=jnp.float32)
        for b, block in enumerate(column_sums(by_taps(sums))):
            out_ref[t, :, b * LANES : (b + 1) * LANES] = block


def begin(shifted, weight):
    _, _, channels, lanes = shifted.shape
    return pl.pallas_call(
        begin_kernel,
        out_shape=jax.ShapeDtypeStruct((PAIR, channels, lanes), jnp.float32),
        in_specs=[VMEM] * 2,
        out_specs=VMEM,
        compiler_params=pltpu.CompilerParams(vmem_limit_bytes=LIMIT),
        cost_estimate=pl.CostEstimate(flops=0, bytes_accessed=0, transcendentals=0),
        name="begin",
    )(shifted, weight)


def conv_kernel(plan, shifted_ref, values_ref, w_ref, columns_ref, *refs):
    layer, pitch, half, received = plan["layer"], plan["pitch"], plan["half"], plan["received"]
    last, sends, rest, rest_sent = plan["last"], plan["sends"], plan["rest"], plan["rest_sent"]
    refs = list(refs)
    begun_ref = refs.pop(0) if plan["begun"] else None
    earlier_refs = [refs.pop(0) for _ in range(plan["inputs"])]
    earlier_ref = refs.pop() if received else earlier_refs[0]
    if received:
        for t in range(PAIR):
            if rest:
                whole = (earlier_refs[0].shape[1] - LANES) // PAIR
                tail = earlier_refs[0][:, PAIR * whole :].astype(jnp.float32)
                tail = tail if t == 0 else pltpu.roll(tail, LANES - t * (LANES // PAIR), 1)
                tail = jnp.where(lane_of(LANES) < rest, tail, 0.0).astype(jnp.bfloat16)
                act = jnp.concatenate([earlier_refs[0][:, t * whole : (t + 1) * whole], tail], axis=1)
            else:
                act = earlier_refs[0][t]
            spread(earlier_ref, t, act, pitch)
    outs = refs
    if plan["builds"]:
        earlier_ref = outs.pop()
        came_ref, near_ref, act_ref = earlier_refs
        done = act_ref.shape[2]

        def add(t, blocks):
            for at in range(0, came_ref.shape[2], LANES):
                b = (done + at) // LANES
                blocks[b] = blocks.get(b, 0.0) + came_ref[t, :, at : at + LANES].astype(jnp.float32)

        add_far(pitch, add, near_ref, act_ref, columns_ref, outs.pop(), earlier_ref)
    _, _, channels, lanes = shifted_ref.shape
    chunks = lanes // LANES
    lane = lane_of(LANES)

    def window(t, b):
        taken = [(earlier_ref, t + a) if t + a < PAIR else (shifted_ref, t + a - PAIR) for a in (2, 1, 0)]
        at = slice(b * LANES, (b + 1) * LANES)
        return jnp.concatenate([ref[j, :, :, at].reshape(3 * channels, LANES) for ref, j in taken], axis=0)

    bias = columns_ref[layer, 1]
    tails = []
    if not last:
        mask = filled(lanes, pitch)
        gain = columns_ref[layer + 1, 0]

    def finish(t, taps):
        totals, acts = [], []
        for b, conv in enumerate(column_sums(taps)):
            at = slice(b * LANES, (b + 1) * LANES)
            if begun_ref is not None:
                conv = conv + begun_ref[t, :, at]
            total = (values_ref[t, :, at].astype(jnp.float32) + conv + bias).astype(jnp.bfloat16)
            totals.append(total.astype(jnp.float32))
            if last:
                continue
            outs[0][t, :, at] = total
            acts.append(activated(totals[-1], gain, mask[:, at]))
            if not sends:
                continue
            if not rest_sent:
                outs[2][t, :, at] = acts[-1]
            elif b < chunks - 1:
                outs[2][:, (t * (chunks - 1) + b) * LANES : (t * (chunks - 1) + b + 1) * LANES] = acts[-1]
            else:
                tail = jnp.where(lane < rest_sent, acts[-1].astype(jnp.float32), 0.0)
                tails.append(tail if t == 0 else pltpu.roll(tail, t * (LANES // PAIR), 1))
        if not last:
            spread(outs[1], t, jnp.concatenate(acts, axis=1), pitch)
            return
        core, _, outer = place()
        skipped = core * (pitch - 1 - half)

        def columns_of(row, to):
            b, low = divmod(row * pitch, LANES)
            shift = lax.rem(to + 2 * LANES - low - skipped, LANES)
            turned = pltpu.roll(totals[b], shift, 1)
            if low + pitch - 1 <= LANES:
                return turned
            return jnp.where(lane < to + LANES - low - skipped, turned, pltpu.roll(totals[b + 1], shift, 1))

        def rows_of(row):
            return jnp.where(lane < half, columns_of(row, 0), columns_of(row + 1, half))

        outermost, inner = rows_of(0), rows_of(2)
        outs[0][t] = jnp.where(outer, outermost, inner).astype(jnp.bfloat16)
        outs[1][t] = jnp.where(outer, inner, outermost).astype(jnp.bfloat16)

    if plan["begun"]:
        depth = 3 * channels
        for t in range(PAIR):
            at = (t + 1) * depth
            lead = at % LANES
            lines = [lines_of(earlier_ref, j) for j in range(PAIR - 1, t - 1, -1)]
            if lead:
                lines.insert(0, jnp.zeros((lead, lanes), jnp.bfloat16))
            sums = jnp.dot(w_ref[:, at - lead :], jnp.concatenate(lines, axis=0), preferred_element_type=jnp.float32)
            finish(t, by_taps(sums))
    else:
        places = [(t, b) for t in range(PAIR) for b in range(chunks)]
        side = TILE // LANES
        taps = {t: [[], [], []] for t in range(PAIR)}
        finished = 0
        for n in range(0, len(places), side):
            rhs = jnp.concatenate([window(t, b) for t, b in places[n : n + side]], axis=1)
            sums = by_taps(jnp.dot(w_ref[...], rhs, preferred_element_type=jnp.float32))
            for i, (t, _) in enumerate(places[n : n + side]):
                for tap in range(3):
                    taps[t][tap].append(sums[tap][i])
            while finished < PAIR and (finished + 1) * chunks <= n + side:
                finish(finished, taps[finished])
                finished += 1
    if sends and rest_sent:
        outs[2][:, PAIR * (chunks - 1) * LANES :] = sum(tails).astype(jnp.bfloat16)


def conv(plan, begun, earlier, shifted, values, weight, columns):
    _, _, channels, lanes = shifted.shape
    pitch, half, received = plan["pitch"], plan["half"], plan["received"]
    if plan["last"]:
        out_shape = (jax.ShapeDtypeStruct((PAIR, channels, LANES), jnp.bfloat16),) * 2
    else:
        out_shape = (
            jax.ShapeDtypeStruct((PAIR, channels, lanes), jnp.bfloat16),
            jax.ShapeDtypeStruct((PAIR, 3, channels, rounded((plan["rows"] - 1) * pitch)), jnp.bfloat16),
        )
        if plan["sends"] and plan["rest_sent"]:
            out_shape += (jax.ShapeDtypeStruct((channels, PAIR * (lanes - LANES) + LANES), jnp.bfloat16),)
        elif plan["sends"]:
            out_shape += out_shape[:1]
    scratch = [pltpu.VMEM((PAIR, 3, channels, lanes), jnp.bfloat16)] * received
    if plan["builds"]:
        out_shape += far_shapes(plan["rows_near"] // 2, pitch - 1 - half, channels, half)
    return pl.pallas_call(
        functools.partial(conv_kernel, plan),
        out_shape=out_shape,
        in_specs=[VMEM] * (4 + len(begun) + len(earlier)),
        out_specs=(VMEM,) * len(out_shape),
        scratch_shapes=scratch,
        compiler_params=pltpu.CompilerParams(vmem_limit_bytes=LIMIT),
        cost_estimate=pl.CostEstimate(
            flops=54 * channels * channels * PAIR * lanes * (1 + plan["builds"]),
            bytes_accessed=2 * weight.size,
            transcendentals=PAIR * channels * lanes,
        ),
        name=f"conv_{plan['layer']}",
    )(shifted, values, weight, columns, *begun, *earlier)


def join_kernel(pair, kept_ref, got_ref, *refs):
    out_ref, lines_ref, sem = refs[-3:]
    _, rows, _, width = lines_ref.shape
    half = width // 2
    core, group, _ = place()
    first = core == 0
    left_half = lane_of(width) < half
    for t in range(PAIR):
        mine, theirs = kept_ref[t].astype(jnp.float32), got_ref[t].astype(jnp.float32)
        left, right = jnp.where(first, mine, theirs), jnp.where(first, theirs, mine)
        lines = (
            jnp.where(left_half, left, pltpu.roll(right, half, 1)),
            jnp.where(left_half, pltpu.roll(left, half, 1), right),
        )
        for j in range(rows):
            lines_ref[t, j + group * (rows - 1 - 2 * j)] = lines[j].astype(jnp.bfloat16)
    copy = pltpu.make_async_copy(lines_ref, out_ref.at[pl.ds(PAIR * pair, PAIR)], sem)
    copy.start()
    copy.wait()


def join(pair, kept, got, shape, *so_far):
    return pl.pallas_call(
        functools.partial(join_kernel, pair),
        out_shape=jax.ShapeDtypeStruct(shape, jnp.bfloat16),
        in_specs=[VMEM, VMEM] + [ANY] * len(so_far),
        out_specs=ANY,
        scratch_shapes=[pltpu.VMEM((PAIR,) + shape[1:], jnp.bfloat16), pltpu.SemaphoreType.DMA],
        input_output_aliases={2: 0} if so_far else {},
        compiler_params=pltpu.CompilerParams(vmem_limit_bytes=LIMIT),
        name="join",
    )(kept, got, *so_far)


def on_device(latents, conv_weight, norm_gains, biases):
    layers = conv_weight.shape[0]
    frames, rows, channels, width = latents.shape
    strips, blocks = lax.axis_size("rows"), lax.axis_size("tm")
    assert strips == 4 and rows == 2 and frames % PAIR == 0 and width == LANES

    def mate_of(block):
        return lax.ppermute(block, "rows", [(i, i ^ 1) for i in range(strips)])

    def earlier_of(block):
        return lax.ppermute(block, "tm", [(i, i + 1) for i in range(blocks - 1)])

    def beyond_of(block):
        return lax.ppermute(block, "rows", [(i, i ^ 2) for i in range(strips)])

    mate = mate_of(latents)
    pairs = frames // PAIR
    own = split(latents)
    far = beyond_of(own[-1])
    row_values = jnp.concatenate([norm_gains, biases], axis=0)
    weight, columns = weights(conv_weight, row_values)
    near_values, near_act, near_sent = near(layers, mate, row_values, own)
    came = [beyond_of(block) for block in near_sent]
    far, weight, columns, near_values, near_act = lax.optimization_barrier(
        (far, weight, columns, near_values, near_act)
    )
    values, shifted = [None] * pairs, [None] * pairs
    values[-1], shifted[-1], send = beyond(layers, columns, far, mate_of(far), near_values[-1], near_act[-1])
    halo, rest = earlier_of(send), 0
    first_begun = begin(shifted[-1], weight[0])
    *came, first_begun = lax.optimization_barrier((*came, first_begun))
    parts = [(came[p], near_values[p], near_act[p]) for p in range(pairs - 1)]
    half = width // 2
    pitch = half + layers + 1
    for layer in range(layers):
        last = layer == layers - 1
        rows_left = 2 * rows + layers - 1 - layer
        results = [None] * pairs
        for p in reversed(range(pairs)):
            builds = layer == 0 and p > 0
            earlier = (halo,) if p == 0 else parts[p - 1] if builds else (shifted[p - 1],)
            waits = builds or (last and p == 0)
            if builds and p == pairs - 1:
                begun = (first_begun,)
            else:
                begun = (begin(shifted[p], weight[layer]),) if waits else ()
            plan = {
                "layer": layer,
                "begun": waits,
                "rows_near": 2 * rows,
                "last": last,
                "sends": p == pairs - 1 and not last,
                "rest_sent": joined(rows_left * pitch),
                "received": p == 0,
                "rest": 0 if p else rest,
                "builds": builds,
                "inputs": len(earlier),
                "pitch": pitch,
                "half": half,
                "rows": rows_left,
            }
            outs = list(conv(plan, begun, earlier, shifted[p], values[p], weight[layer], columns))
            if builds:
                shifted[p - 1], values[p - 1] = outs.pop(), outs.pop()
            results[p] = outs
            if plan["sends"]:
                arriving = earlier_of(outs[2])
        values, shifted = [r[0] for r in results], [r[1] for r in results]
        if not last:
            halo, rest = arriving, joined(rows_left * pitch)
    result = ()
    for p in reversed(range(pairs)):
        result = (join(p, values[p], mate_of(shifted[p]), latents.shape, *result),)
    return result[0]


def solution(mesh):
    in_specs = (P(("clips", "tm"), "rows", None, None), P(), P(), P())
    out_specs = P(("clips", "tm"), "rows", None, None)
    return jax.shard_map(on_device, mesh=mesh, in_specs=in_specs, out_specs=out_specs, check_vma=False)
```

```python
import functools

import jax
import jax.numpy as jnp
from jax import lax
from jax.experimental import pallas as pl
from jax.experimental.pallas import tpu as pltpu
from jax.sharding import PartitionSpec as P

EPSILON = 1e-06
PAIR = 2
LANES = 128
TILE = 256
VMEM = pl.BlockSpec(memory_space=pltpu.VMEM)
ANY = pl.BlockSpec(memory_space=pl.ANY)
LIMIT = 24 * 1024 * 1024
LARGE = 44 * 1024 * 1024


def place():
    strip = lax.axis_index("rows").astype(jnp.int32)
    core, group = strip & 1, strip >> 1
    return core, group, core == group


def rounded(lanes):
    return -(-lanes // LANES) * LANES


def column(row):
    return jnp.transpose(jnp.broadcast_to(row, (LANES, row.shape[1])))


def lane_of(lanes):
    return lax.broadcasted_iota(jnp.int32, (1, lanes), 1)


def filled(lanes, pitch):
    lane = lane_of(lanes)
    gaps = lane < 0
    for end in range(pitch - 1, lanes, pitch):
        gaps = gaps | (lane == end)
    return jnp.where(gaps, 0.0, 1.0)


def activated(values, gain, mask):
    squares = jnp.mean(values * values, axis=0, keepdims=True)
    halved = values * (lax.rsqrt(squares + EPSILON) * (0.5 * mask)) * gain
    return (halved + halved * jnp.tanh(halved)).astype(jnp.bfloat16)


def weights_kernel(w_ref, rows_ref, *refs):
    outs, columns_ref, held_ref, sems = refs[:-3], refs[-3], refs[-2], refs[-1]
    layers, taps, channels_out, ins = w_ref.shape
    step = taps // 3
    places = [(layer, time_tap) for layer in range(layers) for time_tap in range(3)]
    copies = []
    for n, (layer, time_tap) in enumerate(places):
        part = pl.ds(step * time_tap, step)
        copies.append(pltpu.make_async_copy(w_ref.at[layer, part], held_ref.at[n], sems.at[n]))
        copies[-1].start()
    _, flipped, _ = place()
    for layer in range(layers):
        columns_ref[layer, 0] = column(rows_ref[layer : layer + 1, :])
        columns_ref[layer, 1] = column(rows_ref[layers + layer : layers + layer + 1, :])
    for n, (layer, time_tap) in enumerate(places):
        copies[n].wait()
        for row_tap in range(3):
            source = 3 * (row_tap + flipped * (2 - 2 * row_tap))
            at = (3 * (2 - time_tap) + row_tap) * ins
            outs[layer][:, at : at + ins] = held_ref[n, pl.ds(source, 3)].reshape(3 * channels_out, ins)


def weights(conv_weight, rows):
    layers, taps, outs, ins = conv_weight.shape
    one = jax.ShapeDtypeStruct((3 * outs, 9 * ins), conv_weight.dtype)
    results = pl.pallas_call(
        weights_kernel,
        out_shape=(one,) * layers + (jax.ShapeDtypeStruct((layers, 2, outs, LANES), jnp.float32),),
        in_specs=[ANY, VMEM],
        out_specs=(VMEM,) * (layers + 1),
        scratch_shapes=[
            pltpu.VMEM((3 * layers, taps // 3, outs, ins), conv_weight.dtype),
            pltpu.SemaphoreType.DMA((3 * layers,)),
        ],
        compiler_params=pltpu.CompilerParams(vmem_limit_bytes=LARGE),
        cost_estimate=pl.CostEstimate(flops=0, bytes_accessed=4 * conv_weight.size, transcendentals=0),
        name="weights",
    )(conv_weight, rows)
    return results[:-1], results[-1]


def split_kernel(in_ref, *out_refs):
    for p, out_ref in enumerate(out_refs):
        out_ref[...] = in_ref[PAIR * p : PAIR * (p + 1)]


def split(latents):
    pairs = latents.shape[0] // PAIR
    return pl.pallas_call(
        split_kernel,
        out_shape=(jax.ShapeDtypeStruct((PAIR,) + latents.shape[1:], latents.dtype),) * pairs,
        in_specs=[VMEM],
        out_specs=(VMEM,) * pairs,
        compiler_params=pltpu.CompilerParams(vmem_limit_bytes=LIMIT),
        name="split",
    )(latents)


def joined(valid):
    rest = valid % LANES
    return rest if 0 < PAIR * rest <= LANES else 0


def spread(out_ref, index, act, pitch):
    lanes = out_ref.shape[3]
    above = pltpu.roll(act, pitch, 1)
    below = pltpu.roll(act, act.shape[1] - pitch, 1)
    edge = jnp.where(lane_of(LANES) < pitch, 0.0, above[:, :LANES].astype(jnp.float32))
    out_ref[index, 0, :, :LANES] = edge.astype(jnp.bfloat16)
    out_ref[index, 0, :, LANES:] = above[:, LANES:lanes]
    out_ref[index, 1] = act[:, :lanes]
    out_ref[index, 2] = below[:, :lanes]


def placed(blocks, core, row, window, line):
    pitch, width = window + 1, line.shape[1]
    lane = lane_of(LANES)
    block, low = divmod(row * pitch, LANES)
    shift = lax.rem(low + LANES - core * (width - window), LANES)
    turned = pltpu.roll(line, shift, 1)
    here = (lane >= low) & (lane < low + window)
    blocks[block] = blocks.get(block, 0.0) + jnp.where(here, turned, 0.0)
    if low + window > LANES:
        blocks[block + 1] = blocks.get(block + 1, 0.0) + jnp.where(lane < low + window - LANES, turned, 0.0)


def near_kernel(halo, pairs, mate_ref, gains_ref, *refs):
    own_refs, value_refs, act_refs = refs[:pairs], refs[pairs : 2 * pairs], refs[2 * pairs : 3 * pairs]
    send_refs = refs[3 * pairs :]
    frames, rows, _, width = mate_ref.shape
    window = width // 2 + halo
    core, group, outer = place()
    gain = column(gains_ref[0:1, :])
    done = act_refs[0].shape[2]
    mask = filled(done, window + 1)
    for f in range(frames):
        p, t = divmod(f, PAIR)
        blocks, sent = {}, {}
        for row in range(2 * rows):
            at = row % rows
            index = at + group * (rows - 1 - 2 * at)
            own, mate = own_refs[p][t, index], mate_ref[f, index]
            one, two = (own, mate) if row < rows else (mate, own)
            line = jnp.where(outer, one, two).astype(jnp.float32)
            placed(blocks, core, row, window, line)
            there = 4 * rows - 1 - row
            if p < pairs - 1 and there < 2 * rows + halo:
                placed(sent, core, there, window, line)
        for b in sent:
            send_refs[p][t, :, b * LANES - done : (b + 1) * LANES - done] = sent[b].astype(jnp.bfloat16)
        for b in blocks:
            part = slice(b * LANES, (b + 1) * LANES)
            value_refs[p][t, :, part] = blocks[b].astype(jnp.bfloat16)
            if part.stop <= done:
                act_refs[p][t, :, part] = activated(blocks[b], gain, mask[:, part])


def near(halo, mate, gains, own):
    frames, rows, channels, width = mate.shape
    pitch = width // 2 + halo + 1
    lanes = 2 * rows * pitch
    done = lanes // LANES * LANES
    pairs = len(own)
    sent = jax.ShapeDtypeStruct((PAIR, channels, rounded(lanes + halo * pitch) - done), jnp.bfloat16)
    outs = pl.pallas_call(
        functools.partial(near_kernel, halo, pairs),
        out_shape=(jax.ShapeDtypeStruct((PAIR, channels, rounded(lanes)), jnp.bfloat16),) * pairs
        + (jax.ShapeDtypeStruct((PAIR, channels, done), jnp.bfloat16),) * pairs
        + (sent,) * (pairs - 1),
        in_specs=[VMEM] * (2 + pairs),
        out_specs=(VMEM,) * (3 * pairs - 1),
        compiler_params=pltpu.CompilerParams(vmem_limit_bytes=LIMIT),
        cost_estimate=pl.CostEstimate(flops=40 * mate.size, bytes_accessed=8 * mate.size, transcendentals=2 * mate.size),
        name="near",
    )(mate, gains, *own)
    return outs[:pairs], outs[pairs : 2 * pairs], outs[2 * pairs :]


def far_blocks(halo, far_ref, mate_ref, t, blocks):
    _, rows, _, width = far_ref.shape
    core, group, outer = place()
    for row in range(2 * rows, 2 * rows + halo):
        local = 4 * rows - 1 - row
        at = local % rows
        index = at + (1 - group) * (rows - 1 - 2 * at)
        one, two = (mate_ref, far_ref) if local < rows else (far_ref, mate_ref)
        line = jnp.where(outer, one[t, index], two[t, index]).astype(jnp.float32)
        placed(blocks, core, row, width // 2 + halo, line)


def add_far(pitch, add, near_ref, act_ref, columns_ref, values_ref, shifted_ref, send_ref=None):
    lanes, done = values_ref.shape[2], act_ref.shape[2]
    mask = filled(lanes, pitch)
    for t in range(PAIR):
        values_ref[t, :, :done] = near_ref[t, :, :done]
        acts = [act_ref[t]]
        blocks = {done // LANES: near_ref[t, :, done:].astype(jnp.float32)}
        add(t, blocks)
        for b in sorted(blocks):
            part = slice(b * LANES, (b + 1) * LANES)
            values_ref[t, :, part] = blocks[b].astype(jnp.bfloat16)
            acts.append(activated(blocks[b], columns_ref[0, 0], mask[:, part]))
        act = jnp.concatenate(acts, axis=1)
        spread(shifted_ref, t, act, pitch)
        if send_ref is not None:
            send_ref[t] = act


def far_shapes(rows, halo, channels, half):
    pitch = half + halo + 1
    return (
        jax.ShapeDtypeStruct((PAIR, channels, rounded((2 * rows + halo) * pitch)), jnp.bfloat16),
        jax.ShapeDtypeStruct((PAIR, 3, channels, rounded((2 * rows + halo - 1) * pitch)), jnp.bfloat16),
    )


def beyond(halo, columns, *parts):
    far = parts[0]
    _, rows, channels, width = far.shape
    values, shifted = far_shapes(rows, halo, channels, width // 2)

    def kernel(columns_ref, far_ref, mate_ref, near_ref, act_ref, *outs):
        add = functools.partial(far_blocks, halo, far_ref, mate_ref)
        add_far(width // 2 + halo + 1, add, near_ref, act_ref, columns_ref, *outs)

    return pl.pallas_call(
        kernel,
        out_shape=(values, shifted, values),
        in_specs=[VMEM] * 5,
        out_specs=(VMEM,) * 3,
        compiler_params=pltpu.CompilerParams(vmem_limit_bytes=LIMIT),
        cost_estimate=pl.CostEstimate(flops=40 * far.size, bytes_accessed=8 * far.size, transcendentals=2 * far.size),
        name="beyond",
    )(columns, *parts)


def lines_of(ref, frame):
    return ref[frame].reshape(3 * ref.shape[2], ref.shape[3])


def by_taps(sums):
    channels, lanes = sums.shape[0] // 3, sums.shape[1]
    return [
        [sums[tap * channels : (tap + 1) * channels, at : at + LANES] for at in range(0, lanes, LANES)]
        for tap in range(3)
    ]


def column_sums(taps):
    lane = lane_of(LANES)
    left, middle, right = taps
    lefts = [pltpu.roll(block, 1, 1) for block in left]
    rights = [pltpu.roll(block, LANES - 1, 1) for block in right] + [0.0]
    return [
        jnp.where(lane == 0, lefts[b - 1] if b else 0.0, lefts[b])
        + middle[b]
        + jnp.where(lane == LANES - 1, rights[b + 1], rights[b])
        for b in range(len(middle))
    ]


def begin_kernel(shifted_ref, w_ref, out_ref):
    depth = 3 * shifted_ref.shape[2]
    for t in range(PAIR):
        rhs = jnp.concatenate([lines_of(shifted_ref, j) for j in range(t, -1, -1)], axis=0)
        sums = jnp.dot(w_ref[:, : (t + 1) * depth], rhs, preferred_element_type=jnp.float32)
        for b, block in enumerate(column_sums(by_taps(sums))):
            out_ref[t, :, b * LANES : (b + 1) * LANES] = block


def begin(shifted, weight):
    _, _, channels, lanes = shifted.shape
    return pl.pallas_call(
        begin_kernel,
        out_shape=jax.ShapeDtypeStruct((PAIR, channels, lanes), jnp.float32),
        in_specs=[VMEM] * 2,
        out_specs=VMEM,
        compiler_params=pltpu.CompilerParams(vmem_limit_bytes=LIMIT),
        cost_estimate=pl.CostEstimate(flops=0, bytes_accessed=0, transcendentals=0),
        name="begin",
    )(shifted, weight)


def conv_kernel(plan, shifted_ref, values_ref, w_ref, columns_ref, *refs):
    layer, pitch, half, received = plan["layer"], plan["pitch"], plan["half"], plan["received"]
    last, sends, rest, rest_sent = plan["last"], plan["sends"], plan["rest"], plan["rest_sent"]
    refs = list(refs)
    begun_ref = refs.pop(0) if plan["begun"] else None
    earlier_refs = [refs.pop(0) for _ in range(plan["inputs"])]
    earlier_ref = refs.pop() if received else earlier_refs[0]
    if received:
        for t in range(PAIR):
            if rest:
                whole = (earlier_refs[0].shape[1] - LANES) // PAIR
                tail = earlier_refs[0][:, PAIR * whole :].astype(jnp.float32)
                tail = tail if t == 0 else pltpu.roll(tail, LANES - t * (LANES // PAIR), 1)
                tail = jnp.where(lane_of(LANES) < rest, tail, 0.0).astype(jnp.bfloat16)
                act = jnp.concatenate([earlier_refs[0][:, t * whole : (t + 1) * whole], tail], axis=1)
            else:
                act = earlier_refs[0][t]
            spread(earlier_ref, t, act, pitch)
    outs = refs
    if plan["builds"]:
        earlier_ref = outs.pop()
        came_ref, near_ref, act_ref = earlier_refs
        done = act_ref.shape[2]

        def add(t, blocks):
            for at in range(0, came_ref.shape[2], LANES):
                b = (done + at) // LANES
                blocks[b] = blocks.get(b, 0.0) + came_ref[t, :, at : at + LANES].astype(jnp.float32)

        add_far(pitch, add, near_ref, act_ref, columns_ref, outs.pop(), earlier_ref)
    _, _, channels, lanes = shifted_ref.shape
    chunks = lanes // LANES
    lane = lane_of(LANES)

    def window(t, b):
        taken = [(earlier_ref, t + a) if t + a < PAIR else (shifted_ref, t + a - PAIR) for a in (2, 1, 0)]
        at = slice(b * LANES, (b + 1) * LANES)
        return jnp.concatenate([ref[j, :, :, at].reshape(3 * channels, LANES) for ref, j in taken], axis=0)

    bias = columns_ref[layer, 1]
    tails = []
    if not last:
        mask = filled(lanes, pitch)
        gain = columns_ref[layer + 1, 0]

    def finish(t, taps):
        totals, acts = [], []
        for b, conv in enumerate(column_sums(taps)):
            at = slice(b * LANES, (b + 1) * LANES)
            if begun_ref is not None:
                conv = conv + begun_ref[t, :, at]
            total = (values_ref[t, :, at].astype(jnp.float32) + conv + bias).astype(jnp.bfloat16)
            totals.append(total.astype(jnp.float32))
            if last:
                continue
            outs[0][t, :, at] = total
            acts.append(activated(totals[-1], gain, mask[:, at]))
            if not sends:
                continue
            if not rest_sent:
                outs[2][t, :, at] = acts[-1]
            elif b < chunks - 1:
                outs[2][:, (t * (chunks - 1) + b) * LANES : (t * (chunks - 1) + b + 1) * LANES] = acts[-1]
            else:
                tail = jnp.where(lane < rest_sent, acts[-1].astype(jnp.float32), 0.0)
                tails.append(tail if t == 0 else pltpu.roll(tail, t * (LANES // PAIR), 1))
        if not last:
            spread(outs[1], t, jnp.concatenate(acts, axis=1), pitch)
            return
        core, _, outer = place()
        skipped = core * (pitch - 1 - half)

        def columns_of(row, to):
            b, low = divmod(row * pitch, LANES)
            shift = lax.rem(to + 2 * LANES - low - skipped, LANES)
            turned = pltpu.roll(totals[b], shift, 1)
            if low + pitch - 1 <= LANES:
                return turned
            return jnp.where(lane < to + LANES - low - skipped, turned, pltpu.roll(totals[b + 1], shift, 1))

        def rows_of(row):
            return jnp.where(lane < half, columns_of(row, 0), columns_of(row + 1, half))

        outermost, inner = rows_of(0), rows_of(2)
        outs[0][t] = jnp.where(outer, outermost, inner).astype(jnp.bfloat16)
        outs[1][t] = jnp.where(outer, inner, outermost).astype(jnp.bfloat16)

    if plan["begun"]:
        depth = 3 * channels
        for t in range(PAIR):
            at = (t + 1) * depth
            lead = at % LANES
            lines = [lines_of(earlier_ref, j) for j in range(PAIR - 1, t - 1, -1)]
            if lead:
                lines.insert(0, jnp.zeros((lead, lanes), jnp.bfloat16))
            sums = jnp.dot(w_ref[:, at - lead :], jnp.concatenate(lines, axis=0), preferred_element_type=jnp.float32)
            finish(t, by_taps(sums))
    else:
        places = [(t, b) for t in range(PAIR) for b in range(chunks)]
        side = TILE // LANES
        taps = {t: [[], [], []] for t in range(PAIR)}
        finished = 0
        for n in range(0, len(places), side):
            rhs = jnp.concatenate([window(t, b) for t, b in places[n : n + side]], axis=1)
            sums = by_taps(jnp.dot(w_ref[...], rhs, preferred_element_type=jnp.float32))
            for i, (t, _) in enumerate(places[n : n + side]):
                for tap in range(3):
                    taps[t][tap].append(sums[tap][i])
            while finished < PAIR and (finished + 1) * chunks <= n + side:
                finish(finished, taps[finished])
                finished += 1
    if sends and rest_sent:
        outs[2][:, PAIR * (chunks - 1) * LANES :] = sum(tails).astype(jnp.bfloat16)


def conv(plan, begun, earlier, shifted, values, weight, columns):
    _, _, channels, lanes = shifted.shape
    pitch, half, received = plan["pitch"], plan["half"], plan["received"]
    if plan["last"]:
        out_shape = (jax.ShapeDtypeStruct((PAIR, channels, LANES), jnp.bfloat16),) * 2
    else:
        out_shape = (
            jax.ShapeDtypeStruct((PAIR, channels, lanes), jnp.bfloat16),
            jax.ShapeDtypeStruct((PAIR, 3, channels, rounded((plan["rows"] - 1) * pitch)), jnp.bfloat16),
        )
        if plan["sends"] and plan["rest_sent"]:
            out_shape += (jax.ShapeDtypeStruct((channels, PAIR * (lanes - LANES) + LANES), jnp.bfloat16),)
        elif plan["sends"]:
            out_shape += out_shape[:1]
    scratch = [pltpu.VMEM((PAIR, 3, channels, lanes), jnp.bfloat16)] * received
    if plan["builds"]:
        out_shape += far_shapes(plan["rows_near"] // 2, pitch - 1 - half, channels, half)
    return pl.pallas_call(
        functools.partial(conv_kernel, plan),
        out_shape=out_shape,
        in_specs=[VMEM] * (4 + len(begun) + len(earlier)),
        out_specs=(VMEM,) * len(out_shape),
        scratch_shapes=scratch,
        compiler_params=pltpu.CompilerParams(vmem_limit_bytes=LIMIT),
        cost_estimate=pl.CostEstimate(
            flops=54 * channels * channels * PAIR * lanes * (1 + plan["builds"]),
            bytes_accessed=2 * weight.size,
            transcendentals=PAIR * channels * lanes,
        ),
        name=f"conv_{plan['layer']}",
    )(shifted, values, weight, columns, *begun, *earlier)


def join_kernel(pair, kept_ref, got_ref, *refs):
    out_ref, lines_ref, sem = refs[-3:]
    _, rows, _, width = lines_ref.shape
    half = width // 2
    core, group, _ = place()
    first = core == 0
    left_half = lane_of(width) < half
    for t in range(PAIR):
        mine, theirs = kept_ref[t].astype(jnp.float32), got_ref[t].astype(jnp.float32)
        left, right = jnp.where(first, mine, theirs), jnp.where(first, theirs, mine)
        lines = (
            jnp.where(left_half, left, pltpu.roll(right, half, 1)),
            jnp.where(left_half, pltpu.roll(left, half, 1), right),
        )
        for j in range(rows):
            lines_ref[t, j + group * (rows - 1 - 2 * j)] = lines[j].astype(jnp.bfloat16)
    copy = pltpu.make_async_copy(lines_ref, out_ref.at[pl.ds(PAIR * pair, PAIR)], sem)
    copy.start()
    copy.wait()


def join(pair, kept, got, shape, *so_far):
    return pl.pallas_call(
        functools.partial(join_kernel, pair),
        out_shape=jax.ShapeDtypeStruct(shape, jnp.bfloat16),
        in_specs=[VMEM, VMEM] + [ANY] * len(so_far),
        out_specs=ANY,
        scratch_shapes=[pltpu.VMEM((PAIR,) + shape[1:], jnp.bfloat16), pltpu.SemaphoreType.DMA],
        input_output_aliases={2: 0} if so_far else {},
        compiler_params=pltpu.CompilerParams(vmem_limit_bytes=LIMIT),
        name="join",
    )(kept, got, *so_far)


def on_device(latents, conv_weight, norm_gains, biases):
    layers = conv_weight.shape[0]
    frames, rows, channels, width = latents.shape
    strips, blocks = lax.axis_size("rows"), lax.axis_size("tm")
    assert strips == 4 and rows == 2 and frames % PAIR == 0 and width == LANES

    def mate_of(block):
        return lax.ppermute(block, "rows", [(i, i ^ 1) for i in range(strips)])

    def earlier_of(block):
        return lax.ppermute(block, "tm", [(i, i + 1) for i in range(blocks - 1)])

    def beyond_of(block):
        return lax.ppermute(block, "rows", [(i, i ^ 2) for i in range(strips)])

    mate = mate_of(latents)
    pairs = frames // PAIR
    own = split(latents)
    far = beyond_of(own[-1])
    row_values = jnp.concatenate([norm_gains, biases], axis=0)
    weight, columns = weights(conv_weight, row_values)
    near_values, near_act, near_sent = near(layers, mate, row_values, own)
    came = [beyond_of(block) for block in near_sent]
    far, weight, columns, near_values, near_act = lax.optimization_barrier(
        (far, weight, columns, near_values, near_act)
    )
    values, shifted = [None] * pairs, [None] * pairs
    values[-1], shifted[-1], send = beyond(layers, columns, far, mate_of(far), near_values[-1], near_act[-1])
    halo, rest = earlier_of(send), 0
    next_begun = None
    first_begun = begin(shifted[-1], weight[0])
    *came, first_begun = lax.optimization_barrier((*came, first_begun))
    parts = [(came[p], near_values[p], near_act[p]) for p in range(pairs - 1)]
    half = width // 2
    pitch = half + layers + 1
    for layer in range(layers):
        last = layer == layers - 1
        rows_left = 2 * rows + layers - 1 - layer
        results = [None] * pairs
        for p in reversed(range(pairs)):
            builds = layer == 0 and p > 0
            earlier = (halo,) if p == 0 else parts[p - 1] if builds else (shifted[p - 1],)
            waits = builds or (p == 0 and (last or layer == 0))
            if builds and p == pairs - 1:
                begun = (first_begun,)
            elif layer == 0 and p == 0 and next_begun is not None:
                begun = (next_begun,)
            else:
                begun = (begin(shifted[p], weight[layer]),) if waits else ()
            plan = {
                "layer": layer,
                "begun": waits,
                "rows_near": 2 * rows,
                "last": last,
                "sends": p == pairs - 1 and not last,
                "rest_sent": joined(rows_left * pitch),
                "received": p == 0,
                "rest": 0 if p else rest,
                "builds": builds,
                "inputs": len(earlier),
                "pitch": pitch,
                "half": half,
                "rows": rows_left,
            }
            outs = list(conv(plan, begun, earlier, shifted[p], values[p], weight[layer], columns))
            if builds:
                shifted[p - 1], values[p - 1] = outs.pop(), outs.pop()
            results[p] = outs
            if plan["sends"]:
                message = outs[2]
                if layer == 0 and p == 1:
                    next_begun = begin(shifted[0], weight[0])
                    message, next_begun = lax.optimization_barrier((message, next_begun))
                arriving = earlier_of(message)
        values, shifted = [r[0] for r in results], [r[1] for r in results]
        if not last:
            halo, rest = arriving, joined(rows_left * pitch)
    result = ()
    for p in reversed(range(pairs)):
        result = (join(p, values[p], mate_of(shifted[p]), latents.shape, *result),)
    return result[0]


def solution(mesh):
    in_specs = (P(("clips", "tm"), "rows", None, None), P(), P(), P())
    out_specs = P(("clips", "tm"), "rows", None, None)
    return jax.shard_map(on_device, mesh=mesh, in_specs=in_specs, out_specs=out_specs, check_vma=False)
```

```python
import functools

import jax
import jax.numpy as jnp
from jax import lax
from jax.experimental import pallas as pl
from jax.experimental.pallas import tpu as pltpu
from jax.sharding import PartitionSpec as P

EPSILON = 1e-06
PAIR = 2
LANES = 128
TILE = 256
VMEM = pl.BlockSpec(memory_space=pltpu.VMEM)
ANY = pl.BlockSpec(memory_space=pl.ANY)
LIMIT = 24 * 1024 * 1024
LARGE = 44 * 1024 * 1024


def place():
    strip = lax.axis_index("rows").astype(jnp.int32)
    core, group = strip & 1, strip >> 1
    return core, group, core == group


def rounded(lanes):
    return -(-lanes // LANES) * LANES


def column(row):
    return jnp.transpose(jnp.broadcast_to(row, (LANES, row.shape[1])))


def lane_of(lanes):
    return lax.broadcasted_iota(jnp.int32, (1, lanes), 1)


def filled(lanes, pitch):
    lane = lane_of(lanes)
    gaps = lane < 0
    for end in range(pitch - 1, lanes, pitch):
        gaps = gaps | (lane == end)
    return jnp.where(gaps, 0.0, 1.0)


def activated(values, gain, mask):
    squares = jnp.mean(values * values, axis=0, keepdims=True)
    halved = values * (lax.rsqrt(squares + EPSILON) * (0.5 * mask)) * gain
    return (halved + halved * jnp.tanh(halved)).astype(jnp.bfloat16)


def weights_kernel(w_ref, rows_ref, *refs):
    outs, columns_ref, held_ref, sems = refs[:-3], refs[-3], refs[-2], refs[-1]
    layers, taps, channels_out, ins = w_ref.shape
    step = taps // 3
    places = [(layer, time_tap) for layer in range(layers) for time_tap in range(3)]
    copies = []
    for n, (layer, time_tap) in enumerate(places):
        part = pl.ds(step * time_tap, step)
        copies.append(pltpu.make_async_copy(w_ref.at[layer, part], held_ref.at[n], sems.at[n]))
        copies[-1].start()
    _, flipped, _ = place()
    for layer in range(layers):
        columns_ref[layer, 0] = column(rows_ref[layer : layer + 1, :])
        columns_ref[layer, 1] = column(rows_ref[layers + layer : layers + layer + 1, :])
    for n, (layer, time_tap) in enumerate(places):
        copies[n].wait()
        for row_tap in range(3):
            source = 3 * (row_tap + flipped * (2 - 2 * row_tap))
            at = (3 * (2 - time_tap) + row_tap) * ins
            outs[layer][:, at : at + ins] = held_ref[n, pl.ds(source, 3)].reshape(3 * channels_out, ins)


def weights(conv_weight, rows):
    layers, taps, outs, ins = conv_weight.shape
    one = jax.ShapeDtypeStruct((3 * outs, 9 * ins), conv_weight.dtype)
    results = pl.pallas_call(
        weights_kernel,
        out_shape=(one,) * layers + (jax.ShapeDtypeStruct((layers, 2, outs, LANES), jnp.float32),),
        in_specs=[ANY, VMEM],
        out_specs=(VMEM,) * (layers + 1),
        scratch_shapes=[
            pltpu.VMEM((3 * layers, taps // 3, outs, ins), conv_weight.dtype),
            pltpu.SemaphoreType.DMA((3 * layers,)),
        ],
        compiler_params=pltpu.CompilerParams(vmem_limit_bytes=LARGE),
        cost_estimate=pl.CostEstimate(flops=0, bytes_accessed=4 * conv_weight.size, transcendentals=0),
        name="weights",
    )(conv_weight, rows)
    return results[:-1], results[-1]


def split_kernel(in_ref, *out_refs):
    for p, out_ref in enumerate(out_refs):
        out_ref[...] = in_ref[PAIR * p : PAIR * (p + 1)]


def split(latents):
    pairs = latents.shape[0] // PAIR
    return pl.pallas_call(
        split_kernel,
        out_shape=(jax.ShapeDtypeStruct((PAIR,) + latents.shape[1:], latents.dtype),) * pairs,
        in_specs=[VMEM],
        out_specs=(VMEM,) * pairs,
        compiler_params=pltpu.CompilerParams(vmem_limit_bytes=LIMIT),
        name="split",
    )(latents)


def joined(valid):
    rest = valid % LANES
    return rest if 0 < PAIR * rest <= LANES else 0


def spread(out_ref, index, act, pitch):
    lanes = out_ref.shape[3]
    above = pltpu.roll(act, pitch, 1)
    below = pltpu.roll(act, act.shape[1] - pitch, 1)
    edge = jnp.where(lane_of(LANES) < pitch, 0.0, above[:, :LANES].astype(jnp.float32))
    out_ref[index, 0, :, :LANES] = edge.astype(jnp.bfloat16)
    out_ref[index, 0, :, LANES:] = above[:, LANES:lanes]
    out_ref[index, 1] = act[:, :lanes]
    out_ref[index, 2] = below[:, :lanes]


def placed(blocks, core, row, window, line):
    pitch, width = window + 1, line.shape[1]
    lane = lane_of(LANES)
    block, low = divmod(row * pitch, LANES)
    shift = lax.rem(low + LANES - core * (width - window), LANES)
    turned = pltpu.roll(line, shift, 1)
    here = (lane >= low) & (lane < low + window)
    blocks[block] = blocks.get(block, 0.0) + jnp.where(here, turned, 0.0)
    if low + window > LANES:
        blocks[block + 1] = blocks.get(block + 1, 0.0) + jnp.where(lane < low + window - LANES, turned, 0.0)


def near_kernel(halo, pairs, mate_ref, gains_ref, *refs):
    own_refs, value_refs, act_refs = refs[:pairs], refs[pairs : 2 * pairs], refs[2 * pairs : 3 * pairs]
    send_refs = refs[3 * pairs :]
    frames, rows, _, width = mate_ref.shape
    window = width // 2 + halo
    core, group, outer = place()
    gain = column(gains_ref[0:1, :])
    done = act_refs[0].shape[2]
    mask = filled(done, window + 1)
    for f in range(frames):
        p, t = divmod(f, PAIR)
        blocks, sent = {}, {}
        for row in range(2 * rows):
            at = row % rows
            index = at + group * (rows - 1 - 2 * at)
            own, mate = own_refs[p][t, index], mate_ref[f, index]
            one, two = (own, mate) if row < rows else (mate, own)
            line = jnp.where(outer, one, two).astype(jnp.float32)
            placed(blocks, core, row, window, line)
            there = 4 * rows - 1 - row
            if p < pairs - 1 and there < 2 * rows + halo:
                placed(sent, core, there, window, line)
        for b in sent:
            send_refs[p][t, :, b * LANES - done : (b + 1) * LANES - done] = sent[b].astype(jnp.bfloat16)
        for b in blocks:
            part = slice(b * LANES, (b + 1) * LANES)
            value_refs[p][t, :, part] = blocks[b].astype(jnp.bfloat16)
            if part.stop <= done:
                act_refs[p][t, :, part] = activated(blocks[b], gain, mask[:, part])


def near(halo, mate, gains, own):
    frames, rows, channels, width = mate.shape
    pitch = width // 2 + halo + 1
    lanes = 2 * rows * pitch
    done = lanes // LANES * LANES
    pairs = len(own)
    sent = jax.ShapeDtypeStruct((PAIR, channels, rounded(lanes + halo * pitch) - done), jnp.bfloat16)
    outs = pl.pallas_call(
        functools.partial(near_kernel, halo, pairs),
        out_shape=(jax.ShapeDtypeStruct((PAIR, channels, rounded(lanes)), jnp.bfloat16),) * pairs
        + (jax.ShapeDtypeStruct((PAIR, channels, done), jnp.bfloat16),) * pairs
        + (sent,) * (pairs - 1),
        in_specs=[VMEM] * (2 + pairs),
        out_specs=(VMEM,) * (3 * pairs - 1),
        compiler_params=pltpu.CompilerParams(vmem_limit_bytes=LIMIT),
        cost_estimate=pl.CostEstimate(flops=40 * mate.size, bytes_accessed=8 * mate.size, transcendentals=2 * mate.size),
        name="near",
    )(mate, gains, *own)
    return outs[:pairs], outs[pairs : 2 * pairs], outs[2 * pairs :]


def far_blocks(halo, far_ref, mate_ref, t, blocks):
    _, rows, _, width = far_ref.shape
    core, group, outer = place()
    for row in range(2 * rows, 2 * rows + halo):
        local = 4 * rows - 1 - row
        at = local % rows
        index = at + (1 - group) * (rows - 1 - 2 * at)
        one, two = (mate_ref, far_ref) if local < rows else (far_ref, mate_ref)
        line = jnp.where(outer, one[t, index], two[t, index]).astype(jnp.float32)
        placed(blocks, core, row, width // 2 + halo, line)


def add_far(pitch, add, near_ref, act_ref, columns_ref, values_ref, shifted_ref, send_ref=None):
    lanes, done = values_ref.shape[2], act_ref.shape[2]
    mask = filled(lanes, pitch)
    for t in range(PAIR):
        values_ref[t, :, :done] = near_ref[t, :, :done]
        acts = [act_ref[t]]
        blocks = {done // LANES: near_ref[t, :, done:].astype(jnp.float32)}
        add(t, blocks)
        for b in sorted(blocks):
            part = slice(b * LANES, (b + 1) * LANES)
            values_ref[t, :, part] = blocks[b].astype(jnp.bfloat16)
            acts.append(activated(blocks[b], columns_ref[0, 0], mask[:, part]))
        act = jnp.concatenate(acts, axis=1)
        spread(shifted_ref, t, act, pitch)
        if send_ref is not None:
            send_ref[t] = act


def far_shapes(rows, halo, channels, half):
    pitch = half + halo + 1
    return (
        jax.ShapeDtypeStruct((PAIR, channels, rounded((2 * rows + halo) * pitch)), jnp.bfloat16),
        jax.ShapeDtypeStruct((PAIR, 3, channels, rounded((2 * rows + halo - 1) * pitch)), jnp.bfloat16),
    )


def beyond(halo, columns, *parts):
    far = parts[0]
    _, rows, channels, width = far.shape
    values, shifted = far_shapes(rows, halo, channels, width // 2)

    def kernel(columns_ref, far_ref, mate_ref, near_ref, act_ref, *outs):
        add = functools.partial(far_blocks, halo, far_ref, mate_ref)
        add_far(width // 2 + halo + 1, add, near_ref, act_ref, columns_ref, *outs)

    return pl.pallas_call(
        kernel,
        out_shape=(values, shifted, values),
        in_specs=[VMEM] * 5,
        out_specs=(VMEM,) * 3,
        compiler_params=pltpu.CompilerParams(vmem_limit_bytes=LIMIT),
        cost_estimate=pl.CostEstimate(flops=40 * far.size, bytes_accessed=8 * far.size, transcendentals=2 * far.size),
        name="beyond",
    )(columns, *parts)


def lines_of(ref, frame):
    return ref[frame].reshape(3 * ref.shape[2], ref.shape[3])


def by_taps(sums):
    channels, lanes = sums.shape[0] // 3, sums.shape[1]
    return [
        [sums[tap * channels : (tap + 1) * channels, at : at + LANES] for at in range(0, lanes, LANES)]
        for tap in range(3)
    ]


def column_sums(taps):
    lane = lane_of(LANES)
    left, middle, right = taps
    lefts = [pltpu.roll(block, 1, 1) for block in left]
    rights = [pltpu.roll(block, LANES - 1, 1) for block in right] + [0.0]
    return [
        jnp.where(lane == 0, lefts[b - 1] if b else 0.0, lefts[b])
        + middle[b]
        + jnp.where(lane == LANES - 1, rights[b + 1], rights[b])
        for b in range(len(middle))
    ]


def begun_rows(t, channels):
    return (t + 1) * 3 * channels // TILE * TILE


def rows_between(lines, start, stop):
    taken, at = [], 0
    for part in lines:
        low, high = max(start - at, 0), min(stop - at, part.shape[0])
        if low < high:
            taken.append(part[low:high])
        at += part.shape[0]
    return jnp.concatenate(taken, axis=0)


def begin_kernel(shifted_ref, w_ref, out_ref):
    for t in range(PAIR):
        cut = begun_rows(t, shifted_ref.shape[2])
        rhs = rows_between([lines_of(shifted_ref, j) for j in range(t, -1, -1)], 0, cut)
        sums = jnp.dot(w_ref[:, :cut], rhs, preferred_element_type=jnp.float32)
        for b, block in enumerate(column_sums(by_taps(sums))):
            out_ref[t, :, b * LANES : (b + 1) * LANES] = block


def begin(shifted, weight):
    _, _, channels, lanes = shifted.shape
    return pl.pallas_call(
        begin_kernel,
        out_shape=jax.ShapeDtypeStruct((PAIR, channels, lanes), jnp.float32),
        in_specs=[VMEM] * 2,
        out_specs=VMEM,
        compiler_params=pltpu.CompilerParams(vmem_limit_bytes=LIMIT),
        cost_estimate=pl.CostEstimate(flops=0, bytes_accessed=0, transcendentals=0),
        name="begin",
    )(shifted, weight)


def conv_kernel(plan, shifted_ref, values_ref, w_ref, columns_ref, *refs):
    layer, pitch, half, received = plan["layer"], plan["pitch"], plan["half"], plan["received"]
    last, sends, rest, rest_sent = plan["last"], plan["sends"], plan["rest"], plan["rest_sent"]
    refs = list(refs)
    begun_ref = refs.pop(0) if plan["begun"] else None
    earlier_refs = [refs.pop(0) for _ in range(plan["inputs"])]
    earlier_ref = refs.pop() if received else earlier_refs[0]
    if received:
        for t in range(PAIR):
            if rest:
                whole = (earlier_refs[0].shape[1] - LANES) // PAIR
                tail = earlier_refs[0][:, PAIR * whole :].astype(jnp.float32)
                tail = tail if t == 0 else pltpu.roll(tail, LANES - t * (LANES // PAIR), 1)
                tail = jnp.where(lane_of(LANES) < rest, tail, 0.0).astype(jnp.bfloat16)
                act = jnp.concatenate([earlier_refs[0][:, t * whole : (t + 1) * whole], tail], axis=1)
            else:
                act = earlier_refs[0][t]
            spread(earlier_ref, t, act, pitch)
    outs = refs
    if plan["builds"]:
        earlier_ref = outs.pop()
        came_ref, near_ref, act_ref = earlier_refs
        done = act_ref.shape[2]

        def add(t, blocks):
            for at in range(0, came_ref.shape[2], LANES):
                b = (done + at) // LANES
                blocks[b] = blocks.get(b, 0.0) + came_ref[t, :, at : at + LANES].astype(jnp.float32)

        add_far(pitch, add, near_ref, act_ref, columns_ref, outs.pop(), earlier_ref)
    _, _, channels, lanes = shifted_ref.shape
    chunks = lanes // LANES
    lane = lane_of(LANES)

    def window(t, b):
        taken = [(earlier_ref, t + a) if t + a < PAIR else (shifted_ref, t + a - PAIR) for a in (2, 1, 0)]
        at = slice(b * LANES, (b + 1) * LANES)
        return jnp.concatenate([ref[j, :, :, at].reshape(3 * channels, LANES) for ref, j in taken], axis=0)

    bias = columns_ref[layer, 1]
    tails = []
    if not last:
        mask = filled(lanes, pitch)
        gain = columns_ref[layer + 1, 0]

    def finish(t, taps):
        totals, acts = [], []
        for b, conv in enumerate(column_sums(taps)):
            at = slice(b * LANES, (b + 1) * LANES)
            if begun_ref is not None:
                conv = conv + begun_ref[t, :, at]
            total = (values_ref[t, :, at].astype(jnp.float32) + conv + bias).astype(jnp.bfloat16)
            totals.append(total.astype(jnp.float32))
            if last:
                continue
            outs[0][t, :, at] = total
            acts.append(activated(totals[-1], gain, mask[:, at]))
            if not sends:
                continue
            if not rest_sent:
                outs[2][t, :, at] = acts[-1]
            elif b < chunks - 1:
                outs[2][:, (t * (chunks - 1) + b) * LANES : (t * (chunks - 1) + b + 1) * LANES] = acts[-1]
            else:
                tail = jnp.where(lane < rest_sent, acts[-1].astype(jnp.float32), 0.0)
                tails.append(tail if t == 0 else pltpu.roll(tail, t * (LANES // PAIR), 1))
        if not last:
            spread(outs[1], t, jnp.concatenate(acts, axis=1), pitch)
            return
        core, _, outer = place()
        skipped = core * (pitch - 1 - half)

        def columns_of(row, to):
            b, low = divmod(row * pitch, LANES)
            shift = lax.rem(to + 2 * LANES - low - skipped, LANES)
            turned = pltpu.roll(totals[b], shift, 1)
            if low + pitch - 1 <= LANES:
                return turned
            return jnp.where(lane < to + LANES - low - skipped, turned, pltpu.roll(totals[b + 1], shift, 1))

        def rows_of(row):
            return jnp.where(lane < half, columns_of(row, 0), columns_of(row + 1, half))

        outermost, inner = rows_of(0), rows_of(2)
        outs[0][t] = jnp.where(outer, outermost, inner).astype(jnp.bfloat16)
        outs[1][t] = jnp.where(outer, inner, outermost).astype(jnp.bfloat16)

    if plan["begun"]:
        for t in range(PAIR):
            cut = begun_rows(t, channels)
            lines = [lines_of(shifted_ref, j) for j in range(t, -1, -1)]
            lines += [lines_of(earlier_ref, j) for j in range(PAIR - 1, t - 1, -1)]
            rhs = rows_between(lines, cut, w_ref.shape[1])
            sums = jnp.dot(w_ref[:, cut:], rhs, preferred_element_type=jnp.float32)
            finish(t, by_taps(sums))
    else:
        places = [(t, b) for t in range(PAIR) for b in range(chunks)]
        side = TILE // LANES
        taps = {t: [[], [], []] for t in range(PAIR)}
        finished = 0
        for n in range(0, len(places), side):
            rhs = jnp.concatenate([window(t, b) for t, b in places[n : n + side]], axis=1)
            sums = by_taps(jnp.dot(w_ref[...], rhs, preferred_element_type=jnp.float32))
            for i, (t, _) in enumerate(places[n : n + side]):
                for tap in range(3):
                    taps[t][tap].append(sums[tap][i])
            while finished < PAIR and (finished + 1) * chunks <= n + side:
                finish(finished, taps[finished])
                finished += 1
    if sends and rest_sent:
        outs[2][:, PAIR * (chunks - 1) * LANES :] = sum(tails).astype(jnp.bfloat16)


def conv(plan, begun, earlier, shifted, values, weight, columns):
    _, _, channels, lanes = shifted.shape
    pitch, half, received = plan["pitch"], plan["half"], plan["received"]
    if plan["last"]:
        out_shape = (jax.ShapeDtypeStruct((PAIR, channels, LANES), jnp.bfloat16),) * 2
    else:
        out_shape = (
            jax.ShapeDtypeStruct((PAIR, channels, lanes), jnp.bfloat16),
            jax.ShapeDtypeStruct((PAIR, 3, channels, rounded((plan["rows"] - 1) * pitch)), jnp.bfloat16),
        )
        if plan["sends"] and plan["rest_sent"]:
            out_shape += (jax.ShapeDtypeStruct((channels, PAIR * (lanes - LANES) + LANES), jnp.bfloat16),)
        elif plan["sends"]:
            out_shape += out_shape[:1]
    scratch = [pltpu.VMEM((PAIR, 3, channels, lanes), jnp.bfloat16)] * received
    if plan["builds"]:
        out_shape += far_shapes(plan["rows_near"] // 2, pitch - 1 - half, channels, half)
    return pl.pallas_call(
        functools.partial(conv_kernel, plan),
        out_shape=out_shape,
        in_specs=[VMEM] * (4 + len(begun) + len(earlier)),
        out_specs=(VMEM,) * len(out_shape),
        scratch_shapes=scratch,
        compiler_params=pltpu.CompilerParams(vmem_limit_bytes=LIMIT),
        cost_estimate=pl.CostEstimate(
            flops=54 * channels * channels * PAIR * lanes * (1 + plan["builds"]),
            bytes_accessed=2 * weight.size,
            transcendentals=PAIR * channels * lanes,
        ),
        name=f"conv_{plan['layer']}",
    )(shifted, values, weight, columns, *begun, *earlier)


def join_kernel(pair, kept_ref, got_ref, *refs):
    out_ref, lines_ref, sem = refs[-3:]
    _, rows, _, width = lines_ref.shape
    half = width // 2
    core, group, _ = place()
    first = core == 0
    left_half = lane_of(width) < half
    for t in range(PAIR):
        mine, theirs = kept_ref[t].astype(jnp.float32), got_ref[t].astype(jnp.float32)
        left, right = jnp.where(first, mine, theirs), jnp.where(first, theirs, mine)
        lines = (
            jnp.where(left_half, left, pltpu.roll(right, half, 1)),
            jnp.where(left_half, pltpu.roll(left, half, 1), right),
        )
        for j in range(rows):
            lines_ref[t, j + group * (rows - 1 - 2 * j)] = lines[j].astype(jnp.bfloat16)
    copy = pltpu.make_async_copy(lines_ref, out_ref.at[pl.ds(PAIR * pair, PAIR)], sem)
    copy.start()
    copy.wait()


def join(pair, kept, got, shape, *so_far):
    return pl.pallas_call(
        functools.partial(join_kernel, pair),
        out_shape=jax.ShapeDtypeStruct(shape, jnp.bfloat16),
        in_specs=[VMEM, VMEM] + [ANY] * len(so_far),
        out_specs=ANY,
        scratch_shapes=[pltpu.VMEM((PAIR,) + shape[1:], jnp.bfloat16), pltpu.SemaphoreType.DMA],
        input_output_aliases={2: 0} if so_far else {},
        compiler_params=pltpu.CompilerParams(vmem_limit_bytes=LIMIT),
        name="join",
    )(kept, got, *so_far)


def on_device(latents, conv_weight, norm_gains, biases):
    layers = conv_weight.shape[0]
    frames, rows, channels, width = latents.shape
    strips, blocks = lax.axis_size("rows"), lax.axis_size("tm")
    assert strips == 4 and rows == 2 and frames % PAIR == 0 and width == LANES

    def mate_of(block):
        return lax.ppermute(block, "rows", [(i, i ^ 1) for i in range(strips)])

    def earlier_of(block):
        return lax.ppermute(block, "tm", [(i, i + 1) for i in range(blocks - 1)])

    def beyond_of(block):
        return lax.ppermute(block, "rows", [(i, i ^ 2) for i in range(strips)])

    mate = mate_of(latents)
    pairs = frames // PAIR
    own = split(latents)
    far = beyond_of(own[-1])
    row_values = jnp.concatenate([norm_gains, biases], axis=0)
    weight, columns = weights(conv_weight, row_values)
    near_values, near_act, near_sent = near(layers, mate, row_values, own)
    came = [beyond_of(block) for block in near_sent]
    far, weight, columns, near_values, near_act = lax.optimization_barrier(
        (far, weight, columns, near_values, near_act)
    )
    values, shifted = [None] * pairs, [None] * pairs
    values[-1], shifted[-1], send = beyond(layers, columns, far, mate_of(far), near_values[-1], near_act[-1])
    halo, rest = earlier_of(send), 0
    next_begun = layer_begun = None
    first_begun = begin(shifted[-1], weight[0])
    *came, first_begun = lax.optimization_barrier((*came, first_begun))
    parts = [(came[p], near_values[p], near_act[p]) for p in range(pairs - 1)]
    half = width // 2
    pitch = half + layers + 1
    for layer in range(layers):
        last = layer == layers - 1
        rows_left = 2 * rows + layers - 1 - layer
        results = [None] * pairs
        for p in reversed(range(pairs)):
            builds = layer == 0 and p > 0
            earlier = (halo,) if p == 0 else parts[p - 1] if builds else (shifted[p - 1],)
            waits = builds or (p == 0 and (last or layer == 0)) or (layer == 1 and layer_begun is not None and p == pairs - 1)
            if builds and p == pairs - 1:
                begun = (first_begun,)
            elif layer == 0 and p == 0 and next_begun is not None:
                begun = (next_begun,)
            elif layer == 1 and p == pairs - 1 and layer_begun is not None:
                begun = (layer_begun,)
            else:
                begun = (begin(shifted[p], weight[layer]),) if waits else ()
            plan = {
                "layer": layer,
                "begun": waits,
                "rows_near": 2 * rows,
                "last": last,
                "sends": p == pairs - 1 and not last,
                "rest_sent": joined(rows_left * pitch),
                "received": p == 0,
                "rest": 0 if p else rest,
                "builds": builds,
                "inputs": len(earlier),
                "pitch": pitch,
                "half": half,
                "rows": rows_left,
            }
            outs = list(conv(plan, begun, earlier, shifted[p], values[p], weight[layer], columns))
            if builds:
                shifted[p - 1], values[p - 1] = outs.pop(), outs.pop()
            results[p] = outs
            if plan["sends"]:
                message = outs[2]
                if layer == 0 and p == 1:
                    next_begun = begin(shifted[0], weight[0])
                    message, next_begun = lax.optimization_barrier((message, next_begun))
                arriving = earlier_of(message)
                if layer == 0 and p == 1 and not last:
                    layer_begun = begin(outs[1], weight[1])
                    halo, layer_begun = lax.optimization_barrier((halo, layer_begun))
        values, shifted = [r[0] for r in results], [r[1] for r in results]
        if not last:
            halo, rest = arriving, joined(rows_left * pitch)
    result = ()
    for p in reversed(range(pairs)):
        result = (join(p, values[p], mate_of(shifted[p]), latents.shape, *result),)
    return result[0]


def solution(mesh):
    in_specs = (P(("clips", "tm"), "rows", None, None), P(), P(), P())
    out_specs = P(("clips", "tm"), "rows", None, None)
    return jax.shard_map(on_device, mesh=mesh, in_specs=in_specs, out_specs=out_specs, check_vma=False)
```

```python
import functools

import jax
import jax.numpy as jnp
from jax import lax
from jax.experimental import pallas as pl
from jax.experimental.pallas import tpu as pltpu
from jax.sharding import PartitionSpec as P

EPSILON = 1e-06
PAIR = 2
LANES = 128
TILE = 256
VMEM = pl.BlockSpec(memory_space=pltpu.VMEM)
ANY = pl.BlockSpec(memory_space=pl.ANY)
LIMIT = 24 * 1024 * 1024
LARGE = 44 * 1024 * 1024


def place():
    strip = lax.axis_index("rows").astype(jnp.int32)
    core, group = strip & 1, strip >> 1
    return core, group, core == group


def rounded(lanes):
    return -(-lanes // LANES) * LANES


def column(row):
    return jnp.transpose(jnp.broadcast_to(row, (LANES, row.shape[1])))


def lane_of(lanes):
    return lax.broadcasted_iota(jnp.int32, (1, lanes), 1)


def filled(lanes, pitch):
    lane = lane_of(lanes)
    gaps = lane < 0
    for end in range(pitch - 1, lanes, pitch):
        gaps = gaps | (lane == end)
    return jnp.where(gaps, 0.0, 1.0)


def activated(values, gain, mask):
    squares = jnp.mean(values * values, axis=0, keepdims=True)
    halved = values * (lax.rsqrt(squares + EPSILON) * (0.5 * mask)) * gain
    return (halved + halved * jnp.tanh(halved)).astype(jnp.bfloat16)


def weights_kernel(w_ref, rows_ref, *refs):
    outs, columns_ref, held_ref, sems = refs[:-3], refs[-3], refs[-2], refs[-1]
    layers, taps, channels_out, ins = w_ref.shape
    step = taps // 3
    places = [(layer, time_tap) for layer in range(layers) for time_tap in range(3)]
    copies = []
    for n, (layer, time_tap) in enumerate(places):
        part = pl.ds(step * time_tap, step)
        copies.append(pltpu.make_async_copy(w_ref.at[layer, part], held_ref.at[n], sems.at[n]))
        copies[-1].start()
    _, flipped, _ = place()
    for layer in range(layers):
        columns_ref[layer, 0] = column(rows_ref[layer : layer + 1, :])
        columns_ref[layer, 1] = column(rows_ref[layers + layer : layers + layer + 1, :])
    for n, (layer, time_tap) in enumerate(places):
        copies[n].wait()
        for row_tap in range(3):
            source = 3 * (row_tap + flipped * (2 - 2 * row_tap))
            at = (3 * (2 - time_tap) + row_tap) * ins
            outs[layer][:, at : at + ins] = held_ref[n, pl.ds(source, 3)].reshape(3 * channels_out, ins)


def weights(conv_weight, rows):
    layers, taps, outs, ins = conv_weight.shape
    one = jax.ShapeDtypeStruct((3 * outs, 9 * ins), conv_weight.dtype)
    results = pl.pallas_call(
        weights_kernel,
        out_shape=(one,) * layers + (jax.ShapeDtypeStruct((layers, 2, outs, LANES), jnp.float32),),
        in_specs=[ANY, VMEM],
        out_specs=(VMEM,) * (layers + 1),
        scratch_shapes=[
            pltpu.VMEM((3 * layers, taps // 3, outs, ins), conv_weight.dtype),
            pltpu.SemaphoreType.DMA((3 * layers,)),
        ],
        compiler_params=pltpu.CompilerParams(vmem_limit_bytes=LARGE),
        cost_estimate=pl.CostEstimate(flops=0, bytes_accessed=4 * conv_weight.size, transcendentals=0),
        name="weights",
    )(conv_weight, rows)
    return results[:-1], results[-1]


def split_kernel(in_ref, *out_refs):
    for p, out_ref in enumerate(out_refs):
        out_ref[...] = in_ref[PAIR * p : PAIR * (p + 1)]


def split(latents):
    pairs = latents.shape[0] // PAIR
    return pl.pallas_call(
        split_kernel,
        out_shape=(jax.ShapeDtypeStruct((PAIR,) + latents.shape[1:], latents.dtype),) * pairs,
        in_specs=[VMEM],
        out_specs=(VMEM,) * pairs,
        compiler_params=pltpu.CompilerParams(vmem_limit_bytes=LIMIT),
        name="split",
    )(latents)


def joined(valid):
    rest = valid % LANES
    return rest if 0 < PAIR * rest <= LANES else 0


def spread(out_ref, index, act, pitch):
    lanes = out_ref.shape[3]
    above = pltpu.roll(act, pitch, 1)
    below = pltpu.roll(act, act.shape[1] - pitch, 1)
    edge = jnp.where(lane_of(LANES) < pitch, 0.0, above[:, :LANES].astype(jnp.float32))
    out_ref[index, 0, :, :LANES] = edge.astype(jnp.bfloat16)
    out_ref[index, 0, :, LANES:] = above[:, LANES:lanes]
    out_ref[index, 1] = act[:, :lanes]
    out_ref[index, 2] = below[:, :lanes]


def placed(blocks, core, row, window, line):
    pitch, width = window + 1, line.shape[1]
    lane = lane_of(LANES)
    block, low = divmod(row * pitch, LANES)
    shift = lax.rem(low + LANES - core * (width - window), LANES)
    turned = pltpu.roll(line, shift, 1)
    here = (lane >= low) & (lane < low + window)
    blocks[block] = blocks.get(block, 0.0) + jnp.where(here, turned, 0.0)
    if low + window > LANES:
        blocks[block + 1] = blocks.get(block + 1, 0.0) + jnp.where(lane < low + window - LANES, turned, 0.0)


def near_kernel(halo, pairs, mate_ref, gains_ref, *refs):
    own_refs, value_refs, act_refs = refs[:pairs], refs[pairs : 2 * pairs], refs[2 * pairs : 3 * pairs]
    send_refs = refs[3 * pairs :]
    frames, rows, _, width = mate_ref.shape
    window = width // 2 + halo
    core, group, outer = place()
    gain = column(gains_ref[0:1, :])
    done = act_refs[0].shape[2]
    mask = filled(done, window + 1)
    for f in range(frames):
        p, t = divmod(f, PAIR)
        blocks, sent = {}, {}
        for row in range(2 * rows):
            at = row % rows
            index = at + group * (rows - 1 - 2 * at)
            own, mate = own_refs[p][t, index], mate_ref[f, index]
            one, two = (own, mate) if row < rows else (mate, own)
            line = jnp.where(outer, one, two).astype(jnp.float32)
            placed(blocks, core, row, window, line)
            there = 4 * rows - 1 - row
            if p < pairs - 1 and there < 2 * rows + halo:
                placed(sent, core, there, window, line)
        for b in sent:
            send_refs[p][t, :, b * LANES - done : (b + 1) * LANES - done] = sent[b].astype(jnp.bfloat16)
        for b in blocks:
            part = slice(b * LANES, (b + 1) * LANES)
            value_refs[p][t, :, part] = blocks[b].astype(jnp.bfloat16)
            if part.stop <= done:
                act_refs[p][t, :, part] = activated(blocks[b], gain, mask[:, part])


def near(halo, mate, gains, own):
    frames, rows, channels, width = mate.shape
    pitch = width // 2 + halo + 1
    lanes = 2 * rows * pitch
    done = lanes // LANES * LANES
    pairs = len(own)
    sent = jax.ShapeDtypeStruct((PAIR, channels, rounded(lanes + halo * pitch) - done), jnp.bfloat16)
    outs = pl.pallas_call(
        functools.partial(near_kernel, halo, pairs),
        out_shape=(jax.ShapeDtypeStruct((PAIR, channels, rounded(lanes)), jnp.bfloat16),) * pairs
        + (jax.ShapeDtypeStruct((PAIR, channels, done), jnp.bfloat16),) * pairs
        + (sent,) * (pairs - 1),
        in_specs=[VMEM] * (2 + pairs),
        out_specs=(VMEM,) * (3 * pairs - 1),
        compiler_params=pltpu.CompilerParams(vmem_limit_bytes=LIMIT),
        cost_estimate=pl.CostEstimate(flops=40 * mate.size, bytes_accessed=8 * mate.size, transcendentals=2 * mate.size),
        name="near",
    )(mate, gains, *own)
    return outs[:pairs], outs[pairs : 2 * pairs], outs[2 * pairs :]


def far_blocks(halo, far_ref, mate_ref, t, blocks):
    _, rows, _, width = far_ref.shape
    core, group, outer = place()
    for row in range(2 * rows, 2 * rows + halo):
        local = 4 * rows - 1 - row
        at = local % rows
        index = at + (1 - group) * (rows - 1 - 2 * at)
        one, two = (mate_ref, far_ref) if local < rows else (far_ref, mate_ref)
        line = jnp.where(outer, one[t, index], two[t, index]).astype(jnp.float32)
        placed(blocks, core, row, width // 2 + halo, line)


def add_far(pitch, add, near_ref, act_ref, columns_ref, values_ref, shifted_ref, send_ref=None):
    lanes, done = values_ref.shape[2], act_ref.shape[2]
    mask = filled(lanes, pitch)
    for t in range(PAIR):
        values_ref[t, :, :done] = near_ref[t, :, :done]
        acts = [act_ref[t]]
        blocks = {done // LANES: near_ref[t, :, done:].astype(jnp.float32)}
        add(t, blocks)
        for b in sorted(blocks):
            part = slice(b * LANES, (b + 1) * LANES)
            values_ref[t, :, part] = blocks[b].astype(jnp.bfloat16)
            acts.append(activated(blocks[b], columns_ref[0, 0], mask[:, part]))
        act = jnp.concatenate(acts, axis=1)
        spread(shifted_ref, t, act, pitch)
        if send_ref is not None:
            send_ref[t] = act


def far_shapes(rows, halo, channels, half):
    pitch = half + halo + 1
    return (
        jax.ShapeDtypeStruct((PAIR, channels, rounded((2 * rows + halo) * pitch)), jnp.bfloat16),
        jax.ShapeDtypeStruct((PAIR, 3, channels, rounded((2 * rows + halo - 1) * pitch)), jnp.bfloat16),
    )


def beyond(halo, columns, *parts):
    far = parts[0]
    _, rows, channels, width = far.shape
    values, shifted = far_shapes(rows, halo, channels, width // 2)

    def kernel(columns_ref, far_ref, mate_ref, near_ref, act_ref, *outs):
        add = functools.partial(far_blocks, halo, far_ref, mate_ref)
        add_far(width // 2 + halo + 1, add, near_ref, act_ref, columns_ref, *outs)

    return pl.pallas_call(
        kernel,
        out_shape=(values, shifted, values),
        in_specs=[VMEM] * 5,
        out_specs=(VMEM,) * 3,
        compiler_params=pltpu.CompilerParams(vmem_limit_bytes=LIMIT),
        cost_estimate=pl.CostEstimate(flops=40 * far.size, bytes_accessed=8 * far.size, transcendentals=2 * far.size),
        name="beyond",
    )(columns, *parts)


def by_taps(sums):
    channels, lanes = sums.shape[0] // 3, sums.shape[1]
    return [
        [sums[tap * channels : (tap + 1) * channels, at : at + LANES] for at in range(0, lanes, LANES)]
        for tap in range(3)
    ]


def column_sums(taps):
    lane = lane_of(LANES)
    left, middle, right = taps
    lefts = [pltpu.roll(block, 1, 1) for block in left]
    rights = [pltpu.roll(block, LANES - 1, 1) for block in right] + [0.0]
    return [
        jnp.where(lane == 0, lefts[b - 1] if b else 0.0, lefts[b])
        + middle[b]
        + jnp.where(lane == LANES - 1, rights[b + 1], rights[b])
        for b in range(len(middle))
    ]


def begun_rows(t, channels):
    return (t + 1) * 3 * channels // TILE * TILE


def rows_between(lines, start, stop):
    taken, at = [], 0
    for part in lines:
        low, high = max(start - at, 0), min(stop - at, part.shape[0])
        if low < high:
            taken.append(part[low:high])
        at += part.shape[0]
    return jnp.concatenate(taken, axis=0)


def block_lines(ref, frame, b):
    return ref[frame, :, :, b * LANES : (b + 1) * LANES].reshape(3 * ref.shape[2], LANES)


def padded_rows(lines, start, stop, low, high):
    parts = [rows_between(lines, start, stop)]
    if low < start:
        parts.insert(0, jnp.zeros((start - low, LANES), jnp.bfloat16))
    if stop < high:
        parts.append(jnp.zeros((high - stop, LANES), jnp.bfloat16))
    return parts[0] if len(parts) == 1 else jnp.concatenate(parts, axis=0)


def tiled(lanes):
    places = [(t, b) for t in range(PAIR) for b in range(lanes // LANES)]
    side = TILE // LANES
    return [places[n : n + side] for n in range(0, len(places), side)]


def by_frames(lanes, tile_sums, finish):
    taps = {t: [[], [], []] for t in range(PAIR)}
    for places in tiled(lanes):
        sums = by_taps(tile_sums(places))
        for i, (t, b) in enumerate(places):
            for tap in range(3):
                taps[t][tap].append(sums[tap][i])
        for t, b in places:
            if b == lanes // LANES - 1:
                finish(t, taps[t])


def begin_kernel(shifted_ref, w_ref, out_ref):
    _, _, channels, lanes = shifted_ref.shape

    def tile_sums(places):
        depth = max(begun_rows(t, channels) for t, _ in places)
        rhs = [
            padded_rows(
                [block_lines(shifted_ref, j, b) for j in range(t, -1, -1)],
                0,
                begun_rows(t, channels),
                0,
                depth,
            )
            for t, b in places
        ]
        return jnp.dot(w_ref[:, :depth], jnp.concatenate(rhs, axis=1), preferred_element_type=jnp.float32)

    def finish(t, taps):
        for b, block in enumerate(column_sums(taps)):
            out_ref[t, :, b * LANES : (b + 1) * LANES] = block

    by_frames(lanes, tile_sums, finish)


def begin(shifted, weight):
    _, _, channels, lanes = shifted.shape
    return pl.pallas_call(
        begin_kernel,
        out_shape=jax.ShapeDtypeStruct((PAIR, channels, lanes), jnp.float32),
        in_specs=[VMEM] * 2,
        out_specs=VMEM,
        compiler_params=pltpu.CompilerParams(vmem_limit_bytes=LIMIT),
        cost_estimate=pl.CostEstimate(flops=0, bytes_accessed=0, transcendentals=0),
        name="begin",
    )(shifted, weight)


def conv_kernel(plan, shifted_ref, values_ref, w_ref, columns_ref, *refs):
    layer, pitch, half, received = plan["layer"], plan["pitch"], plan["half"], plan["received"]
    last, sends, rest, rest_sent = plan["last"], plan["sends"], plan["rest"], plan["rest_sent"]
    refs = list(refs)
    begun_ref = refs.pop(0) if plan["begun"] else None
    earlier_refs = [refs.pop(0) for _ in range(plan["inputs"])]
    earlier_ref = refs.pop() if received else earlier_refs[0]
    if received:
        for t in range(PAIR):
            if rest:
                whole = (earlier_refs[0].shape[1] - LANES) // PAIR
                tail = earlier_refs[0][:, PAIR * whole :].astype(jnp.float32)
                tail = tail if t == 0 else pltpu.roll(tail, LANES - t * (LANES // PAIR), 1)
                tail = jnp.where(lane_of(LANES) < rest, tail, 0.0).astype(jnp.bfloat16)
                act = jnp.concatenate([earlier_refs[0][:, t * whole : (t + 1) * whole], tail], axis=1)
            else:
                act = earlier_refs[0][t]
            spread(earlier_ref, t, act, pitch)
    outs = refs
    if plan["builds"]:
        earlier_ref = outs.pop()
        came_ref, near_ref, act_ref = earlier_refs
        done = act_ref.shape[2]

        def add(t, blocks):
            for at in range(0, came_ref.shape[2], LANES):
                b = (done + at) // LANES
                blocks[b] = blocks.get(b, 0.0) + came_ref[t, :, at : at + LANES].astype(jnp.float32)

        add_far(pitch, add, near_ref, act_ref, columns_ref, outs.pop(), earlier_ref)
    _, _, channels, lanes = shifted_ref.shape
    chunks = lanes // LANES
    lane = lane_of(LANES)

    bias = columns_ref[layer, 1]
    tails = []
    if not last:
        mask = filled(lanes, pitch)
        gain = columns_ref[layer + 1, 0]

    def finish(t, taps):
        totals, acts = [], []
        for b, conv in enumerate(column_sums(taps)):
            at = slice(b * LANES, (b + 1) * LANES)
            if begun_ref is not None:
                conv = conv + begun_ref[t, :, at]
            total = (values_ref[t, :, at].astype(jnp.float32) + conv + bias).astype(jnp.bfloat16)
            totals.append(total.astype(jnp.float32))
            if last:
                continue
            outs[0][t, :, at] = total
            acts.append(activated(totals[-1], gain, mask[:, at]))
            if not sends:
                continue
            if not rest_sent:
                outs[2][t, :, at] = acts[-1]
            elif b < chunks - 1:
                outs[2][:, (t * (chunks - 1) + b) * LANES : (t * (chunks - 1) + b + 1) * LANES] = acts[-1]
            else:
                tail = jnp.where(lane < rest_sent, acts[-1].astype(jnp.float32), 0.0)
                tails.append(tail if t == 0 else pltpu.roll(tail, t * (LANES // PAIR), 1))
        if not last:
            spread(outs[1], t, jnp.concatenate(acts, axis=1), pitch)
            return
        core, _, outer = place()
        skipped = core * (pitch - 1 - half)

        def columns_of(row, to):
            b, low = divmod(row * pitch, LANES)
            shift = lax.rem(to + 2 * LANES - low - skipped, LANES)
            turned = pltpu.roll(totals[b], shift, 1)
            if low + pitch - 1 <= LANES:
                return turned
            return jnp.where(lane < to + LANES - low - skipped, turned, pltpu.roll(totals[b + 1], shift, 1))

        def rows_of(row):
            return jnp.where(lane < half, columns_of(row, 0), columns_of(row + 1, half))

        outermost, inner = rows_of(0), rows_of(2)
        outs[0][t] = jnp.where(outer, outermost, inner).astype(jnp.bfloat16)
        outs[1][t] = jnp.where(outer, inner, outermost).astype(jnp.bfloat16)

    def tile_sums(places):
        cuts = {t: begun_rows(t, channels) if plan["begun"] else 0 for t, _ in places}
        start, stop = min(cuts.values()), w_ref.shape[1]
        rhs = []
        for t, b in places:
            frames = [(earlier_ref, t + a) if t + a < PAIR else (shifted_ref, t + a - PAIR) for a in (2, 1, 0)]
            rhs.append(padded_rows([block_lines(ref, j, b) for ref, j in frames], cuts[t], stop, start, stop))
        return jnp.dot(w_ref[:, start:], jnp.concatenate(rhs, axis=1), preferred_element_type=jnp.float32)

    by_frames(lanes, tile_sums, finish)
    if sends and rest_sent:
        outs[2][:, PAIR * (chunks - 1) * LANES :] = sum(tails).astype(jnp.bfloat16)


def conv(plan, begun, earlier, shifted, values, weight, columns):
    _, _, channels, lanes = shifted.shape
    pitch, half, received = plan["pitch"], plan["half"], plan["received"]
    if plan["last"]:
        out_shape = (jax.ShapeDtypeStruct((PAIR, channels, LANES), jnp.bfloat16),) * 2
    else:
        out_shape = (
            jax.ShapeDtypeStruct((PAIR, channels, lanes), jnp.bfloat16),
            jax.ShapeDtypeStruct((PAIR, 3, channels, rounded((plan["rows"] - 1) * pitch)), jnp.bfloat16),
        )
        if plan["sends"] and plan["rest_sent"]:
            out_shape += (jax.ShapeDtypeStruct((channels, PAIR * (lanes - LANES) + LANES), jnp.bfloat16),)
        elif plan["sends"]:
            out_shape += out_shape[:1]
    scratch = [pltpu.VMEM((PAIR, 3, channels, lanes), jnp.bfloat16)] * received
    if plan["builds"]:
        out_shape += far_shapes(plan["rows_near"] // 2, pitch - 1 - half, channels, half)
    return pl.pallas_call(
        functools.partial(conv_kernel, plan),
        out_shape=out_shape,
        in_specs=[VMEM] * (4 + len(begun) + len(earlier)),
        out_specs=(VMEM,) * len(out_shape),
        scratch_shapes=scratch,
        compiler_params=pltpu.CompilerParams(vmem_limit_bytes=LIMIT),
        cost_estimate=pl.CostEstimate(
            flops=54 * channels * channels * PAIR * lanes * (1 + plan["builds"]),
            bytes_accessed=2 * weight.size,
            transcendentals=PAIR * channels * lanes,
        ),
        name=f"conv_{plan['layer']}",
    )(shifted, values, weight, columns, *begun, *earlier)


def join_kernel(pair, kept_ref, got_ref, *refs):
    out_ref, lines_ref, sems = refs[-3:]
    _, rows, _, width = lines_ref.shape
    half = width // 2
    core, group, _ = place()
    first = core == 0
    left_half = lane_of(width) < half
    copies = []
    for t in range(PAIR):
        mine, theirs = kept_ref[t].astype(jnp.float32), got_ref[t].astype(jnp.float32)
        left, right = jnp.where(first, mine, theirs), jnp.where(first, theirs, mine)
        lines = (
            jnp.where(left_half, left, pltpu.roll(right, half, 1)),
            jnp.where(left_half, pltpu.roll(left, half, 1), right),
        )
        for j in range(rows):
            lines_ref[t, j + group * (rows - 1 - 2 * j)] = lines[j].astype(jnp.bfloat16)
        copies.append(pltpu.make_async_copy(lines_ref.at[t], out_ref.at[PAIR * pair + t], sems.at[t]))
        copies[-1].start()
    for copy in copies:
        copy.wait()


def join(pair, kept, got, shape, *so_far):
    return pl.pallas_call(
        functools.partial(join_kernel, pair),
        out_shape=jax.ShapeDtypeStruct(shape, jnp.bfloat16),
        in_specs=[VMEM, VMEM] + [ANY] * len(so_far),
        out_specs=ANY,
        scratch_shapes=[pltpu.VMEM((PAIR,) + shape[1:], jnp.bfloat16), pltpu.SemaphoreType.DMA((PAIR,))],
        input_output_aliases={2: 0} if so_far else {},
        compiler_params=pltpu.CompilerParams(vmem_limit_bytes=LIMIT),
        name="join",
    )(kept, got, *so_far)


def on_device(latents, conv_weight, norm_gains, biases):
    layers = conv_weight.shape[0]
    frames, rows, channels, width = latents.shape
    strips, blocks = lax.axis_size("rows"), lax.axis_size("tm")
    assert strips == 4 and rows == 2 and frames % PAIR == 0 and width == LANES

    def mate_of(block):
        return lax.ppermute(block, "rows", [(i, i ^ 1) for i in range(strips)])

    def earlier_of(block):
        return lax.ppermute(block, "tm", [(i, i + 1) for i in range(blocks - 1)])

    def beyond_of(block):
        return lax.ppermute(block, "rows", [(i, i ^ 2) for i in range(strips)])

    mate = mate_of(latents)
    pairs = frames // PAIR
    own = split(latents)
    far = beyond_of(own[-1])
    row_values = jnp.concatenate([norm_gains, biases], axis=0)
    weight, columns = weights(conv_weight, row_values)
    near_values, near_act, near_sent = near(layers, mate, row_values, own)
    came = [beyond_of(block) for block in near_sent]
    far, weight, columns, near_values, near_act = lax.optimization_barrier(
        (far, weight, columns, near_values, near_act)
    )
    values, shifted = [None] * pairs, [None] * pairs
    values[-1], shifted[-1], send = beyond(layers, columns, far, mate_of(far), near_values[-1], near_act[-1])
    halo, rest = earlier_of(send), 0
    next_begun = layer_begun = None
    first_begun = begin(shifted[-1], weight[0])
    *came, first_begun = lax.optimization_barrier((*came, first_begun))
    parts = [(came[p], near_values[p], near_act[p]) for p in range(pairs - 1)]
    half = width // 2
    pitch = half + layers + 1
    for layer in range(layers):
        last = layer == layers - 1
        rows_left = 2 * rows + layers - 1 - layer
        results = [None] * pairs
        for p in reversed(range(pairs)):
            builds = layer == 0 and p > 0
            earlier = (halo,) if p == 0 else parts[p - 1] if builds else (shifted[p - 1],)
            waits = builds or (p == 0 and (last or layer == 0)) or (layer == 1 and layer_begun is not None and p == pairs - 1)
            if builds and p == pairs - 1:
                begun = (first_begun,)
            elif layer == 0 and p == 0 and next_begun is not None:
                begun = (next_begun,)
            elif layer == 1 and p == pairs - 1 and layer_begun is not None:
                begun = (layer_begun,)
            else:
                begun = (begin(shifted[p], weight[layer]),) if waits else ()
            plan = {
                "layer": layer,
                "begun": waits,
                "rows_near": 2 * rows,
                "last": last,
                "sends": p == pairs - 1 and not last,
                "rest_sent": joined(rows_left * pitch),
                "received": p == 0,
                "rest": 0 if p else rest,
                "builds": builds,
                "inputs": len(earlier),
                "pitch": pitch,
                "half": half,
                "rows": rows_left,
            }
            outs = list(conv(plan, begun, earlier, shifted[p], values[p], weight[layer], columns))
            if builds:
                shifted[p - 1], values[p - 1] = outs.pop(), outs.pop()
            results[p] = outs
            if plan["sends"]:
                message = outs[2]
                if layer == 0 and p == 1:
                    next_begun = begin(shifted[0], weight[0])
                    message, next_begun = lax.optimization_barrier((message, next_begun))
                arriving = earlier_of(message)
                if layer == 0 and p == 1 and not last:
                    layer_begun = begin(outs[1], weight[1])
                    halo, layer_begun = lax.optimization_barrier((halo, layer_begun))
        values, shifted = [r[0] for r in results], [r[1] for r in results]
        if not last:
            halo, rest = arriving, joined(rows_left * pitch)
    result = ()
    for p in reversed(range(pairs)):
        result = (join(p, values[p], mate_of(shifted[p]), latents.shape, *result),)
    return result[0]


def solution(mesh):
    in_specs = (P(("clips", "tm"), "rows", None, None), P(), P(), P())
    out_specs = P(("clips", "tm"), "rows", None, None)
    return jax.shard_map(on_device, mesh=mesh, in_specs=in_specs, out_specs=out_specs, check_vma=False)
```

```python
import functools

import jax
import jax.numpy as jnp
from jax import lax
from jax.experimental import pallas as pl
from jax.experimental.pallas import tpu as pltpu
from jax.sharding import PartitionSpec as P

EPSILON = 1e-06
PAIR = 2
LANES = 128
TILE = 256
VMEM = pl.BlockSpec(memory_space=pltpu.VMEM)
ANY = pl.BlockSpec(memory_space=pl.ANY)
LIMIT = 24 * 1024 * 1024
LARGE = 44 * 1024 * 1024


def place():
    strip = lax.axis_index("rows").astype(jnp.int32)
    core, group = strip & 1, strip >> 1
    return core, group, core == group


def rounded(lanes):
    return -(-lanes // LANES) * LANES


def column(row):
    return jnp.transpose(jnp.broadcast_to(row, (LANES, row.shape[1])))


def lane_of(lanes):
    return lax.broadcasted_iota(jnp.int32, (1, lanes), 1)


def filled(lanes, pitch):
    lane = lane_of(lanes)
    gaps = lane < 0
    for end in range(pitch - 1, lanes, pitch):
        gaps = gaps | (lane == end)
    return jnp.where(gaps, 0.0, 1.0)


def activated(values, gain, mask):
    squares = jnp.mean(values * values, axis=0, keepdims=True)
    halved = values * (lax.rsqrt(squares + EPSILON) * (0.5 * mask)) * gain
    return (halved + halved * jnp.tanh(halved)).astype(jnp.bfloat16)


def weights_kernel(w_ref, rows_ref, *refs):
    outs, columns_ref, held_ref, sems = refs[:-3], refs[-3], refs[-2], refs[-1]
    layers, taps, channels_out, ins = w_ref.shape
    step = taps // 3
    places = [(layer, time_tap) for layer in range(layers) for time_tap in range(3)]
    copies = []
    for n, (layer, time_tap) in enumerate(places):
        part = pl.ds(step * time_tap, step)
        copies.append(pltpu.make_async_copy(w_ref.at[layer, part], held_ref.at[n], sems.at[n]))
        copies[-1].start()
    _, flipped, _ = place()
    for layer in range(layers):
        columns_ref[layer, 0] = column(rows_ref[layer : layer + 1, :])
        columns_ref[layer, 1] = column(rows_ref[layers + layer : layers + layer + 1, :])
    for n, (layer, time_tap) in enumerate(places):
        copies[n].wait()
        for row_tap in range(3):
            source = 3 * (row_tap + flipped * (2 - 2 * row_tap))
            at = (3 * (2 - time_tap) + row_tap) * ins
            outs[layer][:, at : at + ins] = held_ref[n, pl.ds(source, 3)].reshape(3 * channels_out, ins)


def weights(conv_weight, rows):
    layers, taps, outs, ins = conv_weight.shape
    one = jax.ShapeDtypeStruct((3 * outs, 9 * ins), conv_weight.dtype)
    results = pl.pallas_call(
        weights_kernel,
        out_shape=(one,) * layers + (jax.ShapeDtypeStruct((layers, 2, outs, LANES), jnp.float32),),
        in_specs=[ANY, VMEM],
        out_specs=(VMEM,) * (layers + 1),
        scratch_shapes=[
            pltpu.VMEM((3 * layers, taps // 3, outs, ins), conv_weight.dtype),
            pltpu.SemaphoreType.DMA((3 * layers,)),
        ],
        compiler_params=pltpu.CompilerParams(vmem_limit_bytes=LARGE),
        cost_estimate=pl.CostEstimate(flops=0, bytes_accessed=4 * conv_weight.size, transcendentals=0),
        name="weights",
    )(conv_weight, rows)
    return results[:-1], results[-1]


def split_kernel(in_ref, *out_refs):
    for p, out_ref in enumerate(out_refs):
        out_ref[...] = in_ref[PAIR * p : PAIR * (p + 1)]


def split(latents):
    pairs = latents.shape[0] // PAIR
    return pl.pallas_call(
        split_kernel,
        out_shape=(jax.ShapeDtypeStruct((PAIR,) + latents.shape[1:], latents.dtype),) * pairs,
        in_specs=[VMEM],
        out_specs=(VMEM,) * pairs,
        compiler_params=pltpu.CompilerParams(vmem_limit_bytes=LIMIT),
        name="split",
    )(latents)


def joined(valid):
    rest = valid % LANES
    return rest if 0 < PAIR * rest <= LANES else 0


def spread(out_ref, index, act, pitch):
    lanes = out_ref.shape[3]
    above = pltpu.roll(act, pitch, 1)
    below = pltpu.roll(act, act.shape[1] - pitch, 1)
    edge = jnp.where(lane_of(LANES) < pitch, 0.0, above[:, :LANES].astype(jnp.float32))
    out_ref[index, 0, :, :LANES] = edge.astype(jnp.bfloat16)
    out_ref[index, 0, :, LANES:] = above[:, LANES:lanes]
    out_ref[index, 1] = act[:, :lanes]
    out_ref[index, 2] = below[:, :lanes]


def placed(blocks, core, row, window, line):
    pitch, width = window + 1, line.shape[1]
    lane = lane_of(LANES)
    block, low = divmod(row * pitch, LANES)
    shift = lax.rem(low + LANES - core * (width - window), LANES)
    turned = moved(line, shift)
    here = (lane >= low) & (lane < low + window)
    blocks[block] = blocks.get(block, 0.0) + jnp.where(here, turned, 0.0)
    if low + window > LANES:
        blocks[block + 1] = blocks.get(block + 1, 0.0) + jnp.where(lane < low + window - LANES, turned, 0.0)


def near_kernel(halo, pairs, mate_ref, gains_ref, *refs):
    own_refs, value_refs, act_refs = refs[:pairs], refs[pairs : 2 * pairs], refs[2 * pairs : 3 * pairs]
    send_refs = refs[3 * pairs :]
    frames, rows, _, width = mate_ref.shape
    window = width // 2 + halo
    core, group, outer = place()
    gain = column(gains_ref[0:1, :])
    done = act_refs[0].shape[2]
    mask = filled(done, window + 1)
    for f in range(frames):
        p, t = divmod(f, PAIR)
        blocks, sent = {}, {}
        for row in range(2 * rows):
            at = row % rows
            index = at + group * (rows - 1 - 2 * at)
            own, mate = own_refs[p][t, index], mate_ref[f, index]
            one, two = (own, mate) if row < rows else (mate, own)
            line = jnp.where(outer, one, two)
            placed(blocks, core, row, window, line)
            there = 4 * rows - 1 - row
            if p < pairs - 1 and there < 2 * rows + halo:
                placed(sent, core, there, window, line)
        for b in sent:
            send_refs[p][t, :, b * LANES - done : (b + 1) * LANES - done] = sent[b].astype(jnp.bfloat16)
        for b in blocks:
            part = slice(b * LANES, (b + 1) * LANES)
            value_refs[p][t, :, part] = blocks[b].astype(jnp.bfloat16)
            if part.stop <= done:
                act_refs[p][t, :, part] = activated(blocks[b], gain, mask[:, part])


def near(halo, mate, gains, own):
    frames, rows, channels, width = mate.shape
    pitch = width // 2 + halo + 1
    lanes = 2 * rows * pitch
    done = lanes // LANES * LANES
    pairs = len(own)
    sent = jax.ShapeDtypeStruct((PAIR, channels, rounded(lanes + halo * pitch) - done), jnp.bfloat16)
    outs = pl.pallas_call(
        functools.partial(near_kernel, halo, pairs),
        out_shape=(jax.ShapeDtypeStruct((PAIR, channels, rounded(lanes)), jnp.bfloat16),) * pairs
        + (jax.ShapeDtypeStruct((PAIR, channels, done), jnp.bfloat16),) * pairs
        + (sent,) * (pairs - 1),
        in_specs=[VMEM] * (2 + pairs),
        out_specs=(VMEM,) * (3 * pairs - 1),
        compiler_params=pltpu.CompilerParams(vmem_limit_bytes=LIMIT),
        cost_estimate=pl.CostEstimate(flops=40 * mate.size, bytes_accessed=8 * mate.size, transcendentals=2 * mate.size),
        name="near",
    )(mate, gains, *own)
    return outs[:pairs], outs[pairs : 2 * pairs], outs[2 * pairs :]


def far_blocks(halo, far_ref, mate_ref, t, blocks):
    _, rows, _, width = far_ref.shape
    core, group, outer = place()
    for row in range(2 * rows, 2 * rows + halo):
        local = 4 * rows - 1 - row
        at = local % rows
        index = at + (1 - group) * (rows - 1 - 2 * at)
        one, two = (mate_ref, far_ref) if local < rows else (far_ref, mate_ref)
        line = jnp.where(outer, one[t, index], two[t, index])
        placed(blocks, core, row, width // 2 + halo, line)


def add_far(pitch, add, near_ref, act_ref, columns_ref, values_ref, shifted_ref, send_ref=None):
    lanes, done = values_ref.shape[2], act_ref.shape[2]
    mask = filled(lanes, pitch)
    for t in range(PAIR):
        values_ref[t, :, :done] = near_ref[t, :, :done]
        acts = [act_ref[t]]
        blocks = {done // LANES: near_ref[t, :, done:].astype(jnp.float32)}
        add(t, blocks)
        for b in sorted(blocks):
            part = slice(b * LANES, (b + 1) * LANES)
            values_ref[t, :, part] = blocks[b].astype(jnp.bfloat16)
            acts.append(activated(blocks[b], columns_ref[0, 0], mask[:, part]))
        act = jnp.concatenate(acts, axis=1)
        spread(shifted_ref, t, act, pitch)
        if send_ref is not None:
            send_ref[t] = act


def far_shapes(rows, halo, channels, half):
    pitch = half + halo + 1
    return (
        jax.ShapeDtypeStruct((PAIR, channels, rounded((2 * rows + halo) * pitch)), jnp.bfloat16),
        jax.ShapeDtypeStruct((PAIR, 3, channels, rounded((2 * rows + halo - 1) * pitch)), jnp.bfloat16),
    )


def beyond(halo, columns, *parts):
    far = parts[0]
    _, rows, channels, width = far.shape
    values, shifted = far_shapes(rows, halo, channels, width // 2)

    def kernel(columns_ref, far_ref, mate_ref, near_ref, act_ref, *outs):
        add = functools.partial(far_blocks, halo, far_ref, mate_ref)
        add_far(width // 2 + halo + 1, add, near_ref, act_ref, columns_ref, *outs)

    return pl.pallas_call(
        kernel,
        out_shape=(values, shifted, values),
        in_specs=[VMEM] * 5,
        out_specs=(VMEM,) * 3,
        compiler_params=pltpu.CompilerParams(vmem_limit_bytes=LIMIT),
        cost_estimate=pl.CostEstimate(flops=40 * far.size, bytes_accessed=8 * far.size, transcendentals=2 * far.size),
        name="beyond",
    )(columns, *parts)


def by_taps(sums):
    channels, lanes = sums.shape[0] // 3, sums.shape[1]
    return [
        [sums[tap * channels : (tap + 1) * channels, at : at + LANES] for at in range(0, lanes, LANES)]
        for tap in range(3)
    ]


def moved(block, shift):
    return pltpu.roll(block, shift, 1).astype(jnp.float32)


def column_sums(taps):
    lane = lane_of(LANES)
    left, middle, right = taps
    lefts = [pltpu.roll(block, 1, 1) for block in left]
    rights = [pltpu.roll(block, LANES - 1, 1) for block in right] + [0.0]
    return [
        jnp.where(lane == 0, lefts[b - 1] if b else 0.0, lefts[b])
        + middle[b]
        + jnp.where(lane == LANES - 1, rights[b + 1], rights[b])
        for b in range(len(middle))
    ]


def begun_rows(t, channels):
    return (t + 1) * 3 * channels // TILE * TILE


def rows_between(lines, start, stop):
    taken, at = [], 0
    for part in lines:
        low, high = max(start - at, 0), min(stop - at, part.shape[0])
        if low < high:
            taken.append(part[low:high])
        at += part.shape[0]
    return jnp.concatenate(taken, axis=0)


def block_lines(ref, frame, b):
    return ref[frame, :, :, b * LANES : (b + 1) * LANES].reshape(3 * ref.shape[2], LANES)


def padded_rows(lines, start, stop, low, high):
    parts = [rows_between(lines, start, stop)]
    if low < start:
        parts.insert(0, jnp.zeros((start - low, LANES), jnp.bfloat16))
    if stop < high:
        parts.append(jnp.zeros((high - stop, LANES), jnp.bfloat16))
    return parts[0] if len(parts) == 1 else jnp.concatenate(parts, axis=0)


def tiled(lanes):
    places = [(t, b) for t in range(PAIR) for b in range(lanes // LANES)]
    side = TILE // LANES
    return [places[n : n + side] for n in range(0, len(places), side)]


def by_frames(lanes, tile_sums, finish):
    taps = {t: [[], [], []] for t in range(PAIR)}
    for places in tiled(lanes):
        sums = by_taps(tile_sums(places))
        for i, (t, b) in enumerate(places):
            for tap in range(3):
                taps[t][tap].append(sums[tap][i])
        for t, b in places:
            if b == lanes // LANES - 1:
                finish(t, taps[t])


def begin_kernel(shifted_ref, w_ref, out_ref):
    _, _, channels, lanes = shifted_ref.shape

    def tile_sums(places):
        depth = max(begun_rows(t, channels) for t, _ in places)
        rhs = [
            padded_rows(
                [block_lines(shifted_ref, j, b) for j in range(t, -1, -1)],
                0,
                begun_rows(t, channels),
                0,
                depth,
            )
            for t, b in places
        ]
        return jnp.dot(w_ref[:, :depth], jnp.concatenate(rhs, axis=1), preferred_element_type=jnp.float32)

    def finish(t, taps):
        for b, block in enumerate(column_sums(taps)):
            out_ref[t, :, b * LANES : (b + 1) * LANES] = block

    by_frames(lanes, tile_sums, finish)


def begin(shifted, weight):
    _, _, channels, lanes = shifted.shape
    return pl.pallas_call(
        begin_kernel,
        out_shape=jax.ShapeDtypeStruct((PAIR, channels, lanes), jnp.float32),
        in_specs=[VMEM] * 2,
        out_specs=VMEM,
        compiler_params=pltpu.CompilerParams(vmem_limit_bytes=LIMIT),
        cost_estimate=pl.CostEstimate(flops=0, bytes_accessed=0, transcendentals=0),
        name="begin",
    )(shifted, weight)


def conv_kernel(plan, shifted_ref, values_ref, w_ref, columns_ref, *refs):
    layer, pitch, half, received = plan["layer"], plan["pitch"], plan["half"], plan["received"]
    last, sends, rest, rest_sent = plan["last"], plan["sends"], plan["rest"], plan["rest_sent"]
    refs = list(refs)
    begun_ref = refs.pop(0) if plan["begun"] else None
    earlier_refs = [refs.pop(0) for _ in range(plan["inputs"])]
    earlier_ref = refs.pop() if received else earlier_refs[0]
    if received:
        for t in range(PAIR):
            if rest:
                whole = (earlier_refs[0].shape[1] - LANES) // PAIR
                tail = earlier_refs[0][:, PAIR * whole :].astype(jnp.float32)
                tail = tail if t == 0 else pltpu.roll(tail, LANES - t * (LANES // PAIR), 1)
                tail = jnp.where(lane_of(LANES) < rest, tail, 0.0).astype(jnp.bfloat16)
                act = jnp.concatenate([earlier_refs[0][:, t * whole : (t + 1) * whole], tail], axis=1)
            else:
                act = earlier_refs[0][t]
            spread(earlier_ref, t, act, pitch)
    outs = refs
    if plan["builds"]:
        earlier_ref = outs.pop()
        came_ref, near_ref, act_ref = earlier_refs
        done = act_ref.shape[2]

        def add(t, blocks):
            for at in range(0, came_ref.shape[2], LANES):
                b = (done + at) // LANES
                blocks[b] = blocks.get(b, 0.0) + came_ref[t, :, at : at + LANES].astype(jnp.float32)

        add_far(pitch, add, near_ref, act_ref, columns_ref, outs.pop(), earlier_ref)
    _, _, channels, lanes = shifted_ref.shape
    chunks = lanes // LANES
    lane = lane_of(LANES)

    bias = columns_ref[layer, 1]
    tails = []
    if not last:
        mask = filled(lanes, pitch)
        gain = columns_ref[layer + 1, 0]

    def finish(t, taps):
        totals, acts = [], []
        for b, conv in enumerate(column_sums(taps)):
            at = slice(b * LANES, (b + 1) * LANES)
            if begun_ref is not None:
                conv = conv + begun_ref[t, :, at]
            total = (values_ref[t, :, at].astype(jnp.float32) + conv + bias).astype(jnp.bfloat16)
            totals.append(total)
            if last:
                continue
            outs[0][t, :, at] = total
            acts.append(activated(total.astype(jnp.float32), gain, mask[:, at]))
            if not sends:
                continue
            if not rest_sent:
                outs[2][t, :, at] = acts[-1]
            elif b < chunks - 1:
                outs[2][:, (t * (chunks - 1) + b) * LANES : (t * (chunks - 1) + b + 1) * LANES] = acts[-1]
            else:
                tail = jnp.where(lane < rest_sent, acts[-1].astype(jnp.float32), 0.0)
                tails.append(tail if t == 0 else pltpu.roll(tail, t * (LANES // PAIR), 1))
        if not last:
            spread(outs[1], t, jnp.concatenate(acts, axis=1), pitch)
            return
        core, _, outer = place()
        skipped = core * (pitch - 1 - half)

        def columns_of(row, to):
            b, low = divmod(row * pitch, LANES)
            shift = lax.rem(to + 2 * LANES - low - skipped, LANES)
            turned = moved(totals[b], shift)
            if low + pitch - 1 <= LANES:
                return turned
            return jnp.where(lane < to + LANES - low - skipped, turned, moved(totals[b + 1], shift))

        def rows_of(row):
            return jnp.where(lane < half, columns_of(row, 0), columns_of(row + 1, half))

        outermost, inner = rows_of(0), rows_of(2)
        outs[0][t] = jnp.where(outer, outermost, inner).astype(jnp.bfloat16)
        outs[1][t] = jnp.where(outer, inner, outermost).astype(jnp.bfloat16)

    def tile_sums(places):
        cuts = {t: begun_rows(t, channels) if plan["begun"] else 0 for t, _ in places}
        start, stop = min(cuts.values()), w_ref.shape[1]
        rhs = []
        for t, b in places:
            frames = [(earlier_ref, t + a) if t + a < PAIR else (shifted_ref, t + a - PAIR) for a in (2, 1, 0)]
            rhs.append(padded_rows([block_lines(ref, j, b) for ref, j in frames], cuts[t], stop, start, stop))
        return jnp.dot(w_ref[:, start:], jnp.concatenate(rhs, axis=1), preferred_element_type=jnp.float32)

    by_frames(lanes, tile_sums, finish)
    if sends and rest_sent:
        outs[2][:, PAIR * (chunks - 1) * LANES :] = sum(tails).astype(jnp.bfloat16)


def conv(plan, begun, earlier, shifted, values, weight, columns):
    _, _, channels, lanes = shifted.shape
    pitch, half, received = plan["pitch"], plan["half"], plan["received"]
    if plan["last"]:
        out_shape = (jax.ShapeDtypeStruct((PAIR, channels, LANES), jnp.bfloat16),) * 2
    else:
        out_shape = (
            jax.ShapeDtypeStruct((PAIR, channels, lanes), jnp.bfloat16),
            jax.ShapeDtypeStruct((PAIR, 3, channels, rounded((plan["rows"] - 1) * pitch)), jnp.bfloat16),
        )
        if plan["sends"] and plan["rest_sent"]:
            out_shape += (jax.ShapeDtypeStruct((channels, PAIR * (lanes - LANES) + LANES), jnp.bfloat16),)
        elif plan["sends"]:
            out_shape += out_shape[:1]
    scratch = [pltpu.VMEM((PAIR, 3, channels, lanes), jnp.bfloat16)] * received
    if plan["builds"]:
        out_shape += far_shapes(plan["rows_near"] // 2, pitch - 1 - half, channels, half)
    return pl.pallas_call(
        functools.partial(conv_kernel, plan),
        out_shape=out_shape,
        in_specs=[VMEM] * (4 + len(begun) + len(earlier)),
        out_specs=(VMEM,) * len(out_shape),
        scratch_shapes=scratch,
        compiler_params=pltpu.CompilerParams(vmem_limit_bytes=LIMIT),
        cost_estimate=pl.CostEstimate(
            flops=54 * channels * channels * PAIR * lanes * (1 + plan["builds"]),
            bytes_accessed=2 * weight.size,
            transcendentals=PAIR * channels * lanes,
        ),
        name=f"conv_{plan['layer']}",
    )(shifted, values, weight, columns, *begun, *earlier)


def join_kernel(pair, kept_ref, got_ref, *refs):
    out_ref, lines_ref, sems = refs[-3:]
    _, rows, _, width = lines_ref.shape
    half = width // 2
    core, group, _ = place()
    first = core == 0
    left_half = lane_of(width) < half
    copies = []
    for t in range(PAIR):
        mine, theirs = kept_ref[t].astype(jnp.float32), got_ref[t].astype(jnp.float32)
        left, right = jnp.where(first, mine, theirs), jnp.where(first, theirs, mine)
        lines = (
            jnp.where(left_half, left, pltpu.roll(right, half, 1)),
            jnp.where(left_half, pltpu.roll(left, half, 1), right),
        )
        for j in range(rows):
            lines_ref[t, j + group * (rows - 1 - 2 * j)] = lines[j].astype(jnp.bfloat16)
        copies.append(pltpu.make_async_copy(lines_ref.at[t], out_ref.at[PAIR * pair + t], sems.at[t]))
        copies[-1].start()
    for copy in copies:
        copy.wait()


def join(pair, kept, got, shape, *so_far):
    return pl.pallas_call(
        functools.partial(join_kernel, pair),
        out_shape=jax.ShapeDtypeStruct(shape, jnp.bfloat16),
        in_specs=[VMEM, VMEM] + [ANY] * len(so_far),
        out_specs=ANY,
        scratch_shapes=[pltpu.VMEM((PAIR,) + shape[1:], jnp.bfloat16), pltpu.SemaphoreType.DMA((PAIR,))],
        input_output_aliases={2: 0} if so_far else {},
        compiler_params=pltpu.CompilerParams(vmem_limit_bytes=LIMIT),
        name="join",
    )(kept, got, *so_far)


def on_device(latents, conv_weight, norm_gains, biases):
    layers = conv_weight.shape[0]
    frames, rows, channels, width = latents.shape
    strips, blocks = lax.axis_size("rows"), lax.axis_size("tm")
    assert strips == 4 and rows == 2 and frames % PAIR == 0 and width == LANES

    def mate_of(block):
        return lax.ppermute(block, "rows", [(i, i ^ 1) for i in range(strips)])

    def earlier_of(block):
        return lax.ppermute(block, "tm", [(i, i + 1) for i in range(blocks - 1)])

    def beyond_of(block):
        return lax.ppermute(block, "rows", [(i, i ^ 2) for i in range(strips)])

    mate = mate_of(latents)
    pairs = frames // PAIR
    own = split(latents)
    far = beyond_of(own[-1])
    row_values = jnp.concatenate([norm_gains, biases], axis=0)
    weight, columns = weights(conv_weight, row_values)
    near_values, near_act, near_sent = near(layers, mate, row_values, own)
    came = [beyond_of(block) for block in near_sent]
    far, weight, columns, near_values, near_act = lax.optimization_barrier(
        (far, weight, columns, near_values, near_act)
    )
    values, shifted = [None] * pairs, [None] * pairs
    values[-1], shifted[-1], send = beyond(layers, columns, far, mate_of(far), near_values[-1], near_act[-1])
    halo, rest = earlier_of(send), 0
    next_begun = layer_begun = None
    first_begun = begin(shifted[-1], weight[0])
    *came, first_begun = lax.optimization_barrier((*came, first_begun))
    parts = [(came[p], near_values[p], near_act[p]) for p in range(pairs - 1)]
    half = width // 2
    pitch = half + layers + 1
    for layer in range(layers):
        last = layer == layers - 1
        rows_left = 2 * rows + layers - 1 - layer
        results = [None] * pairs
        for p in reversed(range(pairs)):
            builds = layer == 0 and p > 0
            earlier = (halo,) if p == 0 else parts[p - 1] if builds else (shifted[p - 1],)
            waits = builds or (p == 0 and (last or layer == 0)) or (layer == 1 and layer_begun is not None and p == pairs - 1)
            if builds and p == pairs - 1:
                begun = (first_begun,)
            elif layer == 0 and p == 0 and next_begun is not None:
                begun = (next_begun,)
            elif layer == 1 and p == pairs - 1 and layer_begun is not None:
                begun = (layer_begun,)
            else:
                begun = (begin(shifted[p], weight[layer]),) if waits else ()
            plan = {
                "layer": layer,
                "begun": waits,
                "rows_near": 2 * rows,
                "last": last,
                "sends": p == pairs - 1 and not last,
                "rest_sent": joined(rows_left * pitch),
                "received": p == 0,
                "rest": 0 if p else rest,
                "builds": builds,
                "inputs": len(earlier),
                "pitch": pitch,
                "half": half,
                "rows": rows_left,
            }
            outs = list(conv(plan, begun, earlier, shifted[p], values[p], weight[layer], columns))
            if builds:
                shifted[p - 1], values[p - 1] = outs.pop(), outs.pop()
            results[p] = outs
            if plan["sends"]:
                message = outs[2]
                if layer == 0 and p == 1:
                    next_begun = begin(shifted[0], weight[0])
                    message, next_begun = lax.optimization_barrier((message, next_begun))
                arriving = earlier_of(message)
                if layer == 0 and p == 1 and not last:
                    layer_begun = begin(outs[1], weight[1])
                    halo, layer_begun = lax.optimization_barrier((halo, layer_begun))
        values, shifted = [r[0] for r in results], [r[1] for r in results]
        if not last:
            halo, rest = arriving, joined(rows_left * pitch)
    result = ()
    for p in reversed(range(pairs)):
        result = (join(p, values[p], mate_of(shifted[p]), latents.shape, *result),)
    return result[0]


def solution(mesh):
    in_specs = (P(("clips", "tm"), "rows", None, None), P(), P(), P())
    out_specs = P(("clips", "tm"), "rows", None, None)
    return jax.shard_map(on_device, mesh=mesh, in_specs=in_specs, out_specs=out_specs, check_vma=False)
```

```python
import functools

import jax
import jax.numpy as jnp
from jax import lax
from jax.experimental import pallas as pl
from jax.experimental.pallas import tpu as pltpu
from jax.sharding import PartitionSpec as P

EPSILON = 1e-06
PAIR = 2
LANES = 128
TILE = 256
VMEM = pl.BlockSpec(memory_space=pltpu.VMEM)
ANY = pl.BlockSpec(memory_space=pl.ANY)
LIMIT = 24 * 1024 * 1024
LARGE = 44 * 1024 * 1024


def place():
    strip = lax.axis_index("rows").astype(jnp.int32)
    core, group = strip & 1, strip >> 1
    return core, group, core == group


def rounded(lanes):
    return -(-lanes // LANES) * LANES


def column(row):
    return jnp.transpose(jnp.broadcast_to(row, (LANES, row.shape[1])))


def lane_of(lanes):
    return lax.broadcasted_iota(jnp.int32, (1, lanes), 1)


def filled(lanes, pitch):
    lane = lane_of(lanes)
    gaps = lane < 0
    for end in range(pitch - 1, lanes, pitch):
        gaps = gaps | (lane == end)
    return jnp.where(gaps, 0.0, 1.0)


def activated(values, gain, mask):
    squares = jnp.mean(values * values, axis=0, keepdims=True)
    halved = values * (lax.rsqrt(squares + EPSILON) * (0.5 * mask)) * gain
    return (halved + halved * jnp.tanh(halved)).astype(jnp.bfloat16)


def weights_kernel(w_ref, rows_ref, *refs):
    outs, columns_ref, held_ref, sems = refs[:-3], refs[-3], refs[-2], refs[-1]
    layers, taps, channels_out, ins = w_ref.shape
    step = taps // 3
    places = [(layer, time_tap) for layer in range(layers) for time_tap in range(3)]
    copies = []
    for n, (layer, time_tap) in enumerate(places):
        part = pl.ds(step * time_tap, step)
        copies.append(pltpu.make_async_copy(w_ref.at[layer, part], held_ref.at[n], sems.at[n]))
        copies[-1].start()
    _, flipped, _ = place()
    for layer in range(layers):
        columns_ref[layer, 0] = column(rows_ref[layer : layer + 1, :])
        columns_ref[layer, 1] = column(rows_ref[layers + layer : layers + layer + 1, :])
    for n, (layer, time_tap) in enumerate(places):
        copies[n].wait()
        for row_tap in range(3):
            source = 3 * (row_tap + flipped * (2 - 2 * row_tap))
            at = (3 * (2 - time_tap) + row_tap) * ins
            outs[layer][:, at : at + ins] = held_ref[n, pl.ds(source, 3)].reshape(3 * channels_out, ins)


def weights(conv_weight, rows):
    layers, taps, outs, ins = conv_weight.shape
    one = jax.ShapeDtypeStruct((3 * outs, 9 * ins), conv_weight.dtype)
    results = pl.pallas_call(
        weights_kernel,
        out_shape=(one,) * layers + (jax.ShapeDtypeStruct((layers, 2, outs, LANES), jnp.float32),),
        in_specs=[ANY, VMEM],
        out_specs=(VMEM,) * (layers + 1),
        scratch_shapes=[
            pltpu.VMEM((3 * layers, taps // 3, outs, ins), conv_weight.dtype),
            pltpu.SemaphoreType.DMA((3 * layers,)),
        ],
        compiler_params=pltpu.CompilerParams(vmem_limit_bytes=LARGE),
        cost_estimate=pl.CostEstimate(flops=0, bytes_accessed=4 * conv_weight.size, transcendentals=0),
        name="weights",
    )(conv_weight, rows)
    return results[:-1], results[-1]


def split_kernel(in_ref, *out_refs):
    for p, out_ref in enumerate(out_refs):
        out_ref[...] = in_ref[PAIR * p : PAIR * (p + 1)]


def split(latents):
    pairs = latents.shape[0] // PAIR
    return pl.pallas_call(
        split_kernel,
        out_shape=(jax.ShapeDtypeStruct((PAIR,) + latents.shape[1:], latents.dtype),) * pairs,
        in_specs=[VMEM],
        out_specs=(VMEM,) * pairs,
        compiler_params=pltpu.CompilerParams(vmem_limit_bytes=LIMIT),
        name="split",
    )(latents)


def joined(valid):
    rest = valid % LANES
    return rest if 0 < PAIR * rest <= LANES else 0


def spread(out_ref, index, act, pitch):
    lanes = out_ref.shape[3]
    above = pltpu.roll(act, pitch, 1)
    below = pltpu.roll(act, act.shape[1] - pitch, 1)
    edge = jnp.where(lane_of(LANES) < pitch, 0.0, above[:, :LANES].astype(jnp.float32))
    out_ref[index, 0, :, :LANES] = edge.astype(jnp.bfloat16)
    out_ref[index, 0, :, LANES:] = above[:, LANES:lanes]
    out_ref[index, 1] = act[:, :lanes]
    out_ref[index, 2] = below[:, :lanes]


def placed(blocks, core, row, window, line):
    pitch, width = window + 1, line.shape[1]
    lane = lane_of(LANES)
    block, low = divmod(row * pitch, LANES)
    shift = lax.rem(low + LANES - core * (width - window), LANES)
    turned = moved(line, shift)
    here = (lane >= low) & (lane < low + window)
    blocks[block] = blocks.get(block, 0.0) + jnp.where(here, turned, 0.0)
    if low + window > LANES:
        blocks[block + 1] = blocks.get(block + 1, 0.0) + jnp.where(lane < low + window - LANES, turned, 0.0)


def near_kernel(halo, pairs, mate_ref, gains_ref, *refs):
    own_refs, value_refs, act_refs = refs[:pairs], refs[pairs : 2 * pairs], refs[2 * pairs : 3 * pairs]
    send_refs = refs[3 * pairs :]
    frames, rows, _, width = mate_ref.shape
    window = width // 2 + halo
    core, group, outer = place()
    gain = column(gains_ref[0:1, :])
    done = act_refs[0].shape[2]
    mask = filled(done, window + 1)
    for f in range(frames):
        p, t = divmod(f, PAIR)
        blocks, sent = {}, {}
        for row in range(2 * rows):
            at = row % rows
            index = at + group * (rows - 1 - 2 * at)
            own, mate = own_refs[p][t, index], mate_ref[f, index]
            one, two = (own, mate) if row < rows else (mate, own)
            line = jnp.where(outer, one, two)
            placed(blocks, core, row, window, line)
            there = 4 * rows - 1 - row
            if p < pairs - 1 and there < 2 * rows + halo:
                placed(sent, core, there, window, line)
        for b in sent:
            send_refs[p][t, :, b * LANES - done : (b + 1) * LANES - done] = sent[b].astype(jnp.bfloat16)
        for b in blocks:
            part = slice(b * LANES, (b + 1) * LANES)
            value_refs[p][t, :, part] = blocks[b].astype(jnp.bfloat16)
            if part.stop <= done:
                act_refs[p][t, :, part] = activated(blocks[b], gain, mask[:, part])


def near(halo, mate, gains, own):
    frames, rows, channels, width = mate.shape
    pitch = width // 2 + halo + 1
    lanes = 2 * rows * pitch
    done = lanes // LANES * LANES
    pairs = len(own)
    sent = jax.ShapeDtypeStruct((PAIR, channels, rounded(lanes + halo * pitch) - done), jnp.bfloat16)
    outs = pl.pallas_call(
        functools.partial(near_kernel, halo, pairs),
        out_shape=(jax.ShapeDtypeStruct((PAIR, channels, rounded(lanes)), jnp.bfloat16),) * pairs
        + (jax.ShapeDtypeStruct((PAIR, channels, done), jnp.bfloat16),) * pairs
        + (sent,) * (pairs - 1),
        in_specs=[VMEM] * (2 + pairs),
        out_specs=(VMEM,) * (3 * pairs - 1),
        compiler_params=pltpu.CompilerParams(vmem_limit_bytes=LIMIT),
        cost_estimate=pl.CostEstimate(flops=40 * mate.size, bytes_accessed=8 * mate.size, transcendentals=2 * mate.size),
        name="near",
    )(mate, gains, *own)
    return outs[:pairs], outs[pairs : 2 * pairs], outs[2 * pairs :]


def far_blocks(halo, far_ref, mate_ref, t, blocks):
    _, rows, _, width = far_ref.shape
    core, group, outer = place()
    for row in range(2 * rows, 2 * rows + halo):
        local = 4 * rows - 1 - row
        at = local % rows
        index = at + (1 - group) * (rows - 1 - 2 * at)
        one, two = (mate_ref, far_ref) if local < rows else (far_ref, mate_ref)
        line = jnp.where(outer, one[t, index], two[t, index])
        placed(blocks, core, row, width // 2 + halo, line)


def add_far(pitch, add, near_ref, act_ref, columns_ref, values_ref, shifted_ref, send_ref=None):
    lanes, done = values_ref.shape[2], act_ref.shape[2]
    mask = filled(lanes, pitch)
    for t in range(PAIR):
        values_ref[t, :, :done] = near_ref[t, :, :done]
        acts = [act_ref[t]]
        blocks = {done // LANES: near_ref[t, :, done:].astype(jnp.float32)}
        add(t, blocks)
        for b in sorted(blocks):
            part = slice(b * LANES, (b + 1) * LANES)
            values_ref[t, :, part] = blocks[b].astype(jnp.bfloat16)
            acts.append(activated(blocks[b], columns_ref[0, 0], mask[:, part]))
        act = jnp.concatenate(acts, axis=1)
        spread(shifted_ref, t, act, pitch)
        if send_ref is not None:
            send_ref[t] = act


def far_shapes(rows, halo, channels, half):
    pitch = half + halo + 1
    return (
        jax.ShapeDtypeStruct((PAIR, channels, rounded((2 * rows + halo) * pitch)), jnp.bfloat16),
        jax.ShapeDtypeStruct((PAIR, 3, channels, rounded((2 * rows + halo - 1) * pitch)), jnp.bfloat16),
    )


def beyond(halo, columns, *parts):
    far = parts[0]
    _, rows, channels, width = far.shape
    values, shifted = far_shapes(rows, halo, channels, width // 2)

    def kernel(columns_ref, far_ref, mate_ref, near_ref, act_ref, *outs):
        add = functools.partial(far_blocks, halo, far_ref, mate_ref)
        add_far(width // 2 + halo + 1, add, near_ref, act_ref, columns_ref, *outs)

    return pl.pallas_call(
        kernel,
        out_shape=(values, shifted, values),
        in_specs=[VMEM] * 5,
        out_specs=(VMEM,) * 3,
        compiler_params=pltpu.CompilerParams(vmem_limit_bytes=LIMIT),
        cost_estimate=pl.CostEstimate(flops=40 * far.size, bytes_accessed=8 * far.size, transcendentals=2 * far.size),
        name="beyond",
    )(columns, *parts)


def by_taps(sums):
    channels, lanes = sums.shape[0] // 3, sums.shape[1]
    return [
        [sums[tap * channels : (tap + 1) * channels, at : at + LANES] for at in range(0, lanes, LANES)]
        for tap in range(3)
    ]


def moved(block, shift):
    return pltpu.roll(block, shift, 1).astype(jnp.float32)


def column_sums(taps):
    lane = lane_of(LANES)
    left, middle, right = taps
    lefts = [pltpu.roll(block, 1, 1) for block in left]
    rights = [pltpu.roll(block, LANES - 1, 1) for block in right] + [0.0]
    return [
        jnp.where(lane == 0, lefts[b - 1] if b else 0.0, lefts[b])
        + middle[b]
        + jnp.where(lane == LANES - 1, rights[b + 1], rights[b])
        for b in range(len(middle))
    ]


def begun_rows(t, channels):
    return (t + 1) * 3 * channels // TILE * TILE


def rows_between(lines, start, stop):
    taken, at = [], 0
    for part in lines:
        low, high = max(start - at, 0), min(stop - at, part.shape[0])
        if low < high:
            taken.append(part[low:high])
        at += part.shape[0]
    return jnp.concatenate(taken, axis=0)


def block_lines(ref, frame, b):
    return ref[frame, :, :, b * LANES : (b + 1) * LANES].reshape(3 * ref.shape[2], LANES)


def padded_rows(lines, start, stop, low, high):
    parts = [rows_between(lines, start, stop)]
    if low < start:
        parts.insert(0, jnp.zeros((start - low, LANES), jnp.bfloat16))
    if stop < high:
        parts.append(jnp.zeros((high - stop, LANES), jnp.bfloat16))
    return parts[0] if len(parts) == 1 else jnp.concatenate(parts, axis=0)


def tiled(lanes):
    places = [(t, b) for t in range(PAIR) for b in range(lanes // LANES)]
    side = TILE // LANES
    return [places[n : n + side] for n in range(0, len(places), side)]


def by_frames(lanes, tile_sums, finish):
    taps = {t: [[], [], []] for t in range(PAIR)}
    for places in tiled(lanes):
        sums = by_taps(tile_sums(places))
        for i, (t, b) in enumerate(places):
            for tap in range(3):
                taps[t][tap].append(sums[tap][i])
        for t, b in places:
            if b == lanes // LANES - 1:
                finish(t, taps[t])


def begin_kernel(shifted_ref, w_ref, out_ref):
    _, _, channels, lanes = shifted_ref.shape

    def tile_sums(places):
        depth = max(begun_rows(t, channels) for t, _ in places)
        rhs = [
            padded_rows(
                [block_lines(shifted_ref, j, b) for j in range(t, -1, -1)],
                0,
                begun_rows(t, channels),
                0,
                depth,
            )
            for t, b in places
        ]
        return jnp.dot(w_ref[:, :depth], jnp.concatenate(rhs, axis=1), preferred_element_type=jnp.float32)

    def finish(t, taps):
        for b, block in enumerate(column_sums(taps)):
            out_ref[t, :, b * LANES : (b + 1) * LANES] = block

    by_frames(lanes, tile_sums, finish)


class Later:
    def __init__(self, shape):
        self.shape, self.dtype, self.value = shape.shape, shape.dtype, None


def now(x):
    return x.value if isinstance(x, Later) else x


class Chain:
    def __init__(self):
        self.steps = []

    def add(self, kernel, inputs, out_shape, scratch, flops):
        outs = [Later(shape) for shape in out_shape]
        self.steps.append((kernel, inputs, outs, out_shape, scratch, flops))
        return outs

    def run(self, name):
        steps, self.steps = self.steps, []
        made = {id(out): n for n, out in enumerate(out for step in steps for out in step[2])}
        arrays = []
        for step in steps:
            for x in step[1]:
                if id(x) not in made and not any(now(x) is y for y in arrays):
                    arrays.append(now(x))
        at = [[("out", made[id(x)]) if id(x) in made else ("in", next(i for i, y in enumerate(arrays) if y is now(x))) for x in step[1]] for step in steps]
        out_shape = [shape for step in steps for shape in step[3]]
        scratch = [shape for step in steps for shape in step[4]]

        def kernel(*refs):
            ins, outs, rest = refs[: len(arrays)], refs[len(arrays) : len(arrays) + len(out_shape)], refs[len(arrays) + len(out_shape) :]
            first, held = 0, 0
            for step, places in zip(steps, at):
                own, kept = outs[first : first + len(step[3])], rest[held : held + len(step[4])]
                first, held = first + len(own), held + len(kept)
                step[0](*[(outs if kind == "out" else ins)[n] for kind, n in places], *own, *kept)

        results = pl.pallas_call(
            kernel,
            out_shape=tuple(out_shape),
            in_specs=[VMEM] * len(arrays),
            out_specs=(VMEM,) * len(out_shape),
            scratch_shapes=scratch,
            compiler_params=pltpu.CompilerParams(vmem_limit_bytes=LIMIT),
            cost_estimate=pl.CostEstimate(flops=sum(step[5] for step in steps), bytes_accessed=0, transcendentals=0),
            name=name,
        )(*arrays)
        for out, value in zip((out for step in steps for out in step[2]), results):
            out.value = value


def begin(chain, shifted, weight):
    _, _, channels, lanes = shifted.shape
    out = jax.ShapeDtypeStruct((PAIR, channels, lanes), jnp.float32)
    return chain.add(begin_kernel, [shifted, weight], [out], [], 0)[0]


def conv_kernel(plan, shifted_ref, values_ref, w_ref, columns_ref, *refs):
    layer, pitch, half, received = plan["layer"], plan["pitch"], plan["half"], plan["received"]
    last, sends, rest, rest_sent = plan["last"], plan["sends"], plan["rest"], plan["rest_sent"]
    refs = list(refs)
    begun_ref = refs.pop(0) if plan["begun"] else None
    earlier_refs = [refs.pop(0) for _ in range(plan["inputs"])]
    earlier_ref = refs.pop() if received else earlier_refs[0]
    if received:
        for t in range(PAIR):
            if rest:
                whole = (earlier_refs[0].shape[1] - LANES) // PAIR
                tail = earlier_refs[0][:, PAIR * whole :].astype(jnp.float32)
                tail = tail if t == 0 else pltpu.roll(tail, LANES - t * (LANES // PAIR), 1)
                tail = jnp.where(lane_of(LANES) < rest, tail, 0.0).astype(jnp.bfloat16)
                act = jnp.concatenate([earlier_refs[0][:, t * whole : (t + 1) * whole], tail], axis=1)
            else:
                act = earlier_refs[0][t]
            spread(earlier_ref, t, act, pitch)
    outs = refs
    if plan["builds"]:
        earlier_ref = outs.pop()
        came_ref, near_ref, act_ref = earlier_refs
        done = act_ref.shape[2]

        def add(t, blocks):
            for at in range(0, came_ref.shape[2], LANES):
                b = (done + at) // LANES
                blocks[b] = blocks.get(b, 0.0) + came_ref[t, :, at : at + LANES].astype(jnp.float32)

        add_far(pitch, add, near_ref, act_ref, columns_ref, outs.pop(), earlier_ref)
    _, _, channels, lanes = shifted_ref.shape
    chunks = lanes // LANES
    lane = lane_of(LANES)

    bias = columns_ref[layer, 1]
    tails = []
    if not last:
        mask = filled(lanes, pitch)
        gain = columns_ref[layer + 1, 0]

    def finish(t, taps):
        totals, acts = [], []
        for b, conv in enumerate(column_sums(taps)):
            at = slice(b * LANES, (b + 1) * LANES)
            if begun_ref is not None:
                conv = conv + begun_ref[t, :, at]
            total = (values_ref[t, :, at].astype(jnp.float32) + conv + bias).astype(jnp.bfloat16)
            totals.append(total)
            if last:
                continue
            outs[0][t, :, at] = total
            acts.append(activated(total.astype(jnp.float32), gain, mask[:, at]))
            if not sends:
                continue
            if not rest_sent:
                outs[2][t, :, at] = acts[-1]
            elif b < chunks - 1:
                outs[2][:, (t * (chunks - 1) + b) * LANES : (t * (chunks - 1) + b + 1) * LANES] = acts[-1]
            else:
                tail = jnp.where(lane < rest_sent, acts[-1].astype(jnp.float32), 0.0)
                tails.append(tail if t == 0 else pltpu.roll(tail, t * (LANES // PAIR), 1))
        if not last:
            spread(outs[1], t, jnp.concatenate(acts, axis=1), pitch)
            return
        core, _, outer = place()
        skipped = core * (pitch - 1 - half)

        def columns_of(row, to):
            b, low = divmod(row * pitch, LANES)
            shift = lax.rem(to + 2 * LANES - low - skipped, LANES)
            turned = moved(totals[b], shift)
            if low + pitch - 1 <= LANES:
                return turned
            return jnp.where(lane < to + LANES - low - skipped, turned, moved(totals[b + 1], shift))

        def rows_of(row):
            return jnp.where(lane < half, columns_of(row, 0), columns_of(row + 1, half))

        outermost, inner = rows_of(0), rows_of(2)
        outs[0][t] = jnp.where(outer, outermost, inner).astype(jnp.bfloat16)
        outs[1][t] = jnp.where(outer, inner, outermost).astype(jnp.bfloat16)

    def tile_sums(places):
        cuts = {t: begun_rows(t, channels) if plan["begun"] else 0 for t, _ in places}
        start, stop = min(cuts.values()), w_ref.shape[1]
        rhs = []
        for t, b in places:
            frames = [(earlier_ref, t + a) if t + a < PAIR else (shifted_ref, t + a - PAIR) for a in (2, 1, 0)]
            rhs.append(padded_rows([block_lines(ref, j, b) for ref, j in frames], cuts[t], stop, start, stop))
        return jnp.dot(w_ref[:, start:], jnp.concatenate(rhs, axis=1), preferred_element_type=jnp.float32)

    by_frames(lanes, tile_sums, finish)
    if sends and rest_sent:
        outs[2][:, PAIR * (chunks - 1) * LANES :] = sum(tails).astype(jnp.bfloat16)


def conv(chain, plan, begun, earlier, shifted, values, weight, columns):
    _, _, channels, lanes = shifted.shape
    pitch, half, received = plan["pitch"], plan["half"], plan["received"]
    if plan["last"]:
        out_shape = (jax.ShapeDtypeStruct((PAIR, channels, LANES), jnp.bfloat16),) * 2
    else:
        out_shape = (
            jax.ShapeDtypeStruct((PAIR, channels, lanes), jnp.bfloat16),
            jax.ShapeDtypeStruct((PAIR, 3, channels, rounded((plan["rows"] - 1) * pitch)), jnp.bfloat16),
        )
        if plan["sends"] and plan["rest_sent"]:
            out_shape += (jax.ShapeDtypeStruct((channels, PAIR * (lanes - LANES) + LANES), jnp.bfloat16),)
        elif plan["sends"]:
            out_shape += out_shape[:1]
    if plan["builds"]:
        out_shape += far_shapes(plan["rows_near"] // 2, pitch - 1 - half, channels, half)
    return chain.add(
        functools.partial(conv_kernel, plan),
        [shifted, values, weight, columns, *begun, *earlier],
        out_shape,
        [pltpu.VMEM((PAIR, 3, channels, lanes), jnp.bfloat16)] * received,
        54 * channels * channels * PAIR * lanes * (1 + plan["builds"]),
    )


def join_kernel(pair, kept_ref, got_ref, *refs):
    out_ref, lines_ref, sems = refs[-3:]
    _, rows, _, width = lines_ref.shape
    half = width // 2
    core, group, _ = place()
    first = core == 0
    left_half = lane_of(width) < half
    copies = []
    for t in range(PAIR):
        mine, theirs = kept_ref[t].astype(jnp.float32), got_ref[t].astype(jnp.float32)
        left, right = jnp.where(first, mine, theirs), jnp.where(first, theirs, mine)
        lines = (
            jnp.where(left_half, left, pltpu.roll(right, half, 1)),
            jnp.where(left_half, pltpu.roll(left, half, 1), right),
        )
        for j in range(rows):
            lines_ref[t, j + group * (rows - 1 - 2 * j)] = lines[j].astype(jnp.bfloat16)
        copies.append(pltpu.make_async_copy(lines_ref.at[t], out_ref.at[PAIR * pair + t], sems.at[t]))
        copies[-1].start()
    for copy in copies:
        copy.wait()


def join(pair, kept, got, shape, *so_far):
    return pl.pallas_call(
        functools.partial(join_kernel, pair),
        out_shape=jax.ShapeDtypeStruct(shape, jnp.bfloat16),
        in_specs=[VMEM, VMEM] + [ANY] * len(so_far),
        out_specs=ANY,
        scratch_shapes=[pltpu.VMEM((PAIR,) + shape[1:], jnp.bfloat16), pltpu.SemaphoreType.DMA((PAIR,))],
        input_output_aliases={2: 0} if so_far else {},
        compiler_params=pltpu.CompilerParams(vmem_limit_bytes=LIMIT),
        name="join",
    )(kept, got, *so_far)


def on_device(latents, conv_weight, norm_gains, biases):
    layers = conv_weight.shape[0]
    frames, rows, channels, width = latents.shape
    strips, blocks = lax.axis_size("rows"), lax.axis_size("tm")
    assert strips == 4 and rows == 2 and frames % PAIR == 0 and width == LANES

    def mate_of(block):
        return lax.ppermute(block, "rows", [(i, i ^ 1) for i in range(strips)])

    def earlier_of(block):
        return lax.ppermute(block, "tm", [(i, i + 1) for i in range(blocks - 1)])

    def beyond_of(block):
        return lax.ppermute(block, "rows", [(i, i ^ 2) for i in range(strips)])

    mate = mate_of(latents)
    pairs = frames // PAIR
    own = split(latents)
    far = beyond_of(own[-1])
    row_values = jnp.concatenate([norm_gains, biases], axis=0)
    weight, columns = weights(conv_weight, row_values)
    near_values, near_act, near_sent = near(layers, mate, row_values, own)
    came = [beyond_of(block) for block in near_sent]
    far, weight, columns, near_values, near_act = lax.optimization_barrier(
        (far, weight, columns, near_values, near_act)
    )
    values, shifted = [None] * pairs, [None] * pairs
    values[-1], shifted[-1], send = beyond(layers, columns, far, mate_of(far), near_values[-1], near_act[-1])
    halo, rest = earlier_of(send), 0
    next_begun = layer_begun = None
    chain = Chain()
    first_begun = begin(chain, shifted[-1], weight[0])
    chain.run("begin")
    first_begun = now(first_begun)
    *came, first_begun = lax.optimization_barrier((*came, first_begun))
    parts = [(came[p], near_values[p], near_act[p]) for p in range(pairs - 1)]
    half = width // 2
    pitch = half + layers + 1
    for layer in range(layers):
        last = layer == layers - 1
        rows_left = 2 * rows + layers - 1 - layer
        results = [None] * pairs
        for p in reversed(range(pairs)):
            builds = layer == 0 and p > 0
            earlier = (halo,) if p == 0 else parts[p - 1] if builds else (shifted[p - 1],)
            begun = ()
            if builds and p == pairs - 1:
                begun = (first_begun,)
            elif layer == 0 and p == 0 and next_begun is not None:
                begun = (next_begun,)
            elif layer == 1 and p == pairs - 1 and layer_begun is not None:
                begun = (layer_begun,)
            elif builds or (p == 0 and (last or layer == 0)):
                begun = (begin(chain, shifted[p], weight[layer]),)
            if last and p == 0:
                chain.run("convs")
            plan = {
                "layer": layer,
                "begun": len(begun) > 0,
                "rows_near": 2 * rows,
                "last": last,
                "sends": p == pairs - 1 and not last,
                "rest_sent": joined(rows_left * pitch),
                "received": p == 0,
                "rest": 0 if p else rest,
                "builds": builds,
                "inputs": len(earlier),
                "pitch": pitch,
                "half": half,
                "rows": rows_left,
            }
            outs = list(conv(chain, plan, begun, earlier, shifted[p], values[p], weight[layer], columns))
            if builds:
                shifted[p - 1], values[p - 1] = outs.pop(), outs.pop()
            results[p] = outs
            if plan["sends"]:
                if layer == 0 and p == 1:
                    next_begun = begin(chain, shifted[0], weight[0])
                chain.run("convs")
                arriving = earlier_of(now(outs[2]))
                if layer == 0 and p == 1:
                    layer_begun = begin(chain, outs[1], weight[1])
                    chain.run("begin")
                    halo, layer_begun = lax.optimization_barrier((halo, now(layer_begun)))
        values, shifted = [r[0] for r in results], [r[1] for r in results]
        if not last:
            halo, rest = arriving, joined(rows_left * pitch)
    chain.run("convs")
    result = ()
    for p in reversed(range(pairs)):
        result = (join(p, now(values[p]), mate_of(now(shifted[p])), latents.shape, *result),)
    return result[0]


def solution(mesh):
    in_specs = (P(("clips", "tm"), "rows", None, None), P(), P(), P())
    out_specs = P(("clips", "tm"), "rows", None, None)
    return jax.shard_map(on_device, mesh=mesh, in_specs=in_specs, out_specs=out_specs, check_vma=False)
```

```python
import functools

import jax
import jax.numpy as jnp
from jax import lax
from jax.experimental import pallas as pl
from jax.experimental.pallas import tpu as pltpu
from jax.sharding import PartitionSpec as P

EPSILON = 1e-06
PAIR = 2
LANES = 128
TILE = 256
VMEM = pl.BlockSpec(memory_space=pltpu.VMEM)
ANY = pl.BlockSpec(memory_space=pl.ANY)
LIMIT = 24 * 1024 * 1024
LARGE = 44 * 1024 * 1024


def place():
    strip = lax.axis_index("rows").astype(jnp.int32)
    core, group = strip & 1, strip >> 1
    return core, group, core == group


def rounded(lanes):
    return -(-lanes // LANES) * LANES


def column(row):
    return jnp.transpose(jnp.broadcast_to(row, (LANES, row.shape[1])))


def lane_of(lanes):
    return lax.broadcasted_iota(jnp.int32, (1, lanes), 1)


def filled(lanes, pitch):
    lane = lane_of(lanes)
    gaps = lane < 0
    for end in range(pitch - 1, lanes, pitch):
        gaps = gaps | (lane == end)
    return jnp.where(gaps, 0.0, 1.0)


def activated(values, gain, mask):
    squares = jnp.mean(values * values, axis=0, keepdims=True)
    halved = values * (lax.rsqrt(squares + EPSILON) * (0.5 * mask)) * gain
    return (halved + halved * jnp.tanh(halved)).astype(jnp.bfloat16)


def weights_kernel(w_ref, rows_ref, *refs):
    outs, columns_ref, held_ref, sems = refs[:-3], refs[-3], refs[-2], refs[-1]
    layers, taps, channels_out, ins = w_ref.shape
    step = taps // 3
    places = [(layer, time_tap) for layer in range(layers) for time_tap in range(3)]
    copies = []
    for n, (layer, time_tap) in enumerate(places):
        part = pl.ds(step * time_tap, step)
        copies.append(pltpu.make_async_copy(w_ref.at[layer, part], held_ref.at[n], sems.at[n]))
        copies[-1].start()
    _, flipped, _ = place()
    for layer in range(layers):
        columns_ref[layer, 0] = column(rows_ref[layer : layer + 1, :])
        columns_ref[layer, 1] = column(rows_ref[layers + layer : layers + layer + 1, :])
    for n, (layer, time_tap) in enumerate(places):
        copies[n].wait()
        for row_tap in range(3):
            source = 3 * (row_tap + flipped * (2 - 2 * row_tap))
            at = (3 * (2 - time_tap) + row_tap) * ins
            outs[layer][:, at : at + ins] = held_ref[n, pl.ds(source, 3)].reshape(3 * channels_out, ins)


def weights(conv_weight, rows):
    layers, taps, outs, ins = conv_weight.shape
    one = jax.ShapeDtypeStruct((3 * outs, 9 * ins), conv_weight.dtype)
    results = pl.pallas_call(
        weights_kernel,
        out_shape=(one,) * layers + (jax.ShapeDtypeStruct((layers, 2, outs, LANES), jnp.float32),),
        in_specs=[ANY, VMEM],
        out_specs=(VMEM,) * (layers + 1),
        scratch_shapes=[
            pltpu.VMEM((3 * layers, taps // 3, outs, ins), conv_weight.dtype),
            pltpu.SemaphoreType.DMA((3 * layers,)),
        ],
        compiler_params=pltpu.CompilerParams(vmem_limit_bytes=LARGE),
        cost_estimate=pl.CostEstimate(flops=0, bytes_accessed=4 * conv_weight.size, transcendentals=0),
        name="weights",
    )(conv_weight, rows)
    return results[:-1], results[-1]


def split_kernel(in_ref, *out_refs):
    for p, out_ref in enumerate(out_refs):
        out_ref[...] = in_ref[PAIR * p : PAIR * (p + 1)]


def split(latents):
    pairs = latents.shape[0] // PAIR
    return pl.pallas_call(
        split_kernel,
        out_shape=(jax.ShapeDtypeStruct((PAIR,) + latents.shape[1:], latents.dtype),) * pairs,
        in_specs=[VMEM],
        out_specs=(VMEM,) * pairs,
        compiler_params=pltpu.CompilerParams(vmem_limit_bytes=LIMIT),
        name="split",
    )(latents)


def folds(channels, rest):
    fits = [n for n in (4, 3, 2) if n * rest <= LANES and channels % (16 * n) == 0]
    return fits[0] if fits else 1


def message_shape(channels, valid):
    whole, rest = divmod(PAIR * valid, LANES)
    lines = whole * channels + (channels // folds(channels, rest) if rest else 0)
    return jax.ShapeDtypeStruct((lines, LANES), jnp.bfloat16)


def write_message(ref, acts, valid):
    channels, width = acts[0].shape
    whole, rest = divmod(PAIR * valid, LANES)
    total = rounded(PAIR * valid)
    if total > width:
        acts = [jnp.concatenate([act, jnp.zeros((channels, total - width), jnp.bfloat16)], axis=1) for act in acts]
    first, second = acts[0], pltpu.roll(acts[1], valid, 1)
    lane = lane_of(LANES)
    for n in range(total // LANES):
        at = slice(n * LANES, (n + 1) * LANES)
        block = first[:, at] if at.stop <= valid else second[:, at]
        if at.start < valid < at.stop:
            mixed = jnp.where(lane < valid - at.start, first[:, at].astype(jnp.float32), second[:, at].astype(jnp.float32))
            block = mixed.astype(jnp.bfloat16)
        if n < whole:
            ref[n * channels : (n + 1) * channels] = block
            continue
        parts = folds(channels, rest)
        size, step = channels // parts, LANES // parts
        kept = jnp.where(lane < rest, block.astype(jnp.float32), 0.0)
        pieces = [kept[i * size : (i + 1) * size] for i in range(parts)]
        ref[n * channels :] = sum(
            piece if i == 0 else pltpu.roll(piece, i * step, 1) for i, piece in enumerate(pieces)
        ).astype(jnp.bfloat16)


def read_message(ref, channels, width, valid):
    whole, rest = divmod(PAIR * valid, LANES)
    blocks = [ref[n * channels : (n + 1) * channels] for n in range(whole)]
    if rest:
        parts = folds(channels, rest)
        folded = ref[whole * channels :]
        pieces = [folded if i == 0 else pltpu.roll(folded, LANES - i * (LANES // parts), 1) for i in range(parts)]
        blocks.append(pieces[0] if parts == 1 else jnp.concatenate(pieces, axis=0))
    both = jnp.concatenate(blocks, axis=1)
    return both[:, :width], pltpu.roll(both, both.shape[1] - valid, 1)[:, :width]


def spread(out_ref, index, act, pitch):
    lanes = out_ref.shape[3]
    above = pltpu.roll(act, pitch, 1)
    below = pltpu.roll(act, act.shape[1] - pitch, 1)
    edge = jnp.where(lane_of(LANES) < pitch, 0.0, above[:, :LANES].astype(jnp.float32))
    out_ref[index, 0, :, :LANES] = edge.astype(jnp.bfloat16)
    out_ref[index, 0, :, LANES:] = above[:, LANES:lanes]
    out_ref[index, 1] = act[:, :lanes]
    out_ref[index, 2] = below[:, :lanes]


def placed(blocks, core, row, window, line):
    pitch, width = window + 1, line.shape[1]
    lane = lane_of(LANES)
    block, low = divmod(row * pitch, LANES)
    shift = lax.rem(low + LANES - core * (width - window), LANES)
    turned = moved(line, shift)
    here = (lane >= low) & (lane < low + window)
    blocks[block] = blocks.get(block, 0.0) + jnp.where(here, turned, 0.0)
    if low + window > LANES:
        blocks[block + 1] = blocks.get(block + 1, 0.0) + jnp.where(lane < low + window - LANES, turned, 0.0)


def near_kernel(halo, pairs, mate_ref, gains_ref, *refs):
    own_refs, value_refs, act_refs = refs[:pairs], refs[pairs : 2 * pairs], refs[2 * pairs : 3 * pairs]
    send_refs = refs[3 * pairs :]
    frames, rows, _, width = mate_ref.shape
    window = width // 2 + halo
    core, group, outer = place()
    gain = column(gains_ref[0:1, :])
    done = act_refs[0].shape[2]
    mask = filled(done, window + 1)
    for f in range(frames):
        p, t = divmod(f, PAIR)
        blocks, sent = {}, {}
        for row in range(2 * rows):
            at = row % rows
            index = at + group * (rows - 1 - 2 * at)
            own, mate = own_refs[p][t, index], mate_ref[f, index]
            one, two = (own, mate) if row < rows else (mate, own)
            line = jnp.where(outer, one, two)
            placed(blocks, core, row, window, line)
            there = 4 * rows - 1 - row
            if p < pairs - 1 and there < 2 * rows + halo:
                placed(sent, core, there, window, line)
        for b in sent:
            send_refs[p][t, :, b * LANES - done : (b + 1) * LANES - done] = sent[b].astype(jnp.bfloat16)
        for b in blocks:
            part = slice(b * LANES, (b + 1) * LANES)
            value_refs[p][t, :, part] = blocks[b].astype(jnp.bfloat16)
            if part.stop <= done:
                act_refs[p][t, :, part] = activated(blocks[b], gain, mask[:, part])


def near(halo, mate, gains, own):
    frames, rows, channels, width = mate.shape
    pitch = width // 2 + halo + 1
    lanes = 2 * rows * pitch
    done = lanes // LANES * LANES
    pairs = len(own)
    sent = jax.ShapeDtypeStruct((PAIR, channels, rounded(lanes + halo * pitch) - done), jnp.bfloat16)
    outs = pl.pallas_call(
        functools.partial(near_kernel, halo, pairs),
        out_shape=(jax.ShapeDtypeStruct((PAIR, channels, rounded(lanes)), jnp.bfloat16),) * pairs
        + (jax.ShapeDtypeStruct((PAIR, channels, done), jnp.bfloat16),) * pairs
        + (sent,) * (pairs - 1),
        in_specs=[VMEM] * (2 + pairs),
        out_specs=(VMEM,) * (3 * pairs - 1),
        compiler_params=pltpu.CompilerParams(vmem_limit_bytes=LIMIT),
        cost_estimate=pl.CostEstimate(flops=40 * mate.size, bytes_accessed=8 * mate.size, transcendentals=2 * mate.size),
        name="near",
    )(mate, gains, *own)
    return outs[:pairs], outs[pairs : 2 * pairs], outs[2 * pairs :]


def far_blocks(halo, far_ref, mate_ref, t, blocks):
    _, rows, _, width = far_ref.shape
    core, group, outer = place()
    for row in range(2 * rows, 2 * rows + halo):
        local = 4 * rows - 1 - row
        at = local % rows
        index = at + (1 - group) * (rows - 1 - 2 * at)
        one, two = (mate_ref, far_ref) if local < rows else (far_ref, mate_ref)
        line = jnp.where(outer, one[t, index], two[t, index])
        placed(blocks, core, row, width // 2 + halo, line)


def add_far(pitch, valid, add, near_ref, act_ref, columns_ref, values_ref, shifted_ref, send_ref=None):
    lanes, done = values_ref.shape[2], act_ref.shape[2]
    mask = filled(lanes, pitch)
    whole_acts = []
    for t in range(PAIR):
        values_ref[t, :, :done] = near_ref[t, :, :done]
        acts = [act_ref[t]]
        blocks = {done // LANES: near_ref[t, :, done:].astype(jnp.float32)}
        add(t, blocks)
        for b in sorted(blocks):
            part = slice(b * LANES, (b + 1) * LANES)
            values_ref[t, :, part] = blocks[b].astype(jnp.bfloat16)
            acts.append(activated(blocks[b], columns_ref[0, 0], mask[:, part]))
        act = jnp.concatenate(acts, axis=1)
        spread(shifted_ref, t, act, pitch)
        whole_acts.append(act)
    if send_ref is not None:
        write_message(send_ref, whole_acts, valid)


def far_shapes(rows, halo, channels, half):
    pitch = half + halo + 1
    return (
        jax.ShapeDtypeStruct((PAIR, channels, rounded((2 * rows + halo) * pitch)), jnp.bfloat16),
        jax.ShapeDtypeStruct((PAIR, 3, channels, rounded((2 * rows + halo - 1) * pitch)), jnp.bfloat16),
    )


def beyond(halo, columns, *parts):
    far = parts[0]
    _, rows, channels, width = far.shape
    values, shifted = far_shapes(rows, halo, channels, width // 2)
    pitch = width // 2 + halo + 1
    valid = (2 * rows + halo) * pitch

    def kernel(columns_ref, far_ref, mate_ref, near_ref, act_ref, *outs):
        add = functools.partial(far_blocks, halo, far_ref, mate_ref)
        add_far(pitch, valid, add, near_ref, act_ref, columns_ref, *outs)

    return pl.pallas_call(
        kernel,
        out_shape=(values, shifted, message_shape(channels, valid)),
        in_specs=[VMEM] * 5,
        out_specs=(VMEM,) * 3,
        compiler_params=pltpu.CompilerParams(vmem_limit_bytes=LIMIT),
        cost_estimate=pl.CostEstimate(flops=40 * far.size, bytes_accessed=8 * far.size, transcendentals=2 * far.size),
        name="beyond",
    )(columns, *parts)


def by_taps(sums):
    channels, lanes = sums.shape[0] // 3, sums.shape[1]
    return [
        [sums[tap * channels : (tap + 1) * channels, at : at + LANES] for at in range(0, lanes, LANES)]
        for tap in range(3)
    ]


def moved(block, shift):
    return pltpu.roll(block, shift, 1).astype(jnp.float32)


def column_sums(taps):
    lane = lane_of(LANES)
    left, middle, right = taps
    lefts = [pltpu.roll(block, 1, 1) for block in left]
    rights = [pltpu.roll(block, LANES - 1, 1) for block in right] + [0.0]
    return [
        jnp.where(lane == 0, lefts[b - 1] if b else 0.0, lefts[b])
        + middle[b]
        + jnp.where(lane == LANES - 1, rights[b + 1], rights[b])
        for b in range(len(middle))
    ]


def begun_rows(t, channels):
    return (t + 1) * 3 * channels // TILE * TILE


def rows_between(lines, start, stop):
    taken, at = [], 0
    for part in lines:
        low, high = max(start - at, 0), min(stop - at, part.shape[0])
        if low < high:
            taken.append(part[low:high])
        at += part.shape[0]
    return jnp.concatenate(taken, axis=0)


def block_lines(ref, frame, b):
    return ref[frame, :, :, b * LANES : (b + 1) * LANES].reshape(3 * ref.shape[2], LANES)


def padded_rows(lines, start, stop, low, high):
    parts = [rows_between(lines, start, stop)]
    if low < start:
        parts.insert(0, jnp.zeros((start - low, LANES), jnp.bfloat16))
    if stop < high:
        parts.append(jnp.zeros((high - stop, LANES), jnp.bfloat16))
    return parts[0] if len(parts) == 1 else jnp.concatenate(parts, axis=0)


def tiled(lanes):
    places = [(t, b) for t in range(PAIR) for b in range(lanes // LANES)]
    side = TILE // LANES
    return [places[n : n + side] for n in range(0, len(places), side)]


def by_frames(lanes, tile_sums, finish):
    taps = {t: [[], [], []] for t in range(PAIR)}
    for places in tiled(lanes):
        sums = by_taps(tile_sums(places))
        for i, (t, b) in enumerate(places):
            for tap in range(3):
                taps[t][tap].append(sums[tap][i])
        for t, b in places:
            if b == lanes // LANES - 1:
                finish(t, taps[t])


def begin_kernel(shifted_ref, w_ref, out_ref):
    _, _, channels, lanes = shifted_ref.shape

    def tile_sums(places):
        depth = max(begun_rows(t, channels) for t, _ in places)
        rhs = [
            padded_rows(
                [block_lines(shifted_ref, j, b) for j in range(t, -1, -1)],
                0,
                begun_rows(t, channels),
                0,
                depth,
            )
            for t, b in places
        ]
        return jnp.dot(w_ref[:, :depth], jnp.concatenate(rhs, axis=1), preferred_element_type=jnp.float32)

    def finish(t, taps):
        for b, block in enumerate(column_sums(taps)):
            out_ref[t, :, b * LANES : (b + 1) * LANES] = block

    by_frames(lanes, tile_sums, finish)


def begin(shifted, weight):
    _, _, channels, lanes = shifted.shape
    return pl.pallas_call(
        begin_kernel,
        out_shape=jax.ShapeDtypeStruct((PAIR, channels, lanes), jnp.float32),
        in_specs=[VMEM] * 2,
        out_specs=VMEM,
        compiler_params=pltpu.CompilerParams(vmem_limit_bytes=LIMIT),
        cost_estimate=pl.CostEstimate(flops=0, bytes_accessed=0, transcendentals=0),
        name="begin",
    )(shifted, weight)


def conv_kernel(plan, shifted_ref, values_ref, w_ref, columns_ref, *refs):
    layer, pitch, half, received = plan["layer"], plan["pitch"], plan["half"], plan["received"]
    last, sends = plan["last"], plan["sends"]
    refs = list(refs)
    begun_ref = refs.pop(0) if plan["begun"] else None
    earlier_refs = [refs.pop(0) for _ in range(plan["inputs"])]
    earlier_ref = refs.pop() if received else earlier_refs[0]
    if received:
        frames = read_message(earlier_refs[0], values_ref.shape[1], values_ref.shape[2], (plan["rows"] + 1) * pitch)
        for t in range(PAIR):
            spread(earlier_ref, t, frames[t], pitch)
    outs = refs
    if plan["builds"]:
        earlier_ref = outs.pop()
        came_ref, near_ref, act_ref = earlier_refs
        done = act_ref.shape[2]

        def add(t, blocks):
            for at in range(0, came_ref.shape[2], LANES):
                b = (done + at) // LANES
                blocks[b] = blocks.get(b, 0.0) + came_ref[t, :, at : at + LANES].astype(jnp.float32)

        add_far(pitch, 0, add, near_ref, act_ref, columns_ref, outs.pop(), earlier_ref)
    _, _, channels, lanes = shifted_ref.shape
    chunks = lanes // LANES
    lane = lane_of(LANES)

    bias = columns_ref[layer, 1]
    whole_acts = []
    if not last:
        mask = filled(lanes, pitch)
        gain = columns_ref[layer + 1, 0]

    def finish(t, taps):
        totals, acts = [], []
        for b, conv in enumerate(column_sums(taps)):
            at = slice(b * LANES, (b + 1) * LANES)
            if begun_ref is not None:
                conv = conv + begun_ref[t, :, at]
            total = (values_ref[t, :, at].astype(jnp.float32) + conv + bias).astype(jnp.bfloat16)
            totals.append(total)
            if last:
                continue
            outs[0][t, :, at] = total
            acts.append(activated(total.astype(jnp.float32), gain, mask[:, at]))
        if not last:
            whole_acts.append(jnp.concatenate(acts, axis=1))
            spread(outs[1], t, whole_acts[-1], pitch)
            return
        core, _, outer = place()
        skipped = core * (pitch - 1 - half)

        def columns_of(row, to):
            b, low = divmod(row * pitch, LANES)
            shift = lax.rem(to + 2 * LANES - low - skipped, LANES)
            turned = moved(totals[b], shift)
            if low + pitch - 1 <= LANES:
                return turned
            return jnp.where(lane < to + LANES - low - skipped, turned, moved(totals[b + 1], shift))

        def rows_of(row):
            return jnp.where(lane < half, columns_of(row, 0), columns_of(row + 1, half))

        outermost, inner = rows_of(0), rows_of(2)
        outs[0][t] = jnp.where(outer, outermost, inner).astype(jnp.bfloat16)
        outs[1][t] = jnp.where(outer, inner, outermost).astype(jnp.bfloat16)

    def tile_sums(places):
        cuts = {t: begun_rows(t, channels) if plan["begun"] else 0 for t, _ in places}
        start, stop = min(cuts.values()), w_ref.shape[1]
        rhs = []
        for t, b in places:
            frames = [(earlier_ref, t + a) if t + a < PAIR else (shifted_ref, t + a - PAIR) for a in (2, 1, 0)]
            rhs.append(padded_rows([block_lines(ref, j, b) for ref, j in frames], cuts[t], stop, start, stop))
        return jnp.dot(w_ref[:, start:], jnp.concatenate(rhs, axis=1), preferred_element_type=jnp.float32)

    by_frames(lanes, tile_sums, finish)
    if sends:
        write_message(outs[2], whole_acts, plan["rows"] * pitch)


def conv(plan, begun, earlier, shifted, values, weight, columns):
    _, _, channels, lanes = shifted.shape
    pitch, half, received = plan["pitch"], plan["half"], plan["received"]
    if plan["last"]:
        out_shape = (jax.ShapeDtypeStruct((PAIR, channels, LANES), jnp.bfloat16),) * 2
    else:
        out_shape = (
            jax.ShapeDtypeStruct((PAIR, channels, lanes), jnp.bfloat16),
            jax.ShapeDtypeStruct((PAIR, 3, channels, rounded((plan["rows"] - 1) * pitch)), jnp.bfloat16),
        )
        if plan["sends"]:
            out_shape += (message_shape(channels, plan["rows"] * pitch),)
    scratch = [pltpu.VMEM((PAIR, 3, channels, lanes), jnp.bfloat16)] * received
    if plan["builds"]:
        out_shape += far_shapes(plan["rows_near"] // 2, pitch - 1 - half, channels, half)
    return pl.pallas_call(
        functools.partial(conv_kernel, plan),
        out_shape=out_shape,
        in_specs=[VMEM] * (4 + len(begun) + len(earlier)),
        out_specs=(VMEM,) * len(out_shape),
        scratch_shapes=scratch,
        compiler_params=pltpu.CompilerParams(vmem_limit_bytes=LIMIT),
        cost_estimate=pl.CostEstimate(
            flops=54 * channels * channels * PAIR * lanes * (1 + plan["builds"]),
            bytes_accessed=2 * weight.size,
            transcendentals=PAIR * channels * lanes,
        ),
        name=f"conv_{plan['layer']}",
    )(shifted, values, weight, columns, *begun, *earlier)


def join_kernel(pair, kept_ref, got_ref, *refs):
    out_ref, lines_ref, sems = refs[-3:]
    _, rows, _, width = lines_ref.shape
    half = width // 2
    core, group, _ = place()
    first = core == 0
    left_half = lane_of(width) < half
    copies = []
    for t in range(PAIR):
        mine, theirs = kept_ref[t].astype(jnp.float32), got_ref[t].astype(jnp.float32)
        left, right = jnp.where(first, mine, theirs), jnp.where(first, theirs, mine)
        lines = (
            jnp.where(left_half, left, pltpu.roll(right, half, 1)),
            jnp.where(left_half, pltpu.roll(left, half, 1), right),
        )
        for j in range(rows):
            lines_ref[t, j + group * (rows - 1 - 2 * j)] = lines[j].astype(jnp.bfloat16)
        copies.append(pltpu.make_async_copy(lines_ref.at[t], out_ref.at[PAIR * pair + t], sems.at[t]))
        copies[-1].start()
    for copy in copies:
        copy.wait()


def join(pair, kept, got, shape, *so_far):
    return pl.pallas_call(
        functools.partial(join_kernel, pair),
        out_shape=jax.ShapeDtypeStruct(shape, jnp.bfloat16),
        in_specs=[VMEM, VMEM] + [ANY] * len(so_far),
        out_specs=ANY,
        scratch_shapes=[pltpu.VMEM((PAIR,) + shape[1:], jnp.bfloat16), pltpu.SemaphoreType.DMA((PAIR,))],
        input_output_aliases={2: 0} if so_far else {},
        compiler_params=pltpu.CompilerParams(vmem_limit_bytes=LIMIT),
        name="join",
    )(kept, got, *so_far)


def on_device(latents, conv_weight, norm_gains, biases):
    layers = conv_weight.shape[0]
    frames, rows, channels, width = latents.shape
    strips, blocks = lax.axis_size("rows"), lax.axis_size("tm")
    assert strips == 4 and rows == 2 and frames % PAIR == 0 and width == LANES

    def mate_of(block):
        return lax.ppermute(block, "rows", [(i, i ^ 1) for i in range(strips)])

    def earlier_of(block):
        return lax.ppermute(block, "tm", [(i, i + 1) for i in range(blocks - 1)])

    def beyond_of(block):
        return lax.ppermute(block, "rows", [(i, i ^ 2) for i in range(strips)])

    mate = mate_of(latents)
    pairs = frames // PAIR
    own = split(latents)
    far = beyond_of(own[-1])
    row_values = jnp.concatenate([norm_gains, biases], axis=0)
    weight, columns = weights(conv_weight, row_values)
    near_values, near_act, near_sent = near(layers, mate, row_values, own)
    came = [beyond_of(block) for block in near_sent]
    far, weight, columns, near_values, near_act = lax.optimization_barrier(
        (far, weight, columns, near_values, near_act)
    )
    values, shifted = [None] * pairs, [None] * pairs
    values[-1], shifted[-1], send = beyond(layers, columns, far, mate_of(far), near_values[-1], near_act[-1])
    halo = earlier_of(send)
    next_begun = layer_begun = None
    first_begun = begin(shifted[-1], weight[0])
    *came, first_begun = lax.optimization_barrier((*came, first_begun))
    parts = [(came[p], near_values[p], near_act[p]) for p in range(pairs - 1)]
    half = width // 2
    pitch = half + layers + 1
    for layer in range(layers):
        last = layer == layers - 1
        rows_left = 2 * rows + layers - 1 - layer
        results = [None] * pairs
        for p in reversed(range(pairs)):
            builds = layer == 0 and p > 0
            earlier = (halo,) if p == 0 else parts[p - 1] if builds else (shifted[p - 1],)
            waits = builds or (p == 0 and (last or layer == 0)) or (layer == 1 and layer_begun is not None and p == pairs - 1)
            if builds and p == pairs - 1:
                begun = (first_begun,)
            elif layer == 0 and p == 0 and next_begun is not None:
                begun = (next_begun,)
            elif layer == 1 and p == pairs - 1 and layer_begun is not None:
                begun = (layer_begun,)
            else:
                begun = (begin(shifted[p], weight[layer]),) if waits else ()
            plan = {
                "layer": layer,
                "begun": waits,
                "rows_near": 2 * rows,
                "last": last,
                "sends": p == pairs - 1 and not last,
                "received": p == 0,
                "builds": builds,
                "inputs": len(earlier),
                "pitch": pitch,
                "half": half,
                "rows": rows_left,
            }
            outs = list(conv(plan, begun, earlier, shifted[p], values[p], weight[layer], columns))
            if builds:
                shifted[p - 1], values[p - 1] = outs.pop(), outs.pop()
            results[p] = outs
            if plan["sends"]:
                message = outs[2]
                if layer == 0 and p == 1:
                    next_begun = begin(shifted[0], weight[0])
                    message, next_begun = lax.optimization_barrier((message, next_begun))
                arriving = earlier_of(message)
                if layer == 0 and p == 1 and not last:
                    layer_begun = begin(outs[1], weight[1])
                    halo, layer_begun = lax.optimization_barrier((halo, layer_begun))
        values, shifted = [r[0] for r in results], [r[1] for r in results]
        if not last:
            halo = arriving
    result = ()
    for p in reversed(range(pairs)):
        result = (join(p, values[p], mate_of(shifted[p]), latents.shape, *result),)
    return result[0]


def solution(mesh):
    in_specs = (P(("clips", "tm"), "rows", None, None), P(), P(), P())
    out_specs = P(("clips", "tm"), "rows", None, None)
    return jax.shard_map(on_device, mesh=mesh, in_specs=in_specs, out_specs=out_specs, check_vma=False)
```

```python
import functools

import jax
import jax.numpy as jnp
from jax import lax
from jax.experimental import pallas as pl
from jax.experimental.pallas import tpu as pltpu
from jax.sharding import PartitionSpec as P

EPSILON = 1e-06
PAIR = 2
LANES = 128
TILE = 256
VMEM = pl.BlockSpec(memory_space=pltpu.VMEM)
ANY = pl.BlockSpec(memory_space=pl.ANY)
LIMIT = 24 * 1024 * 1024
LARGE = 44 * 1024 * 1024


def place():
    strip = lax.axis_index("rows").astype(jnp.int32)
    core, group = strip & 1, strip >> 1
    return core, group, core == group


def rounded(lanes):
    return -(-lanes // LANES) * LANES


def column(row):
    return jnp.transpose(jnp.broadcast_to(row, (LANES, row.shape[1])))


def lane_of(lanes):
    return lax.broadcasted_iota(jnp.int32, (1, lanes), 1)


def filled(lanes, pitch):
    lane = lane_of(lanes)
    gaps = lane < 0
    for end in range(pitch - 1, lanes, pitch):
        gaps = gaps | (lane == end)
    return jnp.where(gaps, 0.0, 1.0)


def activated(values, gain, mask):
    squares = jnp.mean(values * values, axis=0, keepdims=True)
    halved = values * (lax.rsqrt(squares + EPSILON) * (0.5 * mask)) * gain
    return (halved + halved * jnp.tanh(halved)).astype(jnp.bfloat16)


def weights_kernel(w_ref, rows_ref, *refs):
    outs, columns_ref, held_ref, sems = refs[:-3], refs[-3], refs[-2], refs[-1]
    layers, taps, channels_out, ins = w_ref.shape
    step = taps // 3
    places = [(layer, time_tap) for layer in range(layers) for time_tap in range(3)]
    copies = []
    for n, (layer, time_tap) in enumerate(places):
        part = pl.ds(step * time_tap, step)
        copies.append(pltpu.make_async_copy(w_ref.at[layer, part], held_ref.at[n], sems.at[n]))
        copies[-1].start()
    _, flipped, _ = place()
    for layer in range(layers):
        columns_ref[layer, 0] = column(rows_ref[layer : layer + 1, :])
        columns_ref[layer, 1] = column(rows_ref[layers + layer : layers + layer + 1, :])
    for n, (layer, time_tap) in enumerate(places):
        copies[n].wait()
        for row_tap in range(3):
            source = 3 * (row_tap + flipped * (2 - 2 * row_tap))
            at = (3 * (2 - time_tap) + row_tap) * ins
            outs[layer][:, at : at + ins] = held_ref[n, pl.ds(source, 3)].reshape(3 * channels_out, ins)


def weights(conv_weight, rows):
    layers, taps, outs, ins = conv_weight.shape
    one = jax.ShapeDtypeStruct((3 * outs, 9 * ins), conv_weight.dtype)
    results = pl.pallas_call(
        weights_kernel,
        out_shape=(one,) * layers + (jax.ShapeDtypeStruct((layers, 2, outs, LANES), jnp.float32),),
        in_specs=[ANY, VMEM],
        out_specs=(VMEM,) * (layers + 1),
        scratch_shapes=[
            pltpu.VMEM((3 * layers, taps // 3, outs, ins), conv_weight.dtype),
            pltpu.SemaphoreType.DMA((3 * layers,)),
        ],
        compiler_params=pltpu.CompilerParams(vmem_limit_bytes=LARGE),
        cost_estimate=pl.CostEstimate(flops=0, bytes_accessed=4 * conv_weight.size, transcendentals=0),
        name="weights",
    )(conv_weight, rows)
    return results[:-1], results[-1]


def split_kernel(in_ref, *out_refs):
    for p, out_ref in enumerate(out_refs):
        out_ref[...] = in_ref[PAIR * p : PAIR * (p + 1)]


def split(latents):
    pairs = latents.shape[0] // PAIR
    return pl.pallas_call(
        split_kernel,
        out_shape=(jax.ShapeDtypeStruct((PAIR,) + latents.shape[1:], latents.dtype),) * pairs,
        in_specs=[VMEM],
        out_specs=(VMEM,) * pairs,
        compiler_params=pltpu.CompilerParams(vmem_limit_bytes=LIMIT),
        name="split",
    )(latents)


def folds(channels, rest):
    fits = [n for n in (4, 3, 2) if n * rest <= LANES and channels % (16 * n) == 0]
    return fits[0] if fits else 1


def message_shape(channels, valid):
    whole, rest = divmod(PAIR * valid, LANES)
    lines = whole * channels + (channels // folds(channels, rest) if rest else 0)
    return jax.ShapeDtypeStruct((lines, LANES), jnp.bfloat16)


def write_message(ref, acts, valid):
    channels, width = acts[0].shape
    whole, rest = divmod(PAIR * valid, LANES)
    total = rounded(PAIR * valid)
    if total > width:
        acts = [jnp.concatenate([act, jnp.zeros((channels, total - width), jnp.bfloat16)], axis=1) for act in acts]
    first, second = acts[0], pltpu.roll(acts[1], valid, 1)
    lane = lane_of(LANES)
    for n in range(total // LANES):
        at = slice(n * LANES, (n + 1) * LANES)
        block = first[:, at] if at.stop <= valid else second[:, at]
        if at.start < valid < at.stop:
            mixed = jnp.where(lane < valid - at.start, first[:, at].astype(jnp.float32), second[:, at].astype(jnp.float32))
            block = mixed.astype(jnp.bfloat16)
        if n < whole:
            ref[n * channels : (n + 1) * channels] = block
            continue
        parts = folds(channels, rest)
        size, step = channels // parts, LANES // parts
        kept = jnp.where(lane < rest, block.astype(jnp.float32), 0.0)
        pieces = [kept[i * size : (i + 1) * size] for i in range(parts)]
        ref[n * channels :] = sum(
            piece if i == 0 else pltpu.roll(piece, i * step, 1) for i, piece in enumerate(pieces)
        ).astype(jnp.bfloat16)


def read_message(ref, channels, width, valid):
    whole, rest = divmod(PAIR * valid, LANES)
    blocks = [ref[n * channels : (n + 1) * channels] for n in range(whole)]
    if rest:
        parts = folds(channels, rest)
        folded = ref[whole * channels :]
        pieces = [folded if i == 0 else pltpu.roll(folded, LANES - i * (LANES // parts), 1) for i in range(parts)]
        blocks.append(pieces[0] if parts == 1 else jnp.concatenate(pieces, axis=0))
    both = jnp.concatenate(blocks, axis=1)
    return both[:, :width], pltpu.roll(both, both.shape[1] - valid, 1)[:, :width]


def spread(out_ref, index, act, pitch):
    lanes = out_ref.shape[3]
    above = pltpu.roll(act, pitch, 1)
    below = pltpu.roll(act, act.shape[1] - pitch, 1)
    edge = jnp.where(lane_of(LANES) < pitch, 0.0, above[:, :LANES].astype(jnp.float32))
    out_ref[index, 0, :, :LANES] = edge.astype(jnp.bfloat16)
    out_ref[index, 0, :, LANES:] = above[:, LANES:lanes]
    out_ref[index, 1] = act[:, :lanes]
    out_ref[index, 2] = below[:, :lanes]


def placed(blocks, core, row, window, line):
    pitch, width = window + 1, line.shape[1]
    lane = lane_of(LANES)
    block, low = divmod(row * pitch, LANES)
    shift = lax.rem(low + LANES - core * (width - window), LANES)
    turned = moved(line, shift)
    here = (lane >= low) & (lane < low + window)
    blocks[block] = blocks.get(block, 0.0) + jnp.where(here, turned, 0.0)
    if low + window > LANES:
        blocks[block + 1] = blocks.get(block + 1, 0.0) + jnp.where(lane < low + window - LANES, turned, 0.0)


def near_kernel(halo, pairs, mate_ref, gains_ref, *refs):
    own_refs, value_refs, act_refs = refs[:pairs], refs[pairs : 2 * pairs], refs[2 * pairs : 3 * pairs]
    send_refs = refs[3 * pairs :]
    frames, rows, _, width = mate_ref.shape
    window = width // 2 + halo
    core, group, outer = place()
    gain = column(gains_ref[0:1, :])
    done = act_refs[0].shape[2]
    mask = filled(done, window + 1)
    for f in range(frames):
        p, t = divmod(f, PAIR)
        blocks, sent = {}, {}
        for row in range(2 * rows):
            at = row % rows
            index = at + group * (rows - 1 - 2 * at)
            own, mate = own_refs[p][t, index], mate_ref[f, index]
            one, two = (own, mate) if row < rows else (mate, own)
            line = jnp.where(outer, one, two)
            placed(blocks, core, row, window, line)
            there = 4 * rows - 1 - row
            if p < pairs - 1 and there < 2 * rows + halo:
                placed(sent, core, there, window, line)
        for b in sent:
            send_refs[p][t, :, b * LANES - done : (b + 1) * LANES - done] = sent[b].astype(jnp.bfloat16)
        for b in blocks:
            part = slice(b * LANES, (b + 1) * LANES)
            value_refs[p][t, :, part] = blocks[b].astype(jnp.bfloat16)
            if part.stop <= done:
                act_refs[p][t, :, part] = activated(blocks[b], gain, mask[:, part])


def near(halo, mate, gains, own):
    frames, rows, channels, width = mate.shape
    pitch = width // 2 + halo + 1
    lanes = 2 * rows * pitch
    done = lanes // LANES * LANES
    pairs = len(own)
    sent = jax.ShapeDtypeStruct((PAIR, channels, rounded(lanes + halo * pitch) - done), jnp.bfloat16)
    outs = pl.pallas_call(
        functools.partial(near_kernel, halo, pairs),
        out_shape=(jax.ShapeDtypeStruct((PAIR, channels, rounded(lanes)), jnp.bfloat16),) * pairs
        + (jax.ShapeDtypeStruct((PAIR, channels, done), jnp.bfloat16),) * pairs
        + (sent,) * (pairs - 1),
        in_specs=[VMEM] * (2 + pairs),
        out_specs=(VMEM,) * (3 * pairs - 1),
        compiler_params=pltpu.CompilerParams(vmem_limit_bytes=LIMIT),
        cost_estimate=pl.CostEstimate(flops=40 * mate.size, bytes_accessed=8 * mate.size, transcendentals=2 * mate.size),
        name="near",
    )(mate, gains, *own)
    return outs[:pairs], outs[pairs : 2 * pairs], outs[2 * pairs :]


def far_blocks(halo, far_ref, mate_ref, t, blocks):
    _, rows, _, width = far_ref.shape
    core, group, outer = place()
    for row in range(2 * rows, 2 * rows + halo):
        local = 4 * rows - 1 - row
        at = local % rows
        index = at + (1 - group) * (rows - 1 - 2 * at)
        one, two = (mate_ref, far_ref) if local < rows else (far_ref, mate_ref)
        line = jnp.where(outer, one[t, index], two[t, index])
        placed(blocks, core, row, width // 2 + halo, line)


def add_far(pitch, valid, add, near_ref, act_ref, columns_ref, values_ref, shifted_ref, send_ref=None):
    lanes, done = values_ref.shape[2], act_ref.shape[2]
    mask = filled(lanes, pitch)
    whole_acts = []
    for t in range(PAIR):
        values_ref[t, :, :done] = near_ref[t, :, :done]
        acts = [act_ref[t]]
        blocks = {done // LANES: near_ref[t, :, done:].astype(jnp.float32)}
        add(t, blocks)
        for b in sorted(blocks):
            part = slice(b * LANES, (b + 1) * LANES)
            values_ref[t, :, part] = blocks[b].astype(jnp.bfloat16)
            acts.append(activated(blocks[b], columns_ref[0, 0], mask[:, part]))
        act = jnp.concatenate(acts, axis=1)
        spread(shifted_ref, t, act, pitch)
        whole_acts.append(act)
    if send_ref is not None:
        write_message(send_ref, whole_acts, valid)


def far_shapes(rows, halo, channels, half):
    pitch = half + halo + 1
    return (
        jax.ShapeDtypeStruct((PAIR, channels, rounded((2 * rows + halo) * pitch)), jnp.bfloat16),
        jax.ShapeDtypeStruct((PAIR, 3, channels, rounded((2 * rows + halo - 1) * pitch)), jnp.bfloat16),
    )


def beyond(halo, columns, *parts):
    far = parts[0]
    _, rows, channels, width = far.shape
    values, shifted = far_shapes(rows, halo, channels, width // 2)
    pitch = width // 2 + halo + 1
    valid = (2 * rows + halo) * pitch

    def kernel(columns_ref, far_ref, mate_ref, near_ref, act_ref, *outs):
        add = functools.partial(far_blocks, halo, far_ref, mate_ref)
        add_far(pitch, valid, add, near_ref, act_ref, columns_ref, *outs)

    return pl.pallas_call(
        kernel,
        out_shape=(values, shifted, message_shape(channels, valid)),
        in_specs=[VMEM] * 5,
        out_specs=(VMEM,) * 3,
        compiler_params=pltpu.CompilerParams(vmem_limit_bytes=LIMIT),
        cost_estimate=pl.CostEstimate(flops=40 * far.size, bytes_accessed=8 * far.size, transcendentals=2 * far.size),
        name="beyond",
    )(columns, *parts)


def by_taps(sums):
    channels, lanes = sums.shape[0] // 3, sums.shape[1]
    return [
        [sums[tap * channels : (tap + 1) * channels, at : at + LANES] for at in range(0, lanes, LANES)]
        for tap in range(3)
    ]


def moved(block, shift):
    return pltpu.roll(block, shift, 1).astype(jnp.float32)


def column_sums(taps):
    lane = lane_of(LANES)
    left, middle, right = taps
    lefts = [pltpu.roll(block, 1, 1) for block in left]
    rights = [pltpu.roll(block, LANES - 1, 1) for block in right] + [0.0]
    return [
        jnp.where(lane == 0, lefts[b - 1] if b else 0.0, lefts[b])
        + middle[b]
        + jnp.where(lane == LANES - 1, rights[b + 1], rights[b])
        for b in range(len(middle))
    ]


def begun_rows(t, channels):
    return (t + 1) * 3 * channels // TILE * TILE


def rows_between(lines, start, stop):
    taken, at = [], 0
    for part in lines:
        low, high = max(start - at, 0), min(stop - at, part.shape[0])
        if low < high:
            taken.append(part[low:high])
        at += part.shape[0]
    return jnp.concatenate(taken, axis=0)


def block_lines(ref, frame, b):
    return ref[frame, :, :, b * LANES : (b + 1) * LANES].reshape(3 * ref.shape[2], LANES)


def padded_rows(lines, start, stop, low, high):
    parts = [rows_between(lines, start, stop)]
    if low < start:
        parts.insert(0, jnp.zeros((start - low, LANES), jnp.bfloat16))
    if stop < high:
        parts.append(jnp.zeros((high - stop, LANES), jnp.bfloat16))
    return parts[0] if len(parts) == 1 else jnp.concatenate(parts, axis=0)


def tiled(lanes):
    places = [(t, b) for t in range(PAIR) for b in range(lanes // LANES)]
    side = TILE // LANES
    return [places[n : n + side] for n in range(0, len(places), side)]


def by_frames(lanes, tile_sums, finish):
    taps = {t: [[], [], []] for t in range(PAIR)}
    for places in tiled(lanes):
        sums = by_taps(tile_sums(places))
        for i, (t, b) in enumerate(places):
            for tap in range(3):
                taps[t][tap].append(sums[tap][i])
        for t, b in places:
            if b == lanes // LANES - 1:
                finish(t, taps[t])


def begin_kernel(shifted_ref, w_ref, out_ref):
    _, _, channels, lanes = shifted_ref.shape

    def tile_sums(places):
        depth = max(begun_rows(t, channels) for t, _ in places)
        rhs = [
            padded_rows(
                [block_lines(shifted_ref, j, b) for j in range(t, -1, -1)],
                0,
                begun_rows(t, channels),
                0,
                depth,
            )
            for t, b in places
        ]
        return jnp.dot(w_ref[:, :depth], jnp.concatenate(rhs, axis=1), preferred_element_type=jnp.float32)

    def finish(t, taps):
        for b, block in enumerate(column_sums(taps)):
            out_ref[t, :, b * LANES : (b + 1) * LANES] = block

    by_frames(lanes, tile_sums, finish)


class Later:
    def __init__(self, shape):
        self.shape, self.dtype, self.value = shape.shape, shape.dtype, None


def now(x):
    return x.value if isinstance(x, Later) else x


class Chain:
    def __init__(self):
        self.steps = []

    def add(self, kernel, inputs, out_shape, scratch, flops):
        outs = [Later(shape) for shape in out_shape]
        self.steps.append((kernel, inputs, outs, out_shape, scratch, flops))
        return outs

    def run(self, name):
        steps, self.steps = self.steps, []
        made = {id(out): n for n, out in enumerate(out for step in steps for out in step[2])}
        arrays = []
        for step in steps:
            for x in step[1]:
                if id(x) not in made and not any(now(x) is y for y in arrays):
                    arrays.append(now(x))
        at = [[("out", made[id(x)]) if id(x) in made else ("in", next(i for i, y in enumerate(arrays) if y is now(x))) for x in step[1]] for step in steps]
        out_shape = [shape for step in steps for shape in step[3]]
        scratch = [shape for step in steps for shape in step[4]]

        def kernel(*refs):
            ins, outs, rest = refs[: len(arrays)], refs[len(arrays) : len(arrays) + len(out_shape)], refs[len(arrays) + len(out_shape) :]
            first, held = 0, 0
            for step, places in zip(steps, at):
                own, kept = outs[first : first + len(step[3])], rest[held : held + len(step[4])]
                first, held = first + len(own), held + len(kept)
                step[0](*[(outs if kind == "out" else ins)[n] for kind, n in places], *own, *kept)

        results = pl.pallas_call(
            kernel,
            out_shape=tuple(out_shape),
            in_specs=[VMEM] * len(arrays),
            out_specs=(VMEM,) * len(out_shape),
            scratch_shapes=scratch,
            compiler_params=pltpu.CompilerParams(vmem_limit_bytes=LIMIT),
            cost_estimate=pl.CostEstimate(flops=sum(step[5] for step in steps), bytes_accessed=0, transcendentals=0),
            name=name,
        )(*arrays)
        for out, value in zip((out for step in steps for out in step[2]), results):
            out.value = value


def begin(chain, shifted, weight):
    _, _, channels, lanes = shifted.shape
    out = jax.ShapeDtypeStruct((PAIR, channels, lanes), jnp.float32)
    return chain.add(begin_kernel, [shifted, weight], [out], [], 0)[0]


def conv_kernel(plan, shifted_ref, values_ref, w_ref, columns_ref, *refs):
    layer, pitch, half, received = plan["layer"], plan["pitch"], plan["half"], plan["received"]
    last, sends = plan["last"], plan["sends"]
    refs = list(refs)
    begun_ref = refs.pop(0) if plan["begun"] else None
    earlier_refs = [refs.pop(0) for _ in range(plan["inputs"])]
    earlier_ref = refs.pop() if received else earlier_refs[0]
    if received:
        frames = read_message(earlier_refs[0], values_ref.shape[1], values_ref.shape[2], (plan["rows"] + 1) * pitch)
        for t in range(PAIR):
            spread(earlier_ref, t, frames[t], pitch)
    outs = refs
    if plan["builds"]:
        earlier_ref = outs.pop()
        came_ref, near_ref, act_ref = earlier_refs
        done = act_ref.shape[2]

        def add(t, blocks):
            for at in range(0, came_ref.shape[2], LANES):
                b = (done + at) // LANES
                blocks[b] = blocks.get(b, 0.0) + came_ref[t, :, at : at + LANES].astype(jnp.float32)

        add_far(pitch, 0, add, near_ref, act_ref, columns_ref, outs.pop(), earlier_ref)
    _, _, channels, lanes = shifted_ref.shape
    chunks = lanes // LANES
    lane = lane_of(LANES)

    bias = columns_ref[layer, 1]
    whole_acts = []
    if not last:
        mask = filled(lanes, pitch)
        gain = columns_ref[layer + 1, 0]

    def finish(t, taps):
        totals, acts = [], []
        for b, conv in enumerate(column_sums(taps)):
            at = slice(b * LANES, (b + 1) * LANES)
            if begun_ref is not None:
                conv = conv + begun_ref[t, :, at]
            total = (values_ref[t, :, at].astype(jnp.float32) + conv + bias).astype(jnp.bfloat16)
            totals.append(total)
            if last:
                continue
            outs[0][t, :, at] = total
            acts.append(activated(total.astype(jnp.float32), gain, mask[:, at]))
        if not last:
            whole_acts.append(jnp.concatenate(acts, axis=1))
            spread(outs[1], t, whole_acts[-1], pitch)
            return
        core, _, outer = place()
        skipped = core * (pitch - 1 - half)

        def columns_of(row, to):
            b, low = divmod(row * pitch, LANES)
            shift = lax.rem(to + 2 * LANES - low - skipped, LANES)
            turned = moved(totals[b], shift)
            if low + pitch - 1 <= LANES:
                return turned
            return jnp.where(lane < to + LANES - low - skipped, turned, moved(totals[b + 1], shift))

        def rows_of(row):
            return jnp.where(lane < half, columns_of(row, 0), columns_of(row + 1, half))

        outermost, inner = rows_of(0), rows_of(2)
        outs[0][t] = jnp.where(outer, outermost, inner).astype(jnp.bfloat16)
        outs[1][t] = jnp.where(outer, inner, outermost).astype(jnp.bfloat16)

    def tile_sums(places):
        cuts = {t: begun_rows(t, channels) if plan["begun"] else 0 for t, _ in places}
        start, stop = min(cuts.values()), w_ref.shape[1]
        rhs = []
        for t, b in places:
            frames = [(earlier_ref, t + a) if t + a < PAIR else (shifted_ref, t + a - PAIR) for a in (2, 1, 0)]
            rhs.append(padded_rows([block_lines(ref, j, b) for ref, j in frames], cuts[t], stop, start, stop))
        return jnp.dot(w_ref[:, start:], jnp.concatenate(rhs, axis=1), preferred_element_type=jnp.float32)

    by_frames(lanes, tile_sums, finish)
    if sends:
        write_message(outs[2], whole_acts, plan["rows"] * pitch)


def conv(chain, plan, begun, earlier, shifted, values, weight, columns):
    _, _, channels, lanes = shifted.shape
    pitch, half, received = plan["pitch"], plan["half"], plan["received"]
    if plan["last"]:
        out_shape = (jax.ShapeDtypeStruct((PAIR, channels, LANES), jnp.bfloat16),) * 2
    else:
        out_shape = (
            jax.ShapeDtypeStruct((PAIR, channels, lanes), jnp.bfloat16),
            jax.ShapeDtypeStruct((PAIR, 3, channels, rounded((plan["rows"] - 1) * pitch)), jnp.bfloat16),
        )
        if plan["sends"]:
            out_shape += (message_shape(channels, plan["rows"] * pitch),)
    if plan["builds"]:
        out_shape += far_shapes(plan["rows_near"] // 2, pitch - 1 - half, channels, half)
    return chain.add(
        functools.partial(conv_kernel, plan),
        [shifted, values, weight, columns, *begun, *earlier],
        out_shape,
        [pltpu.VMEM((PAIR, 3, channels, lanes), jnp.bfloat16)] * received,
        54 * channels * channels * PAIR * lanes * (1 + plan["builds"]),
    )


def join_kernel(pair, kept_ref, got_ref, *refs):
    out_ref, lines_ref, sems = refs[-3:]
    _, rows, _, width = lines_ref.shape
    half = width // 2
    core, group, _ = place()
    first = core == 0
    left_half = lane_of(width) < half
    copies = []
    for t in range(PAIR):
        mine, theirs = kept_ref[t].astype(jnp.float32), got_ref[t].astype(jnp.float32)
        left, right = jnp.where(first, mine, theirs), jnp.where(first, theirs, mine)
        lines = (
            jnp.where(left_half, left, pltpu.roll(right, half, 1)),
            jnp.where(left_half, pltpu.roll(left, half, 1), right),
        )
        for j in range(rows):
            lines_ref[t, j + group * (rows - 1 - 2 * j)] = lines[j].astype(jnp.bfloat16)
        copies.append(pltpu.make_async_copy(lines_ref.at[t], out_ref.at[PAIR * pair + t], sems.at[t]))
        copies[-1].start()
    for copy in copies:
        copy.wait()


def join(pair, kept, got, shape, *so_far):
    return pl.pallas_call(
        functools.partial(join_kernel, pair),
        out_shape=jax.ShapeDtypeStruct(shape, jnp.bfloat16),
        in_specs=[VMEM, VMEM] + [ANY] * len(so_far),
        out_specs=ANY,
        scratch_shapes=[pltpu.VMEM((PAIR,) + shape[1:], jnp.bfloat16), pltpu.SemaphoreType.DMA((PAIR,))],
        input_output_aliases={2: 0} if so_far else {},
        compiler_params=pltpu.CompilerParams(vmem_limit_bytes=LIMIT),
        name="join",
    )(kept, got, *so_far)


def on_device(latents, conv_weight, norm_gains, biases):
    layers = conv_weight.shape[0]
    frames, rows, channels, width = latents.shape
    strips, blocks = lax.axis_size("rows"), lax.axis_size("tm")
    assert strips == 4 and rows == 2 and frames % PAIR == 0 and width == LANES

    def mate_of(block):
        return lax.ppermute(block, "rows", [(i, i ^ 1) for i in range(strips)])

    def earlier_of(block):
        return lax.ppermute(block, "tm", [(i, i + 1) for i in range(blocks - 1)])

    def beyond_of(block):
        return lax.ppermute(block, "rows", [(i, i ^ 2) for i in range(strips)])

    mate = mate_of(latents)
    pairs = frames // PAIR
    own = split(latents)
    far = beyond_of(own[-1])
    row_values = jnp.concatenate([norm_gains, biases], axis=0)
    weight, columns = weights(conv_weight, row_values)
    near_values, near_act, near_sent = near(layers, mate, row_values, own)
    came = [beyond_of(block) for block in near_sent]
    far, weight, columns, near_values, near_act = lax.optimization_barrier(
        (far, weight, columns, near_values, near_act)
    )
    values, shifted = [None] * pairs, [None] * pairs
    values[-1], shifted[-1], send = beyond(layers, columns, far, mate_of(far), near_values[-1], near_act[-1])
    halo = earlier_of(send)
    next_begun = layer_begun = None
    chain = Chain()
    first_begun = begin(chain, shifted[-1], weight[0])
    chain.run("begin")
    first_begun = now(first_begun)
    *came, first_begun = lax.optimization_barrier((*came, first_begun))
    parts = [(came[p], near_values[p], near_act[p]) for p in range(pairs - 1)]
    half = width // 2
    pitch = half + layers + 1
    for layer in range(layers):
        last = layer == layers - 1
        rows_left = 2 * rows + layers - 1 - layer
        results = [None] * pairs
        for p in reversed(range(pairs)):
            builds = layer == 0 and p > 0
            earlier = (halo,) if p == 0 else parts[p - 1] if builds else (shifted[p - 1],)
            begun = ()
            if builds and p == pairs - 1:
                begun = (first_begun,)
            elif layer == 0 and p == 0 and next_begun is not None:
                begun = (next_begun,)
            elif layer == 1 and p == pairs - 1 and layer_begun is not None:
                begun = (layer_begun,)
            elif builds or (p == 0 and (last or layer == 0)):
                begun = (begin(chain, shifted[p], weight[layer]),)
            if last and p == 0:
                chain.run("convs")
            plan = {
                "layer": layer,
                "begun": len(begun) > 0,
                "rows_near": 2 * rows,
                "last": last,
                "sends": p == pairs - 1 and not last,
                "received": p == 0,
                "builds": builds,
                "inputs": len(earlier),
                "pitch": pitch,
                "half": half,
                "rows": rows_left,
            }
            outs = list(conv(chain, plan, begun, earlier, shifted[p], values[p], weight[layer], columns))
            if builds:
                shifted[p - 1], values[p - 1] = outs.pop(), outs.pop()
            results[p] = outs
            if layer == 0 and p == 0:
                chain.run("convs")
            if plan["sends"]:
                if layer == 0 and p == 1:
                    next_begun = begin(chain, shifted[0], weight[0])
                chain.run("convs")
                arriving = earlier_of(now(outs[2]))
                if layer == 0 and p == 1:
                    layer_begun = begin(chain, outs[1], weight[1])
                    chain.run("begin")
                    halo, layer_begun = lax.optimization_barrier((halo, now(layer_begun)))
        values, shifted = [r[0] for r in results], [r[1] for r in results]
        if not last:
            halo = arriving
    chain.run("convs")
    result = ()
    for p in reversed(range(pairs)):
        result = (join(p, now(values[p]), mate_of(now(shifted[p])), latents.shape, *result),)
    return result[0]


def solution(mesh):
    in_specs = (P(("clips", "tm"), "rows", None, None), P(), P(), P())
    out_specs = P(("clips", "tm"), "rows", None, None)
    return jax.shard_map(on_device, mesh=mesh, in_specs=in_specs, out_specs=out_specs, check_vma=False)
```

```python
import functools

import jax
import jax.numpy as jnp
from jax import lax
from jax.experimental import pallas as pl
from jax.experimental.pallas import tpu as pltpu
from jax.sharding import PartitionSpec as P

EPSILON = 1e-06
PAIR = 2
LANES = 128
TILE = 256
VMEM = pl.BlockSpec(memory_space=pltpu.VMEM)
ANY = pl.BlockSpec(memory_space=pl.ANY)
LIMIT = 24 * 1024 * 1024
LARGE = 44 * 1024 * 1024
WHOLE = 60 * 1024 * 1024


def place():
    strip = lax.axis_index("rows").astype(jnp.int32)
    core, group = strip & 1, strip >> 1
    return core, group, core == group


def rounded(lanes):
    return -(-lanes // LANES) * LANES


def column(row):
    return jnp.transpose(jnp.broadcast_to(row, (LANES, row.shape[1])))


def lane_of(lanes):
    return lax.broadcasted_iota(jnp.int32, (1, lanes), 1)


def filled(lanes, pitch):
    lane = lane_of(lanes)
    gaps = lane < 0
    for end in range(pitch - 1, lanes, pitch):
        gaps = gaps | (lane == end)
    return jnp.where(gaps, 0.0, 1.0)


def activated(values, gain, mask):
    squares = jnp.mean(values * values, axis=0, keepdims=True)
    halved = values * (lax.rsqrt(squares + EPSILON) * (0.5 * mask)) * gain
    return (halved + halved * jnp.tanh(halved)).astype(jnp.bfloat16)


def weights_kernel(w_ref, rows_ref, *refs):
    outs, columns_ref, held_ref, sems = refs[:-3], refs[-3], refs[-2], refs[-1]
    layers, taps, channels_out, ins = w_ref.shape
    step = taps // 3
    places = [(layer, time_tap) for layer in range(layers) for time_tap in range(3)]
    copies = []
    for n, (layer, time_tap) in enumerate(places):
        part = pl.ds(step * time_tap, step)
        copies.append(pltpu.make_async_copy(w_ref.at[layer, part], held_ref.at[n], sems.at[n]))
        copies[-1].start()
    _, flipped, _ = place()
    for layer in range(layers):
        columns_ref[layer, 0] = column(rows_ref[layer : layer + 1, :])
        columns_ref[layer, 1] = column(rows_ref[layers + layer : layers + layer + 1, :])
    for n, (layer, time_tap) in enumerate(places):
        copies[n].wait()
        for row_tap in range(3):
            source = 3 * (row_tap + flipped * (2 - 2 * row_tap))
            at = (3 * (2 - time_tap) + row_tap) * ins
            outs[layer][:, at : at + ins] = held_ref[n, pl.ds(source, 3)].reshape(3 * channels_out, ins)


def weights(conv_weight, rows):
    layers, taps, outs, ins = conv_weight.shape
    one = jax.ShapeDtypeStruct((3 * outs, 9 * ins), conv_weight.dtype)
    results = pl.pallas_call(
        weights_kernel,
        out_shape=(one,) * layers + (jax.ShapeDtypeStruct((layers, 2, outs, LANES), jnp.float32),),
        in_specs=[ANY, VMEM],
        out_specs=(VMEM,) * (layers + 1),
        scratch_shapes=[
            pltpu.VMEM((3 * layers, taps // 3, outs, ins), conv_weight.dtype),
            pltpu.SemaphoreType.DMA((3 * layers,)),
        ],
        compiler_params=pltpu.CompilerParams(vmem_limit_bytes=LARGE),
        cost_estimate=pl.CostEstimate(flops=0, bytes_accessed=4 * conv_weight.size, transcendentals=0),
        name="weights",
    )(conv_weight, rows)
    return results[:-1], results[-1]


def split_kernel(in_ref, *refs):
    out_refs, sems = refs[:-1], refs[-1]
    copies = [
        pltpu.make_async_copy(in_ref.at[pl.ds(PAIR * p, PAIR)], out_ref, sems.at[p]) for p, out_ref in enumerate(out_refs)
    ]
    for copy in reversed(copies):
        copy.start()
    for copy in copies:
        copy.wait()


def split(latents):
    pairs = latents.shape[0] // PAIR
    return pl.pallas_call(
        split_kernel,
        out_shape=(jax.ShapeDtypeStruct((PAIR,) + latents.shape[1:], latents.dtype),) * pairs,
        in_specs=[ANY],
        out_specs=(VMEM,) * pairs,
        scratch_shapes=[pltpu.SemaphoreType.DMA((pairs,))],
        compiler_params=pltpu.CompilerParams(vmem_limit_bytes=WHOLE),
        name="split",
    )(latents)


def folds(channels, rest):
    fits = [n for n in (4, 3, 2) if n * rest <= LANES and channels % (16 * n) == 0]
    return fits[0] if fits else 1


def message_shape(channels, valid):
    whole, rest = divmod(PAIR * valid, LANES)
    lines = whole * channels + (channels // folds(channels, rest) if rest else 0)
    return jax.ShapeDtypeStruct((lines, LANES), jnp.bfloat16)


def write_message(ref, acts, valid):
    channels, width = acts[0].shape
    whole, rest = divmod(PAIR * valid, LANES)
    total = rounded(PAIR * valid)
    if total > width:
        acts = [jnp.concatenate([act, jnp.zeros((channels, total - width), jnp.bfloat16)], axis=1) for act in acts]
    first, second = acts[0], pltpu.roll(acts[1], valid, 1)
    lane = lane_of(LANES)
    for n in range(total // LANES):
        at = slice(n * LANES, (n + 1) * LANES)
        block = first[:, at] if at.stop <= valid else second[:, at]
        if at.start < valid < at.stop:
            mixed = jnp.where(lane < valid - at.start, first[:, at].astype(jnp.float32), second[:, at].astype(jnp.float32))
            block = mixed.astype(jnp.bfloat16)
        if n < whole:
            ref[n * channels : (n + 1) * channels] = block
            continue
        parts = folds(channels, rest)
        size, step = channels // parts, LANES // parts
        kept = jnp.where(lane < rest, block.astype(jnp.float32), 0.0)
        pieces = [kept[i * size : (i + 1) * size] for i in range(parts)]
        ref[n * channels :] = sum(
            piece if i == 0 else pltpu.roll(piece, i * step, 1) for i, piece in enumerate(pieces)
        ).astype(jnp.bfloat16)


def read_message(ref, channels, width, valid):
    whole, rest = divmod(PAIR * valid, LANES)
    blocks = [ref[n * channels : (n + 1) * channels] for n in range(whole)]
    if rest:
        parts = folds(channels, rest)
        folded = ref[whole * channels :]
        pieces = [folded if i == 0 else pltpu.roll(folded, LANES - i * (LANES // parts), 1) for i in range(parts)]
        blocks.append(pieces[0] if parts == 1 else jnp.concatenate(pieces, axis=0))
    both = jnp.concatenate(blocks, axis=1)
    return both[:, :width], pltpu.roll(both, both.shape[1] - valid, 1)[:, :width]


def spread(out_ref, index, act, pitch):
    lanes = out_ref.shape[3]
    above = pltpu.roll(act, pitch, 1)
    below = pltpu.roll(act, act.shape[1] - pitch, 1)
    edge = jnp.where(lane_of(LANES) < pitch, 0.0, above[:, :LANES].astype(jnp.float32))
    out_ref[index, 0, :, :LANES] = edge.astype(jnp.bfloat16)
    out_ref[index, 0, :, LANES:] = above[:, LANES:lanes]
    out_ref[index, 1] = act[:, :lanes]
    out_ref[index, 2] = below[:, :lanes]


def placed(blocks, core, row, window, line):
    pitch, width = window + 1, line.shape[1]
    lane = lane_of(LANES)
    block, low = divmod(row * pitch, LANES)
    shift = lax.rem(low + LANES - core * (width - window), LANES)
    turned = moved(line, shift)
    here = (lane >= low) & (lane < low + window)
    blocks[block] = blocks.get(block, 0.0) + jnp.where(here, turned, 0.0)
    if low + window > LANES:
        blocks[block + 1] = blocks.get(block + 1, 0.0) + jnp.where(lane < low + window - LANES, turned, 0.0)


def near_kernel(halo, pairs, mate_ref, gains_ref, *refs):
    own_refs, value_refs, act_refs = refs[:pairs], refs[pairs : 2 * pairs], refs[2 * pairs : 3 * pairs]
    send_refs = refs[3 * pairs :]
    frames, rows, _, width = mate_ref.shape
    window = width // 2 + halo
    core, group, outer = place()
    gain = column(gains_ref[0:1, :])
    done = act_refs[0].shape[2]
    mask = filled(done, window + 1)
    for f in range(frames):
        p, t = divmod(f, PAIR)
        blocks, sent = {}, {}
        for row in range(2 * rows):
            at = row % rows
            index = at + group * (rows - 1 - 2 * at)
            own, mate = own_refs[p][t, index], mate_ref[f, index]
            one, two = (own, mate) if row < rows else (mate, own)
            line = jnp.where(outer, one, two)
            placed(blocks, core, row, window, line)
            there = 4 * rows - 1 - row
            if p < pairs - 1 and there < 2 * rows + halo:
                placed(sent, core, there, window, line)
        for b in sent:
            send_refs[p][t, :, b * LANES - done : (b + 1) * LANES - done] = sent[b].astype(jnp.bfloat16)
        for b in blocks:
            part = slice(b * LANES, (b + 1) * LANES)
            value_refs[p][t, :, part] = blocks[b].astype(jnp.bfloat16)
            if part.stop <= done:
                act_refs[p][t, :, part] = activated(blocks[b], gain, mask[:, part])


def near(halo, mate, gains, own):
    frames, rows, channels, width = mate.shape
    pitch = width // 2 + halo + 1
    lanes = 2 * rows * pitch
    done = lanes // LANES * LANES
    pairs = len(own)
    sent = jax.ShapeDtypeStruct((PAIR, channels, rounded(lanes + halo * pitch) - done), jnp.bfloat16)
    outs = pl.pallas_call(
        functools.partial(near_kernel, halo, pairs),
        out_shape=(jax.ShapeDtypeStruct((PAIR, channels, rounded(lanes)), jnp.bfloat16),) * pairs
        + (jax.ShapeDtypeStruct((PAIR, channels, done), jnp.bfloat16),) * pairs
        + (sent,) * (pairs - 1),
        in_specs=[VMEM] * (2 + pairs),
        out_specs=(VMEM,) * (3 * pairs - 1),
        compiler_params=pltpu.CompilerParams(vmem_limit_bytes=LIMIT),
        cost_estimate=pl.CostEstimate(flops=40 * mate.size, bytes_accessed=8 * mate.size, transcendentals=2 * mate.size),
        name="near",
    )(mate, gains, *own)
    return outs[:pairs], outs[pairs : 2 * pairs], outs[2 * pairs :]


def far_blocks(halo, far_ref, mate_ref, t, blocks):
    _, rows, _, width = far_ref.shape
    core, group, outer = place()
    for row in range(2 * rows, 2 * rows + halo):
        local = 4 * rows - 1 - row
        at = local % rows
        index = at + (1 - group) * (rows - 1 - 2 * at)
        one, two = (mate_ref, far_ref) if local < rows else (far_ref, mate_ref)
        line = jnp.where(outer, one[t, index], two[t, index])
        placed(blocks, core, row, width // 2 + halo, line)


def add_far(pitch, valid, add, near_ref, act_ref, columns_ref, values_ref, shifted_ref, send_ref=None):
    lanes, done = values_ref.shape[2], act_ref.shape[2]
    mask = filled(lanes, pitch)
    whole_acts = []
    for t in range(PAIR):
        values_ref[t, :, :done] = near_ref[t, :, :done]
        acts = [act_ref[t]]
        blocks = {done // LANES: near_ref[t, :, done:].astype(jnp.float32)}
        add(t, blocks)
        for b in sorted(blocks):
            part = slice(b * LANES, (b + 1) * LANES)
            values_ref[t, :, part] = blocks[b].astype(jnp.bfloat16)
            acts.append(activated(blocks[b], columns_ref[0, 0], mask[:, part]))
        act = jnp.concatenate(acts, axis=1)
        spread(shifted_ref, t, act, pitch)
        whole_acts.append(act)
    if send_ref is not None:
        write_message(send_ref, whole_acts, valid)


def far_shapes(rows, halo, channels, half):
    pitch = half + halo + 1
    return (
        jax.ShapeDtypeStruct((PAIR, channels, rounded((2 * rows + halo) * pitch)), jnp.bfloat16),
        jax.ShapeDtypeStruct((PAIR, 3, channels, rounded((2 * rows + halo - 1) * pitch)), jnp.bfloat16),
    )


def beyond(halo, columns, *parts):
    far = parts[0]
    _, rows, channels, width = far.shape
    values, shifted = far_shapes(rows, halo, channels, width // 2)
    pitch = width // 2 + halo + 1
    valid = (2 * rows + halo) * pitch

    def kernel(columns_ref, far_ref, mate_ref, near_ref, act_ref, *outs):
        add = functools.partial(far_blocks, halo, far_ref, mate_ref)
        add_far(pitch, valid, add, near_ref, act_ref, columns_ref, *outs)

    return pl.pallas_call(
        kernel,
        out_shape=(values, shifted, message_shape(channels, valid)),
        in_specs=[VMEM] * 5,
        out_specs=(VMEM,) * 3,
        compiler_params=pltpu.CompilerParams(vmem_limit_bytes=LIMIT),
        cost_estimate=pl.CostEstimate(flops=40 * far.size, bytes_accessed=8 * far.size, transcendentals=2 * far.size),
        name="beyond",
    )(columns, *parts)


def by_taps(sums):
    channels, lanes = sums.shape[0] // 3, sums.shape[1]
    return [
        [sums[tap * channels : (tap + 1) * channels, at : at + LANES] for at in range(0, lanes, LANES)]
        for tap in range(3)
    ]


def moved(block, shift):
    return pltpu.roll(block, shift, 1).astype(jnp.float32)


def column_sums(taps):
    lane = lane_of(LANES)
    left, middle, right = taps
    lefts = [pltpu.roll(block, 1, 1) for block in left]
    rights = [pltpu.roll(block, LANES - 1, 1) for block in right] + [0.0]
    return [
        jnp.where(lane == 0, lefts[b - 1] if b else 0.0, lefts[b])
        + middle[b]
        + jnp.where(lane == LANES - 1, rights[b + 1], rights[b])
        for b in range(len(middle))
    ]


def begun_rows(t, channels):
    return (t + 1) * 3 * channels // TILE * TILE


def rows_between(lines, start, stop):
    taken, at = [], 0
    for part in lines:
        low, high = max(start - at, 0), min(stop - at, part.shape[0])
        if low < high:
            taken.append(part[low:high])
        at += part.shape[0]
    return jnp.concatenate(taken, axis=0)


def block_lines(ref, frame, b):
    return ref[frame, :, :, b * LANES : (b + 1) * LANES].reshape(3 * ref.shape[2], LANES)


def padded_rows(lines, start, stop, low, high):
    parts = [rows_between(lines, start, stop)]
    if low < start:
        parts.insert(0, jnp.zeros((start - low, LANES), jnp.bfloat16))
    if stop < high:
        parts.append(jnp.zeros((high - stop, LANES), jnp.bfloat16))
    return parts[0] if len(parts) == 1 else jnp.concatenate(parts, axis=0)


def tiled(lanes):
    places = [(t, b) for t in range(PAIR) for b in range(lanes // LANES)]
    side = TILE // LANES
    return [places[n : n + side] for n in range(0, len(places), side)]


def by_frames(lanes, tile_sums, finish):
    taps = {t: [[], [], []] for t in range(PAIR)}
    for places in tiled(lanes):
        sums = by_taps(tile_sums(places))
        for i, (t, b) in enumerate(places):
            for tap in range(3):
                taps[t][tap].append(sums[tap][i])
        for t, b in places:
            if b == lanes // LANES - 1:
                finish(t, taps[t])


def begin_kernel(shifted_ref, w_ref, out_ref):
    _, _, channels, lanes = shifted_ref.shape

    def tile_sums(places):
        depth = max(begun_rows(t, channels) for t, _ in places)
        rhs = [
            padded_rows(
                [block_lines(shifted_ref, j, b) for j in range(t, -1, -1)],
                0,
                begun_rows(t, channels),
                0,
                depth,
            )
            for t, b in places
        ]
        return jnp.dot(w_ref[:, :depth], jnp.concatenate(rhs, axis=1), preferred_element_type=jnp.float32)

    def finish(t, taps):
        for b, block in enumerate(column_sums(taps)):
            out_ref[t, :, b * LANES : (b + 1) * LANES] = block

    by_frames(lanes, tile_sums, finish)


class Later:
    def __init__(self, shape):
        self.shape, self.dtype, self.value = shape.shape, shape.dtype, None


def now(x):
    return x.value if isinstance(x, Later) else x


class Chain:
    def __init__(self):
        self.steps = []

    def add(self, kernel, inputs, out_shape, scratch, flops):
        outs = [Later(shape) for shape in out_shape]
        self.steps.append((kernel, inputs, outs, out_shape, scratch, flops))
        return outs

    def run(self, name):
        steps, self.steps = self.steps, []
        made = {id(out): n for n, out in enumerate(out for step in steps for out in step[2])}
        arrays = []
        for step in steps:
            for x in step[1]:
                if id(x) not in made and not any(now(x) is y for y in arrays):
                    arrays.append(now(x))
        at = [[("out", made[id(x)]) if id(x) in made else ("in", next(i for i, y in enumerate(arrays) if y is now(x))) for x in step[1]] for step in steps]
        out_shape = [shape for step in steps for shape in step[3]]
        scratch = [shape for step in steps for shape in step[4]]

        def kernel(*refs):
            ins, outs, rest = refs[: len(arrays)], refs[len(arrays) : len(arrays) + len(out_shape)], refs[len(arrays) + len(out_shape) :]
            first, held = 0, 0
            for step, places in zip(steps, at):
                own, kept = outs[first : first + len(step[3])], rest[held : held + len(step[4])]
                first, held = first + len(own), held + len(kept)
                step[0](*[(outs if kind == "out" else ins)[n] for kind, n in places], *own, *kept)

        results = pl.pallas_call(
            kernel,
            out_shape=tuple(out_shape),
            in_specs=[VMEM] * len(arrays),
            out_specs=(VMEM,) * len(out_shape),
            scratch_shapes=scratch,
            compiler_params=pltpu.CompilerParams(vmem_limit_bytes=LIMIT),
            cost_estimate=pl.CostEstimate(flops=sum(step[5] for step in steps), bytes_accessed=0, transcendentals=0),
            name=name,
        )(*arrays)
        for out, value in zip((out for step in steps for out in step[2]), results):
            out.value = value


def begin(chain, shifted, weight):
    _, _, channels, lanes = shifted.shape
    out = jax.ShapeDtypeStruct((PAIR, channels, lanes), jnp.float32)
    return chain.add(begin_kernel, [shifted, weight], [out], [], 0)[0]


def conv_kernel(plan, shifted_ref, values_ref, w_ref, columns_ref, *refs):
    layer, pitch, half, received = plan["layer"], plan["pitch"], plan["half"], plan["received"]
    last, sends = plan["last"], plan["sends"]
    refs = list(refs)
    begun_ref = refs.pop(0) if plan["begun"] else None
    earlier_refs = [refs.pop(0) for _ in range(plan["inputs"])]
    earlier_ref = refs.pop() if received else earlier_refs[0]
    if received:
        frames = read_message(earlier_refs[0], values_ref.shape[1], values_ref.shape[2], (plan["rows"] + 1) * pitch)
        for t in range(PAIR):
            spread(earlier_ref, t, frames[t], pitch)
    outs = refs
    if plan["builds"]:
        earlier_ref = outs.pop()
        came_ref, near_ref, act_ref = earlier_refs
        done = act_ref.shape[2]

        def add(t, blocks):
            for at in range(0, came_ref.shape[2], LANES):
                b = (done + at) // LANES
                blocks[b] = blocks.get(b, 0.0) + came_ref[t, :, at : at + LANES].astype(jnp.float32)

        add_far(pitch, 0, add, near_ref, act_ref, columns_ref, outs.pop(), earlier_ref)
    _, _, channels, lanes = shifted_ref.shape
    chunks = lanes // LANES
    lane = lane_of(LANES)

    bias = columns_ref[layer, 1]
    whole_acts = []
    if not last:
        mask = filled(lanes, pitch)
        gain = columns_ref[layer + 1, 0]

    def finish(t, taps):
        totals, acts = [], []
        for b, conv in enumerate(column_sums(taps)):
            at = slice(b * LANES, (b + 1) * LANES)
            if begun_ref is not None:
                conv = conv + begun_ref[t, :, at]
            total = (values_ref[t, :, at].astype(jnp.float32) + conv + bias).astype(jnp.bfloat16)
            totals.append(total)
            if last:
                continue
            outs[0][t, :, at] = total
            acts.append(activated(total.astype(jnp.float32), gain, mask[:, at]))
        if not last:
            whole_acts.append(jnp.concatenate(acts, axis=1))
            spread(outs[1], t, whole_acts[-1], pitch)
            return
        core, _, outer = place()
        skipped = core * (pitch - 1 - half)

        def columns_of(row, to):
            b, low = divmod(row * pitch, LANES)
            shift = lax.rem(to + 2 * LANES - low - skipped, LANES)
            turned = moved(totals[b], shift)
            if low + pitch - 1 <= LANES:
                return turned
            return jnp.where(lane < to + LANES - low - skipped, turned, moved(totals[b + 1], shift))

        def rows_of(row):
            return jnp.where(lane < half, columns_of(row, 0), columns_of(row + 1, half))

        outermost, inner = rows_of(0), rows_of(2)
        outs[0][t] = jnp.where(outer, outermost, inner).astype(jnp.bfloat16)
        outs[1][t] = jnp.where(outer, inner, outermost).astype(jnp.bfloat16)

    def tile_sums(places):
        cuts = {t: begun_rows(t, channels) if plan["begun"] else 0 for t, _ in places}
        start, stop = min(cuts.values()), w_ref.shape[1]
        rhs = []
        for t, b in places:
            frames = [(earlier_ref, t + a) if t + a < PAIR else (shifted_ref, t + a - PAIR) for a in (2, 1, 0)]
            rhs.append(padded_rows([block_lines(ref, j, b) for ref, j in frames], cuts[t], stop, start, stop))
        return jnp.dot(w_ref[:, start:], jnp.concatenate(rhs, axis=1), preferred_element_type=jnp.float32)

    by_frames(lanes, tile_sums, finish)
    if sends:
        write_message(outs[2], whole_acts, plan["rows"] * pitch)


def conv(chain, plan, begun, earlier, shifted, values, weight, columns):
    _, _, channels, lanes = shifted.shape
    pitch, half, received = plan["pitch"], plan["half"], plan["received"]
    if plan["last"]:
        out_shape = (jax.ShapeDtypeStruct((PAIR, channels, LANES), jnp.bfloat16),) * 2
    else:
        out_shape = (
            jax.ShapeDtypeStruct((PAIR, channels, lanes), jnp.bfloat16),
            jax.ShapeDtypeStruct((PAIR, 3, channels, rounded((plan["rows"] - 1) * pitch)), jnp.bfloat16),
        )
        if plan["sends"]:
            out_shape += (message_shape(channels, plan["rows"] * pitch),)
    if plan["builds"]:
        out_shape += far_shapes(plan["rows_near"] // 2, pitch - 1 - half, channels, half)
    return chain.add(
        functools.partial(conv_kernel, plan),
        [shifted, values, weight, columns, *begun, *earlier],
        out_shape,
        [pltpu.VMEM((PAIR, 3, channels, lanes), jnp.bfloat16)] * received,
        54 * channels * channels * PAIR * lanes * (1 + plan["builds"]),
    )


def join_kernel(pair, kept_ref, got_ref, *refs):
    out_ref, lines_ref, sems = refs[-3:]
    _, rows, _, width = lines_ref.shape
    half = width // 2
    core, group, _ = place()
    first = core == 0
    left_half = lane_of(width) < half
    copies = []
    for t in range(PAIR):
        mine, theirs = kept_ref[t].astype(jnp.float32), got_ref[t].astype(jnp.float32)
        left, right = jnp.where(first, mine, theirs), jnp.where(first, theirs, mine)
        lines = (
            jnp.where(left_half, left, pltpu.roll(right, half, 1)),
            jnp.where(left_half, pltpu.roll(left, half, 1), right),
        )
        for j in range(rows):
            lines_ref[t, j + group * (rows - 1 - 2 * j)] = lines[j].astype(jnp.bfloat16)
        copies.append(pltpu.make_async_copy(lines_ref.at[t], out_ref.at[PAIR * pair + t], sems.at[t]))
        copies[-1].start()
    for copy in copies:
        copy.wait()


def join(pair, kept, got, shape, *so_far):
    return pl.pallas_call(
        functools.partial(join_kernel, pair),
        out_shape=jax.ShapeDtypeStruct(shape, jnp.bfloat16),
        in_specs=[VMEM, VMEM] + [ANY] * len(so_far),
        out_specs=ANY,
        scratch_shapes=[pltpu.VMEM((PAIR,) + shape[1:], jnp.bfloat16), pltpu.SemaphoreType.DMA((PAIR,))],
        input_output_aliases={2: 0} if so_far else {},
        compiler_params=pltpu.CompilerParams(vmem_limit_bytes=LIMIT),
        name="join",
    )(kept, got, *so_far)


def on_device(latents, conv_weight, norm_gains, biases):
    layers = conv_weight.shape[0]
    frames, rows, channels, width = latents.shape
    strips, blocks = lax.axis_size("rows"), lax.axis_size("tm")
    assert strips == 4 and rows == 2 and frames % PAIR == 0 and width == LANES

    def mate_of(block):
        return lax.ppermute(block, "rows", [(i, i ^ 1) for i in range(strips)])

    def earlier_of(block):
        return lax.ppermute(block, "tm", [(i, i + 1) for i in range(blocks - 1)])

    def beyond_of(block):
        return lax.ppermute(block, "rows", [(i, i ^ 2) for i in range(strips)])

    mate = mate_of(latents)
    pairs = frames // PAIR
    own = split(latents)
    far = beyond_of(own[-1])
    row_values = jnp.concatenate([norm_gains, biases], axis=0)
    weight, columns = weights(conv_weight, row_values)
    near_values, near_act, near_sent = near(layers, mate, row_values, own)
    came = [beyond_of(block) for block in near_sent]
    far, weight, columns, near_values, near_act = lax.optimization_barrier(
        (far, weight, columns, near_values, near_act)
    )
    values, shifted = [None] * pairs, [None] * pairs
    values[-1], shifted[-1], send = beyond(layers, columns, far, mate_of(far), near_values[-1], near_act[-1])
    halo = earlier_of(send)
    next_begun = layer_begun = None
    chain = Chain()
    first_begun = begin(chain, shifted[-1], weight[0])
    chain.run("begin")
    first_begun = now(first_begun)
    *came, first_begun = lax.optimization_barrier((*came, first_begun))
    parts = [(came[p], near_values[p], near_act[p]) for p in range(pairs - 1)]
    half = width // 2
    pitch = half + layers + 1
    for layer in range(layers):
        last = layer == layers - 1
        rows_left = 2 * rows + layers - 1 - layer
        results = [None] * pairs
        for p in reversed(range(pairs)):
            builds = layer == 0 and p > 0
            earlier = (halo,) if p == 0 else parts[p - 1] if builds else (shifted[p - 1],)
            begun = ()
            if builds and p == pairs - 1:
                begun = (first_begun,)
            elif layer == 0 and p == 0 and next_begun is not None:
                begun = (next_begun,)
            elif layer == 1 and p == pairs - 1 and layer_begun is not None:
                begun = (layer_begun,)
            elif builds or (p == 0 and (last or layer == 0)):
                begun = (begin(chain, shifted[p], weight[layer]),)
            if last and p == 0:
                chain.run("convs")
            plan = {
                "layer": layer,
                "begun": len(begun) > 0,
                "rows_near": 2 * rows,
                "last": last,
                "sends": p == pairs - 1 and not last,
                "received": p == 0,
                "builds": builds,
                "inputs": len(earlier),
                "pitch": pitch,
                "half": half,
                "rows": rows_left,
            }
            outs = list(conv(chain, plan, begun, earlier, shifted[p], values[p], weight[layer], columns))
            if builds:
                shifted[p - 1], values[p - 1] = outs.pop(), outs.pop()
            results[p] = outs
            if layer == 0 and p == 0:
                chain.run("convs")
            if plan["sends"]:
                if layer == 0 and p == 1:
                    next_begun = begin(chain, shifted[0], weight[0])
                chain.run("convs")
                arriving = earlier_of(now(outs[2]))
                if layer == 0 and p == 1:
                    layer_begun = begin(chain, outs[1], weight[1])
                    chain.run("begin")
                    halo, layer_begun = lax.optimization_barrier((halo, now(layer_begun)))
        values, shifted = [r[0] for r in results], [r[1] for r in results]
        if not last:
            halo = arriving
    chain.run("convs")
    result = ()
    for p in reversed(range(pairs)):
        result = (join(p, now(values[p]), mate_of(now(shifted[p])), latents.shape, *result),)
    return result[0]


def solution(mesh):
    in_specs = (P(("clips", "tm"), "rows", None, None), P(), P(), P())
    out_specs = P(("clips", "tm"), "rows", None, None)
    return jax.shard_map(on_device, mesh=mesh, in_specs=in_specs, out_specs=out_specs, check_vma=False)
```

```python
import functools

import jax
import jax.numpy as jnp
from jax import lax
from jax.experimental import pallas as pl
from jax.experimental.pallas import tpu as pltpu
from jax.sharding import PartitionSpec as P

EPSILON = 1e-06
PAIR = 2
LANES = 128
TILE = 256
VMEM = pl.BlockSpec(memory_space=pltpu.VMEM)
ANY = pl.BlockSpec(memory_space=pl.ANY)
LIMIT = 24 * 1024 * 1024
LARGE = 44 * 1024 * 1024


def place():
    strip = lax.axis_index("rows").astype(jnp.int32)
    core, group = strip & 1, strip >> 1
    return core, group, core == group


def rounded(lanes):
    return -(-lanes // LANES) * LANES


def column(row):
    return jnp.transpose(jnp.broadcast_to(row, (LANES, row.shape[1])))


def lane_of(lanes):
    return lax.broadcasted_iota(jnp.int32, (1, lanes), 1)


def filled(lanes, pitch):
    lane = lane_of(lanes)
    gaps = lane < 0
    for end in range(pitch - 1, lanes, pitch):
        gaps = gaps | (lane == end)
    return jnp.where(gaps, 0.0, 1.0)


def activated(values, gain, mask):
    squares = jnp.mean(values * values, axis=0, keepdims=True)
    halved = values * (lax.rsqrt(squares + EPSILON) * (0.5 * mask)) * gain
    return (halved + halved * jnp.tanh(halved)).astype(jnp.bfloat16)


def weights_kernel(w_ref, rows_ref, *refs):
    outs, columns_ref, held_ref, sems = refs[:-3], refs[-3], refs[-2], refs[-1]
    layers, taps, channels_out, ins = w_ref.shape
    step = taps // 3
    places = [(layer, time_tap) for layer in range(layers) for time_tap in range(3)]
    copies = []
    for n, (layer, time_tap) in enumerate(places):
        part = pl.ds(step * time_tap, step)
        copies.append(pltpu.make_async_copy(w_ref.at[layer, part], held_ref.at[n], sems.at[n]))
        copies[-1].start()
    _, flipped, _ = place()
    for layer in range(layers):
        columns_ref[layer, 0] = column(rows_ref[layer : layer + 1, :])
        columns_ref[layer, 1] = column(rows_ref[layers + layer : layers + layer + 1, :])
    for n, (layer, time_tap) in enumerate(places):
        copies[n].wait()
        for row_tap in range(3):
            source = 3 * (row_tap + flipped * (2 - 2 * row_tap))
            at = (3 * (2 - time_tap) + row_tap) * ins
            outs[layer][:, at : at + ins] = held_ref[n, pl.ds(source, 3)].reshape(3 * channels_out, ins)


def weights(conv_weight, rows):
    layers, taps, outs, ins = conv_weight.shape
    one = jax.ShapeDtypeStruct((3 * outs, 9 * ins), conv_weight.dtype)
    results = pl.pallas_call(
        weights_kernel,
        out_shape=(one,) * layers + (jax.ShapeDtypeStruct((layers, 2, outs, LANES), jnp.float32),),
        in_specs=[ANY, VMEM],
        out_specs=(VMEM,) * (layers + 1),
        scratch_shapes=[
            pltpu.VMEM((3 * layers, taps // 3, outs, ins), conv_weight.dtype),
            pltpu.SemaphoreType.DMA((3 * layers,)),
        ],
        compiler_params=pltpu.CompilerParams(vmem_limit_bytes=LARGE),
        cost_estimate=pl.CostEstimate(flops=0, bytes_accessed=4 * conv_weight.size, transcendentals=0),
        name="weights",
    )(conv_weight, rows)
    return results[:-1], results[-1]


def split_kernel(in_ref, *out_refs):
    for p, out_ref in enumerate(out_refs):
        out_ref[...] = in_ref[PAIR * p : PAIR * (p + 1)]


def split(latents):
    pairs = latents.shape[0] // PAIR
    return pl.pallas_call(
        split_kernel,
        out_shape=(jax.ShapeDtypeStruct((PAIR,) + latents.shape[1:], latents.dtype),) * pairs,
        in_specs=[VMEM],
        out_specs=(VMEM,) * pairs,
        compiler_params=pltpu.CompilerParams(vmem_limit_bytes=LIMIT),
        name="split",
    )(latents)


def folds(channels, rest):
    fits = [n for n in (4, 3, 2) if n * rest <= LANES and channels % (16 * n) == 0]
    return fits[0] if fits else 1


def message_shape(channels, valid):
    whole, rest = divmod(PAIR * valid, LANES)
    lines = whole * channels + (channels // folds(channels, rest) if rest else 0)
    return jax.ShapeDtypeStruct((lines, LANES), jnp.bfloat16)


def write_message(ref, acts, valid):
    channels, width = acts[0].shape
    whole, rest = divmod(PAIR * valid, LANES)
    total = rounded(PAIR * valid)
    if total > width:
        acts = [jnp.concatenate([act, jnp.zeros((channels, total - width), jnp.bfloat16)], axis=1) for act in acts]
    first, second = acts[0], pltpu.roll(acts[1], valid, 1)
    lane = lane_of(LANES)
    for n in range(total // LANES):
        at = slice(n * LANES, (n + 1) * LANES)
        block = first[:, at] if at.stop <= valid else second[:, at]
        if at.start < valid < at.stop:
            mixed = jnp.where(lane < valid - at.start, first[:, at].astype(jnp.float32), second[:, at].astype(jnp.float32))
            block = mixed.astype(jnp.bfloat16)
        if n < whole:
            ref[n * channels : (n + 1) * channels] = block
            continue
        parts = folds(channels, rest)
        size, step = channels // parts, LANES // parts
        kept = jnp.where(lane < rest, block.astype(jnp.float32), 0.0)
        pieces = [kept[i * size : (i + 1) * size] for i in range(parts)]
        ref[n * channels :] = sum(
            piece if i == 0 else pltpu.roll(piece, i * step, 1) for i, piece in enumerate(pieces)
        ).astype(jnp.bfloat16)


def read_message(ref, channels, width, valid):
    whole, rest = divmod(PAIR * valid, LANES)
    blocks = [ref[n * channels : (n + 1) * channels] for n in range(whole)]
    if rest:
        parts = folds(channels, rest)
        folded = ref[whole * channels :]
        pieces = [folded if i == 0 else pltpu.roll(folded, LANES - i * (LANES // parts), 1) for i in range(parts)]
        blocks.append(pieces[0] if parts == 1 else jnp.concatenate(pieces, axis=0))
    both = jnp.concatenate(blocks, axis=1)
    return both[:, :width], pltpu.roll(both, both.shape[1] - valid, 1)[:, :width]


def spread(out_ref, index, act, pitch):
    lanes = out_ref.shape[3]
    above = pltpu.roll(act, pitch, 1)
    below = pltpu.roll(act, act.shape[1] - pitch, 1)
    edge = jnp.where(lane_of(LANES) < pitch, 0.0, above[:, :LANES].astype(jnp.float32))
    out_ref[index, 0, :, :LANES] = edge.astype(jnp.bfloat16)
    out_ref[index, 0, :, LANES:] = above[:, LANES:lanes]
    out_ref[index, 1] = act[:, :lanes]
    out_ref[index, 2] = below[:, :lanes]


def placed(blocks, core, row, window, line):
    pitch, width = window + 1, line.shape[1]
    lane = lane_of(LANES)
    block, low = divmod(row * pitch, LANES)
    shift = lax.rem(low + LANES - core * (width - window), LANES)
    turned = moved(line, shift)
    here = (lane >= low) & (lane < low + window)
    blocks[block] = blocks.get(block, 0.0) + jnp.where(here, turned, 0.0)
    if low + window > LANES:
        blocks[block + 1] = blocks.get(block + 1, 0.0) + jnp.where(lane < low + window - LANES, turned, 0.0)


def near_kernel(halo, pairs, mate_ref, gains_ref, *refs):
    own_refs, value_refs, act_refs = refs[:pairs], refs[pairs : 2 * pairs], refs[2 * pairs : 3 * pairs]
    send_refs = refs[3 * pairs :]
    frames, rows, _, width = mate_ref.shape
    window = width // 2 + halo
    core, group, outer = place()
    gain = column(gains_ref[0:1, :])
    done = act_refs[0].shape[2]
    mask = filled(done, window + 1)
    for f in range(frames):
        p, t = divmod(f, PAIR)
        blocks, sent = {}, {}
        for row in range(2 * rows):
            at = row % rows
            index = at + group * (rows - 1 - 2 * at)
            own, mate = own_refs[p][t, index], mate_ref[f, index]
            one, two = (own, mate) if row < rows else (mate, own)
            line = jnp.where(outer, one, two)
            placed(blocks, core, row, window, line)
            there = 4 * rows - 1 - row
            if p < pairs - 1 and there < 2 * rows + halo:
                placed(sent, core, there, window, line)
        for b in sent:
            send_refs[p][t, :, b * LANES - done : (b + 1) * LANES - done] = sent[b].astype(jnp.bfloat16)
        for b in blocks:
            part = slice(b * LANES, (b + 1) * LANES)
            value_refs[p][t, :, part] = blocks[b].astype(jnp.bfloat16)
            if part.stop <= done:
                act_refs[p][t, :, part] = activated(blocks[b], gain, mask[:, part])


def near(halo, mate, gains, own):
    frames, rows, channels, width = mate.shape
    pitch = width // 2 + halo + 1
    lanes = 2 * rows * pitch
    done = lanes // LANES * LANES
    pairs = len(own)
    sent = jax.ShapeDtypeStruct((PAIR, channels, rounded(lanes + halo * pitch) - done), jnp.bfloat16)
    outs = pl.pallas_call(
        functools.partial(near_kernel, halo, pairs),
        out_shape=(jax.ShapeDtypeStruct((PAIR, channels, rounded(lanes)), jnp.bfloat16),) * pairs
        + (jax.ShapeDtypeStruct((PAIR, channels, done), jnp.bfloat16),) * pairs
        + (sent,) * (pairs - 1),
        in_specs=[VMEM] * (2 + pairs),
        out_specs=(VMEM,) * (3 * pairs - 1),
        compiler_params=pltpu.CompilerParams(vmem_limit_bytes=LIMIT),
        cost_estimate=pl.CostEstimate(flops=40 * mate.size, bytes_accessed=8 * mate.size, transcendentals=2 * mate.size),
        name="near",
    )(mate, gains, *own)
    return outs[:pairs], outs[pairs : 2 * pairs], outs[2 * pairs :]


def far_blocks(halo, far_ref, mate_ref, t, blocks):
    _, rows, _, width = far_ref.shape
    core, group, outer = place()
    for row in range(2 * rows, 2 * rows + halo):
        local = 4 * rows - 1 - row
        at = local % rows
        index = at + (1 - group) * (rows - 1 - 2 * at)
        one, two = (mate_ref, far_ref) if local < rows else (far_ref, mate_ref)
        line = jnp.where(outer, one[t, index], two[t, index])
        placed(blocks, core, row, width // 2 + halo, line)


def add_far(pitch, valid, add, near_ref, act_ref, columns_ref, values_ref, shifted_ref, send_ref=None):
    lanes, done = values_ref.shape[2], act_ref.shape[2]
    mask = filled(lanes, pitch)
    whole_acts = []
    for t in range(PAIR):
        values_ref[t, :, :done] = near_ref[t, :, :done]
        acts = [act_ref[t]]
        blocks = {done // LANES: near_ref[t, :, done:].astype(jnp.float32)}
        add(t, blocks)
        for b in sorted(blocks):
            part = slice(b * LANES, (b + 1) * LANES)
            values_ref[t, :, part] = blocks[b].astype(jnp.bfloat16)
            acts.append(activated(blocks[b], columns_ref[0, 0], mask[:, part]))
        act = jnp.concatenate(acts, axis=1)
        spread(shifted_ref, t, act, pitch)
        whole_acts.append(act)
    if send_ref is not None:
        write_message(send_ref, whole_acts, valid)


def far_shapes(rows, halo, channels, half):
    pitch = half + halo + 1
    return (
        jax.ShapeDtypeStruct((PAIR, channels, rounded((2 * rows + halo) * pitch)), jnp.bfloat16),
        jax.ShapeDtypeStruct((PAIR, 3, channels, rounded((2 * rows + halo - 1) * pitch)), jnp.bfloat16),
    )


def beyond(halo, columns, *parts):
    far = parts[0]
    _, rows, channels, width = far.shape
    values, shifted = far_shapes(rows, halo, channels, width // 2)
    pitch = width // 2 + halo + 1
    valid = (2 * rows + halo) * pitch

    def kernel(columns_ref, far_ref, mate_ref, near_ref, act_ref, *outs):
        add = functools.partial(far_blocks, halo, far_ref, mate_ref)
        add_far(pitch, valid, add, near_ref, act_ref, columns_ref, *outs)

    return pl.pallas_call(
        kernel,
        out_shape=(values, shifted, message_shape(channels, valid)),
        in_specs=[VMEM] * 5,
        out_specs=(VMEM,) * 3,
        compiler_params=pltpu.CompilerParams(vmem_limit_bytes=LIMIT),
        cost_estimate=pl.CostEstimate(flops=40 * far.size, bytes_accessed=8 * far.size, transcendentals=2 * far.size),
        name="beyond",
    )(columns, *parts)


def by_taps(sums):
    channels, lanes = sums.shape[0] // 3, sums.shape[1]
    return [
        [sums[tap * channels : (tap + 1) * channels, at : at + LANES] for at in range(0, lanes, LANES)]
        for tap in range(3)
    ]


def moved(block, shift):
    return pltpu.roll(block, shift, 1).astype(jnp.float32)


def column_sums(taps):
    lane = lane_of(LANES)
    left, middle, right = taps
    lefts = [pltpu.roll(block, 1, 1) for block in left]
    rights = [pltpu.roll(block, LANES - 1, 1) for block in right] + [0.0]
    return [
        jnp.where(lane == 0, lefts[b - 1] if b else 0.0, lefts[b])
        + middle[b]
        + jnp.where(lane == LANES - 1, rights[b + 1], rights[b])
        for b in range(len(middle))
    ]


def begun_rows(t, channels):
    return (t + 1) * 3 * channels // TILE * TILE


def rows_between(lines, start, stop):
    taken, at = [], 0
    for part in lines:
        low, high = max(start - at, 0), min(stop - at, part.shape[0])
        if low < high:
            taken.append(part[low:high])
        at += part.shape[0]
    return jnp.concatenate(taken, axis=0)


def block_lines(ref, frame, b):
    return ref[frame, :, :, b * LANES : (b + 1) * LANES].reshape(3 * ref.shape[2], LANES)


def padded_rows(lines, start, stop, low, high):
    parts = [rows_between(lines, start, stop)]
    if low < start:
        parts.insert(0, jnp.zeros((start - low, LANES), jnp.bfloat16))
    if stop < high:
        parts.append(jnp.zeros((high - stop, LANES), jnp.bfloat16))
    return parts[0] if len(parts) == 1 else jnp.concatenate(parts, axis=0)


def tiled(lanes):
    places = [(t, b) for t in range(PAIR) for b in range(lanes // LANES)]
    side = TILE // LANES
    return [places[n : n + side] for n in range(0, len(places), side)]


def by_frames(lanes, tile_sums, finish):
    taps = {t: [[], [], []] for t in range(PAIR)}
    for places in tiled(lanes):
        sums = by_taps(tile_sums(places))
        for i, (t, b) in enumerate(places):
            for tap in range(3):
                taps[t][tap].append(sums[tap][i])
        for t, b in places:
            if b == lanes // LANES - 1:
                finish(t, taps[t])


def begin_kernel(shifted_ref, w_ref, out_ref):
    _, _, channels, lanes = shifted_ref.shape

    def tile_sums(places):
        depth = max(begun_rows(t, channels) for t, _ in places)
        rhs = [
            padded_rows(
                [block_lines(shifted_ref, j, b) for j in range(t, -1, -1)],
                0,
                begun_rows(t, channels),
                0,
                depth,
            )
            for t, b in places
        ]
        return jnp.dot(w_ref[:, :depth], jnp.concatenate(rhs, axis=1), preferred_element_type=jnp.float32)

    def finish(t, taps):
        for b, block in enumerate(column_sums(taps)):
            out_ref[t, :, b * LANES : (b + 1) * LANES] = block

    by_frames(lanes, tile_sums, finish)


class Later:
    def __init__(self, shape):
        self.shape, self.dtype, self.value = shape.shape, shape.dtype, None


def now(x):
    return x.value if isinstance(x, Later) else x


class Chain:
    def __init__(self):
        self.steps = []

    def add(self, kernel, inputs, out_shape, scratch, flops):
        outs = [Later(shape) for shape in out_shape]
        self.steps.append((kernel, inputs, outs, out_shape, scratch, flops))
        return outs

    def run(self, name):
        steps, self.steps = self.steps, []
        made = {id(out): n for n, out in enumerate(out for step in steps for out in step[2])}
        arrays = []
        for step in steps:
            for x in step[1]:
                if id(x) not in made and not any(now(x) is y for y in arrays):
                    arrays.append(now(x))
        at = [[("out", made[id(x)]) if id(x) in made else ("in", next(i for i, y in enumerate(arrays) if y is now(x))) for x in step[1]] for step in steps]
        out_shape = [shape for step in steps for shape in step[3]]
        scratch = [shape for step in steps for shape in step[4]]

        def kernel(*refs):
            ins, outs, rest = refs[: len(arrays)], refs[len(arrays) : len(arrays) + len(out_shape)], refs[len(arrays) + len(out_shape) :]
            first, held = 0, 0
            for step, places in zip(steps, at):
                own, kept = outs[first : first + len(step[3])], rest[held : held + len(step[4])]
                first, held = first + len(own), held + len(kept)
                step[0](*[(outs if kind == "out" else ins)[n] for kind, n in places], *own, *kept)

        results = pl.pallas_call(
            kernel,
            out_shape=tuple(out_shape),
            in_specs=[VMEM] * len(arrays),
            out_specs=(VMEM,) * len(out_shape),
            scratch_shapes=scratch,
            compiler_params=pltpu.CompilerParams(vmem_limit_bytes=LIMIT),
            cost_estimate=pl.CostEstimate(flops=sum(step[5] for step in steps), bytes_accessed=0, transcendentals=0),
            name=name,
        )(*arrays)
        for out, value in zip((out for step in steps for out in step[2]), results):
            out.value = value


def begin(chain, shifted, weight):
    _, _, channels, lanes = shifted.shape
    out = jax.ShapeDtypeStruct((PAIR, channels, lanes), jnp.float32)
    return chain.add(begin_kernel, [shifted, weight], [out], [], 0)[0]


def conv_kernel(plan, shifted_ref, values_ref, w_ref, columns_ref, *refs):
    layer, pitch, half, received = plan["layer"], plan["pitch"], plan["half"], plan["received"]
    last, sends = plan["last"], plan["sends"]
    refs = list(refs)
    begun_ref = refs.pop(0) if plan["begun"] else None
    earlier_refs = [refs.pop(0) for _ in range(plan["inputs"])]
    earlier_ref = refs.pop() if received else earlier_refs[0]
    if received:
        frames = read_message(earlier_refs[0], values_ref.shape[1], values_ref.shape[2], (plan["rows"] + 1) * pitch)
        for t in range(PAIR):
            spread(earlier_ref, t, frames[t], pitch)
    outs = refs
    if plan["builds"]:
        earlier_ref = outs.pop()
        came_ref, near_ref, act_ref = earlier_refs
        done = act_ref.shape[2]

        def add(t, blocks):
            for at in range(0, came_ref.shape[2], LANES):
                b = (done + at) // LANES
                blocks[b] = blocks.get(b, 0.0) + came_ref[t, :, at : at + LANES].astype(jnp.float32)

        add_far(pitch, 0, add, near_ref, act_ref, columns_ref, outs.pop(), earlier_ref)
    _, _, channels, lanes = shifted_ref.shape
    chunks = lanes // LANES
    lane = lane_of(LANES)

    bias = columns_ref[layer, 1]
    whole_acts = []
    if not last:
        mask = filled(lanes, pitch)
        gain = columns_ref[layer + 1, 0]

    def finish(t, taps):
        totals, acts = [], []
        for b, conv in enumerate(column_sums(taps)):
            at = slice(b * LANES, (b + 1) * LANES)
            if begun_ref is not None:
                conv = conv + begun_ref[t, :, at]
            total = (values_ref[t, :, at].astype(jnp.float32) + conv + bias).astype(jnp.bfloat16)
            totals.append(total)
            if last:
                continue
            outs[0][t, :, at] = total
            acts.append(activated(total.astype(jnp.float32), gain, mask[:, at]))
        if not last:
            whole_acts.append(jnp.concatenate(acts, axis=1))
            spread(outs[1], t, whole_acts[-1], pitch)
            return
        core, _, outer = place()
        skipped = core * (pitch - 1 - half)

        def columns_of(row, to):
            b, low = divmod(row * pitch, LANES)
            shift = lax.rem(to + 2 * LANES - low - skipped, LANES)
            turned = moved(totals[b], shift)
            if low + pitch - 1 <= LANES:
                return turned
            return jnp.where(lane < to + LANES - low - skipped, turned, moved(totals[b + 1], shift))

        def rows_of(row):
            return jnp.where(lane < half, columns_of(row, 0), columns_of(row + 1, half))

        outermost, inner = rows_of(0), rows_of(2)
        outs[0][t] = jnp.where(outer, outermost, inner).astype(jnp.bfloat16)
        outs[1][t] = jnp.where(outer, inner, outermost).astype(jnp.bfloat16)

    def tile_sums(places):
        cuts = {t: begun_rows(t, channels) if plan["begun"] else 0 for t, _ in places}
        start, stop = min(cuts.values()), w_ref.shape[1]
        rhs = []
        for t, b in places:
            frames = [(earlier_ref, t + a) if t + a < PAIR else (shifted_ref, t + a - PAIR) for a in (2, 1, 0)]
            rhs.append(padded_rows([block_lines(ref, j, b) for ref, j in frames], cuts[t], stop, start, stop))
        return jnp.dot(w_ref[:, start:], jnp.concatenate(rhs, axis=1), preferred_element_type=jnp.float32)

    by_frames(lanes, tile_sums, finish)
    if sends:
        write_message(outs[2], whole_acts, plan["rows"] * pitch)


def conv(chain, plan, begun, earlier, shifted, values, weight, columns):
    _, _, channels, lanes = shifted.shape
    pitch, half, received = plan["pitch"], plan["half"], plan["received"]
    if plan["last"]:
        out_shape = (jax.ShapeDtypeStruct((PAIR, channels, LANES), jnp.bfloat16),) * 2
    else:
        out_shape = (
            jax.ShapeDtypeStruct((PAIR, channels, lanes), jnp.bfloat16),
            jax.ShapeDtypeStruct((PAIR, 3, channels, rounded((plan["rows"] - 1) * pitch)), jnp.bfloat16),
        )
        if plan["sends"]:
            out_shape += (message_shape(channels, plan["rows"] * pitch),)
    if plan["builds"]:
        out_shape += far_shapes(plan["rows_near"] // 2, pitch - 1 - half, channels, half)
    return chain.add(
        functools.partial(conv_kernel, plan),
        [shifted, values, weight, columns, *begun, *earlier],
        out_shape,
        [pltpu.VMEM((PAIR, 3, channels, lanes), jnp.bfloat16)] * received,
        54 * channels * channels * PAIR * lanes * (1 + plan["builds"]),
    )


def join_kernel(pair, kept_ref, got_ref, *refs):
    out_ref, lines_ref, sems = refs[-3:]
    _, rows, _, width = lines_ref.shape
    half = width // 2
    core, group, _ = place()
    first = core == 0
    left_half = lane_of(width) < half
    copies = []
    for t in range(PAIR):
        mine, theirs = kept_ref[t].astype(jnp.float32), got_ref[t].astype(jnp.float32)
        left, right = jnp.where(first, mine, theirs), jnp.where(first, theirs, mine)
        lines = (
            jnp.where(left_half, left, pltpu.roll(right, half, 1)),
            jnp.where(left_half, pltpu.roll(left, half, 1), right),
        )
        for j in range(rows):
            lines_ref[t, j + group * (rows - 1 - 2 * j)] = lines[j].astype(jnp.bfloat16)
        copies.append(pltpu.make_async_copy(lines_ref.at[t], out_ref.at[PAIR * pair + t], sems.at[t]))
        copies[-1].start()
    for copy in copies:
        copy.wait()


def join(pair, kept, got, shape, *so_far):
    return pl.pallas_call(
        functools.partial(join_kernel, pair),
        out_shape=jax.ShapeDtypeStruct(shape, jnp.bfloat16),
        in_specs=[VMEM, VMEM] + [ANY] * len(so_far),
        out_specs=ANY,
        scratch_shapes=[pltpu.VMEM((PAIR,) + shape[1:], jnp.bfloat16), pltpu.SemaphoreType.DMA((PAIR,))],
        input_output_aliases={2: 0} if so_far else {},
        compiler_params=pltpu.CompilerParams(vmem_limit_bytes=LIMIT),
        name="join",
    )(kept, got, *so_far)


def on_device(latents, conv_weight, norm_gains, biases):
    layers = conv_weight.shape[0]
    frames, rows, channels, width = latents.shape
    strips, blocks = lax.axis_size("rows"), lax.axis_size("tm")
    assert strips == 4 and rows == 2 and frames % PAIR == 0 and width == LANES

    def mate_of(block):
        return lax.ppermute(block, "rows", [(i, i ^ 1) for i in range(strips)])

    def earlier_of(block):
        return lax.ppermute(block, "tm", [(i, i + 1) for i in range(blocks - 1)])

    def beyond_of(block):
        return lax.ppermute(block, "rows", [(i, i ^ 2) for i in range(strips)])

    mate = mate_of(latents)
    pairs = frames // PAIR
    own = split(latents)
    far = beyond_of(own[-1])
    row_values = jnp.concatenate([norm_gains, biases], axis=0)
    weight, columns = weights(conv_weight, row_values)
    near_values, near_act, near_sent = near(layers, mate, row_values, own)
    came = [beyond_of(block) for block in near_sent]
    far, weight, columns, near_values, near_act = lax.optimization_barrier(
        (far, weight, columns, near_values, near_act)
    )
    values, shifted = [None] * pairs, [None] * pairs
    values[-1], shifted[-1], send = beyond(layers, columns, far, mate_of(far), near_values[-1], near_act[-1])
    halo = earlier_of(send)
    next_begun = layer_begun = None
    chain = Chain()
    first_begun = begin(chain, shifted[-1], weight[0])
    chain.run("begin")
    first_begun = now(first_begun)
    *came, first_begun = lax.optimization_barrier((*came, first_begun))
    parts = [(came[p], near_values[p], near_act[p]) for p in range(pairs - 1)]
    half = width // 2
    pitch = half + layers + 1
    for layer in range(layers):
        last = layer == layers - 1
        rows_left = 2 * rows + layers - 1 - layer
        results = [None] * pairs
        for p in reversed(range(pairs)):
            builds = layer == 0 and p > 0
            earlier = (halo,) if p == 0 else parts[p - 1] if builds else (shifted[p - 1],)
            begun = ()
            if builds and p == pairs - 1:
                begun = (first_begun,)
            elif layer == 0 and p == 0 and next_begun is not None:
                begun = (next_begun,)
            elif layer == 1 and p == pairs - 1 and layer_begun is not None:
                begun = (layer_begun,)
            elif builds or (p == 0 and layer == 0):
                begun = (begin(chain, shifted[p], weight[layer]),)
            if last and p == 0:
                chain.run("convs")
            plan = {
                "layer": layer,
                "begun": len(begun) > 0,
                "rows_near": 2 * rows,
                "last": last,
                "sends": p == pairs - 1 and not last,
                "received": p == 0,
                "builds": builds,
                "inputs": len(earlier),
                "pitch": pitch,
                "half": half,
                "rows": rows_left,
            }
            outs = list(conv(chain, plan, begun, earlier, shifted[p], values[p], weight[layer], columns))
            if builds:
                shifted[p - 1], values[p - 1] = outs.pop(), outs.pop()
            results[p] = outs
            if layer == 0 and p == 0:
                chain.run("convs")
            if plan["sends"]:
                if layer == 0 and p == 1:
                    next_begun = begin(chain, shifted[0], weight[0])
                chain.run("convs")
                arriving = earlier_of(now(outs[2]))
                if layer == 0 and p == 1:
                    layer_begun = begin(chain, outs[1], weight[1])
                    chain.run("begin")
                    halo, layer_begun = lax.optimization_barrier((halo, now(layer_begun)))
        values, shifted = [r[0] for r in results], [r[1] for r in results]
        if not last:
            halo = arriving
    chain.run("convs")
    result = ()
    for p in reversed(range(pairs)):
        result = (join(p, now(values[p]), mate_of(now(shifted[p])), latents.shape, *result),)
    return result[0]


def solution(mesh):
    in_specs = (P(("clips", "tm"), "rows", None, None), P(), P(), P())
    out_specs = P(("clips", "tm"), "rows", None, None)
    return jax.shard_map(on_device, mesh=mesh, in_specs=in_specs, out_specs=out_specs, check_vma=False)
```

```python
import functools

import jax
import jax.numpy as jnp
from jax import lax
from jax.experimental import pallas as pl
from jax.experimental.pallas import tpu as pltpu
from jax.sharding import PartitionSpec as P

EPSILON = 1e-06
PAIR = 2
LANES = 128
TILE = 256
VMEM = pl.BlockSpec(memory_space=pltpu.VMEM)
ANY = pl.BlockSpec(memory_space=pl.ANY)
LIMIT = 24 * 1024 * 1024
LARGE = 44 * 1024 * 1024


def place():
    strip = lax.axis_index("rows").astype(jnp.int32)
    core, group = strip & 1, strip >> 1
    return core, group, core == group


def rounded(lanes):
    return -(-lanes // LANES) * LANES


def column(row):
    return jnp.transpose(jnp.broadcast_to(row, (LANES, row.shape[1])))


def lane_of(lanes):
    return lax.broadcasted_iota(jnp.int32, (1, lanes), 1)


def filled(lanes, pitch):
    lane = lane_of(lanes)
    gaps = lane < 0
    for end in range(pitch - 1, lanes, pitch):
        gaps = gaps | (lane == end)
    return jnp.where(gaps, 0.0, 1.0)


def activated(values, gain, mask):
    squares = jnp.mean(values * values, axis=0, keepdims=True)
    halved = values * (lax.rsqrt(squares + EPSILON) * (0.5 * mask)) * gain
    return (halved + halved * jnp.tanh(halved)).astype(jnp.bfloat16)


def weights_kernel(w_ref, rows_ref, *refs):
    outs, columns_ref, held_ref, sems = refs[:-3], refs[-3], refs[-2], refs[-1]
    layers, taps, channels_out, ins = w_ref.shape
    step = taps // 3
    places = [(layer, time_tap) for layer in range(layers) for time_tap in range(3)]
    copies = []
    for n, (layer, time_tap) in enumerate(places):
        part = pl.ds(step * time_tap, step)
        copies.append(pltpu.make_async_copy(w_ref.at[layer, part], held_ref.at[n], sems.at[n]))
        copies[-1].start()
    _, flipped, _ = place()
    for layer in range(layers):
        columns_ref[layer, 0] = column(rows_ref[layer : layer + 1, :])
        columns_ref[layer, 1] = column(rows_ref[layers + layer : layers + layer + 1, :])
    for n, (layer, time_tap) in enumerate(places):
        copies[n].wait()
        for row_tap in range(3):
            source = 3 * (row_tap + flipped * (2 - 2 * row_tap))
            at = (3 * (2 - time_tap) + row_tap) * ins
            outs[layer][:, at : at + ins] = held_ref[n, pl.ds(source, 3)].reshape(3 * channels_out, ins)


def weights(conv_weight, rows):
    layers, taps, outs, ins = conv_weight.shape
    one = jax.ShapeDtypeStruct((3 * outs, 9 * ins), conv_weight.dtype)
    results = pl.pallas_call(
        weights_kernel,
        out_shape=(one,) * layers + (jax.ShapeDtypeStruct((layers, 2, outs, LANES), jnp.float32),),
        in_specs=[ANY, VMEM],
        out_specs=(VMEM,) * (layers + 1),
        scratch_shapes=[
            pltpu.VMEM((3 * layers, taps // 3, outs, ins), conv_weight.dtype),
            pltpu.SemaphoreType.DMA((3 * layers,)),
        ],
        compiler_params=pltpu.CompilerParams(vmem_limit_bytes=LARGE),
        cost_estimate=pl.CostEstimate(flops=0, bytes_accessed=4 * conv_weight.size, transcendentals=0),
        name="weights",
    )(conv_weight, rows)
    return results[:-1], results[-1]


def split_kernel(in_ref, *out_refs):
    for p, out_ref in enumerate(out_refs):
        out_ref[...] = in_ref[PAIR * p : PAIR * (p + 1)]


def split(latents):
    pairs = latents.shape[0] // PAIR
    return pl.pallas_call(
        split_kernel,
        out_shape=(jax.ShapeDtypeStruct((PAIR,) + latents.shape[1:], latents.dtype),) * pairs,
        in_specs=[VMEM],
        out_specs=(VMEM,) * pairs,
        compiler_params=pltpu.CompilerParams(vmem_limit_bytes=LIMIT),
        name="split",
    )(latents)


def folds(channels, rest):
    fits = [n for n in (4, 3, 2) if n * rest <= LANES and channels % (16 * n) == 0]
    return fits[0] if fits else 1


def message_shape(channels, valid):
    whole, rest = divmod(PAIR * valid, LANES)
    lines = whole * channels + (channels // folds(channels, rest) if rest else 0)
    return jax.ShapeDtypeStruct((lines, LANES), jnp.bfloat16)


def write_message(ref, acts, valid):
    channels, width = acts[0].shape
    whole, rest = divmod(PAIR * valid, LANES)
    total = rounded(PAIR * valid)
    if total > width:
        acts = [jnp.concatenate([act, jnp.zeros((channels, total - width), jnp.bfloat16)], axis=1) for act in acts]
    first, second = acts[0], pltpu.roll(acts[1], valid, 1)
    lane = lane_of(LANES)
    for n in range(total // LANES):
        at = slice(n * LANES, (n + 1) * LANES)
        block = first[:, at] if at.stop <= valid else second[:, at]
        if at.start < valid < at.stop:
            mixed = jnp.where(lane < valid - at.start, first[:, at].astype(jnp.float32), second[:, at].astype(jnp.float32))
            block = mixed.astype(jnp.bfloat16)
        if n < whole:
            ref[n * channels : (n + 1) * channels] = block
            continue
        parts = folds(channels, rest)
        size, step = channels // parts, LANES // parts
        kept = jnp.where(lane < rest, block.astype(jnp.float32), 0.0)
        pieces = [kept[i * size : (i + 1) * size] for i in range(parts)]
        ref[n * channels :] = sum(
            piece if i == 0 else pltpu.roll(piece, i * step, 1) for i, piece in enumerate(pieces)
        ).astype(jnp.bfloat16)


def read_message(ref, channels, width, valid):
    whole, rest = divmod(PAIR * valid, LANES)
    blocks = [ref[n * channels : (n + 1) * channels] for n in range(whole)]
    if rest:
        parts = folds(channels, rest)
        folded = ref[whole * channels :]
        pieces = [folded if i == 0 else pltpu.roll(folded, LANES - i * (LANES // parts), 1) for i in range(parts)]
        blocks.append(pieces[0] if parts == 1 else jnp.concatenate(pieces, axis=0))
    both = jnp.concatenate(blocks, axis=1)
    return both[:, :width], pltpu.roll(both, both.shape[1] - valid, 1)[:, :width]


def spread(out_ref, index, act, pitch):
    lanes = out_ref.shape[3]
    above = pltpu.roll(act, pitch, 1)
    below = pltpu.roll(act, act.shape[1] - pitch, 1)
    edge = jnp.where(lane_of(LANES) < pitch, 0.0, above[:, :LANES].astype(jnp.float32))
    out_ref[index, 0, :, :LANES] = edge.astype(jnp.bfloat16)
    out_ref[index, 0, :, LANES:] = above[:, LANES:lanes]
    out_ref[index, 1] = act[:, :lanes]
    out_ref[index, 2] = below[:, :lanes]


def placed(blocks, core, row, window, line):
    pitch, width = window + 1, line.shape[1]
    lane = lane_of(LANES)
    block, low = divmod(row * pitch, LANES)
    shift = lax.rem(low + LANES - core * (width - window), LANES)
    turned = moved(line, shift)
    here = (lane >= low) & (lane < low + window)
    blocks[block] = blocks.get(block, 0.0) + jnp.where(here, turned, 0.0)
    if low + window > LANES:
        blocks[block + 1] = blocks.get(block + 1, 0.0) + jnp.where(lane < low + window - LANES, turned, 0.0)


def near_kernel(halo, pairs, mate_ref, gains_ref, *refs):
    own_refs, value_refs, act_refs = refs[:pairs], refs[pairs : 2 * pairs], refs[2 * pairs : 3 * pairs]
    send_refs = refs[3 * pairs :]
    frames, rows, _, width = mate_ref.shape
    window = width // 2 + halo
    core, group, outer = place()
    gain = column(gains_ref[0:1, :])
    done = act_refs[0].shape[2]
    mask = filled(done, window + 1)
    for f in range(frames):
        p, t = divmod(f, PAIR)
        blocks, sent = {}, {}
        for row in range(2 * rows):
            at = row % rows
            index = at + group * (rows - 1 - 2 * at)
            own, mate = own_refs[p][t, index], mate_ref[f, index]
            one, two = (own, mate) if row < rows else (mate, own)
            line = jnp.where(outer, one, two)
            placed(blocks, core, row, window, line)
            there = 4 * rows - 1 - row
            if p < pairs - 1 and there < 2 * rows + halo:
                placed(sent, core, there, window, line)
        for b in sent:
            send_refs[p][t, :, b * LANES - done : (b + 1) * LANES - done] = sent[b].astype(jnp.bfloat16)
        for b in blocks:
            part = slice(b * LANES, (b + 1) * LANES)
            value_refs[p][t, :, part] = blocks[b].astype(jnp.bfloat16)
            if part.stop <= done:
                act_refs[p][t, :, part] = activated(blocks[b], gain, mask[:, part])


def near(halo, mate, gains, own):
    frames, rows, channels, width = mate.shape
    pitch = width // 2 + halo + 1
    lanes = 2 * rows * pitch
    done = lanes // LANES * LANES
    pairs = len(own)
    sent = jax.ShapeDtypeStruct((PAIR, channels, rounded(lanes + halo * pitch) - done), jnp.bfloat16)
    outs = pl.pallas_call(
        functools.partial(near_kernel, halo, pairs),
        out_shape=(jax.ShapeDtypeStruct((PAIR, channels, rounded(lanes)), jnp.bfloat16),) * pairs
        + (jax.ShapeDtypeStruct((PAIR, channels, done), jnp.bfloat16),) * pairs
        + (sent,) * (pairs - 1),
        in_specs=[VMEM] * (2 + pairs),
        out_specs=(VMEM,) * (3 * pairs - 1),
        compiler_params=pltpu.CompilerParams(vmem_limit_bytes=LIMIT),
        cost_estimate=pl.CostEstimate(flops=40 * mate.size, bytes_accessed=8 * mate.size, transcendentals=2 * mate.size),
        name="near",
    )(mate, gains, *own)
    return outs[:pairs], outs[pairs : 2 * pairs], outs[2 * pairs :]


def far_blocks(halo, far_ref, mate_ref, t, blocks):
    _, rows, _, width = far_ref.shape
    core, group, outer = place()
    for row in range(2 * rows, 2 * rows + halo):
        local = 4 * rows - 1 - row
        at = local % rows
        index = at + (1 - group) * (rows - 1 - 2 * at)
        one, two = (mate_ref, far_ref) if local < rows else (far_ref, mate_ref)
        line = jnp.where(outer, one[t, index], two[t, index])
        placed(blocks, core, row, width // 2 + halo, line)


def add_far(pitch, valid, add, near_ref, act_ref, columns_ref, values_ref, shifted_ref, send_ref=None):
    lanes, done = values_ref.shape[2], act_ref.shape[2]
    mask = filled(lanes, pitch)
    whole_acts = []
    for t in range(PAIR):
        values_ref[t, :, :done] = near_ref[t, :, :done]
        acts = [act_ref[t]]
        blocks = {done // LANES: near_ref[t, :, done:].astype(jnp.float32)}
        add(t, blocks)
        for b in sorted(blocks):
            part = slice(b * LANES, (b + 1) * LANES)
            values_ref[t, :, part] = blocks[b].astype(jnp.bfloat16)
            acts.append(activated(blocks[b], columns_ref[0, 0], mask[:, part]))
        act = jnp.concatenate(acts, axis=1)
        if send_ref is None:
            spread(shifted_ref, t, act, pitch)
        else:
            shifted_ref[t] = act
        whole_acts.append(act)
    if send_ref is not None:
        write_message(send_ref, whole_acts, valid)


def far_shapes(rows, halo, channels, half):
    pitch = half + halo + 1
    return (
        jax.ShapeDtypeStruct((PAIR, channels, rounded((2 * rows + halo) * pitch)), jnp.bfloat16),
        jax.ShapeDtypeStruct((PAIR, 3, channels, rounded((2 * rows + halo - 1) * pitch)), jnp.bfloat16),
    )


def beyond(halo, columns, *parts):
    far = parts[0]
    _, rows, channels, width = far.shape
    values, _ = far_shapes(rows, halo, channels, width // 2)
    pitch = width // 2 + halo + 1
    valid = (2 * rows + halo) * pitch

    def kernel(columns_ref, far_ref, mate_ref, near_ref, act_ref, *outs):
        add = functools.partial(far_blocks, halo, far_ref, mate_ref)
        add_far(pitch, valid, add, near_ref, act_ref, columns_ref, *outs)

    return pl.pallas_call(
        kernel,
        out_shape=(values, values, message_shape(channels, valid)),
        in_specs=[VMEM] * 5,
        out_specs=(VMEM,) * 3,
        compiler_params=pltpu.CompilerParams(vmem_limit_bytes=LIMIT),
        cost_estimate=pl.CostEstimate(flops=40 * far.size, bytes_accessed=8 * far.size, transcendentals=2 * far.size),
        name="beyond",
    )(columns, *parts)


def by_taps(sums):
    channels, lanes = sums.shape[0] // 3, sums.shape[1]
    return [
        [sums[tap * channels : (tap + 1) * channels, at : at + LANES] for at in range(0, lanes, LANES)]
        for tap in range(3)
    ]


def moved(block, shift):
    return pltpu.roll(block, shift, 1).astype(jnp.float32)


def column_sums(taps):
    lane = lane_of(LANES)
    left, middle, right = taps
    lefts = [pltpu.roll(block, 1, 1) for block in left]
    rights = [pltpu.roll(block, LANES - 1, 1) for block in right] + [0.0]
    return [
        jnp.where(lane == 0, lefts[b - 1] if b else 0.0, lefts[b])
        + middle[b]
        + jnp.where(lane == LANES - 1, rights[b + 1], rights[b])
        for b in range(len(middle))
    ]


def begun_rows(t, channels):
    return (t + 1) * 3 * channels // TILE * TILE


def rows_between(lines, start, stop):
    taken, at = [], 0
    for part in lines:
        low, high = max(start - at, 0), min(stop - at, part.shape[0])
        if low < high:
            taken.append(part[low:high])
        at += part.shape[0]
    return jnp.concatenate(taken, axis=0)


def block_lines(ref, frame, b):
    return ref[frame, :, :, b * LANES : (b + 1) * LANES].reshape(3 * ref.shape[2], LANES)


def padded_rows(lines, start, stop, low, high):
    parts = [rows_between(lines, start, stop)]
    if low < start:
        parts.insert(0, jnp.zeros((start - low, LANES), jnp.bfloat16))
    if stop < high:
        parts.append(jnp.zeros((high - stop, LANES), jnp.bfloat16))
    return parts[0] if len(parts) == 1 else jnp.concatenate(parts, axis=0)


def tiled(lanes):
    places = [(t, b) for t in range(PAIR) for b in range(lanes // LANES)]
    side = TILE // LANES
    return [places[n : n + side] for n in range(0, len(places), side)]


def by_frames(lanes, tile_sums, finish):
    taps = {t: [[], [], []] for t in range(PAIR)}
    for places in tiled(lanes):
        sums = by_taps(tile_sums(places))
        for i, (t, b) in enumerate(places):
            for tap in range(3):
                taps[t][tap].append(sums[tap][i])
        for t, b in places:
            if b == lanes // LANES - 1:
                finish(t, taps[t])


def begin_kernel(shifted_ref, w_ref, out_ref):
    _, _, channels, lanes = shifted_ref.shape

    def tile_sums(places):
        depth = max(begun_rows(t, channels) for t, _ in places)
        rhs = [
            padded_rows(
                [block_lines(shifted_ref, j, b) for j in range(t, -1, -1)],
                0,
                begun_rows(t, channels),
                0,
                depth,
            )
            for t, b in places
        ]
        return jnp.dot(w_ref[:, :depth], jnp.concatenate(rhs, axis=1), preferred_element_type=jnp.float32)

    def finish(t, taps):
        for b, block in enumerate(column_sums(taps)):
            out_ref[t, :, b * LANES : (b + 1) * LANES] = block

    by_frames(lanes, tile_sums, finish)


class Later:
    def __init__(self, shape):
        self.shape, self.dtype, self.value = shape.shape, shape.dtype, None


def now(x):
    return x.value if isinstance(x, Later) else x


class Chain:
    def __init__(self):
        self.steps = []

    def add(self, kernel, inputs, out_shape, scratch, flops):
        outs = [Later(shape) for shape in out_shape]
        self.steps.append((kernel, inputs, outs, out_shape, scratch, flops))
        return outs

    def run(self, name):
        steps, self.steps = self.steps, []
        made = {id(out): n for n, out in enumerate(out for step in steps for out in step[2])}
        arrays = []
        for step in steps:
            for x in step[1]:
                if id(x) not in made and not any(now(x) is y for y in arrays):
                    arrays.append(now(x))
        at = [[("out", made[id(x)]) if id(x) in made else ("in", next(i for i, y in enumerate(arrays) if y is now(x))) for x in step[1]] for step in steps]
        out_shape = [shape for step in steps for shape in step[3]]
        scratch = [shape for step in steps for shape in step[4]]

        def kernel(*refs):
            ins, outs, rest = refs[: len(arrays)], refs[len(arrays) : len(arrays) + len(out_shape)], refs[len(arrays) + len(out_shape) :]
            first, held = 0, 0
            for step, places in zip(steps, at):
                own, kept = outs[first : first + len(step[3])], rest[held : held + len(step[4])]
                first, held = first + len(own), held + len(kept)
                step[0](*[(outs if kind == "out" else ins)[n] for kind, n in places], *own, *kept)

        results = pl.pallas_call(
            kernel,
            out_shape=tuple(out_shape),
            in_specs=[VMEM] * len(arrays),
            out_specs=(VMEM,) * len(out_shape),
            scratch_shapes=scratch,
            compiler_params=pltpu.CompilerParams(vmem_limit_bytes=LIMIT),
            cost_estimate=pl.CostEstimate(flops=sum(step[5] for step in steps), bytes_accessed=0, transcendentals=0),
            name=name,
        )(*arrays)
        for out, value in zip((out for step in steps for out in step[2]), results):
            out.value = value


def spread_kernel(pitch, act_ref, shifted_ref):
    for t in range(PAIR):
        spread(shifted_ref, t, act_ref[t], pitch)


def begin(chain, shifted, weight):
    _, _, channels, lanes = shifted.shape
    out = jax.ShapeDtypeStruct((PAIR, channels, lanes), jnp.float32)
    return chain.add(begin_kernel, [shifted, weight], [out], [], 0)[0]


def conv_kernel(plan, shifted_ref, values_ref, w_ref, columns_ref, *refs):
    layer, pitch, half, received = plan["layer"], plan["pitch"], plan["half"], plan["received"]
    last, sends = plan["last"], plan["sends"]
    refs = list(refs)
    begun_ref = refs.pop(0) if plan["begun"] else None
    earlier_refs = [refs.pop(0) for _ in range(plan["inputs"])]
    earlier_ref = refs.pop() if received else earlier_refs[0]
    if received:
        frames = read_message(earlier_refs[0], values_ref.shape[1], values_ref.shape[2], (plan["rows"] + 1) * pitch)
        for t in range(PAIR):
            spread(earlier_ref, t, frames[t], pitch)
    outs = refs
    if plan["builds"]:
        earlier_ref = outs.pop()
        came_ref, near_ref, act_ref = earlier_refs
        done = act_ref.shape[2]

        def add(t, blocks):
            for at in range(0, came_ref.shape[2], LANES):
                b = (done + at) // LANES
                blocks[b] = blocks.get(b, 0.0) + came_ref[t, :, at : at + LANES].astype(jnp.float32)

        add_far(pitch, 0, add, near_ref, act_ref, columns_ref, outs.pop(), earlier_ref)
    _, _, channels, lanes = shifted_ref.shape
    chunks = lanes // LANES
    lane = lane_of(LANES)

    bias = columns_ref[layer, 1]
    whole_acts = []
    if not last:
        mask = filled(lanes, pitch)
        gain = columns_ref[layer + 1, 0]

    def finish(t, taps):
        totals, acts = [], []
        for b, conv in enumerate(column_sums(taps)):
            at = slice(b * LANES, (b + 1) * LANES)
            if begun_ref is not None:
                conv = conv + begun_ref[t, :, at]
            total = (values_ref[t, :, at].astype(jnp.float32) + conv + bias).astype(jnp.bfloat16)
            totals.append(total)
            if last:
                continue
            outs[0][t, :, at] = total
            acts.append(activated(total.astype(jnp.float32), gain, mask[:, at]))
        if not last:
            whole_acts.append(jnp.concatenate(acts, axis=1))
            spread(outs[1], t, whole_acts[-1], pitch)
            return
        core, _, outer = place()
        skipped = core * (pitch - 1 - half)

        def columns_of(row, to):
            b, low = divmod(row * pitch, LANES)
            shift = lax.rem(to + 2 * LANES - low - skipped, LANES)
            turned = moved(totals[b], shift)
            if low + pitch - 1 <= LANES:
                return turned
            return jnp.where(lane < to + LANES - low - skipped, turned, moved(totals[b + 1], shift))

        def rows_of(row):
            return jnp.where(lane < half, columns_of(row, 0), columns_of(row + 1, half))

        outermost, inner = rows_of(0), rows_of(2)
        outs[0][t] = jnp.where(outer, outermost, inner).astype(jnp.bfloat16)
        outs[1][t] = jnp.where(outer, inner, outermost).astype(jnp.bfloat16)

    def tile_sums(places):
        cuts = {t: begun_rows(t, channels) if plan["begun"] else 0 for t, _ in places}
        start, stop = min(cuts.values()), w_ref.shape[1]
        rhs = []
        for t, b in places:
            frames = [(earlier_ref, t + a) if t + a < PAIR else (shifted_ref, t + a - PAIR) for a in (2, 1, 0)]
            rhs.append(padded_rows([block_lines(ref, j, b) for ref, j in frames], cuts[t], stop, start, stop))
        return jnp.dot(w_ref[:, start:], jnp.concatenate(rhs, axis=1), preferred_element_type=jnp.float32)

    by_frames(lanes, tile_sums, finish)
    if sends:
        write_message(outs[2], whole_acts, plan["rows"] * pitch)


def conv(chain, plan, begun, earlier, shifted, values, weight, columns):
    _, _, channels, lanes = shifted.shape
    pitch, half, received = plan["pitch"], plan["half"], plan["received"]
    if plan["last"]:
        out_shape = (jax.ShapeDtypeStruct((PAIR, channels, LANES), jnp.bfloat16),) * 2
    else:
        out_shape = (
            jax.ShapeDtypeStruct((PAIR, channels, lanes), jnp.bfloat16),
            jax.ShapeDtypeStruct((PAIR, 3, channels, rounded((plan["rows"] - 1) * pitch)), jnp.bfloat16),
        )
        if plan["sends"]:
            out_shape += (message_shape(channels, plan["rows"] * pitch),)
    if plan["builds"]:
        out_shape += far_shapes(plan["rows_near"] // 2, pitch - 1 - half, channels, half)
    return chain.add(
        functools.partial(conv_kernel, plan),
        [shifted, values, weight, columns, *begun, *earlier],
        out_shape,
        [pltpu.VMEM((PAIR, 3, channels, lanes), jnp.bfloat16)] * received,
        54 * channels * channels * PAIR * lanes * (1 + plan["builds"]),
    )


def join_kernel(pair, kept_ref, got_ref, *refs):
    out_ref, lines_ref, sems = refs[-3:]
    _, rows, _, width = lines_ref.shape
    half = width // 2
    core, group, _ = place()
    first = core == 0
    left_half = lane_of(width) < half
    copies = []
    for t in range(PAIR):
        mine, theirs = kept_ref[t].astype(jnp.float32), got_ref[t].astype(jnp.float32)
        left, right = jnp.where(first, mine, theirs), jnp.where(first, theirs, mine)
        lines = (
            jnp.where(left_half, left, pltpu.roll(right, half, 1)),
            jnp.where(left_half, pltpu.roll(left, half, 1), right),
        )
        for j in range(rows):
            lines_ref[t, j + group * (rows - 1 - 2 * j)] = lines[j].astype(jnp.bfloat16)
        copies.append(pltpu.make_async_copy(lines_ref.at[t], out_ref.at[PAIR * pair + t], sems.at[t]))
        copies[-1].start()
    for copy in copies:
        copy.wait()


def join(pair, kept, got, shape, *so_far):
    return pl.pallas_call(
        functools.partial(join_kernel, pair),
        out_shape=jax.ShapeDtypeStruct(shape, jnp.bfloat16),
        in_specs=[VMEM, VMEM] + [ANY] * len(so_far),
        out_specs=ANY,
        scratch_shapes=[pltpu.VMEM((PAIR,) + shape[1:], jnp.bfloat16), pltpu.SemaphoreType.DMA((PAIR,))],
        input_output_aliases={2: 0} if so_far else {},
        compiler_params=pltpu.CompilerParams(vmem_limit_bytes=LIMIT),
        name="join",
    )(kept, got, *so_far)


def on_device(latents, conv_weight, norm_gains, biases):
    layers = conv_weight.shape[0]
    frames, rows, channels, width = latents.shape
    strips, blocks = lax.axis_size("rows"), lax.axis_size("tm")
    assert strips == 4 and rows == 2 and frames % PAIR == 0 and width == LANES

    def mate_of(block):
        return lax.ppermute(block, "rows", [(i, i ^ 1) for i in range(strips)])

    def earlier_of(block):
        return lax.ppermute(block, "tm", [(i, i + 1) for i in range(blocks - 1)])

    def beyond_of(block):
        return lax.ppermute(block, "rows", [(i, i ^ 2) for i in range(strips)])

    mate = mate_of(latents)
    pairs = frames // PAIR
    own = split(latents)
    far = beyond_of(own[-1])
    row_values = jnp.concatenate([norm_gains, biases], axis=0)
    weight, columns = weights(conv_weight, row_values)
    near_values, near_act, near_sent = near(layers, mate, row_values, own)
    came = [beyond_of(block) for block in near_sent]
    far, weight, columns, near_values, near_act = lax.optimization_barrier(
        (far, weight, columns, near_values, near_act)
    )
    values, shifted = [None] * pairs, [None] * pairs
    values[-1], last_act, send = beyond(layers, columns, far, mate_of(far), near_values[-1], near_act[-1])
    halo = earlier_of(send)
    next_begun = layer_begun = None
    chain = Chain()
    shift_shape = far_shapes(rows, layers, channels, width // 2)[1]
    spread_last = functools.partial(spread_kernel, width // 2 + layers + 1)
    shifted[-1] = chain.add(spread_last, [last_act], [shift_shape], [], 0)[0]
    first_begun = begin(chain, shifted[-1], weight[0])
    chain.run("begin")
    shifted[-1], first_begun = now(shifted[-1]), now(first_begun)
    *came, first_begun = lax.optimization_barrier((*came, first_begun))
    parts = [(came[p], near_values[p], near_act[p]) for p in range(pairs - 1)]
    half = width // 2
    pitch = half + layers + 1
    for layer in range(layers):
        last = layer == layers - 1
        rows_left = 2 * rows + layers - 1 - layer
        results = [None] * pairs
        for p in reversed(range(pairs)):
            builds = layer == 0 and p > 0
            earlier = (halo,) if p == 0 else parts[p - 1] if builds else (shifted[p - 1],)
            begun = ()
            if builds and p == pairs - 1:
                begun = (first_begun,)
            elif layer == 0 and p == 0 and next_begun is not None:
                begun = (next_begun,)
            elif layer == 1 and p == pairs - 1 and layer_begun is not None:
                begun = (layer_begun,)
            elif builds or (p == 0 and (last or layer == 0)):
                begun = (begin(chain, shifted[p], weight[layer]),)
            if last and p == 0:
                chain.run("convs")
            plan = {
                "layer": layer,
                "begun": len(begun) > 0,
                "rows_near": 2 * rows,
                "last": last,
                "sends": p == pairs - 1 and not last,
                "received": p == 0,
                "builds": builds,
                "inputs": len(earlier),
                "pitch": pitch,
                "half": half,
                "rows": rows_left,
            }
            outs = list(conv(chain, plan, begun, earlier, shifted[p], values[p], weight[layer], columns))
            if builds:
                shifted[p - 1], values[p - 1] = outs.pop(), outs.pop()
            results[p] = outs
            if layer == 0 and p == 0:
                chain.run("convs")
            if plan["sends"]:
                if layer == 0 and p == 1:
                    next_begun = begin(chain, shifted[0], weight[0])
                chain.run("convs")
                arriving = earlier_of(now(outs[2]))
                if layer == 0 and p == 1:
                    layer_begun = begin(chain, outs[1], weight[1])
                    chain.run("begin")
                    halo, layer_begun = lax.optimization_barrier((halo, now(layer_begun)))
        values, shifted = [r[0] for r in results], [r[1] for r in results]
        if not last:
            halo = arriving
    chain.run("convs")
    result = ()
    for p in reversed(range(pairs)):
        result = (join(p, now(values[p]), mate_of(now(shifted[p])), latents.shape, *result),)
    return result[0]


def solution(mesh):
    in_specs = (P(("clips", "tm"), "rows", None, None), P(), P(), P())
    out_specs = P(("clips", "tm"), "rows", None, None)
    return jax.shard_map(on_device, mesh=mesh, in_specs=in_specs, out_specs=out_specs, check_vma=False)
```

```python
import functools

import jax
import jax.numpy as jnp
from jax import lax
from jax.experimental import pallas as pl
from jax.experimental.pallas import tpu as pltpu
from jax.sharding import PartitionSpec as P

EPSILON = 1e-06
PAIR = 2
LANES = 128
TILE = 256
VMEM = pl.BlockSpec(memory_space=pltpu.VMEM)
ANY = pl.BlockSpec(memory_space=pl.ANY)
LIMIT = 24 * 1024 * 1024
LARGE = 44 * 1024 * 1024


def place():
    strip = lax.axis_index("rows").astype(jnp.int32)
    core, group = strip & 1, strip >> 1
    return core, group, core == group


def rounded(lanes):
    return -(-lanes // LANES) * LANES


def column(row):
    return jnp.transpose(jnp.broadcast_to(row, (LANES, row.shape[1])))


def lane_of(lanes):
    return lax.broadcasted_iota(jnp.int32, (1, lanes), 1)


def filled(lanes, pitch):
    lane = lane_of(lanes)
    gaps = lane < 0
    for end in range(pitch - 1, lanes, pitch):
        gaps = gaps | (lane == end)
    return jnp.where(gaps, 0.0, 1.0)


def activated(values, gain, mask):
    squares = jnp.mean(values * values, axis=0, keepdims=True)
    halved = values * (lax.rsqrt(squares + EPSILON) * (0.5 * mask)) * gain
    return (halved + halved * jnp.tanh(halved)).astype(jnp.bfloat16)


def weights_kernel(w_ref, rows_ref, *refs):
    outs, columns_ref, held_ref, sems = refs[:-3], refs[-3], refs[-2], refs[-1]
    layers, taps, channels_out, ins = w_ref.shape
    step = taps // 3
    places = [(layer, time_tap) for layer in range(layers) for time_tap in range(3)]
    copies = []
    for n, (layer, time_tap) in enumerate(places):
        part = pl.ds(step * time_tap, step)
        copies.append(pltpu.make_async_copy(w_ref.at[layer, part], held_ref.at[n], sems.at[n]))
        copies[-1].start()
    _, flipped, _ = place()
    for layer in range(layers):
        columns_ref[layer, 0] = column(rows_ref[layer : layer + 1, :])
        columns_ref[layer, 1] = column(rows_ref[layers + layer : layers + layer + 1, :])
    for n, (layer, time_tap) in enumerate(places):
        copies[n].wait()
        for row_tap in range(3):
            source = 3 * (row_tap + flipped * (2 - 2 * row_tap))
            at = (3 * (2 - time_tap) + row_tap) * ins
            outs[layer][:, at : at + ins] = held_ref[n, pl.ds(source, 3)].reshape(3 * channels_out, ins)


def weights(conv_weight, rows):
    layers, taps, outs, ins = conv_weight.shape
    one = jax.ShapeDtypeStruct((3 * outs, 9 * ins), conv_weight.dtype)
    results = pl.pallas_call(
        weights_kernel,
        out_shape=(one,) * layers + (jax.ShapeDtypeStruct((layers, 2, outs, LANES), jnp.float32),),
        in_specs=[ANY, VMEM],
        out_specs=(VMEM,) * (layers + 1),
        scratch_shapes=[
            pltpu.VMEM((3 * layers, taps // 3, outs, ins), conv_weight.dtype),
            pltpu.SemaphoreType.DMA((3 * layers,)),
        ],
        compiler_params=pltpu.CompilerParams(vmem_limit_bytes=LARGE),
        cost_estimate=pl.CostEstimate(flops=0, bytes_accessed=4 * conv_weight.size, transcendentals=0),
        name="weights",
    )(conv_weight, rows)
    return results[:-1], results[-1]


def split_kernel(in_ref, *out_refs):
    for p, out_ref in enumerate(out_refs):
        out_ref[...] = in_ref[PAIR * p : PAIR * (p + 1)]


def split(latents):
    pairs = latents.shape[0] // PAIR
    return pl.pallas_call(
        split_kernel,
        out_shape=(jax.ShapeDtypeStruct((PAIR,) + latents.shape[1:], latents.dtype),) * pairs,
        in_specs=[VMEM],
        out_specs=(VMEM,) * pairs,
        compiler_params=pltpu.CompilerParams(vmem_limit_bytes=LIMIT),
        name="split",
    )(latents)


def folds(channels, rest):
    fits = [n for n in (4, 3, 2) if n * rest <= LANES and channels % (16 * n) == 0]
    return fits[0] if fits else 1


def message_shape(channels, valid):
    whole, rest = divmod(PAIR * valid, LANES)
    lines = whole * channels + (channels // folds(channels, rest) if rest else 0)
    return jax.ShapeDtypeStruct((lines, LANES), jnp.bfloat16)


def write_message(ref, acts, valid):
    channels, width = acts[0].shape
    whole, rest = divmod(PAIR * valid, LANES)
    total = rounded(PAIR * valid)
    if total > width:
        acts = [jnp.concatenate([act, jnp.zeros((channels, total - width), jnp.bfloat16)], axis=1) for act in acts]
    first, second = acts[0], pltpu.roll(acts[1], valid, 1)
    lane = lane_of(LANES)
    for n in range(total // LANES):
        at = slice(n * LANES, (n + 1) * LANES)
        block = first[:, at] if at.stop <= valid else second[:, at]
        if at.start < valid < at.stop:
            mixed = jnp.where(lane < valid - at.start, first[:, at].astype(jnp.float32), second[:, at].astype(jnp.float32))
            block = mixed.astype(jnp.bfloat16)
        if n < whole:
            ref[n * channels : (n + 1) * channels] = block
            continue
        parts = folds(channels, rest)
        size, step = channels // parts, LANES // parts
        kept = jnp.where(lane < rest, block.astype(jnp.float32), 0.0)
        pieces = [kept[i * size : (i + 1) * size] for i in range(parts)]
        ref[n * channels :] = sum(
            piece if i == 0 else pltpu.roll(piece, i * step, 1) for i, piece in enumerate(pieces)
        ).astype(jnp.bfloat16)


def read_message(ref, channels, width, valid):
    whole, rest = divmod(PAIR * valid, LANES)
    blocks = [ref[n * channels : (n + 1) * channels] for n in range(whole)]
    if rest:
        parts = folds(channels, rest)
        folded = ref[whole * channels :]
        pieces = [folded if i == 0 else pltpu.roll(folded, LANES - i * (LANES // parts), 1) for i in range(parts)]
        blocks.append(pieces[0] if parts == 1 else jnp.concatenate(pieces, axis=0))
    both = jnp.concatenate(blocks, axis=1)
    return both[:, :width], pltpu.roll(both, both.shape[1] - valid, 1)[:, :width]


def spread(out_ref, index, act, pitch):
    lanes = out_ref.shape[3]
    above = pltpu.roll(act, pitch, 1)
    below = pltpu.roll(act, act.shape[1] - pitch, 1)
    edge = jnp.where(lane_of(LANES) < pitch, 0.0, above[:, :LANES].astype(jnp.float32))
    out_ref[index, 0, :, :LANES] = edge.astype(jnp.bfloat16)
    out_ref[index, 0, :, LANES:] = above[:, LANES:lanes]
    out_ref[index, 1] = act[:, :lanes]
    out_ref[index, 2] = below[:, :lanes]


def placed(blocks, core, row, window, line):
    pitch, width = window + 1, line.shape[1]
    lane = lane_of(LANES)
    block, low = divmod(row * pitch, LANES)
    shift = lax.rem(low + LANES - core * (width - window), LANES)
    turned = moved(line, shift)
    here = (lane >= low) & (lane < low + window)
    blocks[block] = blocks.get(block, 0.0) + jnp.where(here, turned, 0.0)
    if low + window > LANES:
        blocks[block + 1] = blocks.get(block + 1, 0.0) + jnp.where(lane < low + window - LANES, turned, 0.0)


def near_kernel(halo, pairs, mate_ref, gains_ref, *refs):
    own_refs, value_refs, act_refs = refs[:pairs], refs[pairs : 2 * pairs], refs[2 * pairs : 3 * pairs]
    send_refs = refs[3 * pairs :]
    frames, rows, _, width = mate_ref.shape
    window = width // 2 + halo
    core, group, outer = place()
    gain = column(gains_ref[0:1, :])
    done = act_refs[0].shape[2]
    mask = filled(done, window + 1)
    for f in range(frames):
        p, t = divmod(f, PAIR)
        blocks, sent = {}, {}
        for row in range(2 * rows):
            at = row % rows
            index = at + group * (rows - 1 - 2 * at)
            own, mate = own_refs[p][t, index], mate_ref[f, index]
            one, two = (own, mate) if row < rows else (mate, own)
            line = jnp.where(outer, one, two)
            placed(blocks, core, row, window, line)
            there = 4 * rows - 1 - row
            if p < pairs - 1 and there < 2 * rows + halo:
                placed(sent, core, there, window, line)
        for b in sent:
            send_refs[p][t, :, b * LANES - done : (b + 1) * LANES - done] = sent[b].astype(jnp.bfloat16)
        for b in blocks:
            part = slice(b * LANES, (b + 1) * LANES)
            value_refs[p][t, :, part] = blocks[b].astype(jnp.bfloat16)
            if part.stop <= done:
                act_refs[p][t, :, part] = activated(blocks[b], gain, mask[:, part])


def near(halo, mate, gains, own):
    frames, rows, channels, width = mate.shape
    pitch = width // 2 + halo + 1
    lanes = 2 * rows * pitch
    done = lanes // LANES * LANES
    pairs = len(own)
    sent = jax.ShapeDtypeStruct((PAIR, channels, rounded(lanes + halo * pitch) - done), jnp.bfloat16)
    outs = pl.pallas_call(
        functools.partial(near_kernel, halo, pairs),
        out_shape=(jax.ShapeDtypeStruct((PAIR, channels, rounded(lanes)), jnp.bfloat16),) * pairs
        + (jax.ShapeDtypeStruct((PAIR, channels, done), jnp.bfloat16),) * pairs
        + (sent,) * (pairs - 1),
        in_specs=[VMEM] * (2 + pairs),
        out_specs=(VMEM,) * (3 * pairs - 1),
        compiler_params=pltpu.CompilerParams(vmem_limit_bytes=LIMIT),
        cost_estimate=pl.CostEstimate(flops=40 * mate.size, bytes_accessed=8 * mate.size, transcendentals=2 * mate.size),
        name="near",
    )(mate, gains, *own)
    return outs[:pairs], outs[pairs : 2 * pairs], outs[2 * pairs :]


def far_blocks(halo, far_ref, mate_ref, t, blocks):
    _, rows, _, width = far_ref.shape
    core, group, outer = place()
    for row in range(2 * rows, 2 * rows + halo):
        local = 4 * rows - 1 - row
        at = local % rows
        index = at + (1 - group) * (rows - 1 - 2 * at)
        one, two = (mate_ref, far_ref) if local < rows else (far_ref, mate_ref)
        line = jnp.where(outer, one[t, index], two[t, index])
        placed(blocks, core, row, width // 2 + halo, line)


def add_far(pitch, valid, add, near_ref, act_ref, columns_ref, values_ref, shifted_ref, send_ref=None):
    lanes, done = values_ref.shape[2], act_ref.shape[2]
    mask = filled(lanes, pitch)
    whole_acts = []
    for t in range(PAIR):
        values_ref[t, :, :done] = near_ref[t, :, :done]
        acts = [act_ref[t]]
        blocks = {done // LANES: near_ref[t, :, done:].astype(jnp.float32)}
        add(t, blocks)
        for b in sorted(blocks):
            part = slice(b * LANES, (b + 1) * LANES)
            values_ref[t, :, part] = blocks[b].astype(jnp.bfloat16)
            acts.append(activated(blocks[b], columns_ref[0, 0], mask[:, part]))
        act = jnp.concatenate(acts, axis=1)
        if send_ref is None:
            spread(shifted_ref, t, act, pitch)
        else:
            shifted_ref[t] = act
        whole_acts.append(act)
    if send_ref is not None:
        write_message(send_ref, whole_acts, valid)


def far_shapes(rows, halo, channels, half):
    pitch = half + halo + 1
    return (
        jax.ShapeDtypeStruct((PAIR, channels, rounded((2 * rows + halo) * pitch)), jnp.bfloat16),
        jax.ShapeDtypeStruct((PAIR, 3, channels, rounded((2 * rows + halo - 1) * pitch)), jnp.bfloat16),
    )


def beyond(halo, columns, *parts):
    far = parts[0]
    _, rows, channels, width = far.shape
    values, _ = far_shapes(rows, halo, channels, width // 2)
    pitch = width // 2 + halo + 1
    valid = (2 * rows + halo) * pitch

    def kernel(columns_ref, far_ref, mate_ref, near_ref, act_ref, *outs):
        add = functools.partial(far_blocks, halo, far_ref, mate_ref)
        add_far(pitch, valid, add, near_ref, act_ref, columns_ref, *outs)

    return pl.pallas_call(
        kernel,
        out_shape=(values, values, message_shape(channels, valid)),
        in_specs=[VMEM] * 5,
        out_specs=(VMEM,) * 3,
        compiler_params=pltpu.CompilerParams(vmem_limit_bytes=LIMIT),
        cost_estimate=pl.CostEstimate(flops=40 * far.size, bytes_accessed=8 * far.size, transcendentals=2 * far.size),
        name="beyond",
    )(columns, *parts)


def by_taps(sums):
    channels, lanes = sums.shape[0] // 3, sums.shape[1]
    return [
        [sums[tap * channels : (tap + 1) * channels, at : at + LANES] for at in range(0, lanes, LANES)]
        for tap in range(3)
    ]


def moved(block, shift):
    return pltpu.roll(block, shift, 1).astype(jnp.float32)


def column_sums(taps):
    lane = lane_of(LANES)
    left, middle, right = taps
    lefts = [pltpu.roll(block, 1, 1) for block in left]
    rights = [pltpu.roll(block, LANES - 1, 1) for block in right] + [0.0]
    return [
        jnp.where(lane == 0, lefts[b - 1] if b else 0.0, lefts[b])
        + middle[b]
        + jnp.where(lane == LANES - 1, rights[b + 1], rights[b])
        for b in range(len(middle))
    ]


def begun_rows(t, channels):
    return (t + 1) * 3 * channels // TILE * TILE


def rows_between(lines, start, stop):
    taken, at = [], 0
    for part in lines:
        low, high = max(start - at, 0), min(stop - at, part.shape[0])
        if low < high:
            taken.append(part[low:high])
        at += part.shape[0]
    return jnp.concatenate(taken, axis=0)


def block_lines(ref, frame, b):
    return ref[frame, :, :, b * LANES : (b + 1) * LANES].reshape(3 * ref.shape[2], LANES)


def padded_rows(lines, start, stop, low, high):
    parts = [rows_between(lines, start, stop)]
    if low < start:
        parts.insert(0, jnp.zeros((start - low, LANES), jnp.bfloat16))
    if stop < high:
        parts.append(jnp.zeros((high - stop, LANES), jnp.bfloat16))
    return parts[0] if len(parts) == 1 else jnp.concatenate(parts, axis=0)


def tiled(lanes):
    places = [(t, b) for t in range(PAIR) for b in range(lanes // LANES)]
    side = TILE // LANES
    return [places[n : n + side] for n in range(0, len(places), side)]


def by_frames(lanes, tile_sums, finish):
    taps = {t: [[], [], []] for t in range(PAIR)}
    for places in tiled(lanes):
        sums = by_taps(tile_sums(places))
        for i, (t, b) in enumerate(places):
            for tap in range(3):
                taps[t][tap].append(sums[tap][i])
        for t, b in places:
            if b == lanes // LANES - 1:
                finish(t, taps[t])


def begin_kernel(shifted_ref, w_ref, out_ref):
    _, _, channels, lanes = shifted_ref.shape

    def tile_sums(places):
        depth = max(begun_rows(t, channels) for t, _ in places)
        rhs = [
            padded_rows(
                [block_lines(shifted_ref, j, b) for j in range(t, -1, -1)],
                0,
                begun_rows(t, channels),
                0,
                depth,
            )
            for t, b in places
        ]
        return jnp.dot(w_ref[:, :depth], jnp.concatenate(rhs, axis=1), preferred_element_type=jnp.float32)

    def finish(t, taps):
        for b, block in enumerate(column_sums(taps)):
            out_ref[t, :, b * LANES : (b + 1) * LANES] = block

    by_frames(lanes, tile_sums, finish)


class Later:
    def __init__(self, shape):
        self.shape, self.dtype, self.value = shape.shape, shape.dtype, None


def now(x):
    return x.value if isinstance(x, Later) else x


class Chain:
    def __init__(self):
        self.steps = []

    def add(self, kernel, inputs, out_shape, scratch, flops):
        outs = [Later(shape) for shape in out_shape]
        self.steps.append((kernel, inputs, outs, out_shape, scratch, flops))
        return outs

    def run(self, name):
        steps, self.steps = self.steps, []
        made = {id(out): n for n, out in enumerate(out for step in steps for out in step[2])}
        arrays = []
        for step in steps:
            for x in step[1]:
                if id(x) not in made and not any(now(x) is y for y in arrays):
                    arrays.append(now(x))
        at = [[("out", made[id(x)]) if id(x) in made else ("in", next(i for i, y in enumerate(arrays) if y is now(x))) for x in step[1]] for step in steps]
        out_shape = [shape for step in steps for shape in step[3]]
        scratch = [shape for step in steps for shape in step[4]]

        def kernel(*refs):
            ins, outs, rest = refs[: len(arrays)], refs[len(arrays) : len(arrays) + len(out_shape)], refs[len(arrays) + len(out_shape) :]
            first, held = 0, 0
            for step, places in zip(steps, at):
                own, kept = outs[first : first + len(step[3])], rest[held : held + len(step[4])]
                first, held = first + len(own), held + len(kept)
                step[0](*[(outs if kind == "out" else ins)[n] for kind, n in places], *own, *kept)

        results = pl.pallas_call(
            kernel,
            out_shape=tuple(out_shape),
            in_specs=[VMEM] * len(arrays),
            out_specs=(VMEM,) * len(out_shape),
            scratch_shapes=scratch,
            compiler_params=pltpu.CompilerParams(vmem_limit_bytes=LIMIT),
            cost_estimate=pl.CostEstimate(flops=sum(step[5] for step in steps), bytes_accessed=0, transcendentals=0),
            name=name,
        )(*arrays)
        for out, value in zip((out for step in steps for out in step[2]), results):
            out.value = value


def spread_kernel(pitch, act_ref, shifted_ref):
    for t in range(PAIR):
        spread(shifted_ref, t, act_ref[t], pitch)


def begin(chain, shifted, weight):
    _, _, channels, lanes = shifted.shape
    out = jax.ShapeDtypeStruct((PAIR, channels, lanes), jnp.float32)
    return chain.add(begin_kernel, [shifted, weight], [out], [], 0)[0]


def conv_kernel(plan, shifted_ref, values_ref, w_ref, columns_ref, *refs):
    layer, pitch, half, received = plan["layer"], plan["pitch"], plan["half"], plan["received"]
    last, sends = plan["last"], plan["sends"]
    refs = list(refs)
    begun_ref = refs.pop(0) if plan["begun"] else None
    earlier_refs = [refs.pop(0) for _ in range(plan["inputs"])]
    earlier_ref = refs.pop() if received else earlier_refs[0]
    if received:
        frames = read_message(earlier_refs[0], values_ref.shape[1], values_ref.shape[2], (plan["rows"] + 1) * pitch)
        for t in range(PAIR):
            spread(earlier_ref, t, frames[t], pitch)
    outs = refs
    if plan["builds"]:
        earlier_ref = outs.pop()
        came_ref, near_ref, act_ref = earlier_refs
        done = act_ref.shape[2]

        def add(t, blocks):
            for at in range(0, came_ref.shape[2], LANES):
                b = (done + at) // LANES
                blocks[b] = blocks.get(b, 0.0) + came_ref[t, :, at : at + LANES].astype(jnp.float32)

        add_far(pitch, 0, add, near_ref, act_ref, columns_ref, outs.pop(), earlier_ref)
    _, _, channels, lanes = shifted_ref.shape
    chunks = lanes // LANES
    lane = lane_of(LANES)

    bias = columns_ref[layer, 1]
    whole_acts = []
    if not last:
        mask = filled(lanes, pitch)
        gain = columns_ref[layer + 1, 0]

    def finish(t, taps):
        totals, acts = [], []
        for b, conv in enumerate(column_sums(taps)):
            at = slice(b * LANES, (b + 1) * LANES)
            if begun_ref is not None:
                conv = conv + begun_ref[t, :, at]
            total = (values_ref[t, :, at].astype(jnp.float32) + conv + bias).astype(jnp.bfloat16)
            totals.append(total)
            if last:
                continue
            outs[0][t, :, at] = total
            acts.append(activated(total.astype(jnp.float32), gain, mask[:, at]))
        if not last:
            whole_acts.append(jnp.concatenate(acts, axis=1))
            spread(outs[1], t, whole_acts[-1], pitch)
            return
        core, _, outer = place()
        skipped = core * (pitch - 1 - half)

        def columns_of(row, to):
            b, low = divmod(row * pitch, LANES)
            shift = lax.rem(to + 2 * LANES - low - skipped, LANES)
            turned = moved(totals[b], shift)
            if low + pitch - 1 <= LANES:
                return turned
            return jnp.where(lane < to + LANES - low - skipped, turned, moved(totals[b + 1], shift))

        def rows_of(row):
            return jnp.where(lane < half, columns_of(row, 0), columns_of(row + 1, half))

        outermost, inner = rows_of(0), rows_of(2)
        outs[0][t] = jnp.where(outer, outermost, inner).astype(jnp.bfloat16)
        outs[1][t] = jnp.where(outer, inner, outermost).astype(jnp.bfloat16)

    def tile_sums(places):
        cuts = {t: begun_rows(t, channels) if plan["begun"] else 0 for t, _ in places}
        start, stop = min(cuts.values()), w_ref.shape[1]
        rhs = []
        for t, b in places:
            frames = [(earlier_ref, t + a) if t + a < PAIR else (shifted_ref, t + a - PAIR) for a in (2, 1, 0)]
            rhs.append(padded_rows([block_lines(ref, j, b) for ref, j in frames], cuts[t], stop, start, stop))
        return jnp.dot(w_ref[:, start:], jnp.concatenate(rhs, axis=1), preferred_element_type=jnp.float32)

    by_frames(lanes, tile_sums, finish)
    if sends:
        write_message(outs[2], whole_acts, plan["rows"] * pitch)


def conv(chain, plan, begun, earlier, shifted, values, weight, columns):
    _, _, channels, lanes = shifted.shape
    pitch, half, received = plan["pitch"], plan["half"], plan["received"]
    if plan["last"]:
        out_shape = (jax.ShapeDtypeStruct((PAIR, channels, LANES), jnp.bfloat16),) * 2
    else:
        out_shape = (
            jax.ShapeDtypeStruct((PAIR, channels, lanes), jnp.bfloat16),
            jax.ShapeDtypeStruct((PAIR, 3, channels, rounded((plan["rows"] - 1) * pitch)), jnp.bfloat16),
        )
        if plan["sends"]:
            out_shape += (message_shape(channels, plan["rows"] * pitch),)
    if plan["builds"]:
        out_shape += far_shapes(plan["rows_near"] // 2, pitch - 1 - half, channels, half)
    return chain.add(
        functools.partial(conv_kernel, plan),
        [shifted, values, weight, columns, *begun, *earlier],
        out_shape,
        [pltpu.VMEM((PAIR, 3, channels, lanes), jnp.bfloat16)] * received,
        54 * channels * channels * PAIR * lanes * (1 + plan["builds"]),
    )


def join_kernel(pair, kept_ref, got_ref, *refs):
    out_ref, lines_ref, sems = refs[-3:]
    _, rows, _, width = lines_ref.shape
    half = width // 2
    core, group, _ = place()
    first = core == 0
    left_half = lane_of(width) < half
    copies = []
    for t in range(PAIR):
        mine, theirs = kept_ref[t].astype(jnp.float32), got_ref[t].astype(jnp.float32)
        left, right = jnp.where(first, mine, theirs), jnp.where(first, theirs, mine)
        lines = (
            jnp.where(left_half, left, pltpu.roll(right, half, 1)),
            jnp.where(left_half, pltpu.roll(left, half, 1), right),
        )
        for j in range(rows):
            lines_ref[t, j + group * (rows - 1 - 2 * j)] = lines[j].astype(jnp.bfloat16)
        copies.append(pltpu.make_async_copy(lines_ref.at[t], out_ref.at[PAIR * pair + t], sems.at[t]))
        copies[-1].start()
    for copy in copies:
        copy.wait()


def join(pair, kept, got, shape, *so_far):
    return pl.pallas_call(
        functools.partial(join_kernel, pair),
        out_shape=jax.ShapeDtypeStruct(shape, jnp.bfloat16),
        in_specs=[VMEM, VMEM] + [ANY] * len(so_far),
        out_specs=ANY,
        scratch_shapes=[pltpu.VMEM((PAIR,) + shape[1:], jnp.bfloat16), pltpu.SemaphoreType.DMA((PAIR,))],
        input_output_aliases={2: 0} if so_far else {},
        compiler_params=pltpu.CompilerParams(vmem_limit_bytes=LIMIT),
        name="join",
    )(kept, got, *so_far)


def on_device(latents, conv_weight, norm_gains, biases):
    layers = conv_weight.shape[0]
    frames, rows, channels, width = latents.shape
    strips, blocks = lax.axis_size("rows"), lax.axis_size("tm")
    assert strips == 4 and rows == 2 and frames % PAIR == 0 and width == LANES

    def mate_of(block):
        return lax.ppermute(block, "rows", [(i, i ^ 1) for i in range(strips)])

    def earlier_of(block):
        return lax.ppermute(block, "tm", [(i, i + 1) for i in range(blocks - 1)])

    def beyond_of(block):
        return lax.ppermute(block, "rows", [(i, i ^ 2) for i in range(strips)])

    pairs = frames // PAIR
    own = split(latents)
    far = beyond_of(own[-1])
    whole, *own = lax.optimization_barrier((latents, *own))
    mate = mate_of(whole)
    row_values = jnp.concatenate([norm_gains, biases], axis=0)
    weight, columns = weights(conv_weight, row_values)
    near_values, near_act, near_sent = near(layers, mate, row_values, own)
    came = [beyond_of(block) for block in near_sent]
    far, weight, columns, near_values, near_act = lax.optimization_barrier(
        (far, weight, columns, near_values, near_act)
    )
    values, shifted = [None] * pairs, [None] * pairs
    values[-1], last_act, send = beyond(layers, columns, far, mate_of(far), near_values[-1], near_act[-1])
    halo = earlier_of(send)
    next_begun = layer_begun = None
    chain = Chain()
    shift_shape = far_shapes(rows, layers, channels, width // 2)[1]
    spread_last = functools.partial(spread_kernel, width // 2 + layers + 1)
    shifted[-1] = chain.add(spread_last, [last_act], [shift_shape], [], 0)[0]
    first_begun = begin(chain, shifted[-1], weight[0])
    chain.run("begin")
    shifted[-1], first_begun = now(shifted[-1]), now(first_begun)
    *came, first_begun = lax.optimization_barrier((*came, first_begun))
    parts = [(came[p], near_values[p], near_act[p]) for p in range(pairs - 1)]
    half = width // 2
    pitch = half + layers + 1
    for layer in range(layers):
        last = layer == layers - 1
        rows_left = 2 * rows + layers - 1 - layer
        results = [None] * pairs
        for p in reversed(range(pairs)):
            builds = layer == 0 and p > 0
            earlier = (halo,) if p == 0 else parts[p - 1] if builds else (shifted[p - 1],)
            begun = ()
            if builds and p == pairs - 1:
                begun = (first_begun,)
            elif layer == 0 and p == 0 and next_begun is not None:
                begun = (next_begun,)
            elif layer == 1 and p == pairs - 1 and layer_begun is not None:
                begun = (layer_begun,)
            elif builds or (p == 0 and (last or layer == 0)):
                begun = (begin(chain, shifted[p], weight[layer]),)
            if last and p == 0:
                chain.run("convs")
            plan = {
                "layer": layer,
                "begun": len(begun) > 0,
                "rows_near": 2 * rows,
                "last": last,
                "sends": p == pairs - 1 and not last,
                "received": p == 0,
                "builds": builds,
                "inputs": len(earlier),
                "pitch": pitch,
                "half": half,
                "rows": rows_left,
            }
            outs = list(conv(chain, plan, begun, earlier, shifted[p], values[p], weight[layer], columns))
            if builds:
                shifted[p - 1], values[p - 1] = outs.pop(), outs.pop()
            results[p] = outs
            if layer == 0 and p == 0:
                chain.run("convs")
            if plan["sends"]:
                if layer == 0 and p == 1:
                    next_begun = begin(chain, shifted[0], weight[0])
                chain.run("convs")
                arriving = earlier_of(now(outs[2]))
                if layer == 0 and p == 1:
                    layer_begun = begin(chain, outs[1], weight[1])
                    chain.run("begin")
                    halo, layer_begun = lax.optimization_barrier((halo, now(layer_begun)))
        values, shifted = [r[0] for r in results], [r[1] for r in results]
        if not last:
            halo = arriving
    chain.run("convs")
    result = ()
    for p in reversed(range(pairs)):
        result = (join(p, now(values[p]), mate_of(now(shifted[p])), latents.shape, *result),)
    return result[0]


def solution(mesh):
    in_specs = (P(("clips", "tm"), "rows", None, None), P(), P(), P())
    out_specs = P(("clips", "tm"), "rows", None, None)
    return jax.shard_map(on_device, mesh=mesh, in_specs=in_specs, out_specs=out_specs, check_vma=False)
```
